32 devices in a mesh: scen: 2 (over x), row: 8 (over z, y), col: 2 (over core).
Axes of the slice: x: 2, y: 2, z: 4, core: 2. Of those that a mesh axis runs over, the one named last changes fastest.
Arguments:
- slip_deficit: float32 [4096, 512], P(('row', 'col'), 'scen'), parts along dimension 1, may hold values from -6 to 6
- state_var: float32 [4096, 512], P(('row', 'col'), 'scen'), parts along dimension 1, may hold values from -0.5 to 0.5
- tau_load: float32 [4096, 512], P(('row', 'col'), 'scen'), parts along dimension 1, may hold values from -4 to 4
- sigma_base: float32 [4096], P(('row', 'col')), may hold values from 1 to 3
- a_coef: float32 [4096], P(('row', 'col')), may hold values from 0.5 to 1
- b_coef: float32 [4096], P(('row', 'col')), may hold values from 0.5 to 1
- v_basis: bfloat16 [16, 16, 32, 256], P('row', 'col'), may hold values from -0.375 to 0.375
- u_basis: bfloat16 [2, 16, 16, 32, 256], P(None, 'row', 'col'), may hold values from -0.25 to 0.25
- dense_blocks: bfloat16 [2, 16, 4, 256, 256], P(None, 'row', 'col'), may hold values from -0.25 to 0.25
- block_ranks: int32 [16, 16], P('row', 'col'), may hold values from 0 to 32, as said below
- near_index: int32 [16, 4], P('row', 'col'), may hold values from 0 to 15, as said below
Outputs:
- mean_rate: float32 [4096, 512], P(('row', 'col'), 'scen'), parts along dimension 1
- mean_change: float32 [4096, 512], P(('row', 'col'), 'scen'), parts along dimension 1
The draws below stay inside these ranges and needn't reach their ends.
There are 2 independent parts, one for each index of `scen`. The reference program is written for one: setup_inputs(seed, part) draws one part's arguments, and reference() takes and returns one part's arrays. A program takes and returns all parts, laid end to end along the dimension named above; an argument that names none is the same for every part. Nothing has to cross between parts.
Inputs may be any that keep to these rules, and one draw needn't show every extreme that they name: `near_index`: row p names 4 different column blocks; entries j * 2 to (j + 1) * 2 - 1 lie in column tile j, from j * 8 to (j + 1) * 8 - 1; the column block that holds element block p is among them. `block_ranks`: 0 exactly on the blocks that near_index names for that row; every other block has a rank of 8 or more.
All inputs are finite; a program needn't handle non-finite values.
Results may differ from the reference program's by a relative error of at most 0.0041.
Values may be sent and summed in bfloat16 or wider, within the bound.
No kernel may reach another device: no remote copies, remote signals or barrier semaphores. Data moves between devices by JAX's collectives and lax.ppermute only.
A program may use at most 128 MiB of HBM per device.

```python
import jax
import jax.numpy as jnp
from jax import lax

BLOCK = 256
RANK = 32
SLOTS = 2
NEWTON = 2
ENS = 256
TILE_BLOCKS = 8
COL_TILES = 2
NBLK = 16
NEAR = 4
ELEMS = 4096


def pick_near(key):
    shape = (NBLK, COL_TILES, TILE_BLOCKS)
    scores = jax.random.randint(key, shape, 0, 1 << 20)
    tile_pos = lax.broadcasted_iota(jnp.int32, shape, 2)
    row_pos = lax.broadcasted_iota(jnp.int32, shape, 0)
    part_pos = lax.broadcasted_iota(jnp.int32, shape, 1)
    own_block = (part_pos == row_pos % COL_TILES) & (tile_pos == row_pos // COL_TILES)
    scores = jnp.where(own_block, -1, scores * TILE_BLOCKS + tile_pos)
    order = jnp.argsort(scores, axis=2)[:, :, :SLOTS].astype(jnp.int32)
    near = part_pos[:, :, :SLOTS] * TILE_BLOCKS + order
    return near.reshape(NBLK, COL_TILES * SLOTS).astype(jnp.int32)


def draw_near_index(key, part):
    return pick_near(key)


def draw_block_ranks(key, part):
    near = pick_near(key)
    key = jax.random.fold_in(key, 7)
    ranks = jax.random.randint(key, (NBLK, NBLK), RANK // 4, RANK + 1).astype(jnp.int32)
    column_pos = lax.broadcasted_iota(jnp.int32, (NBLK, NEAR, NBLK), 2)
    is_near = jnp.any(near[:, :, None] == column_pos, axis=1)
    return jnp.where(is_near, 0, ranks).astype(jnp.int32)


def level_of(rng, dims, pieces, least, high):
    factor_of, own = 1.0, jax.random.fold_in(rng, 6)
    for axis_at, blocks in pieces:
        draws = jnp.exp(jax.random.uniform(jax.random.fold_in(own, axis_at), (blocks,), jnp.float32, least / len(pieces), high / len(pieces)))
        factor_of = factor_of * jnp.repeat(draws, dims[axis_at] // blocks).reshape([-1 if axis == axis_at else 1 for axis in range(len(dims))])
    return factor_of


def bell_draw(stream_key, shape, spread, reach, cuts=(), kind=jnp.bfloat16):
    entries = spread * jax.random.normal(stream_key, shape, jnp.float32)
    if cuts:
        entries = entries * level_of(stream_key, shape, cuts, -0.22, 0.18)
    return jnp.clip(entries, -reach, reach).astype(kind)


def setup_inputs(seed: int = 0, part: int = 0) -> dict:
    keys = jax.random.split(jax.random.key(seed), 12)
    part_splits = jax.random.split(jax.random.fold_in(keys[11], part), 12)
    return {
        "slip_deficit": bell_draw(part_splits[0], (ELEMS, ENS), 1.0, 6.0, ((0, 16),), jnp.float32),
        "state_var": jnp.clip(jax.random.uniform(part_splits[1], (ELEMS, ENS), jnp.float32, -0.5, 0.5) * level_of(part_splits[1], (ELEMS, ENS), ((0, 16),), -0.4, 0.0), -0.5, 0.5),
        "tau_load": bell_draw(part_splits[2], (ELEMS, ENS), 1.0, 4.0, ((0, 16),), jnp.float32),
        "sigma_base": jnp.clip(1.0 + 2.0 * jax.random.uniform(keys[3], (ELEMS,), jnp.float32) ** level_of(keys[3], (ELEMS,), ((0, 16),), -0.2, 0.2), 1.0, 3.0),
        "a_coef": jnp.clip(0.5 + 0.5 * jax.random.uniform(keys[4], (ELEMS,), jnp.float32) ** level_of(keys[4], (ELEMS,), ((0, 16),), -0.2, 0.2), 0.5, 1.0),
        "b_coef": jnp.clip(0.5 + 0.5 * jax.random.uniform(keys[5], (ELEMS,), jnp.float32) ** level_of(keys[5], (ELEMS,), ((0, 16),), -0.2, 0.2), 0.5, 1.0),
        "v_basis": bell_draw(keys[6], (NBLK, NBLK, RANK, BLOCK), BLOCK ** -0.5, 0.375, ((0, 8), (1, 2))),
        "u_basis": bell_draw(keys[7], (2, NBLK, NBLK, RANK, BLOCK), (NBLK * RANK) ** -0.5, 0.25, ((1, 8), (2, 2))),
        "dense_blocks": bell_draw(keys[8], (2, NBLK, NEAR, BLOCK, BLOCK), (2 * BLOCK) ** -0.5, 0.25, ((1, 8), (2, 2))),
        "block_ranks": draw_block_ranks(jax.random.fold_in(keys[11], 71), part),
        "near_index": draw_near_index(jax.random.fold_in(keys[11], 71), part),
    }


damping = 0.5
sigma_floor = 0.5
section_step = 0.1

def inverse_sinh(value):
    magnitude = jnp.abs(value)
    result = jnp.log(magnitude + jnp.sqrt(magnitude * magnitude + 1.0))
    return jnp.where(value < 0.0, -result, result)

def lattice_apply(field_half, v_basis, u_basis, dense_blocks, block_ranks, near_index):
    columns = field_half.reshape(TILE_BLOCKS, COL_TILES, BLOCK, ENS).transpose(1, 0, 2, 3).reshape(NBLK, BLOCK, ENS)
    columns_wide = columns.astype(jnp.float32)

    def one_row(row_block):
        v_row = lax.dynamic_index_in_dim(v_basis, row_block, 0, keepdims=False).astype(jnp.float32)
        u_row = lax.dynamic_index_in_dim(u_basis, row_block, 1, keepdims=False).astype(jnp.float32)
        d_row = lax.dynamic_index_in_dim(dense_blocks, row_block, 1, keepdims=False).astype(jnp.float32)
        r_row = lax.dynamic_index_in_dim(block_ranks, row_block, 0, keepdims=False)
        n_row = lax.dynamic_index_in_dim(near_index, row_block, 0, keepdims=False)
        projected = jnp.einsum('qkb,qbe->qke', v_row, columns_wide)
        inside = lax.broadcasted_iota(jnp.int32, (NBLK, RANK), 1) < r_row[:, None]
        projected = jnp.where(inside[:, :, None], projected, 0.0).astype(jnp.bfloat16)
        far_part = jnp.einsum('cqkb,qke->cbe', u_row, projected.astype(jnp.float32))
        picked = columns_wide[n_row.astype(jnp.int32)]
        near_part = jnp.einsum('csab,sbe->cae', d_row, picked)
        return far_part + near_part
    rows_out = lax.map(one_row, jnp.arange(NBLK, dtype=jnp.int32))
    joined = rows_out.transpose(1, 0, 2, 3).reshape(2, ELEMS, ENS)
    return (joined[0], joined[1])

def friction(shear, normal, state, tau_load, sigma_base, a_coef, b_coef):
    a_wide = a_coef[:, None]
    b_wide = b_coef[:, None]
    tau = tau_load + shear
    sigma = jnp.maximum(sigma_base[:, None] + normal, sigma_floor)
    weight = jnp.exp(-state / a_wide)
    first = tau / (sigma * a_wide)
    second = inverse_sinh(tau / (2.0 * damping * weight))
    slope = jnp.where(jnp.abs(first) < jnp.abs(second), first, second)
    for newton_step in range(NEWTON):
        excess = sigma * a_wide * slope + 2.0 * damping * weight * jnp.sinh(slope) - tau
        deriv = sigma * a_wide + 2.0 * damping * weight * jnp.cosh(slope)
        slope = slope - excess / deriv
    rate = 2.0 * weight * jnp.sinh(slope)
    change = b_wide * (jnp.exp(-state / b_wide) - jnp.abs(rate))
    return (rate, change)

def reference(slip_deficit, state_var, tau_load, sigma_base, a_coef, b_coef, v_basis, u_basis, dense_blocks, block_ranks, near_index):
    slip_half = slip_deficit.astype(jnp.bfloat16)
    stress_one, normal_one = lattice_apply(slip_half, v_basis, u_basis, dense_blocks, block_ranks, near_index)
    rate_one, change_one = friction(stress_one, normal_one, state_var, tau_load, sigma_base, a_coef, b_coef)
    rate_half = rate_one.astype(jnp.bfloat16)
    stress_add, normal_add = lattice_apply(rate_half, v_basis, u_basis, dense_blocks, block_ranks, near_index)
    stress_two = stress_one + section_step * stress_add
    normal_two = normal_one + section_step * normal_add
    state_two = state_var + section_step * change_one
    rate_two, change_two = friction(stress_two, normal_two, state_two, tau_load, sigma_base, a_coef, b_coef)
    return ((rate_one + rate_two) * 0.5, (change_one + change_two) * 0.5)
```

```python
import functools

import jax
import jax.numpy as jnp
from jax import lax
from jax.experimental import pallas as pl
from jax.experimental.pallas import tpu as pltpu
from jax.sharding import PartitionSpec as P

NEWTON = 2
RING_LIMIT = 16

damping = 0.5
sigma_floor = 0.5
section_step = 0.1


def ring_rows(count):
    return list(range(0, count, 2)) + list(range(1, count, 2))[::-1]


def ring_gather(block, count):
    me = lax.axis_index("row")
    if count > RING_LIMIT:
        whole = lax.all_gather(block, "row", axis=0)
        return [(jnp.int32(r), [whole[r]]) for r in range(count)]
    ring = ring_rows(count)
    place = [ring.index(r) for r in range(count)]
    up = [(ring[i], ring[(i + 1) % count]) for i in range(count)]
    down = [(ring[(i + 1) % count], ring[i]) for i in range(count)]
    table = jnp.array(ring, jnp.int32)
    my_place = jnp.array(place, jnp.int32)[me]

    def row_at(shift):
        return table[(my_place + shift) % count]

    found = [(row_at(0), [block])]
    from_left = from_right = block
    steps = (count - 1) // 2
    for step in range(1, steps + 1):
        from_left = lax.ppermute(from_left, "row", up)
        from_right = lax.ppermute(from_right, "row", down)
        found.append((row_at(-step), [from_left]))
        found.append((row_at(step), [from_right]))
    if count % 2 == 0:
        half = block.shape[0] // 2
        if steps == 0:
            found.append((row_at(1), [lax.ppermute(block, "row", up)]))
        else:
            top = lax.ppermute(from_left[:half], "row", up)
            low = lax.ppermute(from_right[half:], "row", down)
            found.append((row_at(steps + 1), [top, low]))
    return found


def lattice_kernel(pieces, order_ref, rank_ref, near_ref, pick_ref, *refs):
    total = sum(pieces)
    blocks = refs[:total]
    v_ref, u_ref, d_ref, out_ref, x_all, v_mine, u_mine, d_mine, proj, x_sem, w_sem = refs[total:]
    count, size = x_all.shape[0], x_all.shape[1]
    rank_count = v_mine.shape[1]
    slots = d_mine.shape[1]
    row = pick_ref[0]
    copies = []
    at = 0
    for place, parts in enumerate(pieces):
        tall = size // parts
        for part in range(parts):
            copies.append(
                pltpu.make_async_copy(
                    blocks[at], x_all.at[order_ref[place], pl.ds(part * tall, tall)], x_sem.at[at]
                )
            )
            at += 1
    weights = [
        pltpu.make_async_copy(v_ref.at[row], v_mine, w_sem.at[0]),
        pltpu.make_async_copy(d_ref.at[:, row], d_mine, w_sem.at[1]),
        pltpu.make_async_copy(u_ref.at[:, row], u_mine, w_sem.at[2]),
    ]
    for copy in copies + weights:
        copy.start()
    for copy in copies:
        copy.wait()
    weights[0].wait()
    for q in range(count):
        part = jnp.dot(v_mine[q], x_all[q], preferred_element_type=jnp.float32)
        inside = lax.broadcasted_iota(jnp.int32, part.shape, 0) < rank_ref[row, q]
        proj[pl.ds(q * rank_count, rank_count), :] = jnp.where(inside, part, 0.0).astype(proj.dtype)
    weights[1].wait()
    weights[2].wait()
    picked = [x_all[near_ref[row, s]] for s in range(slots)]
    for kind in range(u_mine.shape[0]):
        u_flat = u_mine[kind].reshape(count * rank_count, size)
        sums = lax.dot_general(
            u_flat, proj[...], (((0,), (0,)), ((), ())), preferred_element_type=jnp.float32
        )
        for s in range(slots):
            sums += jnp.dot(d_mine[kind, s], picked[s], preferred_element_type=jnp.float32)
        out_ref[kind] = sums.astype(out_ref.dtype)


def lattice_row(found, order, ranks, near, row, v_basis, u_basis, dense_blocks, kind):
    pieces = tuple(len(parts) for _, parts in found)
    blocks = [part for _, parts in found for part in parts]
    kinds, _, count, rank_count, size = u_basis.shape
    slots = dense_blocks.shape[2]
    members = blocks[0].shape[1]
    half = blocks[0].dtype
    smem = pl.BlockSpec(memory_space=pltpu.SMEM)
    far = pl.BlockSpec(memory_space=pl.ANY)
    return pl.pallas_call(
        functools.partial(lattice_kernel, pieces),
        out_shape=jax.ShapeDtypeStruct((kinds, size, members), kind),
        in_specs=[smem] * 4 + [far] * (len(blocks) + 3),
        out_specs=pl.BlockSpec(memory_space=pltpu.VMEM),
        scratch_shapes=[
            pltpu.VMEM((count, size, members), half),
            pltpu.VMEM((count, rank_count, size), half),
            pltpu.VMEM((kinds, count, rank_count, size), half),
            pltpu.VMEM((kinds, slots, size, size), half),
            pltpu.VMEM((count * rank_count, members), half),
            pltpu.SemaphoreType.DMA((len(blocks),)),
            pltpu.SemaphoreType.DMA((3,)),
        ],
        compiler_params=pltpu.CompilerParams(vmem_limit_bytes=40 * 1024 * 1024),
        cost_estimate=pl.CostEstimate(
            flops=2 * size * members * (count * rank_count * 3 + kinds * slots * size),
            bytes_accessed=4 * 1024 * 1024,
            transcendentals=0,
        ),
    )(order, ranks, near, row, *blocks, v_basis, u_basis, dense_blocks)


def inverse_sinh(value):
    magnitude = jnp.abs(value)
    result = jnp.log(magnitude + jnp.sqrt(magnitude * magnitude + 1.0))
    return jnp.where(value < 0.0, -result, result)


def sinh_cosh(value):
    grown = jnp.exp(value)
    shrunk = 1.0 / grown
    square = value * value
    small = value * (
        1.0 + square * (1 / 6 + square * (1 / 120 + square * (1 / 5040 + square * (1 / 362880))))
    )
    sinh = jnp.where(square < 1.0, small, 0.5 * (grown - shrunk))
    return sinh, 0.5 * (grown + shrunk)


def friction(shear, normal, state, tau_load, sigma_base, a_wide, b_wide):
    tau = tau_load + shear
    sigma = jnp.maximum(sigma_base + normal, sigma_floor)
    weight = jnp.exp(-state / a_wide)
    stiff = sigma * a_wide
    first = tau / stiff
    second = inverse_sinh(tau / (2.0 * damping * weight))
    slope = jnp.where(jnp.abs(first) < jnp.abs(second), first, second)
    for newton_step in range(NEWTON):
        sinh, cosh = sinh_cosh(slope)
        excess = stiff * slope + 2.0 * damping * weight * sinh - tau
        deriv = stiff + 2.0 * damping * weight * cosh
        slope = slope - excess / deriv
    rate = 2.0 * weight * sinh_cosh(slope)[0]
    change = b_wide * (jnp.exp(-state / b_wide) - jnp.abs(rate))
    return (rate, change)


def section_one_kernel(own, other, state, tau, coef, stress, normal, rate, change, rate_half):
    size, members = state.shape
    step = min(size, 64)

    @pl.loop(0, size // step)
    def _(index):
        rows = pl.ds(pl.multiple_of(index * step, step), step)
        shear = own[0, rows, :] + other[0, rows, :].astype(jnp.float32)
        press = own[1, rows, :] + other[1, rows, :].astype(jnp.float32)
        stress[rows, :] = shear
        normal[rows, :] = press
        first, second = friction(
            shear, press, state[rows, :], tau[rows, :], coef[rows, 0:1], coef[rows, 1:2], coef[rows, 2:3]
        )
        rate[rows, :] = first
        change[rows, :] = second
        rate_half[rows, :] = first.astype(rate_half.dtype)


def section_two_kernel(own, other, state, tau, coef, stress, normal, rate, change, mean_rate, mean_change):
    size, members = state.shape
    step = min(size, 64)

    @pl.loop(0, size // step)
    def _(index):
        rows = pl.ds(pl.multiple_of(index * step, step), step)
        shear = stress[rows, :] + section_step * (own[0, rows, :] + other[0, rows, :].astype(jnp.float32))
        press = normal[rows, :] + section_step * (own[1, rows, :] + other[1, rows, :].astype(jnp.float32))
        first, second = friction(
            shear,
            press,
            state[rows, :] + section_step * change[rows, :],
            tau[rows, :],
            coef[rows, 0:1],
            coef[rows, 1:2],
            coef[rows, 2:3],
        )
        mean_rate[rows, :] = (rate[rows, :] + first) * 0.5
        mean_change[rows, :] = (change[rows, :] + second) * 0.5


def section(kernel, outs, *args):
    vmem = pl.BlockSpec(memory_space=pltpu.VMEM)
    return pl.pallas_call(
        kernel,
        out_shape=outs,
        in_specs=[vmem] * len(args),
        out_specs=tuple([vmem] * len(outs)),
        compiler_params=pltpu.CompilerParams(vmem_limit_bytes=24 * 1024 * 1024),
        cost_estimate=pl.CostEstimate(
            flops=200 * outs[0].size, bytes_accessed=8 * 4 * outs[0].size, transcendentals=12 * outs[0].size
        ),
    )(*args)


def body(
    slip_deficit,
    state_var,
    tau_load,
    sigma_base,
    a_coef,
    b_coef,
    v_basis,
    u_basis,
    dense_blocks,
    block_ranks,
    near_index,
):
    count = lax.axis_size("row")
    col = lax.axis_index("col")
    near = near_index - col * count
    coef = jnp.stack([sigma_base, a_coef, b_coef], axis=1)
    mine, twin = col.reshape(1), (1 - col).reshape(1)
    swap = [(0, 1), (1, 0)]

    def lattice(field_half):
        found = ring_gather(field_half, count)
        order = jnp.stack([row for row, _ in found])

        def one(row, kind):
            return lattice_row(
                found, order, block_ranks, near, row, v_basis, u_basis, dense_blocks, kind
            )

        other = lax.ppermute(one(twin, jnp.bfloat16), "col", swap)
        return one(mine, jnp.float32), other

    full = jax.ShapeDtypeStruct(slip_deficit.shape, jnp.float32)
    narrow = jax.ShapeDtypeStruct(slip_deficit.shape, jnp.bfloat16)
    own, other = lattice(slip_deficit.astype(jnp.bfloat16))
    stress, normal, rate, change, rate_half = section(
        section_one_kernel, (full, full, full, full, narrow), own, other, state_var, tau_load, coef
    )
    own, other = lattice(rate_half)
    return section(
        section_two_kernel,
        (full, full),
        own,
        other,
        state_var,
        tau_load,
        coef,
        stress,
        normal,
        rate,
        change,
    )


def solution(mesh):
    placed = (
        P(("row", "col"), "scen"),
        P(("row", "col"), "scen"),
        P(("row", "col"), "scen"),
        P(("row", "col")),
        P(("row", "col")),
        P(("row", "col")),
        P("row", "col", None, None),
        P(None, "row", "col", None, None),
        P(None, "row", "col", None, None),
        P("row", "col"),
        P("row", "col"),
    )
    return jax.shard_map(
        body,
        mesh=mesh,
        in_specs=placed,
        out_specs=(P(("row", "col"), "scen"), P(("row", "col"), "scen")),
        check_vma=False,
    )
```

```python
import functools

import jax
import jax.numpy as jnp
from jax import lax
from jax.experimental import pallas as pl
from jax.experimental.pallas import tpu as pltpu
from jax.sharding import PartitionSpec as P

NEWTON = 2
RING_LIMIT = 16

damping = 0.5
sigma_floor = 0.5
section_step = 0.1


def ring_rows(count):
    return list(range(0, count, 2)) + list(range(1, count, 2))[::-1]


def row_met(turn, row, col, count):
    place = jnp.where(row % 2 == 0, row // 2, count - 1 - row // 2)
    place = lax.rem(place + turn * (2 * col - 1) + count, count)
    return jnp.where(place < count // 2, 2 * place, 2 * (count - 1 - place) + 1)


def ring_gather(block, count, cols):
    ring = ring_rows(count)
    hops = [(ring[i], ring[(i + 1) % count]) for i in range(count)]

    def way(turn):
        return [
            ((a, b) if (c + turn) % 2 == 0 else (b, a), c) for c in range(cols) for a, b in hops
        ]

    ahead, back = ([(a * cols + c, b * cols + c) for (a, b), c in way(turn)] for turn in (0, 1))
    first = second = block
    found = [block]
    for _ in range((count - 1) // 2):
        first = lax.ppermute(first, ("row", "col"), ahead)
        second = lax.ppermute(second, ("row", "col"), back)
        found += [first, second]
    half = block.shape[0] // 2
    top = lax.ppermute(first[:half], ("row", "col"), ahead)
    low = lax.ppermute(second[half:], ("row", "col"), back)
    return found, [top, low]


def arrivals(count):
    return [0] + [sign * step for step in range(1, (count - 1) // 2 + 1) for sign in (1, -1)]


def near_kernel(count, turns, ring, row_ref, col_ref, rank_ref, near_ref, v_ref, d_ref, *refs):
    blocks = refs[: len(turns)]
    proj_ref, sums_ref, picked = refs[len(turns) :]
    rank_count = v_ref.shape[2]
    row, col = row_ref[0], col_ref[0]
    rows, slots = near_ref.shape
    met = [row_met(turn, row, col, count) if ring else turn for turn in turns]
    proj_ref[...] = jnp.zeros_like(proj_ref)
    picked[...] = jnp.zeros_like(picked)
    for q, block in zip(met, blocks):
        for p in range(rows):
            part = jnp.dot(v_ref[p, q], block[...], preferred_element_type=jnp.float32)
            inside = lax.broadcasted_iota(jnp.int32, part.shape, 0) < rank_ref[p, q]
            at = pl.ds(pl.multiple_of(q * rank_count, rank_count), rank_count)
            proj_ref[p, at, :] = jnp.where(inside, part, 0.0).astype(proj_ref.dtype)
            for s in range(slots):

                @pl.when(near_ref[p, s] - col * count == q)
                def _():
                    picked[p * slots + s] = block[...]

    for p in range(rows):
        for kind in range(d_ref.shape[0]):
            total = jnp.dot(d_ref[kind, p, 0], picked[p * slots], preferred_element_type=jnp.float32)
            for s in range(1, slots):
                total += jnp.dot(
                    d_ref[kind, p, s], picked[p * slots + s], preferred_element_type=jnp.float32
                )
            sums_ref[p, kind] = total


def finish_kernel(
    count, turn, ring, swap, row_ref, col_ref, rank_ref, near_ref, v_ref, u_ref, d_ref, proj_ref, sums_ref, *refs
):
    parts = refs[:-2]
    out_ref, proj = refs[-2:]
    rank_count = v_ref.shape[2]
    row, col = row_ref[0], col_ref[0]
    slots = near_ref.shape[1]
    p = 1 - col if swap else col
    q = row_met(turn, row, col, count) if ring else turn
    tall = v_ref.shape[3] // len(parts)

    def times(weights):
        pieces = [
            jnp.dot(weights[:, i * tall : (i + 1) * tall], part[...], preferred_element_type=jnp.float32)
            for i, part in enumerate(parts)
        ]
        return sum(pieces[1:], pieces[0])

    proj[...] = proj_ref[p]
    last = times(v_ref[p, q])
    inside = lax.broadcasted_iota(jnp.int32, last.shape, 0) < rank_ref[p, q]
    at = pl.ds(pl.multiple_of(q * rank_count, rank_count), rank_count)
    proj[at, :] = jnp.where(inside, last, 0.0).astype(proj.dtype)
    for kind in range(u_ref.shape[0]):
        total = sums_ref[p, kind] + jnp.dot(
            u_ref[kind, p], proj[...], preferred_element_type=jnp.float32
        )
        out_ref[kind] = total.astype(out_ref.dtype)
    for s in range(slots):

        @pl.when(near_ref[p, s] - col * count == q)
        def _():
            for kind in range(u_ref.shape[0]):
                total = out_ref[kind].astype(jnp.float32) + times(d_ref[kind, p, s])
                out_ref[kind] = total.astype(out_ref.dtype)


def on_core(kernel, outs, scalars, arrays, scratch, flops):
    smem, vmem = pl.BlockSpec(memory_space=pltpu.SMEM), pl.BlockSpec(memory_space=pltpu.VMEM)
    return pl.pallas_call(
        kernel,
        out_shape=outs,
        in_specs=[smem] * len(scalars) + [vmem] * len(arrays),
        out_specs=jax.tree.map(lambda _: vmem, outs),
        scratch_shapes=scratch,
        compiler_params=pltpu.CompilerParams(vmem_limit_bytes=32 * 1024 * 1024),
        cost_estimate=pl.CostEstimate(
            flops=flops, bytes_accessed=sum(a.size * a.dtype.itemsize for a in arrays), transcendentals=0
        ),
    )(*scalars, *arrays)


def inverse_sinh(value):
    magnitude = jnp.abs(value)
    result = jnp.log(magnitude + jnp.sqrt(magnitude * magnitude + 1.0))
    return jnp.where(value < 0.0, -result, result)


def sinh_cosh(value):
    grown = jnp.exp(value)
    shrunk = 1.0 / grown
    square = value * value
    small = value * (
        1.0 + square * (1 / 6 + square * (1 / 120 + square * (1 / 5040 + square * (1 / 362880))))
    )
    sinh = jnp.where(square < 1.0, small, 0.5 * (grown - shrunk))
    return sinh, 0.5 * (grown + shrunk)


def friction(shear, normal, state, tau_load, sigma_base, a_wide, b_wide):
    tau = tau_load + shear
    sigma = jnp.maximum(sigma_base + normal, sigma_floor)
    weight = jnp.exp(-state / a_wide)
    stiff = sigma * a_wide
    first = tau / stiff
    second = inverse_sinh(tau / (2.0 * damping * weight))
    slope = jnp.where(jnp.abs(first) < jnp.abs(second), first, second)
    for newton_step in range(NEWTON):
        sinh, cosh = sinh_cosh(slope)
        excess = stiff * slope + 2.0 * damping * weight * sinh - tau
        deriv = stiff + 2.0 * damping * weight * cosh
        slope = slope - excess / deriv
    rate = 2.0 * weight * sinh_cosh(slope)[0]
    change = b_wide * (jnp.exp(-state / b_wide) - jnp.abs(rate))
    return (rate, change)


def section_one_kernel(own, other, state, tau, coef, stress, normal, rate, change, rate_half):
    size, members = state.shape
    step = min(size, 64)

    @pl.loop(0, size // step)
    def _(index):
        rows = pl.ds(pl.multiple_of(index * step, step), step)
        shear = own[0, rows, :] + other[0, rows, :].astype(jnp.float32)
        press = own[1, rows, :] + other[1, rows, :].astype(jnp.float32)
        stress[rows, :] = shear
        normal[rows, :] = press
        first, second = friction(
            shear, press, state[rows, :], tau[rows, :], coef[rows, 0:1], coef[rows, 1:2], coef[rows, 2:3]
        )
        rate[rows, :] = first
        change[rows, :] = second
        rate_half[rows, :] = first.astype(rate_half.dtype)


def section_two_kernel(own, other, state, tau, coef, stress, normal, rate, change, mean_rate, mean_change):
    size, members = state.shape
    step = min(size, 64)

    @pl.loop(0, size // step)
    def _(index):
        rows = pl.ds(pl.multiple_of(index * step, step), step)
        shear = stress[rows, :] + section_step * (own[0, rows, :] + other[0, rows, :].astype(jnp.float32))
        press = normal[rows, :] + section_step * (own[1, rows, :] + other[1, rows, :].astype(jnp.float32))
        first, second = friction(
            shear,
            press,
            state[rows, :] + section_step * change[rows, :],
            tau[rows, :],
            coef[rows, 0:1],
            coef[rows, 1:2],
            coef[rows, 2:3],
        )
        mean_rate[rows, :] = (rate[rows, :] + first) * 0.5
        mean_change[rows, :] = (change[rows, :] + second) * 0.5


def section(kernel, outs, *args):
    vmem = pl.BlockSpec(memory_space=pltpu.VMEM)
    return pl.pallas_call(
        kernel,
        out_shape=outs,
        in_specs=[vmem] * len(args),
        out_specs=tuple([vmem] * len(outs)),
        compiler_params=pltpu.CompilerParams(vmem_limit_bytes=24 * 1024 * 1024),
        cost_estimate=pl.CostEstimate(
            flops=200 * outs[0].size, bytes_accessed=8 * 4 * outs[0].size, transcendentals=12 * outs[0].size
        ),
    )(*args)


def body(
    slip_deficit,
    state_var,
    tau_load,
    sigma_base,
    a_coef,
    b_coef,
    v_basis,
    u_basis,
    dense_blocks,
    block_ranks,
    near_index,
):
    count, cols = lax.axis_size("row"), lax.axis_size("col")
    size, members = slip_deficit.shape
    kinds, rows, _, rank_count, _ = u_basis.shape
    slots = near_index.shape[1]
    ring = cols == 2 and count % 2 == 0 and 4 <= count <= RING_LIMIT
    coef = jnp.stack([sigma_base, a_coef, b_coef], axis=1)
    u_turned = jnp.swapaxes(u_basis.reshape(kinds, rows, count * rank_count, size), 2, 3)
    scalars = (
        lax.axis_index("row").reshape(1),
        lax.axis_index("col").reshape(1),
        block_ranks,
        near_index,
    )
    swap = [(0, 1), (1, 0)]
    narrow = jnp.bfloat16

    def lattice(field_half):
        if ring:
            found, last = ring_gather(field_half, count, cols)
            turns, turn = arrivals(count), count // 2
        else:
            whole = lax.all_gather(field_half, "row", axis=0)
            found, last = [whole[r] for r in range(count - 1)], [whole[count - 1]]
            turns, turn = list(range(count - 1)), count - 1
        proj, sums = on_core(
            functools.partial(near_kernel, count, turns, ring),
            (
                jax.ShapeDtypeStruct((rows, count * rank_count, members), narrow),
                jax.ShapeDtypeStruct((rows, kinds, size, members), jnp.float32),
            ),
            scalars,
            (v_basis, dense_blocks, *found),
            [pltpu.VMEM((rows * slots, size, members), narrow)],
            2 * rows * size * members * (count * rank_count + kinds * slots * size),
        )

        def finish(twin, kind):
            return on_core(
                functools.partial(finish_kernel, count, turn, ring, twin),
                jax.ShapeDtypeStruct((kinds, size, members), kind),
                scalars,
                (v_basis, u_turned, dense_blocks, proj, sums, *last),
                [pltpu.VMEM((count * rank_count, members), narrow)],
                2 * kinds * size * members * count * rank_count,
            )

        other = lax.ppermute(finish(True, narrow), "col", swap)
        return finish(False, jnp.float32), other

    full = jax.ShapeDtypeStruct(slip_deficit.shape, jnp.float32)
    half = jax.ShapeDtypeStruct(slip_deficit.shape, narrow)
    own, other = lattice(slip_deficit.astype(narrow))
    stress, normal, rate, change, rate_half = section(
        section_one_kernel, (full, full, full, full, half), own, other, state_var, tau_load, coef
    )
    own, other = lattice(rate_half)
    return section(
        section_two_kernel,
        (full, full),
        own,
        other,
        state_var,
        tau_load,
        coef,
        stress,
        normal,
        rate,
        change,
    )


def solution(mesh):
    placed = (
        P(("row", "col"), "scen"),
        P(("row", "col"), "scen"),
        P(("row", "col"), "scen"),
        P(("row", "col")),
        P(("row", "col")),
        P(("row", "col")),
        P("row", "col", None, None),
        P(None, "row", "col", None, None),
        P(None, "row", "col", None, None),
        P("row", "col"),
        P("row", "col"),
    )
    return jax.shard_map(
        body,
        mesh=mesh,
        in_specs=placed,
        out_specs=(P(("row", "col"), "scen"), P(("row", "col"), "scen")),
        check_vma=False,
    )
```

```python
import functools

import jax
import jax.numpy as jnp
from jax import lax
from jax.experimental import pallas as pl
from jax.experimental.pallas import tpu as pltpu
from jax.sharding import PartitionSpec as P

NEWTON = 2
DIRECT_LIMIT = 16
LATE = 4

damping = 0.5
sigma_floor = 0.5
section_step = 0.1


def arrivals(count, direct):
    if not direct:
        return list(range(count))
    length = count // 2
    shifts = list(range(length - 1, 0, -1))
    early = [(0, 0), (0, 1)] + [(shift, 0) for shift in shifts[:-1]]
    late = [(shift, 0) for shift in shifts[-1:]] + [(shift, 1) for shift in shifts[-1:]]
    return early + late + [(shift, 1) for shift in shifts[:-1]]


def row_met(spot, row, count):
    if not isinstance(spot, tuple):
        return spot
    shift, other = spot
    z, y = row // 2, row % 2
    return lax.rem(z - shift + count // 2, count // 2) * 2 + (1 - y if other else y)


def gather_direct(block, count):
    length = count // 2

    def along(shift, other, data):
        hops = [
            (z * 2 + y, (z + shift) % length * 2 + (1 - y if other else y))
            for z in range(length)
            for y in range(2)
        ]
        return lax.ppermute(data, "row", hops)

    shifts = list(range(length - 1, 0, -1))
    far, last = {}, []
    across = along(0, 1, block)
    for shift in shifts[:-1]:
        far[shift] = along(shift, 0, block)
    if shifts:
        held = block
        if far:
            held, _ = lax.optimization_barrier((block, far[shifts[0]]))
        last = [along(shifts[-1], 0, held), along(shifts[-1], 1, held)]
    passed = [along(0, 1, far[shift]) for shift in shifts[:-1]]
    return [block, across, *far.values(), *last, *passed]


def narrow_kernel(wide_ref, narrow_ref):
    narrow_ref[...] = wide_ref[...].astype(narrow_ref.dtype)


def prepare_kernel(
    spots, row_ref, rank_ref, v_ref, u_ref, sigma_ref, a_ref, b_ref, state_ref, v_out, u_out, coef_out, weight_out, decay_out
):
    kinds, rows, count, rank_count, size = u_ref.shape
    row = row_ref[0]
    met = [row_met(spot, row, count) for spot in spots]
    for at, q in enumerate(met):
        for p in range(rows):
            inside = lax.broadcasted_iota(jnp.int32, (rank_count, size), 0) < rank_ref[p, q]
            v_out[at, p] = jnp.where(inside, v_ref[p, q].astype(jnp.float32), 0.0).astype(v_out.dtype)
    for p in range(rows):
        for kind in range(kinds):
            for first in range(0, count, 4):
                group = [u_ref[kind, p, q] for q in met[first : first + 4]]
                turned = jnp.concatenate(group, axis=0).astype(jnp.float32).T
                u_out[p, kind * size : (kind + 1) * size, first * rank_count : (first + len(group)) * rank_count] = (
                    turned.astype(u_out.dtype)
                )
    lanes = coef_out.shape[2]
    for at, ref in enumerate((sigma_ref, a_ref, b_ref)):
        coef_out[at] = jnp.broadcast_to(ref[...], (lanes, size)).T
    for first in range(0, state_ref.shape[1], lanes):
        part = slice(first, first + lanes)
        state = state_ref[:, part]
        weight_out[:, part] = jnp.exp(-state / coef_out[1])
        decay_out[:, part] = jnp.exp(-state / coef_out[2])


def sums_kernel(spots, first, pick, before, row_ref, col_ref, near_ref, v_ref, u_ref, d_ref, *refs):
    blocks = refs[: len(spots)]
    refs = refs[len(spots) :]
    if before:
        sums_ref, refs = refs[0], refs[1:]
    out_ref, x_all, proj, total = refs
    count, rows, rank_count, size = v_ref.shape
    kinds, slots = d_ref.shape[0], near_ref.shape[1]
    row, col = row_ref[0], col_ref[0]
    met = [row_met(spot, row, count) for spot in spots]
    chosen = list(range(rows)) if pick is None else [col if pick == 0 else 1 - col]
    for at, block in enumerate(blocks):
        x_all[at] = block[...]
    for at, block in enumerate(blocks):
        if pick is None:
            weights = v_ref[first + at].reshape(rows * rank_count, size)
        else:
            weights = v_ref[first + at, chosen[0]]
        part = jnp.dot(weights, block[...], preferred_element_type=jnp.float32).astype(proj.dtype)
        for place in range(len(chosen)):
            proj[place, at * rank_count : (at + 1) * rank_count, :] = part[
                place * rank_count : (place + 1) * rank_count
            ]
    lanes = slice(first * rank_count, (first + len(blocks)) * rank_count)
    for place, p in enumerate(chosen):
        gained = jnp.dot(u_ref[p, :, lanes], proj[place], preferred_element_type=jnp.float32)
        for kind in range(kinds):
            piece = gained[kind * size : (kind + 1) * size]
            total[place, kind] = sums_ref[p, kind] + piece if before else piece
    for place, p in enumerate(chosen):
        for s in range(slots):
            near = near_ref[p, s] - col * count
            at = sum(jnp.where(near == q, i, 0) for i, q in enumerate(met))
            hit = sum(jnp.where(near == q, 1, 0) for q in met)

            @pl.when(hit > 0)
            def _():
                block = x_all[at]
                for kind in range(kinds):
                    total[place, kind] += jnp.dot(
                        d_ref[kind, p, s], block, preferred_element_type=jnp.float32
                    )
    for place in range(len(chosen)):
        for kind in range(kinds):
            if pick is None:
                out_ref[place, kind] = total[place, kind]
            else:
                out_ref[kind] = total[place, kind].astype(out_ref.dtype)


def inverse_sinh(value):
    magnitude = jnp.abs(value)
    result = jnp.log(magnitude + jnp.sqrt(magnitude * magnitude + 1.0))
    return jnp.where(value < 0.0, -result, result)


def sinh_cosh(value):
    grown = jnp.exp(value)
    shrunk = jnp.exp(-value)
    square = value * value
    small = value * (
        1.0 + square * (1 / 6 + square * (1 / 120 + square * (1 / 5040 + square * (1 / 362880))))
    )
    sinh = jnp.where(square < 1.0, small, 0.5 * (grown - shrunk))
    return sinh, 0.5 * (grown + shrunk)


def friction(shear, normal, weight, decay, tau_load, sigma_base, a_wide, b_wide):
    tau = tau_load + shear
    sigma = jnp.maximum(sigma_base + normal, sigma_floor)
    stiff = sigma * a_wide
    first = tau / stiff
    second = inverse_sinh(tau / (2.0 * damping * weight))
    slope = jnp.where(jnp.abs(first) < jnp.abs(second), first, second)
    for newton_step in range(NEWTON):
        sinh, cosh = sinh_cosh(slope)
        excess = stiff * slope + 2.0 * damping * weight * sinh - tau
        deriv = stiff + 2.0 * damping * weight * cosh
        slope = slope - excess / deriv
    rate = 2.0 * weight * sinh_cosh(slope)[0]
    change = b_wide * (decay - jnp.abs(rate))
    return (rate, change)


def over_pieces(size, members, lanes, work):
    step = min(size, 16)

    @pl.loop(0, size // step)
    def _(index):
        rows = pl.ds(pl.multiple_of(index * step, step), step)
        for first in range(0, members, lanes):
            work(rows, slice(first, first + lanes))


def section_one_kernel(own, other, weight, decay, tau, coef, stress, normal, rate, change, rate_half):
    size, members = tau.shape

    def work(rows, part):
        shear = own[0, rows, part] + other[0, rows, part].astype(jnp.float32)
        press = own[1, rows, part] + other[1, rows, part].astype(jnp.float32)
        stress[rows, part] = shear
        normal[rows, part] = press
        first, second = friction(
            shear,
            press,
            weight[rows, part],
            decay[rows, part],
            tau[rows, part],
            coef[0, rows, :],
            coef[1, rows, :],
            coef[2, rows, :],
        )
        rate[rows, part] = first
        change[rows, part] = second
        rate_half[rows, part] = first.astype(rate_half.dtype)

    over_pieces(size, members, coef.shape[2], work)


def section_two_kernel(
    own, other, state, tau, coef, stress, normal, rate, change, mean_rate, mean_change
):
    size, members = tau.shape

    def work(rows, part):
        shear = own[0, rows, part] + other[0, rows, part].astype(jnp.float32)
        press = own[1, rows, part] + other[1, rows, part].astype(jnp.float32)
        sigma, a_wide, b_wide = coef[0, rows, :], coef[1, rows, :], coef[2, rows, :]
        later = state[rows, part] + section_step * change[rows, part]
        first, second = friction(
            stress[rows, part] + section_step * shear,
            normal[rows, part] + section_step * press,
            jnp.exp(-later / a_wide),
            jnp.exp(-later / b_wide),
            tau[rows, part],
            sigma,
            a_wide,
            b_wide,
        )
        mean_rate[rows, part] = (rate[rows, part] + first) * 0.5
        mean_change[rows, part] = (change[rows, part] + second) * 0.5

    over_pieces(size, members, coef.shape[2], work)


def on_core(kernel, outs, scalars, arrays, scratch=(), flops=0, room=16):
    smem, vmem = pl.BlockSpec(memory_space=pltpu.SMEM), pl.BlockSpec(memory_space=pltpu.VMEM)
    return pl.pallas_call(
        kernel,
        out_shape=outs,
        in_specs=[smem] * len(scalars) + [vmem] * len(arrays),
        out_specs=jax.tree.map(lambda _: vmem, outs),
        scratch_shapes=list(scratch),
        compiler_params=pltpu.CompilerParams(vmem_limit_bytes=room * 1024 * 1024),
        cost_estimate=pl.CostEstimate(
            flops=flops, bytes_accessed=sum(a.size * a.dtype.itemsize for a in arrays), transcendentals=0
        ),
    )(*scalars, *arrays)


def body(
    slip_deficit,
    state_var,
    tau_load,
    sigma_base,
    a_coef,
    b_coef,
    v_basis,
    u_basis,
    dense_blocks,
    block_ranks,
    near_index,
):
    count = lax.axis_size("row")
    size, members = slip_deficit.shape
    kinds, rows, _, rank_count, _ = u_basis.shape
    direct = count % 2 == 0 and count <= DIRECT_LIMIT
    spots = arrivals(count, direct)
    early = max(count - LATE, 0)
    room = 16 if direct else 40
    lanes = min(members, 128)
    narrow, wide = jnp.bfloat16, jnp.float32
    row, col = lax.axis_index("row").reshape(1), lax.axis_index("col").reshape(1)
    swap = [(0, 1), (1, 0)]

    def shaped(*shape, kind=wide):
        return jax.ShapeDtypeStruct(shape, kind)

    full = shaped(size, members)
    v_met, u_met, coef, weight, decay = on_core(
        functools.partial(prepare_kernel, spots),
        (
            shaped(count, rows, rank_count, size, kind=narrow),
            shaped(rows, kinds * size, count * rank_count, kind=narrow),
            shaped(3, size, lanes),
            full,
            full,
        ),
        (row, block_ranks),
        (
            v_basis,
            u_basis,
            sigma_base.reshape(1, size),
            a_coef.reshape(1, size),
            b_coef.reshape(1, size),
            state_var,
        ),
        room=room,
    )

    def add(blocks, first, pick, before, kind):
        held = rows if pick is None else 1
        lead = (rows, kinds) if pick is None else (kinds,)
        return on_core(
            functools.partial(
                sums_kernel, spots[first : first + len(blocks)], first, pick, before is not None
            ),
            shaped(*lead, size, members, kind=kind),
            (row, col, near_index),
            (v_met, u_met, dense_blocks, *blocks, *(() if before is None else (before,))),
            (
                pltpu.VMEM((len(blocks), size, members), narrow),
                pltpu.VMEM((held, len(blocks) * rank_count, members), narrow),
                pltpu.VMEM((held, kinds, size, members), wide),
            ),
            2 * held * size * members * rank_count * len(blocks) * 3,
            room,
        )

    def lattice(field_half):
        if direct:
            blocks = gather_direct(field_half, count)
        else:
            whole = lax.all_gather(field_half, "row", axis=0)
            blocks = [whole[r] for r in range(count)]
        sums = add(blocks[:early], 0, None, None, wide) if early else None
        other = lax.ppermute(add(blocks[early:], early, 1, sums, narrow), "col", swap)
        return add(blocks[early:], early, 0, sums, wide), other

    slip_half = on_core(narrow_kernel, shaped(size, members, kind=narrow), (), (slip_deficit,))
    own, other = lattice(slip_half)
    stress, normal, rate, change, rate_half = on_core(
        section_one_kernel,
        (full, full, full, full, shaped(size, members, kind=narrow)),
        (),
        (own, other, weight, decay, tau_load, coef),
        flops=200 * size * members,
    )
    own, other = lattice(rate_half)
    return on_core(
        section_two_kernel,
        (full, full),
        (),
        (own, other, state_var, tau_load, coef, stress, normal, rate, change),
        flops=200 * size * members,
    )


def solution(mesh):
    placed = (
        P(("row", "col"), "scen"),
        P(("row", "col"), "scen"),
        P(("row", "col"), "scen"),
        P(("row", "col")),
        P(("row", "col")),
        P(("row", "col")),
        P("row", "col", None, None),
        P(None, "row", "col", None, None),
        P(None, "row", "col", None, None),
        P("row", "col"),
        P("row", "col"),
    )
    return jax.shard_map(
        body,
        mesh=mesh,
        in_specs=placed,
        out_specs=(P(("row", "col"), "scen"), P(("row", "col"), "scen")),
        check_vma=False,
    )
```

```python
import functools

import jax
import jax.numpy as jnp
from jax import lax
from jax.experimental import pallas as pl
from jax.experimental.pallas import tpu as pltpu
from jax.sharding import PartitionSpec as P

NEWTON = 2
DIRECT_LIMIT = 16
LATE = 4

damping = 0.5
sigma_floor = 0.5
section_step = 0.1


def arrivals(count, direct):
    if not direct:
        return list(range(count))
    length = count // 2
    shifts = list(range(length - 1, 0, -1))
    early = [(0, 0), (0, 1)] + [(shift, 0) for shift in shifts[:-1]]
    late = [(shift, 0) for shift in shifts[-1:]] + [(shift, 1) for shift in shifts[-1:]]
    return early + late + [(shift, 1) for shift in shifts[:-1]]


def row_met(spot, row, count):
    if not isinstance(spot, tuple):
        return spot
    shift, other = spot
    z, y = row // 2, row % 2
    return lax.rem(z - shift + count // 2, count // 2) * 2 + (1 - y if other else y)


def gather_direct(block, count):
    length = count // 2

    def along(shift, other, data):
        hops = [
            (z * 2 + y, (z + shift) % length * 2 + (1 - y if other else y))
            for z in range(length)
            for y in range(2)
        ]
        return lax.ppermute(data, "row", hops)

    shifts = list(range(length - 1, 0, -1))
    far, last = {}, []
    across = along(0, 1, block)
    for shift in shifts[:-1]:
        far[shift] = along(shift, 0, block)
    if shifts:
        last = [along(shifts[-1], 0, block), along(shifts[-1], 1, block)]
    passed = [along(0, 1, far[shift]) for shift in shifts[:-1]]
    return [block, across, *far.values(), *last, *passed]


PIECES = 4


def row_pieces(size):
    tall = size // PIECES
    return [pl.ds(at * tall, tall) for at in range(PIECES)]


def narrow_kernel(wide_ref, narrow_ref, held, sem):
    copies = [
        pltpu.make_async_copy(wide_ref.at[part], held.at[part], sem.at[at])
        for at, part in enumerate(row_pieces(held.shape[0]))
    ]
    for copy in copies:
        copy.start()
    for copy, part in zip(copies, row_pieces(held.shape[0])):
        copy.wait()
        narrow_ref[part, :] = held[part, :].astype(narrow_ref.dtype)


def prepare_kernel(spots, row_ref, *refs):
    far, (v_out, u_out, coef_out, weight_out, decay_out), near, sem = refs[:7], refs[7:12], refs[12:19], refs[19]
    copies = [
        pltpu.make_async_copy(source, held, sem.at[at])
        for at, (source, held) in enumerate(zip(far, near))
    ]
    for copy in copies:
        copy.start()
    for copy in copies:
        copy.wait()
    rank_ref, v_ref, u_ref, sigma_ref, a_ref, b_ref, state_ref = near
    kinds, rows, count, rank_count, size = u_ref.shape
    row = row_ref[0]
    met = [row_met(spot, row, count) for spot in spots]
    for at, q in enumerate(met):
        for p in range(rows):
            inside = lax.broadcasted_iota(jnp.int32, (rank_count, size), 0) < rank_ref[p, q]
            v_out[at, p] = jnp.where(inside, v_ref[p, q].astype(jnp.float32), 0.0).astype(v_out.dtype)
    for p in range(rows):
        for kind in range(kinds):
            for first in range(0, count, 4):
                group = [u_ref[kind, p, q] for q in met[first : first + 4]]
                turned = jnp.concatenate(group, axis=0).astype(jnp.float32).T
                u_out[p, kind * size : (kind + 1) * size, first * rank_count : (first + len(group)) * rank_count] = (
                    turned.astype(u_out.dtype)
                )
    lanes = coef_out.shape[2]
    for at, ref in enumerate((sigma_ref, a_ref, b_ref)):
        coef_out[at] = jnp.broadcast_to(ref[...], (lanes, size)).T
    for first in range(0, state_ref.shape[1], lanes):
        part = slice(first, first + lanes)
        state = state_ref[:, part]
        weight_out[:, part] = jnp.exp(-state / coef_out[1])
        decay_out[:, part] = jnp.exp(-state / coef_out[2])


def sums_kernel(spots, first, pick, before, row_ref, col_ref, near_ref, v_ref, u_ref, d_ref, *refs):
    blocks = refs[: len(spots)]
    refs = refs[len(spots) :]
    if before:
        sums_ref, refs = refs[0], refs[1:]
    out_ref, x_all, proj, total = refs
    count, rows, rank_count, size = v_ref.shape
    kinds, slots = d_ref.shape[0], near_ref.shape[1]
    row, col = row_ref[0], col_ref[0]
    met = [row_met(spot, row, count) for spot in spots]
    chosen = list(range(rows)) if pick is None else [col if pick == 0 else 1 - col]
    for at, block in enumerate(blocks):
        x_all[at] = block[...]
    for at, block in enumerate(blocks):
        if pick is None:
            weights = v_ref[first + at].reshape(rows * rank_count, size)
        else:
            weights = v_ref[first + at, chosen[0]]
        part = jnp.dot(weights, block[...], preferred_element_type=jnp.float32).astype(proj.dtype)
        for place in range(len(chosen)):
            proj[place, at * rank_count : (at + 1) * rank_count, :] = part[
                place * rank_count : (place + 1) * rank_count
            ]
    lanes = slice(first * rank_count, (first + len(blocks)) * rank_count)
    for place, p in enumerate(chosen):
        gained = jnp.dot(u_ref[p, :, lanes], proj[place], preferred_element_type=jnp.float32)
        for kind in range(kinds):
            piece = gained[kind * size : (kind + 1) * size]
            total[place, kind] = sums_ref[p, kind] + piece if before else piece
    for place, p in enumerate(chosen):
        for s in range(slots):
            near = near_ref[p, s] - col * count
            at = sum(jnp.where(near == q, i, 0) for i, q in enumerate(met))
            hit = sum(jnp.where(near == q, 1, 0) for q in met)

            @pl.when(hit > 0)
            def _():
                block = x_all[at]
                for kind in range(kinds):
                    total[place, kind] += jnp.dot(
                        d_ref[kind, p, s], block, preferred_element_type=jnp.float32
                    )
    for place in range(len(chosen)):
        for kind in range(kinds):
            if pick is None:
                out_ref[place, kind] = total[place, kind]
            else:
                out_ref[kind] = total[place, kind].astype(out_ref.dtype)


def inverse_sinh(value):
    magnitude = jnp.abs(value)
    result = jnp.log(magnitude + jnp.sqrt(magnitude * magnitude + 1.0))
    return jnp.where(value < 0.0, -result, result)


def sinh_cosh(value):
    grown = jnp.exp(value)
    shrunk = jnp.exp(-value)
    square = value * value
    small = value * (
        1.0 + square * (1 / 6 + square * (1 / 120 + square * (1 / 5040 + square * (1 / 362880))))
    )
    sinh = jnp.where(square < 1.0, small, 0.5 * (grown - shrunk))
    return sinh, 0.5 * (grown + shrunk)


def friction(shear, normal, weight, decay, tau_load, sigma_base, a_wide, b_wide):
    tau = tau_load + shear
    sigma = jnp.maximum(sigma_base + normal, sigma_floor)
    stiff = sigma * a_wide
    first = tau / stiff
    second = inverse_sinh(tau / (2.0 * damping * weight))
    slope = jnp.where(jnp.abs(first) < jnp.abs(second), first, second)
    for newton_step in range(NEWTON):
        sinh, cosh = sinh_cosh(slope)
        excess = stiff * slope + 2.0 * damping * weight * sinh - tau
        deriv = stiff + 2.0 * damping * weight * cosh
        slope = slope - excess / deriv
    rate = 2.0 * weight * sinh_cosh(slope)[0]
    change = b_wide * (decay - jnp.abs(rate))
    return (rate, change)


def over_pieces(begin, tall, members, lanes, work):
    step = min(tall, 16)

    @pl.loop(0, tall // step)
    def _(index):
        rows = pl.ds(pl.multiple_of(begin + index * step, step), step)
        for first in range(0, members, lanes):
            work(rows, slice(first, first + lanes))


def section_one_kernel(own, other, weight, decay, tau, coef, stress, normal, rate, change, rate_half):
    size, members = tau.shape

    def work(rows, part):
        shear = own[0, rows, part] + other[0, rows, part].astype(jnp.float32)
        press = own[1, rows, part] + other[1, rows, part].astype(jnp.float32)
        stress[rows, part] = shear
        normal[rows, part] = press
        first, second = friction(
            shear,
            press,
            weight[rows, part],
            decay[rows, part],
            tau[rows, part],
            coef[0, rows, :],
            coef[1, rows, :],
            coef[2, rows, :],
        )
        rate[rows, part] = first
        change[rows, part] = second
        rate_half[rows, part] = first.astype(rate_half.dtype)

    over_pieces(0, size, members, coef.shape[2], work)


def section_two_kernel(
    own, other, state, tau, coef, stress, normal, rate, change, rate_out, change_out, mean_rate, mean_change, sem
):
    size, members = tau.shape

    def work(rows, part):
        shear = own[0, rows, part] + other[0, rows, part].astype(jnp.float32)
        press = own[1, rows, part] + other[1, rows, part].astype(jnp.float32)
        sigma, a_wide, b_wide = coef[0, rows, :], coef[1, rows, :], coef[2, rows, :]
        later = state[rows, part] + section_step * change[rows, part]
        first, second = friction(
            stress[rows, part] + section_step * shear,
            normal[rows, part] + section_step * press,
            jnp.exp(-later / a_wide),
            jnp.exp(-later / b_wide),
            tau[rows, part],
            sigma,
            a_wide,
            b_wide,
        )
        mean_rate[rows, part] = (rate[rows, part] + first) * 0.5
        mean_change[rows, part] = (change[rows, part] + second) * 0.5

    copies = []
    for at, part in enumerate(row_pieces(size)):
        over_pieces(part.start, part.size, members, coef.shape[2], work)
        for kind, (held, out) in enumerate(((mean_rate, rate_out), (mean_change, change_out))):
            copies.append(pltpu.make_async_copy(held.at[part], out.at[part], sem.at[kind, at]))
            copies[-1].start()
    for copy in copies:
        copy.wait()


def on_core(kernel, outs, scalars, arrays, scratch=(), flops=0, room=16, far=(), out_far=False):
    smem, vmem = pl.BlockSpec(memory_space=pltpu.SMEM), pl.BlockSpec(memory_space=pltpu.VMEM)
    hbm = pl.BlockSpec(memory_space=pl.ANY)
    arrays = (*(pltpu.with_memory_space_constraint(a, pltpu.HBM) for a in far), *arrays)
    return pl.pallas_call(
        kernel,
        out_shape=outs,
        in_specs=[smem] * len(scalars) + [hbm] * len(far) + [vmem] * (len(arrays) - len(far)),
        out_specs=jax.tree.map(lambda _: hbm if out_far else vmem, outs),
        scratch_shapes=list(scratch),
        compiler_params=pltpu.CompilerParams(vmem_limit_bytes=room * 1024 * 1024),
        cost_estimate=pl.CostEstimate(
            flops=flops, bytes_accessed=sum(a.size * a.dtype.itemsize for a in arrays), transcendentals=0
        ),
    )(*scalars, *arrays)


def body(
    slip_deficit,
    state_var,
    tau_load,
    sigma_base,
    a_coef,
    b_coef,
    v_basis,
    u_basis,
    dense_blocks,
    block_ranks,
    near_index,
):
    count = lax.axis_size("row")
    size, members = slip_deficit.shape
    kinds, rows, _, rank_count, _ = u_basis.shape
    direct = count % 2 == 0 and count <= DIRECT_LIMIT
    spots = arrivals(count, direct)
    early = max(count - LATE, 0)
    room = 16 if direct else 40
    lanes = min(members, 128)
    narrow, wide = jnp.bfloat16, jnp.float32
    row, col = lax.axis_index("row").reshape(1), lax.axis_index("col").reshape(1)
    swap = [(0, 1), (1, 0)]

    def shaped(*shape, kind=wide):
        return jax.ShapeDtypeStruct(shape, kind)

    full = shaped(size, members)
    v_met, u_met, coef, weight, decay = on_core(
        functools.partial(prepare_kernel, spots),
        (
            shaped(count, rows, rank_count, size, kind=narrow),
            shaped(rows, kinds * size, count * rank_count, kind=narrow),
            shaped(3, size, lanes),
            full,
            full,
        ),
        (row,),
        (),
        (
            pltpu.SMEM(block_ranks.shape, jnp.int32),
            pltpu.VMEM(v_basis.shape, narrow),
            pltpu.VMEM(u_basis.shape, narrow),
            *[pltpu.VMEM((1, size), wide)] * 3,
            pltpu.VMEM((size, members), wide),
            pltpu.SemaphoreType.DMA((7,)),
        ),
        room=room,
        far=(
            block_ranks,
            v_basis,
            u_basis,
            sigma_base.reshape(1, size),
            a_coef.reshape(1, size),
            b_coef.reshape(1, size),
            state_var,
        ),
    )

    def add(blocks, first, pick, before, kind):
        held = rows if pick is None else 1
        lead = (rows, kinds) if pick is None else (kinds,)
        return on_core(
            functools.partial(
                sums_kernel, spots[first : first + len(blocks)], first, pick, before is not None
            ),
            shaped(*lead, size, members, kind=kind),
            (row, col, near_index),
            (v_met, u_met, dense_blocks, *blocks, *(() if before is None else (before,))),
            (
                pltpu.VMEM((len(blocks), size, members), narrow),
                pltpu.VMEM((held, len(blocks) * rank_count, members), narrow),
                pltpu.VMEM((held, kinds, size, members), wide),
            ),
            2 * held * size * members * rank_count * len(blocks) * 3,
            room,
        )

    def lattice(field_half):
        if direct:
            blocks = gather_direct(field_half, count)
        else:
            whole = lax.all_gather(field_half, "row", axis=0)
            blocks = [whole[r] for r in range(count)]
        sums = add(blocks[:early], 0, None, None, wide) if early else None
        other = lax.ppermute(add(blocks[early:], early, 1, sums, narrow), "col", swap)
        return add(blocks[early:], early, 0, sums, wide), other

    slip_half = on_core(
        narrow_kernel,
        shaped(size, members, kind=narrow),
        (),
        (),
        (pltpu.VMEM((size, members), wide), pltpu.SemaphoreType.DMA((PIECES,))),
        far=(slip_deficit,),
    )
    own, other = lattice(slip_half)
    stress, normal, rate, change, rate_half = on_core(
        section_one_kernel,
        (full, full, full, full, shaped(size, members, kind=narrow)),
        (),
        (own, other, weight, decay, tau_load, coef),
        flops=200 * size * members,
    )
    own, other = lattice(rate_half)
    return on_core(
        section_two_kernel,
        (full, full),
        (),
        (own, other, state_var, tau_load, coef, stress, normal, rate, change),
        (
            pltpu.VMEM((size, members), wide),
            pltpu.VMEM((size, members), wide),
            pltpu.SemaphoreType.DMA((2, PIECES)),
        ),
        flops=200 * size * members,
        out_far=True,
    )


def solution(mesh):
    placed = (
        P(("row", "col"), "scen"),
        P(("row", "col"), "scen"),
        P(("row", "col"), "scen"),
        P(("row", "col")),
        P(("row", "col")),
        P(("row", "col")),
        P("row", "col", None, None),
        P(None, "row", "col", None, None),
        P(None, "row", "col", None, None),
        P("row", "col"),
        P("row", "col"),
    )
    return jax.shard_map(
        body,
        mesh=mesh,
        in_specs=placed,
        out_specs=(P(("row", "col"), "scen"), P(("row", "col"), "scen")),
        check_vma=False,
    )
```

```python
import functools

import jax
import jax.numpy as jnp
from jax import lax
from jax.experimental import pallas as pl
from jax.experimental.pallas import tpu as pltpu
from jax.sharding import PartitionSpec as P

NEWTON = 2
DIRECT_LIMIT = 16
LATE = 3
TILE = 128

damping = 0.5
sigma_floor = 0.5
section_step = 0.1


def arrivals(count, direct):
    if not direct:
        return list(range(count))
    length = count // 2
    shifts = list(range(length - 1, 0, -1))
    return [(0, 0), (0, 1)] + [(shift, 0) for shift in shifts] + [(shift, 1) for shift in shifts[::-1]]


def columns(first, last, early, rank_count):
    gap = -early * rank_count % TILE if first >= early else 0
    return slice(first * rank_count + gap, last * rank_count + gap)


def row_met(spot, row, count):
    if not isinstance(spot, tuple):
        return spot
    shift, other = spot
    z, y = row // 2, row % 2
    return lax.rem(z - shift + count // 2, count // 2) * 2 + (1 - y if other else y)


def gather_direct(block, count):
    length = count // 2

    def along(shift, other, data):
        hops = [
            (z * 2 + y, (z + shift) % length * 2 + (1 - y if other else y))
            for z in range(length)
            for y in range(2)
        ]
        return lax.ppermute(data, "row", hops)

    shifts = list(range(length - 1, 0, -1))
    far = [along(shift, 0, block) for shift in shifts[:-1]]
    across = along(0, 1, block)
    passed = [along(0, 1, data) for data in far]
    near = []
    if shifts:
        after = lax.optimization_barrier((block, across))[0]
        near = [along(shifts[-1], 0, after)]
        after = lax.optimization_barrier((block, far[0]))[0] if far else block
        passed.append(along(shifts[-1], 1, after))
    return [block, across, *far, *near, *passed[::-1]]


PIECES = 4


def row_pieces(size):
    tall = size // PIECES
    return [pl.ds(at * tall, tall) for at in range(PIECES)]


def narrow_kernel(wide_ref, narrow_ref, held, sem):
    copies = [
        pltpu.make_async_copy(wide_ref.at[part], held.at[part], sem.at[at])
        for at, part in enumerate(row_pieces(held.shape[0]))
    ]
    for copy in copies:
        copy.start()
    for copy, part in zip(copies, row_pieces(held.shape[0])):
        copy.wait()
        narrow_ref[part, :] = held[part, :].astype(narrow_ref.dtype)


def prepare_kernel(spots, early, row_ref, *refs):
    far, (v_out, u_out, coef_out, weight_out, decay_out), near, sem = refs[:7], refs[7:12], refs[12:19], refs[19]
    copies = [
        pltpu.make_async_copy(source, held, sem.at[at])
        for at, (source, held) in enumerate(zip(far, near))
    ]
    for copy in copies:
        copy.start()
    for copy in copies:
        copy.wait()
    rank_ref, v_ref, u_ref, sigma_ref, a_ref, b_ref, state_ref = near
    kinds, rows, count, rank_count, size = u_ref.shape
    row = row_ref[0]
    met = [row_met(spot, row, count) for spot in spots]
    for at, q in enumerate(met):
        for p in range(rows):
            inside = lax.broadcasted_iota(jnp.int32, (rank_count, size), 0) < rank_ref[p, q]
            v_out[at, p] = jnp.where(inside, v_ref[p, q].astype(jnp.float32), 0.0).astype(v_out.dtype)
    for p in range(rows):
        for kind in range(kinds):
            for first, last in ((0, early), (early, count)):
                group = [u_ref[kind, p, q] for q in met[first:last]]
                if not group:
                    continue
                spare = -len(group) * rank_count % TILE
                if spare:
                    group.append(jnp.zeros((spare, size), u_ref.dtype))
                turned = jnp.concatenate(group, axis=0).astype(jnp.float32).T
                start = columns(first, last, early, rank_count).start
                u_out[p, kind * size : (kind + 1) * size, start : start + turned.shape[1]] = turned.astype(
                    u_out.dtype
                )
    lanes = coef_out.shape[2]
    for at, ref in enumerate((sigma_ref, a_ref, b_ref)):
        coef_out[at] = jnp.broadcast_to(ref[...], (lanes, size)).T
    for first in range(0, state_ref.shape[1], lanes):
        part = slice(first, first + lanes)
        state = state_ref[:, part]
        weight_out[:, part] = jnp.exp(-state / coef_out[1])
        decay_out[:, part] = jnp.exp(-state / coef_out[2])


def sums_kernel(spots, first, early, pick, before, row_ref, col_ref, near_ref, v_ref, u_ref, d_ref, *refs):
    blocks = refs[: len(spots)]
    refs = refs[len(spots) :]
    if before:
        sums_ref, refs = refs[0], refs[1:]
    out_ref, x_all, proj, total = refs
    count, rows, rank_count, size = v_ref.shape
    kinds, slots = d_ref.shape[0], near_ref.shape[1]
    row, col = row_ref[0], col_ref[0]
    met = [row_met(spot, row, count) for spot in spots]
    chosen = list(range(rows)) if pick is None else [col if pick == 0 else 1 - col]
    for at, block in enumerate(blocks):
        x_all[at] = block[...]
    for at, block in enumerate(blocks):
        if pick is None:
            weights = v_ref[first + at].reshape(rows * rank_count, size)
        else:
            weights = v_ref[first + at, chosen[0]]
        part = jnp.dot(weights, block[...], preferred_element_type=jnp.float32).astype(proj.dtype)
        for place in range(len(chosen)):
            proj[place, at * rank_count : (at + 1) * rank_count, :] = part[
                place * rank_count : (place + 1) * rank_count
            ]
    lanes = columns(first, first + len(blocks), early, rank_count)
    for place, p in enumerate(chosen):
        gained = jnp.dot(u_ref[p, :, lanes], proj[place], preferred_element_type=jnp.float32)
        for kind in range(kinds):
            piece = gained[kind * size : (kind + 1) * size]
            total[place, kind] = sums_ref[p, kind] + piece if before else piece
    for place, p in enumerate(chosen):
        for s in range(slots):
            near = near_ref[p, s] - col * count
            at = sum(jnp.where(near == q, i, 0) for i, q in enumerate(met))
            hit = sum(jnp.where(near == q, 1, 0) for q in met)

            @pl.when(hit > 0)
            def _():
                block = x_all[at]
                for kind in range(kinds):
                    total[place, kind] += jnp.dot(
                        d_ref[kind, p, s], block, preferred_element_type=jnp.float32
                    )
    for place in range(len(chosen)):
        for kind in range(kinds):
            if pick is None:
                out_ref[place, kind] = total[place, kind]
            else:
                out_ref[kind] = total[place, kind].astype(out_ref.dtype)


def inverse_sinh(value):
    magnitude = jnp.abs(value)
    result = jnp.log(magnitude + jnp.sqrt(magnitude * magnitude + 1.0))
    return jnp.where(value < 0.0, -result, result)


def sinh_cosh(value):
    grown = jnp.exp(value)
    shrunk = jnp.exp(-value)
    square = value * value
    small = value * (
        1.0 + square * (1 / 6 + square * (1 / 120 + square * (1 / 5040 + square * (1 / 362880))))
    )
    sinh = jnp.where(square < 1.0, small, 0.5 * (grown - shrunk))
    return sinh, 0.5 * (grown + shrunk)


def friction(shear, normal, weight, decay, tau_load, sigma_base, a_wide, b_wide):
    tau = tau_load + shear
    sigma = jnp.maximum(sigma_base + normal, sigma_floor)
    stiff = sigma * a_wide
    first = tau / stiff
    second = inverse_sinh(tau / (2.0 * damping * weight))
    slope = jnp.where(jnp.abs(first) < jnp.abs(second), first, second)
    for newton_step in range(NEWTON):
        sinh, cosh = sinh_cosh(slope)
        excess = stiff * slope + 2.0 * damping * weight * sinh - tau
        deriv = stiff + 2.0 * damping * weight * cosh
        slope = slope - excess / deriv
    rate = 2.0 * weight * sinh_cosh(slope)[0]
    change = b_wide * (decay - jnp.abs(rate))
    return (rate, change)


def over_pieces(begin, tall, members, lanes, work):
    step = min(tall, 16)

    @pl.loop(0, tall // step)
    def _(index):
        rows = pl.ds(pl.multiple_of(begin + index * step, step), step)
        for first in range(0, members, lanes):
            work(rows, slice(first, first + lanes))


def section_one_kernel(own, other, weight, decay, tau, coef, stress, normal, rate, change, rate_half):
    size, members = tau.shape

    def work(rows, part):
        shear = own[0, rows, part] + other[0, rows, part].astype(jnp.float32)
        press = own[1, rows, part] + other[1, rows, part].astype(jnp.float32)
        stress[rows, part] = shear
        normal[rows, part] = press
        first, second = friction(
            shear,
            press,
            weight[rows, part],
            decay[rows, part],
            tau[rows, part],
            coef[0, rows, :],
            coef[1, rows, :],
            coef[2, rows, :],
        )
        rate[rows, part] = first
        change[rows, part] = second
        rate_half[rows, part] = first.astype(rate_half.dtype)

    over_pieces(0, size, members, coef.shape[2], work)


def section_two_kernel(
    own, other, state, tau, coef, stress, normal, rate, change, rate_out, change_out, mean_rate, mean_change, sem
):
    size, members = tau.shape

    def work(rows, part):
        shear = own[0, rows, part] + other[0, rows, part].astype(jnp.float32)
        press = own[1, rows, part] + other[1, rows, part].astype(jnp.float32)
        sigma, a_wide, b_wide = coef[0, rows, :], coef[1, rows, :], coef[2, rows, :]
        later = state[rows, part] + section_step * change[rows, part]
        first, second = friction(
            stress[rows, part] + section_step * shear,
            normal[rows, part] + section_step * press,
            jnp.exp(-later / a_wide),
            jnp.exp(-later / b_wide),
            tau[rows, part],
            sigma,
            a_wide,
            b_wide,
        )
        mean_rate[rows, part] = (rate[rows, part] + first) * 0.5
        mean_change[rows, part] = (change[rows, part] + second) * 0.5

    copies = []
    for at, part in enumerate(row_pieces(size)):
        over_pieces(part.start, part.size, members, coef.shape[2], work)
        for kind, (held, out) in enumerate(((mean_rate, rate_out), (mean_change, change_out))):
            copies.append(pltpu.make_async_copy(held.at[part], out.at[part], sem.at[kind, at]))
            copies[-1].start()
    for copy in copies:
        copy.wait()


def on_core(kernel, outs, scalars, arrays, scratch=(), flops=0, room=16, far=(), out_far=False):
    smem, vmem = pl.BlockSpec(memory_space=pltpu.SMEM), pl.BlockSpec(memory_space=pltpu.VMEM)
    hbm = pl.BlockSpec(memory_space=pl.ANY)
    arrays = (*(pltpu.with_memory_space_constraint(a, pltpu.HBM) for a in far), *arrays)
    return pl.pallas_call(
        kernel,
        out_shape=outs,
        in_specs=[smem] * len(scalars) + [hbm] * len(far) + [vmem] * (len(arrays) - len(far)),
        out_specs=jax.tree.map(lambda _: hbm if out_far else vmem, outs),
        scratch_shapes=list(scratch),
        compiler_params=pltpu.CompilerParams(vmem_limit_bytes=room * 1024 * 1024),
        cost_estimate=pl.CostEstimate(
            flops=flops, bytes_accessed=sum(a.size * a.dtype.itemsize for a in arrays), transcendentals=0
        ),
    )(*scalars, *arrays)


def body(
    slip_deficit,
    state_var,
    tau_load,
    sigma_base,
    a_coef,
    b_coef,
    v_basis,
    u_basis,
    dense_blocks,
    block_ranks,
    near_index,
):
    count = lax.axis_size("row")
    size, members = slip_deficit.shape
    kinds, rows, _, rank_count, _ = u_basis.shape
    direct = count % 2 == 0 and count <= DIRECT_LIMIT
    spots = arrivals(count, direct)
    early = max(count - LATE, 0)
    width = -(-columns(early, count, early, rank_count).stop // TILE) * TILE
    room = 16 if direct else 40
    lanes = min(members, 128)
    narrow, wide = jnp.bfloat16, jnp.float32
    row, col = lax.axis_index("row").reshape(1), lax.axis_index("col").reshape(1)
    swap = [(0, 1), (1, 0)]

    def shaped(*shape, kind=wide):
        return jax.ShapeDtypeStruct(shape, kind)

    full = shaped(size, members)
    v_met, u_met, coef, weight, decay = on_core(
        functools.partial(prepare_kernel, spots, early),
        (
            shaped(count, rows, rank_count, size, kind=narrow),
            shaped(rows, kinds * size, width, kind=narrow),
            shaped(3, size, lanes),
            full,
            full,
        ),
        (row,),
        (),
        (
            pltpu.SMEM(block_ranks.shape, jnp.int32),
            pltpu.VMEM(v_basis.shape, narrow),
            pltpu.VMEM(u_basis.shape, narrow),
            *[pltpu.VMEM((1, size), wide)] * 3,
            pltpu.VMEM((size, members), wide),
            pltpu.SemaphoreType.DMA((7,)),
        ),
        room=room,
        far=(
            block_ranks,
            v_basis,
            u_basis,
            sigma_base.reshape(1, size),
            a_coef.reshape(1, size),
            b_coef.reshape(1, size),
            state_var,
        ),
    )

    def add(blocks, first, pick, before, kind):
        held = rows if pick is None else 1
        lead = (rows, kinds) if pick is None else (kinds,)
        return on_core(
            functools.partial(
                sums_kernel, spots[first : first + len(blocks)], first, early, pick, before is not None
            ),
            shaped(*lead, size, members, kind=kind),
            (row, col, near_index),
            (v_met, u_met, dense_blocks, *blocks, *(() if before is None else (before,))),
            (
                pltpu.VMEM((len(blocks), size, members), narrow),
                pltpu.VMEM((held, len(blocks) * rank_count, members), narrow),
                pltpu.VMEM((held, kinds, size, members), wide),
            ),
            2 * held * size * members * rank_count * len(blocks) * 3,
            room,
        )

    def lattice(field_half):
        if direct:
            blocks = gather_direct(field_half, count)
        else:
            whole = lax.all_gather(field_half, "row", axis=0)
            blocks = [whole[r] for r in range(count)]
        sums = add(blocks[:early], 0, None, None, wide) if early else None
        other = lax.ppermute(add(blocks[early:], early, 1, sums, narrow), "col", swap)
        return add(blocks[early:], early, 0, sums, wide), other

    slip_half = on_core(
        narrow_kernel,
        shaped(size, members, kind=narrow),
        (),
        (),
        (pltpu.VMEM((size, members), wide), pltpu.SemaphoreType.DMA((PIECES,))),
        far=(slip_deficit,),
    )
    own, other = lattice(slip_half)
    stress, normal, rate, change, rate_half = on_core(
        section_one_kernel,
        (full, full, full, full, shaped(size, members, kind=narrow)),
        (),
        (own, other, weight, decay, tau_load, coef),
        flops=200 * size * members,
    )
    own, other = lattice(rate_half)
    return on_core(
        section_two_kernel,
        (full, full),
        (),
        (own, other, state_var, tau_load, coef, stress, normal, rate, change),
        (
            pltpu.VMEM((size, members), wide),
            pltpu.VMEM((size, members), wide),
            pltpu.SemaphoreType.DMA((2, PIECES)),
        ),
        flops=200 * size * members,
        out_far=True,
    )


def solution(mesh):
    placed = (
        P(("row", "col"), "scen"),
        P(("row", "col"), "scen"),
        P(("row", "col"), "scen"),
        P(("row", "col")),
        P(("row", "col")),
        P(("row", "col")),
        P("row", "col", None, None),
        P(None, "row", "col", None, None),
        P(None, "row", "col", None, None),
        P("row", "col"),
        P("row", "col"),
    )
    return jax.shard_map(
        body,
        mesh=mesh,
        in_specs=placed,
        out_specs=(P(("row", "col"), "scen"), P(("row", "col"), "scen")),
        check_vma=False,
    )
```

```python
import functools

import jax
import jax.numpy as jnp
from jax import lax
from jax.experimental import pallas as pl
from jax.experimental.pallas import tpu as pltpu
from jax.sharding import PartitionSpec as P

NEWTON = 2
DIRECT_LIMIT = 16
TILE = 128

damping = 0.5
sigma_floor = 0.5
section_step = 0.1


def arrivals(count, direct):
    if not direct:
        cuts = [0, max(count - 4, 1), max(count - 2, 1), count]
        groups = [list(range(first, last)) for first, last in zip(cuts, cuts[1:])]
        return [group for group in groups if group]
    length = count // 2
    split = length // 2
    whole = [shift for shift in range(1, length) if shift != split]
    first = [(0, 0), (0, 1)] + [(shift, 0) for shift in whole]
    passed = [(shift, 1) for shift in whole]
    return [group for group in (first, passed, [(split, 0), (split, 1)]) if group]


def row_met(spot, row, count):
    if not isinstance(spot, tuple):
        return spot
    shift, other = spot
    z, y = row // 2, row % 2
    return lax.rem(z - shift + count // 2, count // 2) * 2 + (1 - y if other else y)


def gather_direct(block, top, low, count):
    length = count // 2
    split = length // 2

    def along(shift, other, data):
        hops = [
            (z * 2 + y, (z + shift) % length * 2 + (1 - y if other else y))
            for z in range(length)
            for y in range(2)
        ]
        return lax.ppermute(data, "row", hops)

    whole = [along(shift, 0, block) for shift in range(1, length) if shift != split]
    split_top = along(split, 0, top)
    across = along(0, 1, block)
    split_low, split_far = along(split, 0, low), along(split, 1, low)
    passed = [along(0, 1, data) for data in whole]
    far_top = along(0, 1, split_top)
    groups = [[(block,), (across,)] + [(data,) for data in whole]]
    groups += [[(data,) for data in passed]] if passed else []
    return groups + [[(split_top, split_low), (far_top, split_far)]]


PIECES = 4


def row_pieces(size):
    tall = size // PIECES
    return [pl.ds(at * tall, tall) for at in range(PIECES)]


def store_half(outs, rows, part, value):
    whole, top, low = outs
    whole[rows, part] = value
    half = top.shape[0]

    @pl.when(rows.start < half)
    def _():
        top[rows, part] = value

    @pl.when(rows.start >= half)
    def _():
        low[pl.ds(pl.multiple_of(rows.start - half, 16), rows.size), part] = value


def narrow_kernel(wide_ref, whole, top, low, held, sem):
    copies = [
        pltpu.make_async_copy(wide_ref.at[part], held.at[part], sem.at[at])
        for at, part in enumerate(row_pieces(held.shape[0]))
    ]
    for copy in copies:
        copy.start()
    for copy, part in zip(copies, row_pieces(held.shape[0])):
        copy.wait()
        store_half((whole, top, low), part, slice(None), held[part, :].astype(whole.dtype))


def prepare_kernel(groups, row_ref, *refs):
    far, (v_out, u_out, coef_out, weight_out, decay_out), near, sem = refs[:7], refs[7:12], refs[12:19], refs[19]
    copies = [
        pltpu.make_async_copy(source, held, sem.at[at])
        for at, (source, held) in enumerate(zip(far, near))
    ]
    for copy in copies:
        copy.start()
    for copy in copies:
        copy.wait()
    rank_ref, v_ref, u_ref, sigma_ref, a_ref, b_ref, state_ref = near
    kinds, rows, count, rank_count, size = u_ref.shape
    row = row_ref[0]
    met = [row_met(spot, row, count) for group in groups for spot in group]
    for at, q in enumerate(met):
        for p in range(rows):
            inside = lax.broadcasted_iota(jnp.int32, (rank_count, size), 0) < rank_ref[p, q]
            v_out[at, p] = jnp.where(inside, v_ref[p, q].astype(jnp.float32), 0.0).astype(v_out.dtype)
    for p in range(rows):
        for kind in range(kinds):
            first = start = 0
            for spots in groups:
                group = [u_ref[kind, p, q] for q in met[first : first + len(spots)]]
                spare = -len(group) * rank_count % TILE
                if spare:
                    group.append(jnp.zeros((spare, size), u_ref.dtype))
                turned = jnp.concatenate(group, axis=0).astype(jnp.float32).T
                stop = start + turned.shape[1]
                u_out[p, kind * size : (kind + 1) * size, start:stop] = turned.astype(u_out.dtype)
                first, start = first + len(spots), stop
    lanes = coef_out.shape[2]
    for at, ref in enumerate((sigma_ref, a_ref, b_ref)):
        coef_out[at] = jnp.broadcast_to(ref[...], (lanes, size)).T
    for first in range(0, state_ref.shape[1], lanes):
        part = slice(first, first + lanes)
        state = state_ref[:, part]
        weight_out[:, part] = jnp.exp(-state / coef_out[1])
        decay_out[:, part] = jnp.exp(-state / coef_out[2])


def sums_kernel(spots, pieces, first, start, pick, before, row_ref, col_ref, near_ref, v_ref, u_ref, d_ref, *refs):
    blocks = [refs[sum(pieces[:at]) : sum(pieces[: at + 1])] for at in range(len(pieces))]
    refs = refs[sum(pieces) :]
    if before:
        sums_ref, refs = refs[0], refs[1:]
    out_ref, x_all, proj, total = refs
    count, rows, rank_count, size = v_ref.shape
    kinds, slots = d_ref.shape[0], near_ref.shape[1]
    row, col = row_ref[0], col_ref[0]
    met = [row_met(spot, row, count) for spot in spots]
    chosen = list(range(rows)) if pick is None else [col if pick == 0 else 1 - col]
    for at, parts in enumerate(blocks):
        tall = size // len(parts)
        for place, part in enumerate(parts):
            x_all[at, place * tall : (place + 1) * tall, :] = part[...]
    for at in range(len(blocks)):
        if pick is None:
            weights = v_ref[first + at].reshape(rows * rank_count, size)
        else:
            weights = v_ref[first + at, chosen[0]]
        part = jnp.dot(weights, x_all[at], preferred_element_type=jnp.float32).astype(proj.dtype)
        for place in range(len(chosen)):
            proj[place, at * rank_count : (at + 1) * rank_count, :] = part[
                place * rank_count : (place + 1) * rank_count
            ]
    lanes = slice(start, start + len(blocks) * rank_count)
    for place, p in enumerate(chosen):
        gained = jnp.dot(u_ref[p, :, lanes], proj[place], preferred_element_type=jnp.float32)
        for kind in range(kinds):
            piece = gained[kind * size : (kind + 1) * size]
            total[place, kind] = sums_ref[p, kind] + piece if before else piece
    for place, p in enumerate(chosen):
        for s in range(slots):
            near = near_ref[p, s] - col * count
            at = sum(jnp.where(near == q, i, 0) for i, q in enumerate(met))
            hit = sum(jnp.where(near == q, 1, 0) for q in met)

            @pl.when(hit > 0)
            def _():
                block = x_all[at]
                for kind in range(kinds):
                    total[place, kind] += jnp.dot(
                        d_ref[kind, p, s], block, preferred_element_type=jnp.float32
                    )
    for place in range(len(chosen)):
        for kind in range(kinds):
            if pick is None:
                out_ref[place, kind] = total[place, kind]
            else:
                out_ref[kind] = total[place, kind].astype(out_ref.dtype)


def inverse_sinh(value):
    magnitude = jnp.abs(value)
    result = jnp.log(magnitude + jnp.sqrt(magnitude * magnitude + 1.0))
    return jnp.where(value < 0.0, -result, result)


def sinh_cosh(value):
    grown = jnp.exp(value)
    shrunk = jnp.exp(-value)
    square = value * value
    small = value * (
        1.0 + square * (1 / 6 + square * (1 / 120 + square * (1 / 5040 + square * (1 / 362880))))
    )
    sinh = jnp.where(square < 1.0, small, 0.5 * (grown - shrunk))
    return sinh, 0.5 * (grown + shrunk)


def friction(shear, normal, weight, decay, tau_load, sigma_base, a_wide, b_wide):
    tau = tau_load + shear
    sigma = jnp.maximum(sigma_base + normal, sigma_floor)
    stiff = sigma * a_wide
    first = tau / stiff
    second = inverse_sinh(tau / (2.0 * damping * weight))
    slope = jnp.where(jnp.abs(first) < jnp.abs(second), first, second)
    for newton_step in range(NEWTON):
        sinh, cosh = sinh_cosh(slope)
        excess = stiff * slope + 2.0 * damping * weight * sinh - tau
        deriv = stiff + 2.0 * damping * weight * cosh
        slope = slope - excess / deriv
    rate = 2.0 * weight * sinh_cosh(slope)[0]
    change = b_wide * (decay - jnp.abs(rate))
    return (rate, change)


def over_pieces(begin, tall, members, lanes, work):
    step = min(tall, 16)

    @pl.loop(0, tall // step)
    def _(index):
        rows = pl.ds(pl.multiple_of(begin + index * step, step), step)
        for first in range(0, members, lanes):
            work(rows, slice(first, first + lanes))


def section_one_kernel(own, other, weight, decay, tau, coef, stress, normal, rate, change, *rate_half):
    size, members = tau.shape

    def work(rows, part):
        shear = own[0, rows, part] + other[0, rows, part].astype(jnp.float32)
        press = own[1, rows, part] + other[1, rows, part].astype(jnp.float32)
        stress[rows, part] = shear
        normal[rows, part] = press
        first, second = friction(
            shear,
            press,
            weight[rows, part],
            decay[rows, part],
            tau[rows, part],
            coef[0, rows, :],
            coef[1, rows, :],
            coef[2, rows, :],
        )
        rate[rows, part] = first
        change[rows, part] = second
        store_half(rate_half, rows, part, first.astype(rate_half[0].dtype))

    over_pieces(0, size, members, coef.shape[2], work)


def section_two_kernel(
    own, other, state, tau, coef, stress, normal, rate, change, rate_out, change_out, mean_rate, mean_change, sem
):
    size, members = tau.shape

    def work(rows, part):
        shear = own[0, rows, part] + other[0, rows, part].astype(jnp.float32)
        press = own[1, rows, part] + other[1, rows, part].astype(jnp.float32)
        sigma, a_wide, b_wide = coef[0, rows, :], coef[1, rows, :], coef[2, rows, :]
        later = state[rows, part] + section_step * change[rows, part]
        first, second = friction(
            stress[rows, part] + section_step * shear,
            normal[rows, part] + section_step * press,
            jnp.exp(-later / a_wide),
            jnp.exp(-later / b_wide),
            tau[rows, part],
            sigma,
            a_wide,
            b_wide,
        )
        mean_rate[rows, part] = (rate[rows, part] + first) * 0.5
        mean_change[rows, part] = (change[rows, part] + second) * 0.5

    copies = []
    for at, part in enumerate(row_pieces(size)):
        over_pieces(part.start, part.size, members, coef.shape[2], work)
        for kind, (held, out) in enumerate(((mean_rate, rate_out), (mean_change, change_out))):
            copies.append(pltpu.make_async_copy(held.at[part], out.at[part], sem.at[kind, at]))
            copies[-1].start()
    for copy in copies:
        copy.wait()


def on_core(kernel, outs, scalars, arrays, scratch=(), flops=0, room=16, far=(), out_far=False):
    smem, vmem = pl.BlockSpec(memory_space=pltpu.SMEM), pl.BlockSpec(memory_space=pltpu.VMEM)
    hbm = pl.BlockSpec(memory_space=pl.ANY)
    arrays = (*(pltpu.with_memory_space_constraint(a, pltpu.HBM) for a in far), *arrays)
    return pl.pallas_call(
        kernel,
        out_shape=outs,
        in_specs=[smem] * len(scalars) + [hbm] * len(far) + [vmem] * (len(arrays) - len(far)),
        out_specs=jax.tree.map(lambda _: hbm if out_far else vmem, outs),
        scratch_shapes=list(scratch),
        compiler_params=pltpu.CompilerParams(vmem_limit_bytes=room * 1024 * 1024),
        cost_estimate=pl.CostEstimate(
            flops=flops, bytes_accessed=sum(a.size * a.dtype.itemsize for a in arrays), transcendentals=0
        ),
    )(*scalars, *arrays)


def body(
    slip_deficit,
    state_var,
    tau_load,
    sigma_base,
    a_coef,
    b_coef,
    v_basis,
    u_basis,
    dense_blocks,
    block_ranks,
    near_index,
):
    count = lax.axis_size("row")
    size, members = slip_deficit.shape
    kinds, rows, _, rank_count, _ = u_basis.shape
    direct = count % 2 == 0 and 4 <= count <= DIRECT_LIMIT
    groups = arrivals(count, direct)
    firsts = [sum(len(group) for group in groups[:at]) for at in range(len(groups))]
    tiles = [-(-len(group) * rank_count // TILE) * TILE for group in groups]
    starts = [sum(tiles[:at]) for at in range(len(groups))]
    room = 16 if direct else 40
    lanes = min(members, 128)
    narrow, wide = jnp.bfloat16, jnp.float32
    row, col = lax.axis_index("row").reshape(1), lax.axis_index("col").reshape(1)
    swap = [(0, 1), (1, 0)]

    def shaped(*shape, kind=wide):
        return jax.ShapeDtypeStruct(shape, kind)

    full = shaped(size, members)
    v_met, u_met, coef, weight, decay = on_core(
        functools.partial(prepare_kernel, groups),
        (
            shaped(count, rows, rank_count, size, kind=narrow),
            shaped(rows, kinds * size, sum(tiles), kind=narrow),
            shaped(3, size, lanes),
            full,
            full,
        ),
        (row,),
        (),
        (
            pltpu.SMEM(block_ranks.shape, jnp.int32),
            pltpu.VMEM(v_basis.shape, narrow),
            pltpu.VMEM(u_basis.shape, narrow),
            *[pltpu.VMEM((1, size), wide)] * 3,
            pltpu.VMEM((size, members), wide),
            pltpu.SemaphoreType.DMA((7,)),
        ),
        room=room,
        far=(
            block_ranks,
            v_basis,
            u_basis,
            sigma_base.reshape(1, size),
            a_coef.reshape(1, size),
            b_coef.reshape(1, size),
            state_var,
        ),
    )

    def add(blocks, at, pick, before, kind):
        held = rows if pick is None else 1
        lead = (rows, kinds) if pick is None else (kinds,)
        pieces = tuple(len(parts) for parts in blocks)
        return on_core(
            functools.partial(
                sums_kernel, groups[at], pieces, firsts[at], starts[at], pick, before is not None
            ),
            shaped(*lead, size, members, kind=kind),
            (row, col, near_index),
            (
                v_met,
                u_met,
                dense_blocks,
                *[part for parts in blocks for part in parts],
                *(() if before is None else (before,)),
            ),
            (
                pltpu.VMEM((len(blocks), size, members), narrow),
                pltpu.VMEM((held, len(blocks) * rank_count, members), narrow),
                pltpu.VMEM((held, kinds, size, members), wide),
            ),
            2 * held * size * members * rank_count * len(blocks) * 3,
            room,
        )

    def lattice(block, top, low):
        if direct:
            found = gather_direct(block, top, low, count)
        else:
            whole = lax.all_gather(block, "row", axis=0)
            found = [[(whole[r],) for r in group] for group in groups]
        sums = None
        for at in range(len(groups) - 1):
            sums = add(found[at], at, None, sums, wide)
        other = lax.ppermute(add(found[-1], len(groups) - 1, 1, sums, narrow), "col", swap)
        return add(found[-1], len(groups) - 1, 0, sums, wide), other

    halves = (
        shaped(size, members, kind=narrow),
        shaped(size // 2, members, kind=narrow),
        shaped(size // 2, members, kind=narrow),
    )
    slip_half = on_core(
        narrow_kernel,
        halves,
        (),
        (),
        (pltpu.VMEM((size, members), wide), pltpu.SemaphoreType.DMA((PIECES,))),
        far=(slip_deficit,),
    )
    own, other = lattice(*slip_half)
    stress, normal, rate, change, *rate_half = on_core(
        section_one_kernel,
        (full, full, full, full, *halves),
        (),
        (own, other, weight, decay, tau_load, coef),
        flops=200 * size * members,
    )
    own, other = lattice(*rate_half)
    return on_core(
        section_two_kernel,
        (full, full),
        (),
        (own, other, state_var, tau_load, coef, stress, normal, rate, change),
        (
            pltpu.VMEM((size, members), wide),
            pltpu.VMEM((size, members), wide),
            pltpu.SemaphoreType.DMA((2, PIECES)),
        ),
        flops=200 * size * members,
        out_far=True,
    )


def solution(mesh):
    placed = (
        P(("row", "col"), "scen"),
        P(("row", "col"), "scen"),
        P(("row", "col"), "scen"),
        P(("row", "col")),
        P(("row", "col")),
        P(("row", "col")),
        P("row", "col", None, None),
        P(None, "row", "col", None, None),
        P(None, "row", "col", None, None),
        P("row", "col"),
        P("row", "col"),
    )
    return jax.shard_map(
        body,
        mesh=mesh,
        in_specs=placed,
        out_specs=(P(("row", "col"), "scen"), P(("row", "col"), "scen")),
        check_vma=False,
    )
```

```python
import functools

import jax
import jax.numpy as jnp
from jax import lax
from jax.experimental import pallas as pl
from jax.experimental.pallas import tpu as pltpu
from jax.sharding import PartitionSpec as P

NEWTON = 2
DIRECT_COUNTS = (4, 8)
LATE = 4

damping = 0.5
sigma_floor = 0.5
section_step = 0.1


def arrivals(count, direct):
    if not direct:
        return list(range(count))
    return [0, 1, 4, 2, 3, 5, 6, 7] if count == 8 else [0, 1, 2, 3]


def row_met(spot, row, direct):
    return jnp.bitwise_xor(row, spot) if direct else spot


def gather_direct(block, count):
    def swapped(mask, data):
        return lax.ppermute(data, "row", [(row, row ^ mask) for row in range(count)])

    found = {0: block}
    for mask in (4, 1, 2, 3) if count == 8 else (1, 2, 3):
        found[mask] = swapped(mask, block)
    if count == 8:
        for mask in (1, 2, 3):
            found[4 + mask] = swapped(mask, found[4])
    return [found[mask] for mask in arrivals(count, True)]


PIECES = 4


def row_pieces(size):
    tall = size // PIECES
    return [pl.ds(at * tall, tall) for at in range(PIECES)]


def narrow_kernel(wide_ref, narrow_ref, held, sem):
    copies = [
        pltpu.make_async_copy(wide_ref.at[part], held.at[part], sem.at[at])
        for at, part in enumerate(row_pieces(held.shape[0]))
    ]
    for copy in copies:
        copy.start()
    for copy, part in zip(copies, row_pieces(held.shape[0])):
        copy.wait()
        narrow_ref[part, :] = held[part, :].astype(narrow_ref.dtype)


def prepare_kernel(spots, direct, row_ref, *refs):
    far, (v_out, u_out, coef_out, weight_out, decay_out), near, sem = refs[:7], refs[7:12], refs[12:19], refs[19]
    copies = [
        pltpu.make_async_copy(source, held, sem.at[at])
        for at, (source, held) in enumerate(zip(far, near))
    ]
    for copy in copies:
        copy.start()
    for copy in copies:
        copy.wait()
    rank_ref, v_ref, u_ref, sigma_ref, a_ref, b_ref, state_ref = near
    kinds, rows, count, rank_count, size = u_ref.shape
    row = row_ref[0]
    met = [row_met(spot, row, direct) for spot in spots]
    for at, q in enumerate(met):
        for p in range(rows):
            inside = lax.broadcasted_iota(jnp.int32, (rank_count, size), 0) < rank_ref[p, q]
            v_out[at, p] = jnp.where(inside, v_ref[p, q].astype(jnp.float32), 0.0).astype(v_out.dtype)
    for p in range(rows):
        for kind in range(kinds):
            for first in range(0, count, 4):
                group = [u_ref[kind, p, q] for q in met[first : first + 4]]
                turned = jnp.concatenate(group, axis=0).astype(jnp.float32).T
                u_out[p, kind * size : (kind + 1) * size, first * rank_count : (first + len(group)) * rank_count] = (
                    turned.astype(u_out.dtype)
                )
    lanes = coef_out.shape[2]
    for at, ref in enumerate((sigma_ref, a_ref, b_ref)):
        coef_out[at] = jnp.broadcast_to(ref[...], (lanes, size)).T
    for first in range(0, state_ref.shape[1], lanes):
        part = slice(first, first + lanes)
        state = state_ref[:, part]
        weight_out[:, part] = jnp.exp(-state / coef_out[1])
        decay_out[:, part] = jnp.exp(-state / coef_out[2])


def sums_kernel(spots, direct, first, pick, before, row_ref, col_ref, near_ref, v_ref, u_ref, d_ref, *refs):
    blocks = refs[: len(spots)]
    refs = refs[len(spots) :]
    if before:
        sums_ref, refs = refs[0], refs[1:]
    out_ref, x_all, proj, total = refs
    count, rows, rank_count, size = v_ref.shape
    kinds, slots = d_ref.shape[0], near_ref.shape[1]
    row, col = row_ref[0], col_ref[0]
    met = [row_met(spot, row, direct) for spot in spots]
    chosen = list(range(rows)) if pick is None else [col if pick == 0 else 1 - col]
    for at, block in enumerate(blocks):
        x_all[at] = block[...]
    for at, block in enumerate(blocks):
        if pick is None:
            weights = v_ref[first + at].reshape(rows * rank_count, size)
        else:
            weights = v_ref[first + at, chosen[0]]
        part = jnp.dot(weights, block[...], preferred_element_type=jnp.float32).astype(proj.dtype)
        for place in range(len(chosen)):
            proj[place, at * rank_count : (at + 1) * rank_count, :] = part[
                place * rank_count : (place + 1) * rank_count
            ]
    lanes = slice(first * rank_count, (first + len(blocks)) * rank_count)
    for place, p in enumerate(chosen):
        gained = jnp.dot(u_ref[p, :, lanes], proj[place], preferred_element_type=jnp.float32)
        for kind in range(kinds):
            piece = gained[kind * size : (kind + 1) * size]
            total[place, kind] = sums_ref[p, kind] + piece if before else piece
    for place, p in enumerate(chosen):
        for s in range(slots):
            near = near_ref[p, s] - col * count
            at = sum(jnp.where(near == q, i, 0) for i, q in enumerate(met))
            hit = sum(jnp.where(near == q, 1, 0) for q in met)

            @pl.when(hit > 0)
            def _():
                block = x_all[at]
                for kind in range(kinds):
                    total[place, kind] += jnp.dot(
                        d_ref[kind, p, s], block, preferred_element_type=jnp.float32
                    )
    for place in range(len(chosen)):
        for kind in range(kinds):
            if pick is None:
                out_ref[place, kind] = total[place, kind]
            else:
                out_ref[kind] = total[place, kind].astype(out_ref.dtype)


def inverse_sinh(value):
    magnitude = jnp.abs(value)
    result = jnp.log(magnitude + jnp.sqrt(magnitude * magnitude + 1.0))
    return jnp.where(value < 0.0, -result, result)


def sinh_cosh(value):
    grown = jnp.exp(value)
    shrunk = jnp.exp(-value)
    square = value * value
    small = value * (
        1.0 + square * (1 / 6 + square * (1 / 120 + square * (1 / 5040 + square * (1 / 362880))))
    )
    sinh = jnp.where(square < 1.0, small, 0.5 * (grown - shrunk))
    return sinh, 0.5 * (grown + shrunk)


def friction(shear, normal, weight, decay, tau_load, sigma_base, a_wide, b_wide):
    tau = tau_load + shear
    sigma = jnp.maximum(sigma_base + normal, sigma_floor)
    stiff = sigma * a_wide
    first = tau / stiff
    second = inverse_sinh(tau / (2.0 * damping * weight))
    slope = jnp.where(jnp.abs(first) < jnp.abs(second), first, second)
    for newton_step in range(NEWTON):
        sinh, cosh = sinh_cosh(slope)
        excess = stiff * slope + 2.0 * damping * weight * sinh - tau
        deriv = stiff + 2.0 * damping * weight * cosh
        slope = slope - excess / deriv
    rate = 2.0 * weight * sinh_cosh(slope)[0]
    change = b_wide * (decay - jnp.abs(rate))
    return (rate, change)


def over_pieces(begin, tall, members, lanes, work):
    step = min(tall, 16)

    @pl.loop(0, tall // step)
    def _(index):
        rows = pl.ds(pl.multiple_of(begin + index * step, step), step)
        for first in range(0, members, lanes):
            work(rows, slice(first, first + lanes))


def section_one_kernel(own, other, weight, decay, tau, coef, stress, normal, rate, change, rate_half):
    size, members = tau.shape

    def work(rows, part):
        shear = own[0, rows, part] + other[0, rows, part].astype(jnp.float32)
        press = own[1, rows, part] + other[1, rows, part].astype(jnp.float32)
        stress[rows, part] = shear
        normal[rows, part] = press
        first, second = friction(
            shear,
            press,
            weight[rows, part],
            decay[rows, part],
            tau[rows, part],
            coef[0, rows, :],
            coef[1, rows, :],
            coef[2, rows, :],
        )
        rate[rows, part] = first
        change[rows, part] = second
        rate_half[rows, part] = first.astype(rate_half.dtype)

    over_pieces(0, size, members, coef.shape[2], work)


def section_two_kernel(
    own, other, state, tau, coef, stress, normal, rate, change, rate_out, change_out, mean_rate, mean_change, sem
):
    size, members = tau.shape

    def work(rows, part):
        shear = own[0, rows, part] + other[0, rows, part].astype(jnp.float32)
        press = own[1, rows, part] + other[1, rows, part].astype(jnp.float32)
        sigma, a_wide, b_wide = coef[0, rows, :], coef[1, rows, :], coef[2, rows, :]
        later = state[rows, part] + section_step * change[rows, part]
        first, second = friction(
            stress[rows, part] + section_step * shear,
            normal[rows, part] + section_step * press,
            jnp.exp(-later / a_wide),
            jnp.exp(-later / b_wide),
            tau[rows, part],
            sigma,
            a_wide,
            b_wide,
        )
        mean_rate[rows, part] = (rate[rows, part] + first) * 0.5
        mean_change[rows, part] = (change[rows, part] + second) * 0.5

    copies = []
    for at, part in enumerate(row_pieces(size)):
        over_pieces(part.start, part.size, members, coef.shape[2], work)
        for kind, (held, out) in enumerate(((mean_rate, rate_out), (mean_change, change_out))):
            copies.append(pltpu.make_async_copy(held.at[part], out.at[part], sem.at[kind, at]))
            copies[-1].start()
    for copy in copies:
        copy.wait()


def on_core(kernel, outs, scalars, arrays, scratch=(), flops=0, room=16, far=(), out_far=False):
    smem, vmem = pl.BlockSpec(memory_space=pltpu.SMEM), pl.BlockSpec(memory_space=pltpu.VMEM)
    hbm = pl.BlockSpec(memory_space=pl.ANY)
    arrays = (*(pltpu.with_memory_space_constraint(a, pltpu.HBM) for a in far), *arrays)
    return pl.pallas_call(
        kernel,
        out_shape=outs,
        in_specs=[smem] * len(scalars) + [hbm] * len(far) + [vmem] * (len(arrays) - len(far)),
        out_specs=jax.tree.map(lambda _: hbm if out_far else vmem, outs),
        scratch_shapes=list(scratch),
        compiler_params=pltpu.CompilerParams(vmem_limit_bytes=room * 1024 * 1024),
        cost_estimate=pl.CostEstimate(
            flops=flops, bytes_accessed=sum(a.size * a.dtype.itemsize for a in arrays), transcendentals=0
        ),
    )(*scalars, *arrays)


def body(
    slip_deficit,
    state_var,
    tau_load,
    sigma_base,
    a_coef,
    b_coef,
    v_basis,
    u_basis,
    dense_blocks,
    block_ranks,
    near_index,
):
    count = lax.axis_size("row")
    size, members = slip_deficit.shape
    kinds, rows, _, rank_count, _ = u_basis.shape
    direct = count in DIRECT_COUNTS
    spots = arrivals(count, direct)
    early = max(count - LATE, 0)
    room = 16 if direct else 40
    lanes = min(members, 128)
    narrow, wide = jnp.bfloat16, jnp.float32
    row, col = lax.axis_index("row").reshape(1), lax.axis_index("col").reshape(1)
    swap = [(0, 1), (1, 0)]

    def shaped(*shape, kind=wide):
        return jax.ShapeDtypeStruct(shape, kind)

    full = shaped(size, members)
    v_met, u_met, coef, weight, decay = on_core(
        functools.partial(prepare_kernel, spots, direct),
        (
            shaped(count, rows, rank_count, size, kind=narrow),
            shaped(rows, kinds * size, count * rank_count, kind=narrow),
            shaped(3, size, lanes),
            full,
            full,
        ),
        (row,),
        (),
        (
            pltpu.SMEM(block_ranks.shape, jnp.int32),
            pltpu.VMEM(v_basis.shape, narrow),
            pltpu.VMEM(u_basis.shape, narrow),
            *[pltpu.VMEM((1, size), wide)] * 3,
            pltpu.VMEM((size, members), wide),
            pltpu.SemaphoreType.DMA((7,)),
        ),
        room=room,
        far=(
            block_ranks,
            v_basis,
            u_basis,
            sigma_base.reshape(1, size),
            a_coef.reshape(1, size),
            b_coef.reshape(1, size),
            state_var,
        ),
    )

    def add(blocks, first, pick, before, kind):
        held = rows if pick is None else 1
        lead = (rows, kinds) if pick is None else (kinds,)
        return on_core(
            functools.partial(
                sums_kernel, spots[first : first + len(blocks)], direct, first, pick, before is not None
            ),
            shaped(*lead, size, members, kind=kind),
            (row, col, near_index),
            (v_met, u_met, dense_blocks, *blocks, *(() if before is None else (before,))),
            (
                pltpu.VMEM((len(blocks), size, members), narrow),
                pltpu.VMEM((held, len(blocks) * rank_count, members), narrow),
                pltpu.VMEM((held, kinds, size, members), wide),
            ),
            2 * held * size * members * rank_count * len(blocks) * 3,
            room,
        )

    def lattice(field_half):
        if direct:
            blocks = gather_direct(field_half, count)
        else:
            whole = lax.all_gather(field_half, "row", axis=0)
            blocks = [whole[r] for r in range(count)]
        sums = add(blocks[:early], 0, None, None, wide) if early else None
        other = lax.ppermute(add(blocks[early:], early, 1, sums, narrow), "col", swap)
        return add(blocks[early:], early, 0, sums, wide), other

    slip_half = on_core(
        narrow_kernel,
        shaped(size, members, kind=narrow),
        (),
        (),
        (pltpu.VMEM((size, members), wide), pltpu.SemaphoreType.DMA((PIECES,))),
        far=(slip_deficit,),
    )
    own, other = lattice(slip_half)
    stress, normal, rate, change, rate_half = on_core(
        section_one_kernel,
        (full, full, full, full, shaped(size, members, kind=narrow)),
        (),
        (own, other, weight, decay, tau_load, coef),
        flops=200 * size * members,
    )
    own, other = lattice(rate_half)
    return on_core(
        section_two_kernel,
        (full, full),
        (),
        (own, other, state_var, tau_load, coef, stress, normal, rate, change),
        (
            pltpu.VMEM((size, members), wide),
            pltpu.VMEM((size, members), wide),
            pltpu.SemaphoreType.DMA((2, PIECES)),
        ),
        flops=200 * size * members,
        out_far=True,
    )


def solution(mesh):
    placed = (
        P(("row", "col"), "scen"),
        P(("row", "col"), "scen"),
        P(("row", "col"), "scen"),
        P(("row", "col")),
        P(("row", "col")),
        P(("row", "col")),
        P("row", "col", None, None),
        P(None, "row", "col", None, None),
        P(None, "row", "col", None, None),
        P("row", "col"),
        P("row", "col"),
    )
    return jax.shard_map(
        body,
        mesh=mesh,
        in_specs=placed,
        out_specs=(P(("row", "col"), "scen"), P(("row", "col"), "scen")),
        check_vma=False,
    )
```

```python
import functools

import jax
import jax.numpy as jnp
from jax import lax
from jax.experimental import pallas as pl
from jax.experimental.pallas import tpu as pltpu
from jax.sharding import PartitionSpec as P

NEWTON = 2
DIRECT_COUNTS = (4, 8)
LATE = 4

damping = 0.5
sigma_floor = 0.5
section_step = 0.1


def arrivals(count, direct):
    if not direct:
        return list(range(count))
    return [0, 1, 4, 2, 3, 5, 6, 7] if count == 8 else [0, 1, 2, 3]


def row_met(spot, row, direct):
    return jnp.bitwise_xor(row, spot) if direct else spot


def gather_direct(block, count):
    def swapped(mask, data):
        return lax.ppermute(data, "row", [(row, row ^ mask) for row in range(count)])

    found = {0: block}
    for mask in (4, 1, 2, 3) if count == 8 else (1, 2, 3):
        found[mask] = swapped(mask, block)
    if count == 8:
        for mask in (1, 2, 3):
            found[4 + mask] = swapped(mask, found[4])
    return [found[mask] for mask in arrivals(count, True)]


PIECES = 4


def row_pieces(size):
    tall = size // PIECES
    return [pl.ds(at * tall, tall) for at in range(PIECES)]


def narrow_kernel(wide_ref, narrow_ref, held, sem):
    copies = [
        pltpu.make_async_copy(wide_ref.at[part], held.at[part], sem.at[at])
        for at, part in enumerate(row_pieces(held.shape[0]))
    ]
    for copy in copies:
        copy.start()
    for copy, part in zip(copies, row_pieces(held.shape[0])):
        copy.wait()
        narrow_ref[part, :] = held[part, :].astype(narrow_ref.dtype)


def prepare_kernel(spots, direct, *refs):
    far, (v_out, u_out, coef_out, weight_out, decay_out), near, sem = refs[:7], refs[7:12], refs[12:19], refs[19]
    copies = [
        pltpu.make_async_copy(source, held, sem.at[at])
        for at, (source, held) in enumerate(zip(far, near))
    ]
    for copy in copies:
        copy.start()
    for copy in copies:
        copy.wait()
    rank_ref, v_ref, u_ref, sigma_ref, a_ref, b_ref, state_ref = near
    kinds, rows, count, rank_count, size = u_ref.shape
    row = lax.axis_index("row")
    met = [row_met(spot, row, direct) for spot in spots]
    for at, q in enumerate(met):
        for p in range(rows):
            inside = lax.broadcasted_iota(jnp.int32, (rank_count, size), 0) < rank_ref[p, q]
            v_out[at, p] = jnp.where(inside, v_ref[p, q].astype(jnp.float32), 0.0).astype(v_out.dtype)
    for p in range(rows):
        for kind in range(kinds):
            for first in range(0, count, 4):
                group = [u_ref[kind, p, q] for q in met[first : first + 4]]
                turned = jnp.concatenate(group, axis=0).astype(jnp.float32).T
                u_out[p, kind * size : (kind + 1) * size, first * rank_count : (first + len(group)) * rank_count] = (
                    turned.astype(u_out.dtype)
                )
    lanes = coef_out.shape[2]
    for at, values in enumerate((sigma_ref[...], a_ref[...], b_ref[...], 1.0 / a_ref[...], 1.0 / b_ref[...])):
        coef_out[at] = jnp.broadcast_to(values, (lanes, size)).T
    for first in range(0, state_ref.shape[1], lanes):
        part = slice(first, first + lanes)
        state = state_ref[:, part]
        weight_out[:, part] = jnp.exp(-state * coef_out[3])
        decay_out[:, part] = jnp.exp(-state * coef_out[4])


def sums_kernel(spots, direct, first, pick, before, near_any, v_ref, u_ref, d_ref, *refs):
    blocks = refs[: len(spots)]
    refs = refs[len(spots) :]
    if before:
        sums_ref, refs = refs[0], refs[1:]
    out_ref, x_all, proj, near_ref, near_sem = refs[:5]
    total = refs[5] if pick == 1 else out_ref
    count, rows, rank_count, size = v_ref.shape
    kinds, slots = d_ref.shape[0], near_ref.shape[1]
    near_copy = pltpu.make_async_copy(near_any, near_ref, near_sem)
    near_copy.start()
    row, col = lax.axis_index("row"), lax.axis_index("col")
    met = [row_met(spot, row, direct) for spot in spots]
    chosen = list(range(rows)) if pick is None else [col if pick == 0 else 1 - col]
    places = [(place,) for place in range(rows)] if pick is None else [()]
    for at, block in enumerate(blocks):
        if pick is None:
            weights = v_ref[first + at].reshape(rows * rank_count, size)
        else:
            weights = v_ref[first + at, chosen[0]]
        part = jnp.dot(weights, block[...], preferred_element_type=jnp.float32).astype(proj.dtype)
        for place in range(len(chosen)):
            proj[place, at * rank_count : (at + 1) * rank_count, :] = part[
                place * rank_count : (place + 1) * rank_count
            ]
    for at, block in enumerate(blocks):
        x_all[at] = block[...]
    lanes = slice(first * rank_count, (first + len(blocks)) * rank_count)
    for place, p in enumerate(chosen):
        gained = jnp.dot(u_ref[p, :, lanes], proj[place], preferred_element_type=jnp.float32)
        for kind in range(kinds):
            piece = gained[kind * size : (kind + 1) * size]
            total[*places[place], kind] = sums_ref[p, kind] + piece if before else piece
    near_copy.wait()
    for place, p in enumerate(chosen):
        for s in range(slots):
            near = near_ref[p, s] - col * count
            at = sum(jnp.where(near == q, i, 0) for i, q in enumerate(met))
            hit = sum(jnp.where(near == q, 1, 0) for q in met)

            @pl.when(hit > 0)
            def _():
                block = x_all[at]
                for kind in range(kinds):
                    total[*places[place], kind] += jnp.dot(
                        d_ref[kind, p, s], block, preferred_element_type=jnp.float32
                    )
    if pick == 1:
        out_ref[...] = total[...].astype(out_ref.dtype)


def inverse(value):
    rough = pl.reciprocal(value, approx=True)
    return rough * (2.0 - value * rough)


def sinh_cosh(value):
    grown = jnp.exp(value)
    shrunk = inverse(grown)
    square = value * value
    small = value * (1.0 + square * (1 / 6 + square * (1 / 120)))
    sinh = jnp.where(square < 0.25, small, 0.5 * (grown - shrunk))
    return sinh, 0.5 * (grown + shrunk)


def friction(shear, normal, weight, decay, tau_load, sigma_base, a_wide, b_wide):
    tau = tau_load + shear
    size = jnp.abs(tau)
    stiff = jnp.maximum(sigma_base + normal, sigma_floor) * a_wide
    double = 2.0 * damping * weight
    drive = size * inverse(double)
    square = drive * drive + 1.0
    slope = jnp.minimum(size * inverse(stiff), jnp.log(drive + square * lax.rsqrt(square)))
    for newton_step in range(NEWTON):
        sinh, cosh = sinh_cosh(slope)
        excess = stiff * slope + double * sinh - size
        slope = slope - excess * inverse(stiff + double * cosh)
    rate = 2.0 * weight * sinh_cosh(slope)[0]
    change = b_wide * (decay - jnp.abs(rate))
    return (jnp.where(tau < 0.0, -rate, rate), change)


def over_pieces(begin, tall, members, lanes, work):
    step = min(tall, 32)

    @pl.loop(0, tall // step)
    def _(index):
        rows = pl.ds(pl.multiple_of(begin + index * step, step), step)
        for first in range(0, members, lanes):
            work(rows, slice(first, first + lanes))


def section_one_kernel(own, other, weight, decay, tau, coef, stress, normal, rate, change, rate_half):
    size, members = tau.shape

    def work(rows, part):
        shear = own[0, rows, part] + other[0, rows, part].astype(jnp.float32)
        press = own[1, rows, part] + other[1, rows, part].astype(jnp.float32)
        stress[rows, part] = shear
        normal[rows, part] = press
        first, second = friction(
            shear,
            press,
            weight[rows, part],
            decay[rows, part],
            tau[rows, part],
            coef[0, rows, :],
            coef[1, rows, :],
            coef[2, rows, :],
        )
        rate[rows, part] = first
        change[rows, part] = second
        rate_half[rows, part] = first.astype(rate_half.dtype)

    over_pieces(0, size, members, coef.shape[2], work)


def section_two_kernel(
    own, other, state, tau, coef, stress, normal, rate, change, rate_out, change_out, mean_rate, mean_change, sem
):
    size, members = tau.shape

    def work(rows, part):
        shear = own[0, rows, part] + other[0, rows, part].astype(jnp.float32)
        press = own[1, rows, part] + other[1, rows, part].astype(jnp.float32)
        sigma, a_wide, b_wide = coef[0, rows, :], coef[1, rows, :], coef[2, rows, :]
        later = state[rows, part] + section_step * change[rows, part]
        first, second = friction(
            stress[rows, part] + section_step * shear,
            normal[rows, part] + section_step * press,
            jnp.exp(-later * coef[3, rows, :]),
            jnp.exp(-later * coef[4, rows, :]),
            tau[rows, part],
            sigma,
            a_wide,
            b_wide,
        )
        mean_rate[rows, part] = (rate[rows, part] + first) * 0.5
        mean_change[rows, part] = (change[rows, part] + second) * 0.5

    copies = []
    for at, part in enumerate(row_pieces(size)):
        over_pieces(part.start, part.size, members, coef.shape[2], work)
        for kind, (held, out) in enumerate(((mean_rate, rate_out), (mean_change, change_out))):
            copies.append(pltpu.make_async_copy(held.at[part], out.at[part], sem.at[kind, at]))
            copies[-1].start()
    for copy in copies:
        copy.wait()


def on_core(kernel, outs, arrays, scratch=(), flops=0, room=16, far=(), out_far=False):
    vmem, hbm = pl.BlockSpec(memory_space=pltpu.VMEM), pl.BlockSpec(memory_space=pl.ANY)
    arrays = (*(pltpu.with_memory_space_constraint(a, pltpu.HBM) for a in far), *arrays)
    return pl.pallas_call(
        kernel,
        out_shape=outs,
        in_specs=[hbm] * len(far) + [vmem] * (len(arrays) - len(far)),
        out_specs=jax.tree.map(lambda _: hbm if out_far else vmem, outs),
        scratch_shapes=list(scratch),
        compiler_params=pltpu.CompilerParams(vmem_limit_bytes=room * 1024 * 1024),
        cost_estimate=pl.CostEstimate(
            flops=flops, bytes_accessed=sum(a.size * a.dtype.itemsize for a in arrays), transcendentals=0
        ),
    )(*arrays)


def body(
    slip_deficit,
    state_var,
    tau_load,
    sigma_base,
    a_coef,
    b_coef,
    v_basis,
    u_basis,
    dense_blocks,
    block_ranks,
    near_index,
):
    count = lax.axis_size("row")
    size, members = slip_deficit.shape
    kinds, rows, _, rank_count, _ = u_basis.shape
    direct = count in DIRECT_COUNTS
    spots = arrivals(count, direct)
    early = max(count - LATE, 0)
    room = 16 if direct else 40
    lanes = min(members, 128)
    narrow, wide = jnp.bfloat16, jnp.float32
    swap = [(0, 1), (1, 0)]

    def shaped(*shape, kind=wide):
        return jax.ShapeDtypeStruct(shape, kind)

    full = shaped(size, members)
    v_met, u_met, coef, weight, decay = on_core(
        functools.partial(prepare_kernel, spots, direct),
        (
            shaped(count, rows, rank_count, size, kind=narrow),
            shaped(rows, kinds * size, count * rank_count, kind=narrow),
            shaped(5, size, lanes),
            full,
            full,
        ),
        (),
        (
            pltpu.SMEM(block_ranks.shape, jnp.int32),
            pltpu.VMEM(v_basis.shape, narrow),
            pltpu.VMEM(u_basis.shape, narrow),
            *[pltpu.VMEM((1, size), wide)] * 3,
            pltpu.VMEM((size, members), wide),
            pltpu.SemaphoreType.DMA((7,)),
        ),
        room=room,
        far=(
            block_ranks,
            v_basis,
            u_basis,
            sigma_base.reshape(1, size),
            a_coef.reshape(1, size),
            b_coef.reshape(1, size),
            state_var,
        ),
    )

    def add(blocks, first, pick, before, kind):
        held = rows if pick is None else 1
        lead = (rows, kinds) if pick is None else (kinds,)
        return on_core(
            functools.partial(
                sums_kernel, spots[first : first + len(blocks)], direct, first, pick, before is not None
            ),
            shaped(*lead, size, members, kind=kind),
            (v_met, u_met, dense_blocks, *blocks, *(() if before is None else (before,))),
            (
                pltpu.VMEM((len(blocks), size, members), narrow),
                pltpu.VMEM((held, len(blocks) * rank_count, members), narrow),
                pltpu.SMEM(near_index.shape, jnp.int32),
                pltpu.SemaphoreType.DMA(()),
                *([pltpu.VMEM((kinds, size, members), wide)] if pick == 1 else []),
            ),
            2 * held * size * members * rank_count * len(blocks) * 3,
            room,
            far=(near_index,),
        )

    def lattice(field_half):
        if direct:
            blocks = gather_direct(field_half, count)
        else:
            whole = lax.all_gather(field_half, "row", axis=0)
            blocks = [whole[r] for r in range(count)]
        sums = add(blocks[:early], 0, None, None, wide) if early else None
        other = lax.ppermute(add(blocks[early:], early, 1, sums, narrow), "col", swap)
        return add(blocks[early:], early, 0, sums, wide), other

    slip_half = on_core(
        narrow_kernel,
        shaped(size, members, kind=narrow),
        (),
        (pltpu.VMEM((size, members), wide), pltpu.SemaphoreType.DMA((PIECES,))),
        far=(slip_deficit,),
    )
    own, other = lattice(slip_half)
    stress, normal, rate, change, rate_half = on_core(
        section_one_kernel,
        (full, full, full, full, shaped(size, members, kind=narrow)),
        (own, other, weight, decay, tau_load, coef),
        flops=200 * size * members,
    )
    own, other = lattice(rate_half)
    return on_core(
        section_two_kernel,
        (full, full),
        (own, other, state_var, tau_load, coef, stress, normal, rate, change),
        (
            pltpu.VMEM((size, members), wide),
            pltpu.VMEM((size, members), wide),
            pltpu.SemaphoreType.DMA((2, PIECES)),
        ),
        flops=200 * size * members,
        out_far=True,
    )


def solution(mesh):
    placed = (
        P(("row", "col"), "scen"),
        P(("row", "col"), "scen"),
        P(("row", "col"), "scen"),
        P(("row", "col")),
        P(("row", "col")),
        P(("row", "col")),
        P("row", "col", None, None),
        P(None, "row", "col", None, None),
        P(None, "row", "col", None, None),
        P("row", "col"),
        P("row", "col"),
    )
    return jax.shard_map(
        body,
        mesh=mesh,
        in_specs=placed,
        out_specs=(P(("row", "col"), "scen"), P(("row", "col"), "scen")),
        check_vma=False,
    )
```

```python
import functools

import jax
import jax.numpy as jnp
from jax import lax
from jax.experimental import pallas as pl
from jax.experimental.pallas import tpu as pltpu
from jax.sharding import PartitionSpec as P

NEWTON = 2
DIRECT_COUNTS = (4, 8)
LATE = 4

damping = 0.5
sigma_floor = 0.5
section_step = 0.1


def arrivals(count, direct):
    if not direct:
        return list(range(count))
    return [0, 1, 2, 4, 3, 7, 5, 6] if count == 8 else [0, 1, 2, 3]


def row_met(spot, row, direct):
    return jnp.bitwise_xor(row, spot) if direct else spot


def gather_direct(block, count):
    def swapped(mask, data):
        return lax.ppermute(data, "row", [(row, row ^ mask) for row in range(count)])

    found = {0: block}
    for mask in (4, 1, 2, 3, 7) if count == 8 else (1, 2, 3):
        found[mask] = swapped(mask, block)
    if count == 8:
        for mask in (1, 2):
            found[4 + mask] = swapped(mask, found[4])
    return [found[mask] for mask in arrivals(count, True)]


PIECES = 4


def row_pieces(size):
    tall = size // PIECES
    return [pl.ds(at * tall, tall) for at in range(PIECES)]


def narrow_kernel(wide_ref, narrow_ref, held, sem):
    copies = [
        pltpu.make_async_copy(wide_ref.at[part], held.at[part], sem.at[at])
        for at, part in enumerate(row_pieces(held.shape[0]))
    ]
    for copy in copies:
        copy.start()
    for copy, part in zip(copies, row_pieces(held.shape[0])):
        copy.wait()
        narrow_ref[part, :] = held[part, :].astype(narrow_ref.dtype)


def prepare_kernel(spots, direct, *refs):
    far, (v_out, u_out, coef_out, weight_out, decay_out), near, sem = refs[:7], refs[7:12], refs[12:19], refs[19]
    copies = [
        pltpu.make_async_copy(source, held, sem.at[at])
        for at, (source, held) in enumerate(zip(far, near))
    ]
    for copy in copies:
        copy.start()
    for copy in copies:
        copy.wait()
    rank_ref, v_ref, u_ref, sigma_ref, a_ref, b_ref, state_ref = near
    kinds, rows, count, rank_count, size = u_ref.shape
    row = lax.axis_index("row")
    met = [row_met(spot, row, direct) for spot in spots]
    for at, q in enumerate(met):
        for p in range(rows):
            inside = lax.broadcasted_iota(jnp.int32, (rank_count, size), 0) < rank_ref[p, q]
            v_out[at, p] = jnp.where(inside, v_ref[p, q].astype(jnp.float32), 0.0).astype(v_out.dtype)
    for p in range(rows):
        for kind in range(kinds):
            for first in range(0, count, 4):
                group = [u_ref[kind, p, q] for q in met[first : first + 4]]
                turned = jnp.concatenate(group, axis=0).astype(jnp.float32).T
                u_out[p, kind * size : (kind + 1) * size, first * rank_count : (first + len(group)) * rank_count] = (
                    turned.astype(u_out.dtype)
                )
    lanes = coef_out.shape[2]
    for at, values in enumerate((sigma_ref[...], a_ref[...], b_ref[...], 1.0 / a_ref[...], 1.0 / b_ref[...])):
        coef_out[at] = jnp.broadcast_to(values, (lanes, size)).T
    for first in range(0, state_ref.shape[1], lanes):
        part = slice(first, first + lanes)
        state = state_ref[:, part]
        weight_out[:, part] = jnp.exp(-state * coef_out[3])
        decay_out[:, part] = jnp.exp(-state * coef_out[4])


def sums_kernel(spots, direct, first, pick, before, near_any, v_ref, u_ref, d_ref, *refs):
    blocks = refs[: len(spots)]
    refs = refs[len(spots) :]
    if before:
        sums_ref, refs = refs[0], refs[1:]
    out_ref, x_all, proj, near_ref, near_sem = refs[:5]
    total = refs[5] if pick == 1 else out_ref
    count, rows, rank_count, size = v_ref.shape
    kinds, slots = d_ref.shape[0], near_ref.shape[1]
    near_copy = pltpu.make_async_copy(near_any, near_ref, near_sem)
    near_copy.start()
    row, col = lax.axis_index("row"), lax.axis_index("col")
    met = [row_met(spot, row, direct) for spot in spots]
    chosen = list(range(rows)) if pick is None else [col if pick == 0 else 1 - col]
    places = [(place,) for place in range(rows)] if pick is None else [()]
    for at, block in enumerate(blocks):
        if pick is None:
            weights = v_ref[first + at].reshape(rows * rank_count, size)
        else:
            weights = v_ref[first + at, chosen[0]]
        part = jnp.dot(weights, block[...], preferred_element_type=jnp.float32).astype(proj.dtype)
        for place in range(len(chosen)):
            proj[place, at * rank_count : (at + 1) * rank_count, :] = part[
                place * rank_count : (place + 1) * rank_count
            ]
    for at, block in enumerate(blocks):
        x_all[at] = block[...]
    lanes = slice(first * rank_count, (first + len(blocks)) * rank_count)
    for place, p in enumerate(chosen):
        gained = jnp.dot(u_ref[p, :, lanes], proj[place], preferred_element_type=jnp.float32)
        for kind in range(kinds):
            piece = gained[kind * size : (kind + 1) * size]
            total[*places[place], kind] = sums_ref[p, kind] + piece if before else piece
    near_copy.wait()
    for place, p in enumerate(chosen):
        for s in range(slots):
            near = near_ref[p, s] - col * count
            at = sum(jnp.where(near == q, i, 0) for i, q in enumerate(met))
            hit = sum(jnp.where(near == q, 1, 0) for q in met)

            @pl.when(hit > 0)
            def _():
                block = x_all[at]
                for kind in range(kinds):
                    total[*places[place], kind] += jnp.dot(
                        d_ref[kind, p, s], block, preferred_element_type=jnp.float32
                    )
    if pick == 1:
        out_ref[...] = total[...].astype(out_ref.dtype)


def inverse(value):
    rough = pl.reciprocal(value, approx=True)
    return rough * (2.0 - value * rough)


def sinh_cosh(value):
    grown = jnp.exp(value)
    shrunk = inverse(grown)
    square = value * value
    small = value * (1.0 + square * (1 / 6 + square * (1 / 120)))
    sinh = jnp.where(square < 0.25, small, 0.5 * (grown - shrunk))
    return sinh, 0.5 * (grown + shrunk)


def friction(shear, normal, weight, decay, tau_load, sigma_base, a_wide, b_wide):
    tau = tau_load + shear
    size = jnp.abs(tau)
    stiff = jnp.maximum(sigma_base + normal, sigma_floor) * a_wide
    double = 2.0 * damping * weight
    drive = size * inverse(double)
    square = drive * drive + 1.0
    slope = jnp.minimum(size * inverse(stiff), jnp.log(drive + square * lax.rsqrt(square)))
    for newton_step in range(NEWTON):
        sinh, cosh = sinh_cosh(slope)
        excess = stiff * slope + double * sinh - size
        slope = slope - excess * inverse(stiff + double * cosh)
    rate = 2.0 * weight * sinh_cosh(slope)[0]
    change = b_wide * (decay - jnp.abs(rate))
    return (jnp.where(tau < 0.0, -rate, rate), change)


def over_pieces(begin, tall, members, lanes, work):
    step = min(tall, 32)

    @pl.loop(0, tall // step)
    def _(index):
        rows = pl.ds(pl.multiple_of(begin + index * step, step), step)
        for first in range(0, members, lanes):
            work(rows, slice(first, first + lanes))


def section_one_kernel(own, other, weight, decay, tau, coef, stress, normal, rate, change, rate_half):
    size, members = tau.shape

    def work(rows, part):
        shear = own[0, rows, part] + other[0, rows, part].astype(jnp.float32)
        press = own[1, rows, part] + other[1, rows, part].astype(jnp.float32)
        stress[rows, part] = shear
        normal[rows, part] = press
        first, second = friction(
            shear,
            press,
            weight[rows, part],
            decay[rows, part],
            tau[rows, part],
            coef[0, rows, :],
            coef[1, rows, :],
            coef[2, rows, :],
        )
        rate[rows, part] = first
        change[rows, part] = second
        rate_half[rows, part] = first.astype(rate_half.dtype)

    over_pieces(0, size, members, coef.shape[2], work)


def section_two_kernel(
    own, other, state, tau, coef, stress, normal, rate, change, rate_out, change_out, mean_rate, mean_change, sem
):
    size, members = tau.shape

    def work(rows, part):
        shear = own[0, rows, part] + other[0, rows, part].astype(jnp.float32)
        press = own[1, rows, part] + other[1, rows, part].astype(jnp.float32)
        sigma, a_wide, b_wide = coef[0, rows, :], coef[1, rows, :], coef[2, rows, :]
        later = state[rows, part] + section_step * change[rows, part]
        first, second = friction(
            stress[rows, part] + section_step * shear,
            normal[rows, part] + section_step * press,
            jnp.exp(-later * coef[3, rows, :]),
            jnp.exp(-later * coef[4, rows, :]),
            tau[rows, part],
            sigma,
            a_wide,
            b_wide,
        )
        mean_rate[rows, part] = (rate[rows, part] + first) * 0.5
        mean_change[rows, part] = (change[rows, part] + second) * 0.5

    copies = []
    for at, part in enumerate(row_pieces(size)):
        over_pieces(part.start, part.size, members, coef.shape[2], work)
        for kind, (held, out) in enumerate(((mean_rate, rate_out), (mean_change, change_out))):
            copies.append(pltpu.make_async_copy(held.at[part], out.at[part], sem.at[kind, at]))
            copies[-1].start()
    for copy in copies:
        copy.wait()


def on_core(kernel, outs, arrays, scratch=(), flops=0, room=16, far=(), out_far=False):
    vmem, hbm = pl.BlockSpec(memory_space=pltpu.VMEM), pl.BlockSpec(memory_space=pl.ANY)
    arrays = (*(pltpu.with_memory_space_constraint(a, pltpu.HBM) for a in far), *arrays)
    return pl.pallas_call(
        kernel,
        out_shape=outs,
        in_specs=[hbm] * len(far) + [vmem] * (len(arrays) - len(far)),
        out_specs=jax.tree.map(lambda _: hbm if out_far else vmem, outs),
        scratch_shapes=list(scratch),
        compiler_params=pltpu.CompilerParams(vmem_limit_bytes=room * 1024 * 1024),
        cost_estimate=pl.CostEstimate(
            flops=flops, bytes_accessed=sum(a.size * a.dtype.itemsize for a in arrays), transcendentals=0
        ),
    )(*arrays)


def body(
    slip_deficit,
    state_var,
    tau_load,
    sigma_base,
    a_coef,
    b_coef,
    v_basis,
    u_basis,
    dense_blocks,
    block_ranks,
    near_index,
):
    count = lax.axis_size("row")
    size, members = slip_deficit.shape
    kinds, rows, _, rank_count, _ = u_basis.shape
    direct = count in DIRECT_COUNTS
    spots = arrivals(count, direct)
    early = max(count - LATE, 0)
    room = 16 if direct else 40
    lanes = min(members, 128)
    narrow, wide = jnp.bfloat16, jnp.float32
    swap = [(0, 1), (1, 0)]

    def shaped(*shape, kind=wide):
        return jax.ShapeDtypeStruct(shape, kind)

    full = shaped(size, members)
    v_met, u_met, coef, weight, decay = on_core(
        functools.partial(prepare_kernel, spots, direct),
        (
            shaped(count, rows, rank_count, size, kind=narrow),
            shaped(rows, kinds * size, count * rank_count, kind=narrow),
            shaped(5, size, lanes),
            full,
            full,
        ),
        (),
        (
            pltpu.SMEM(block_ranks.shape, jnp.int32),
            pltpu.VMEM(v_basis.shape, narrow),
            pltpu.VMEM(u_basis.shape, narrow),
            *[pltpu.VMEM((1, size), wide)] * 3,
            pltpu.VMEM((size, members), wide),
            pltpu.SemaphoreType.DMA((7,)),
        ),
        room=room,
        far=(
            block_ranks,
            v_basis,
            u_basis,
            sigma_base.reshape(1, size),
            a_coef.reshape(1, size),
            b_coef.reshape(1, size),
            state_var,
        ),
    )

    def add(blocks, first, pick, before, kind):
        held = rows if pick is None else 1
        lead = (rows, kinds) if pick is None else (kinds,)
        return on_core(
            functools.partial(
                sums_kernel, spots[first : first + len(blocks)], direct, first, pick, before is not None
            ),
            shaped(*lead, size, members, kind=kind),
            (v_met, u_met, dense_blocks, *blocks, *(() if before is None else (before,))),
            (
                pltpu.VMEM((len(blocks), size, members), narrow),
                pltpu.VMEM((held, len(blocks) * rank_count, members), narrow),
                pltpu.SMEM(near_index.shape, jnp.int32),
                pltpu.SemaphoreType.DMA(()),
                *([pltpu.VMEM((kinds, size, members), wide)] if pick == 1 else []),
            ),
            2 * held * size * members * rank_count * len(blocks) * 3,
            room,
            far=(near_index,),
        )

    def lattice(field_half):
        if direct:
            blocks = gather_direct(field_half, count)
        else:
            whole = lax.all_gather(field_half, "row", axis=0)
            blocks = [whole[r] for r in range(count)]
        sums = add(blocks[:early], 0, None, None, wide) if early else None
        other = lax.ppermute(add(blocks[early:], early, 1, sums, narrow), "col", swap)
        return add(blocks[early:], early, 0, sums, wide), other

    slip_half = on_core(
        narrow_kernel,
        shaped(size, members, kind=narrow),
        (),
        (pltpu.VMEM((size, members), wide), pltpu.SemaphoreType.DMA((PIECES,))),
        far=(slip_deficit,),
    )
    own, other = lattice(slip_half)
    stress, normal, rate, change, rate_half = on_core(
        section_one_kernel,
        (full, full, full, full, shaped(size, members, kind=narrow)),
        (own, other, weight, decay, tau_load, coef),
        flops=200 * size * members,
    )
    own, other = lattice(rate_half)
    return on_core(
        section_two_kernel,
        (full, full),
        (own, other, state_var, tau_load, coef, stress, normal, rate, change),
        (
            pltpu.VMEM((size, members), wide),
            pltpu.VMEM((size, members), wide),
            pltpu.SemaphoreType.DMA((2, PIECES)),
        ),
        flops=200 * size * members,
        out_far=True,
    )


def solution(mesh):
    placed = (
        P(("row", "col"), "scen"),
        P(("row", "col"), "scen"),
        P(("row", "col"), "scen"),
        P(("row", "col")),
        P(("row", "col")),
        P(("row", "col")),
        P("row", "col", None, None),
        P(None, "row", "col", None, None),
        P(None, "row", "col", None, None),
        P("row", "col"),
        P("row", "col"),
    )
    return jax.shard_map(
        body,
        mesh=mesh,
        in_specs=placed,
        out_specs=(P(("row", "col"), "scen"), P(("row", "col"), "scen")),
        check_vma=False,
    )
```

```python
import functools

import jax
import jax.numpy as jnp
from jax import lax
from jax.experimental import pallas as pl
from jax.experimental.pallas import tpu as pltpu
from jax.sharding import PartitionSpec as P

NEWTON = 2
DIRECT_COUNTS = (4, 8)
TILE = 128

damping = 0.5
sigma_floor = 0.5
section_step = 0.1


def arrivals(count, direct):
    if not direct:
        cuts = [0, max(count - 4, 0), count]
        return [list(range(first, last)) for first, last in zip(cuts, cuts[1:]) if last > first]
    return [[0, 1, 4], [2, 3], [7, 5, 6]] if count == 8 else [[0, 1], [2, 3]]


def row_met(spot, row, direct):
    return jnp.bitwise_xor(row, spot) if direct else spot


def gather_direct(block, count):
    def swapped(mask, data):
        return lax.ppermute(data, "row", [(row, row ^ mask) for row in range(count)])

    found = {0: block}
    for mask in (4, 1, 2, 3, 7) if count == 8 else (1, 2, 3):
        found[mask] = swapped(mask, block)
    if count == 8:
        for mask in (1, 2):
            found[4 + mask] = swapped(mask, found[4])
    return [[found[mask] for mask in group] for group in arrivals(count, True)]


PIECES = 4


def row_pieces(size):
    tall = size // PIECES
    return [pl.ds(at * tall, tall) for at in range(PIECES)]


def narrow_kernel(wide_ref, narrow_ref, held, sem):
    copies = [
        pltpu.make_async_copy(wide_ref.at[part], held.at[part], sem.at[at])
        for at, part in enumerate(row_pieces(held.shape[0]))
    ]
    for copy in copies:
        copy.start()
    for copy, part in zip(copies, row_pieces(held.shape[0])):
        copy.wait()
        narrow_ref[part, :] = held[part, :].astype(narrow_ref.dtype)


def prepare_kernel(groups, direct, *refs):
    far, (v_out, u_out, coef_out, weight_out, decay_out), near, sem = refs[:7], refs[7:12], refs[12:19], refs[19]
    copies = [
        pltpu.make_async_copy(source, held, sem.at[at])
        for at, (source, held) in enumerate(zip(far, near))
    ]
    for copy in copies:
        copy.start()
    for copy in copies:
        copy.wait()
    rank_ref, v_ref, u_ref, sigma_ref, a_ref, b_ref, state_ref = near
    kinds, rows, count, rank_count, size = u_ref.shape
    row = lax.axis_index("row")
    met = [row_met(spot, row, direct) for group in groups for spot in group]
    for at, q in enumerate(met):
        for p in range(rows):
            inside = lax.broadcasted_iota(jnp.int32, (rank_count, size), 0) < rank_ref[p, q]
            v_out[at, p] = jnp.where(inside, v_ref[p, q].astype(jnp.float32), 0.0).astype(v_out.dtype)
    for p in range(rows):
        for kind in range(kinds):
            first = start = 0
            for spots in groups:
                group = [u_ref[kind, p, q] for q in met[first : first + len(spots)]]
                spare = -len(group) * rank_count % TILE
                if spare:
                    group.append(jnp.zeros((spare, size), u_ref.dtype))
                turned = jnp.concatenate(group, axis=0).astype(jnp.float32).T
                stop = start + turned.shape[1]
                u_out[p, kind * size : (kind + 1) * size, start:stop] = turned.astype(u_out.dtype)
                first, start = first + len(spots), stop
    lanes = coef_out.shape[2]
    for at, values in enumerate((sigma_ref[...], a_ref[...], b_ref[...], 1.0 / a_ref[...], 1.0 / b_ref[...])):
        coef_out[at] = jnp.broadcast_to(values, (lanes, size)).T
    for first in range(0, state_ref.shape[1], lanes):
        part = slice(first, first + lanes)
        state = state_ref[:, part]
        weight_out[:, part] = jnp.exp(-state * coef_out[3])
        decay_out[:, part] = jnp.exp(-state * coef_out[4])


def sums_kernel(spots, direct, first, start, pick, before, near_any, v_ref, u_ref, d_ref, *refs):
    blocks = refs[: len(spots)]
    refs = refs[len(spots) :]
    if before:
        sums_ref, refs = refs[0], refs[1:]
    out_ref, x_all, proj, near_ref, near_sem = refs[:5]
    total = refs[5] if pick == 1 else out_ref
    count, rows, rank_count, size = v_ref.shape
    kinds, slots = d_ref.shape[0], near_ref.shape[1]
    near_copy = pltpu.make_async_copy(near_any, near_ref, near_sem)
    near_copy.start()
    row, col = lax.axis_index("row"), lax.axis_index("col")
    met = [row_met(spot, row, direct) for spot in spots]
    chosen = list(range(rows)) if pick is None else [col if pick == 0 else 1 - col]
    places = [(place,) for place in range(rows)] if pick is None else [()]
    for at, block in enumerate(blocks):
        if pick is None:
            weights = v_ref[first + at].reshape(rows * rank_count, size)
        else:
            weights = v_ref[first + at, chosen[0]]
        part = jnp.dot(weights, block[...], preferred_element_type=jnp.float32).astype(proj.dtype)
        for place in range(len(chosen)):
            proj[place, at * rank_count : (at + 1) * rank_count, :] = part[
                place * rank_count : (place + 1) * rank_count
            ]
    for at, block in enumerate(blocks):
        x_all[at] = block[...]
    lanes = slice(start, start + len(blocks) * rank_count)
    for place, p in enumerate(chosen):
        gained = jnp.dot(u_ref[p, :, lanes], proj[place], preferred_element_type=jnp.float32)
        for kind in range(kinds):
            piece = gained[kind * size : (kind + 1) * size]
            total[*places[place], kind] = sums_ref[p, kind] + piece if before else piece
    near_copy.wait()
    for place, p in enumerate(chosen):
        for s in range(slots):
            near = near_ref[p, s] - col * count
            at = sum(jnp.where(near == q, i, 0) for i, q in enumerate(met))
            hit = sum(jnp.where(near == q, 1, 0) for q in met)

            @pl.when(hit > 0)
            def _():
                block = x_all[at]
                for kind in range(kinds):
                    total[*places[place], kind] += jnp.dot(
                        d_ref[kind, p, s], block, preferred_element_type=jnp.float32
                    )
    if pick == 1:
        out_ref[...] = total[...].astype(out_ref.dtype)


def inverse(value):
    rough = pl.reciprocal(value, approx=True)
    return rough * (2.0 - value * rough)


def sinh_cosh(value):
    grown = jnp.exp(value)
    shrunk = inverse(grown)
    square = value * value
    small = value * (1.0 + square * (1 / 6 + square * (1 / 120)))
    sinh = jnp.where(square < 0.25, small, 0.5 * (grown - shrunk))
    return sinh, 0.5 * (grown + shrunk)


def friction(shear, normal, weight, decay, tau_load, sigma_base, a_wide, b_wide):
    tau = tau_load + shear
    size = jnp.abs(tau)
    stiff = jnp.maximum(sigma_base + normal, sigma_floor) * a_wide
    double = 2.0 * damping * weight
    drive = size * inverse(double)
    square = drive * drive + 1.0
    slope = jnp.minimum(size * inverse(stiff), jnp.log(drive + square * lax.rsqrt(square)))
    for newton_step in range(NEWTON):
        sinh, cosh = sinh_cosh(slope)
        excess = stiff * slope + double * sinh - size
        slope = slope - excess * inverse(stiff + double * cosh)
    rate = 2.0 * weight * sinh_cosh(slope)[0]
    change = b_wide * (decay - jnp.abs(rate))
    return (jnp.where(tau < 0.0, -rate, rate), change)


def over_pieces(begin, tall, members, lanes, work):
    step = min(tall, 32)

    @pl.loop(0, tall // step)
    def _(index):
        rows = pl.ds(pl.multiple_of(begin + index * step, step), step)
        for first in range(0, members, lanes):
            work(rows, slice(first, first + lanes))


def section_one_kernel(own, other, weight, decay, tau, coef, stress, normal, rate, change, rate_half):
    size, members = tau.shape

    def work(rows, part):
        shear = own[0, rows, part] + other[0, rows, part].astype(jnp.float32)
        press = own[1, rows, part] + other[1, rows, part].astype(jnp.float32)
        stress[rows, part] = shear
        normal[rows, part] = press
        first, second = friction(
            shear,
            press,
            weight[rows, part],
            decay[rows, part],
            tau[rows, part],
            coef[0, rows, :],
            coef[1, rows, :],
            coef[2, rows, :],
        )
        rate[rows, part] = first
        change[rows, part] = second
        rate_half[rows, part] = first.astype(rate_half.dtype)

    over_pieces(0, size, members, coef.shape[2], work)


def section_two_kernel(
    own, other, state, tau, coef, stress, normal, rate, change, rate_out, change_out, mean_rate, mean_change, sem
):
    size, members = tau.shape

    def work(rows, part):
        shear = own[0, rows, part] + other[0, rows, part].astype(jnp.float32)
        press = own[1, rows, part] + other[1, rows, part].astype(jnp.float32)
        sigma, a_wide, b_wide = coef[0, rows, :], coef[1, rows, :], coef[2, rows, :]
        later = state[rows, part] + section_step * change[rows, part]
        first, second = friction(
            stress[rows, part] + section_step * shear,
            normal[rows, part] + section_step * press,
            jnp.exp(-later * coef[3, rows, :]),
            jnp.exp(-later * coef[4, rows, :]),
            tau[rows, part],
            sigma,
            a_wide,
            b_wide,
        )
        mean_rate[rows, part] = (rate[rows, part] + first) * 0.5
        mean_change[rows, part] = (change[rows, part] + second) * 0.5

    copies = []
    for at, part in enumerate(row_pieces(size)):
        over_pieces(part.start, part.size, members, coef.shape[2], work)
        for kind, (held, out) in enumerate(((mean_rate, rate_out), (mean_change, change_out))):
            copies.append(pltpu.make_async_copy(held.at[part], out.at[part], sem.at[kind, at]))
            copies[-1].start()
    for copy in copies:
        copy.wait()


def on_core(kernel, outs, arrays, scratch=(), flops=0, room=16, far=(), out_far=False):
    vmem, hbm = pl.BlockSpec(memory_space=pltpu.VMEM), pl.BlockSpec(memory_space=pl.ANY)
    arrays = (*(pltpu.with_memory_space_constraint(a, pltpu.HBM) for a in far), *arrays)
    return pl.pallas_call(
        kernel,
        out_shape=outs,
        in_specs=[hbm] * len(far) + [vmem] * (len(arrays) - len(far)),
        out_specs=jax.tree.map(lambda _: hbm if out_far else vmem, outs),
        scratch_shapes=list(scratch),
        compiler_params=pltpu.CompilerParams(vmem_limit_bytes=room * 1024 * 1024),
        cost_estimate=pl.CostEstimate(
            flops=flops, bytes_accessed=sum(a.size * a.dtype.itemsize for a in arrays), transcendentals=0
        ),
    )(*arrays)


def body(
    slip_deficit,
    state_var,
    tau_load,
    sigma_base,
    a_coef,
    b_coef,
    v_basis,
    u_basis,
    dense_blocks,
    block_ranks,
    near_index,
):
    count = lax.axis_size("row")
    size, members = slip_deficit.shape
    kinds, rows, _, rank_count, _ = u_basis.shape
    direct = count in DIRECT_COUNTS
    groups = arrivals(count, direct)
    firsts = [sum(len(group) for group in groups[:at]) for at in range(len(groups))]
    tiles = [-(-len(group) * rank_count // TILE) * TILE for group in groups]
    starts = [sum(tiles[:at]) for at in range(len(groups))]
    room = 16 if direct else 40
    lanes = min(members, 128)
    narrow, wide = jnp.bfloat16, jnp.float32
    swap = [(0, 1), (1, 0)]

    def shaped(*shape, kind=wide):
        return jax.ShapeDtypeStruct(shape, kind)

    full = shaped(size, members)
    v_met, u_met, coef, weight, decay = on_core(
        functools.partial(prepare_kernel, groups, direct),
        (
            shaped(count, rows, rank_count, size, kind=narrow),
            shaped(rows, kinds * size, sum(tiles), kind=narrow),
            shaped(5, size, lanes),
            full,
            full,
        ),
        (),
        (
            pltpu.SMEM(block_ranks.shape, jnp.int32),
            pltpu.VMEM(v_basis.shape, narrow),
            pltpu.VMEM(u_basis.shape, narrow),
            *[pltpu.VMEM((1, size), wide)] * 3,
            pltpu.VMEM((size, members), wide),
            pltpu.SemaphoreType.DMA((7,)),
        ),
        room=room,
        far=(
            block_ranks,
            v_basis,
            u_basis,
            sigma_base.reshape(1, size),
            a_coef.reshape(1, size),
            b_coef.reshape(1, size),
            state_var,
        ),
    )

    def add(blocks, at, pick, before, kind):
        held = rows if pick is None else 1
        lead = (rows, kinds) if pick is None else (kinds,)
        return on_core(
            functools.partial(
                sums_kernel, groups[at], direct, firsts[at], starts[at], pick, before is not None
            ),
            shaped(*lead, size, members, kind=kind),
            (v_met, u_met, dense_blocks, *blocks, *(() if before is None else (before,))),
            (
                pltpu.VMEM((len(blocks), size, members), narrow),
                pltpu.VMEM((held, len(blocks) * rank_count, members), narrow),
                pltpu.SMEM(near_index.shape, jnp.int32),
                pltpu.SemaphoreType.DMA(()),
                *([pltpu.VMEM((kinds, size, members), wide)] if pick == 1 else []),
            ),
            2 * held * size * members * rank_count * len(blocks) * 3,
            room,
            far=(near_index,),
        )

    def lattice(field_half):
        if direct:
            found = gather_direct(field_half, count)
        else:
            whole = lax.all_gather(field_half, "row", axis=0)
            found = [[whole[r] for r in group] for group in groups]
        sums, end = None, len(groups) - 1
        for at in range(end):
            sums = add(found[at], at, None, sums, wide)
        other = lax.ppermute(add(found[end], end, 1, sums, narrow), "col", swap)
        return add(found[end], end, 0, sums, wide), other

    slip_half = on_core(
        narrow_kernel,
        shaped(size, members, kind=narrow),
        (),
        (pltpu.VMEM((size, members), wide), pltpu.SemaphoreType.DMA((PIECES,))),
        far=(slip_deficit,),
    )
    own, other = lattice(slip_half)
    stress, normal, rate, change, rate_half = on_core(
        section_one_kernel,
        (full, full, full, full, shaped(size, members, kind=narrow)),
        (own, other, weight, decay, tau_load, coef),
        flops=200 * size * members,
    )
    own, other = lattice(rate_half)
    return on_core(
        section_two_kernel,
        (full, full),
        (own, other, state_var, tau_load, coef, stress, normal, rate, change),
        (
            pltpu.VMEM((size, members), wide),
            pltpu.VMEM((size, members), wide),
            pltpu.SemaphoreType.DMA((2, PIECES)),
        ),
        flops=200 * size * members,
        out_far=True,
    )


def solution(mesh):
    placed = (
        P(("row", "col"), "scen"),
        P(("row", "col"), "scen"),
        P(("row", "col"), "scen"),
        P(("row", "col")),
        P(("row", "col")),
        P(("row", "col")),
        P("row", "col", None, None),
        P(None, "row", "col", None, None),
        P(None, "row", "col", None, None),
        P("row", "col"),
        P("row", "col"),
    )
    return jax.shard_map(
        body,
        mesh=mesh,
        in_specs=placed,
        out_specs=(P(("row", "col"), "scen"), P(("row", "col"), "scen")),
        check_vma=False,
    )
```

```python
import functools

import jax
import jax.numpy as jnp
from jax import lax
from jax.experimental import pallas as pl
from jax.experimental.pallas import tpu as pltpu
from jax.sharding import PartitionSpec as P

NEWTON = 2
DIRECT_COUNTS = (4, 8)
TILE = 128

damping = 0.5
sigma_floor = 0.5
section_step = 0.1


def arrivals(count, direct):
    if not direct:
        cuts = [0, max(count - 4, 0), count]
        return [list(range(first, last)) for first, last in zip(cuts, cuts[1:]) if last > first]
    return [[0, 1, 4, 2], [7, 3, 5, 6]] if count == 8 else [[0, 1], [2, 3]]


def row_met(spot, row, direct):
    return jnp.bitwise_xor(row, spot) if direct else spot


def gather_direct(block, count):
    def swapped(mask, data):
        return lax.ppermute(data, "row", [(row, row ^ mask) for row in range(count)])

    found = {0: block}
    for mask in (4, 2, 1, 7) if count == 8 else (2, 1):
        found[mask] = swapped(mask, block)
    if count == 8:
        for mask in (1, 2):
            found[4 + mask] = swapped(mask, found[4])
    found[3] = swapped(1, found[2])
    return [[found[mask] for mask in group] for group in arrivals(count, True)]


PIECES = 4


def row_pieces(size):
    tall = size // PIECES
    return [pl.ds(at * tall, tall) for at in range(PIECES)]


def narrow_kernel(wide_ref, narrow_ref, held, sem):
    copies = [
        pltpu.make_async_copy(wide_ref.at[part], held.at[part], sem.at[at])
        for at, part in enumerate(row_pieces(held.shape[0]))
    ]
    for copy in copies:
        copy.start()
    for copy, part in zip(copies, row_pieces(held.shape[0])):
        copy.wait()
        narrow_ref[part, :] = held[part, :].astype(narrow_ref.dtype)


def prepare_kernel(groups, direct, *refs):
    far, (v_out, u_out, coef_out, weight_out, decay_out), near, sem = refs[:7], refs[7:12], refs[12:19], refs[19]
    copies = [
        pltpu.make_async_copy(source, held, sem.at[at])
        for at, (source, held) in enumerate(zip(far, near))
    ]
    for copy in copies:
        copy.start()
    for copy in copies:
        copy.wait()
    rank_ref, v_ref, u_ref, sigma_ref, a_ref, b_ref, state_ref = near
    kinds, rows, count, rank_count, size = u_ref.shape
    row = lax.axis_index("row")
    met = [row_met(spot, row, direct) for group in groups for spot in group]
    for at, q in enumerate(met):
        for p in range(rows):
            inside = lax.broadcasted_iota(jnp.int32, (rank_count, size), 0) < rank_ref[p, q]
            v_out[at, p] = jnp.where(inside, v_ref[p, q].astype(jnp.float32), 0.0).astype(v_out.dtype)
    for p in range(rows):
        for kind in range(kinds):
            first = start = 0
            for spots in groups:
                group = [u_ref[kind, p, q] for q in met[first : first + len(spots)]]
                spare = -len(group) * rank_count % TILE
                if spare:
                    group.append(jnp.zeros((spare, size), u_ref.dtype))
                turned = jnp.concatenate(group, axis=0).astype(jnp.float32).T
                stop = start + turned.shape[1]
                u_out[p, kind * size : (kind + 1) * size, start:stop] = turned.astype(u_out.dtype)
                first, start = first + len(spots), stop
    lanes = coef_out.shape[2]
    for at, values in enumerate((sigma_ref[...], a_ref[...], b_ref[...], 1.0 / a_ref[...], 1.0 / b_ref[...])):
        coef_out[at] = jnp.broadcast_to(values, (lanes, size)).T
    for first in range(0, state_ref.shape[1], lanes):
        part = slice(first, first + lanes)
        state = state_ref[:, part]
        weight_out[:, part] = jnp.exp(-state * coef_out[3])
        decay_out[:, part] = jnp.exp(-state * coef_out[4])


def sums_kernel(spots, direct, first, start, pick, before, near_any, v_ref, u_ref, d_ref, *refs):
    blocks = refs[: len(spots)]
    refs = refs[len(spots) :]
    if before:
        sums_ref, refs = refs[0], refs[1:]
    out_ref, x_all, proj, near_ref, near_sem = refs[:5]
    total = refs[5] if pick == 1 else out_ref
    count, rows, rank_count, size = v_ref.shape
    kinds, slots = d_ref.shape[0], near_ref.shape[1]
    near_copy = pltpu.make_async_copy(near_any, near_ref, near_sem)
    near_copy.start()
    row, col = lax.axis_index("row"), lax.axis_index("col")
    met = [row_met(spot, row, direct) for spot in spots]
    chosen = list(range(rows)) if pick is None else [col if pick == 0 else 1 - col]
    places = [(place,) for place in range(rows)] if pick is None else [()]
    for at, block in enumerate(blocks):
        if pick is None:
            weights = v_ref[first + at].reshape(rows * rank_count, size)
        else:
            weights = v_ref[first + at, chosen[0]]
        part = jnp.dot(weights, block[...], preferred_element_type=jnp.float32).astype(proj.dtype)
        for place in range(len(chosen)):
            proj[place, at * rank_count : (at + 1) * rank_count, :] = part[
                place * rank_count : (place + 1) * rank_count
            ]
    for at, block in enumerate(blocks):
        x_all[at] = block[...]
    lanes = slice(start, start + len(blocks) * rank_count)
    for place, p in enumerate(chosen):
        gained = jnp.dot(u_ref[p, :, lanes], proj[place], preferred_element_type=jnp.float32)
        for kind in range(kinds):
            piece = gained[kind * size : (kind + 1) * size]
            total[*places[place], kind] = sums_ref[p, kind] + piece if before else piece
    near_copy.wait()
    for place, p in enumerate(chosen):
        for s in range(slots):
            near = near_ref[p, s] - col * count
            at = sum(jnp.where(near == q, i, 0) for i, q in enumerate(met))
            hit = sum(jnp.where(near == q, 1, 0) for q in met)

            @pl.when(hit > 0)
            def _():
                block = x_all[at]
                for kind in range(kinds):
                    total[*places[place], kind] += jnp.dot(
                        d_ref[kind, p, s], block, preferred_element_type=jnp.float32
                    )
    if pick == 1:
        out_ref[...] = total[...].astype(out_ref.dtype)


def inverse(value):
    rough = pl.reciprocal(value, approx=True)
    return rough * (2.0 - value * rough)


def sinh_cosh(value):
    grown = jnp.exp(value)
    shrunk = inverse(grown)
    square = value * value
    small = value * (1.0 + square * (1 / 6 + square * (1 / 120)))
    sinh = jnp.where(square < 0.25, small, 0.5 * (grown - shrunk))
    return sinh, 0.5 * (grown + shrunk)


def friction(shear, normal, weight, decay, tau_load, sigma_base, a_wide, b_wide):
    tau = tau_load + shear
    size = jnp.abs(tau)
    stiff = jnp.maximum(sigma_base + normal, sigma_floor) * a_wide
    double = 2.0 * damping * weight
    drive = size * inverse(double)
    square = drive * drive + 1.0
    slope = jnp.minimum(size * inverse(stiff), jnp.log(drive + square * lax.rsqrt(square)))
    for newton_step in range(NEWTON):
        sinh, cosh = sinh_cosh(slope)
        excess = stiff * slope + double * sinh - size
        slope = slope - excess * inverse(stiff + double * cosh)
    rate = 2.0 * weight * sinh_cosh(slope)[0]
    change = b_wide * (decay - jnp.abs(rate))
    return (jnp.where(tau < 0.0, -rate, rate), change)


def over_pieces(begin, tall, members, lanes, work):
    step = min(tall, 32)

    @pl.loop(0, tall // step)
    def _(index):
        rows = pl.ds(pl.multiple_of(begin + index * step, step), step)
        for first in range(0, members, lanes):
            work(rows, slice(first, first + lanes))


def section_one_kernel(own, other, weight, decay, tau, coef, stress, normal, rate, change, rate_half):
    size, members = tau.shape

    def work(rows, part):
        shear = own[0, rows, part] + other[0, rows, part].astype(jnp.float32)
        press = own[1, rows, part] + other[1, rows, part].astype(jnp.float32)
        stress[rows, part] = shear
        normal[rows, part] = press
        first, second = friction(
            shear,
            press,
            weight[rows, part],
            decay[rows, part],
            tau[rows, part],
            coef[0, rows, :],
            coef[1, rows, :],
            coef[2, rows, :],
        )
        rate[rows, part] = first
        change[rows, part] = second
        rate_half[rows, part] = first.astype(rate_half.dtype)

    over_pieces(0, size, members, coef.shape[2], work)


def section_two_kernel(
    own, other, state, tau, coef, stress, normal, rate, change, rate_out, change_out, mean_rate, mean_change, sem
):
    size, members = tau.shape

    def work(rows, part):
        shear = own[0, rows, part] + other[0, rows, part].astype(jnp.float32)
        press = own[1, rows, part] + other[1, rows, part].astype(jnp.float32)
        sigma, a_wide, b_wide = coef[0, rows, :], coef[1, rows, :], coef[2, rows, :]
        later = state[rows, part] + section_step * change[rows, part]
        first, second = friction(
            stress[rows, part] + section_step * shear,
            normal[rows, part] + section_step * press,
            jnp.exp(-later * coef[3, rows, :]),
            jnp.exp(-later * coef[4, rows, :]),
            tau[rows, part],
            sigma,
            a_wide,
            b_wide,
        )
        mean_rate[rows, part] = (rate[rows, part] + first) * 0.5
        mean_change[rows, part] = (change[rows, part] + second) * 0.5

    copies = []
    for at, part in enumerate(row_pieces(size)):
        over_pieces(part.start, part.size, members, coef.shape[2], work)
        for kind, (held, out) in enumerate(((mean_rate, rate_out), (mean_change, change_out))):
            copies.append(pltpu.make_async_copy(held.at[part], out.at[part], sem.at[kind, at]))
            copies[-1].start()
    for copy in copies:
        copy.wait()


def on_core(kernel, outs, arrays, scratch=(), flops=0, room=16, far=(), out_far=False):
    vmem, hbm = pl.BlockSpec(memory_space=pltpu.VMEM), pl.BlockSpec(memory_space=pl.ANY)
    arrays = (*(pltpu.with_memory_space_constraint(a, pltpu.HBM) for a in far), *arrays)
    return pl.pallas_call(
        kernel,
        out_shape=outs,
        in_specs=[hbm] * len(far) + [vmem] * (len(arrays) - len(far)),
        out_specs=jax.tree.map(lambda _: hbm if out_far else vmem, outs),
        scratch_shapes=list(scratch),
        compiler_params=pltpu.CompilerParams(vmem_limit_bytes=room * 1024 * 1024),
        cost_estimate=pl.CostEstimate(
            flops=flops, bytes_accessed=sum(a.size * a.dtype.itemsize for a in arrays), transcendentals=0
        ),
    )(*arrays)


def body(
    slip_deficit,
    state_var,
    tau_load,
    sigma_base,
    a_coef,
    b_coef,
    v_basis,
    u_basis,
    dense_blocks,
    block_ranks,
    near_index,
):
    count = lax.axis_size("row")
    size, members = slip_deficit.shape
    kinds, rows, _, rank_count, _ = u_basis.shape
    direct = count in DIRECT_COUNTS
    groups = arrivals(count, direct)
    firsts = [sum(len(group) for group in groups[:at]) for at in range(len(groups))]
    tiles = [-(-len(group) * rank_count // TILE) * TILE for group in groups]
    starts = [sum(tiles[:at]) for at in range(len(groups))]
    room = 16 if direct else 40
    lanes = min(members, 128)
    narrow, wide = jnp.bfloat16, jnp.float32
    swap = [(0, 1), (1, 0)]

    def shaped(*shape, kind=wide):
        return jax.ShapeDtypeStruct(shape, kind)

    full = shaped(size, members)
    v_met, u_met, coef, weight, decay = on_core(
        functools.partial(prepare_kernel, groups, direct),
        (
            shaped(count, rows, rank_count, size, kind=narrow),
            shaped(rows, kinds * size, sum(tiles), kind=narrow),
            shaped(5, size, lanes),
            full,
            full,
        ),
        (),
        (
            pltpu.SMEM(block_ranks.shape, jnp.int32),
            pltpu.VMEM(v_basis.shape, narrow),
            pltpu.VMEM(u_basis.shape, narrow),
            *[pltpu.VMEM((1, size), wide)] * 3,
            pltpu.VMEM((size, members), wide),
            pltpu.SemaphoreType.DMA((7,)),
        ),
        room=room,
        far=(
            block_ranks,
            v_basis,
            u_basis,
            sigma_base.reshape(1, size),
            a_coef.reshape(1, size),
            b_coef.reshape(1, size),
            state_var,
        ),
    )

    def add(blocks, at, pick, before, kind):
        held = rows if pick is None else 1
        lead = (rows, kinds) if pick is None else (kinds,)
        return on_core(
            functools.partial(
                sums_kernel, groups[at], direct, firsts[at], starts[at], pick, before is not None
            ),
            shaped(*lead, size, members, kind=kind),
            (v_met, u_met, dense_blocks, *blocks, *(() if before is None else (before,))),
            (
                pltpu.VMEM((len(blocks), size, members), narrow),
                pltpu.VMEM((held, len(blocks) * rank_count, members), narrow),
                pltpu.SMEM(near_index.shape, jnp.int32),
                pltpu.SemaphoreType.DMA(()),
                *([pltpu.VMEM((kinds, size, members), wide)] if pick == 1 else []),
            ),
            2 * held * size * members * rank_count * len(blocks) * 3,
            room,
            far=(near_index,),
        )

    def lattice(field_half):
        if direct:
            found = gather_direct(field_half, count)
        else:
            whole = lax.all_gather(field_half, "row", axis=0)
            found = [[whole[r] for r in group] for group in groups]
        sums, end = None, len(groups) - 1
        for at in range(end):
            sums = add(found[at], at, None, sums, wide)
        other = lax.ppermute(add(found[end], end, 1, sums, narrow), "col", swap)
        return add(found[end], end, 0, sums, wide), other

    slip_half = on_core(
        narrow_kernel,
        shaped(size, members, kind=narrow),
        (),
        (pltpu.VMEM((size, members), wide), pltpu.SemaphoreType.DMA((PIECES,))),
        far=(slip_deficit,),
    )
    own, other = lattice(slip_half)
    stress, normal, rate, change, rate_half = on_core(
        section_one_kernel,
        (full, full, full, full, shaped(size, members, kind=narrow)),
        (own, other, weight, decay, tau_load, coef),
        flops=200 * size * members,
    )
    own, other = lattice(rate_half)
    return on_core(
        section_two_kernel,
        (full, full),
        (own, other, state_var, tau_load, coef, stress, normal, rate, change),
        (
            pltpu.VMEM((size, members), wide),
            pltpu.VMEM((size, members), wide),
            pltpu.SemaphoreType.DMA((2, PIECES)),
        ),
        flops=200 * size * members,
        out_far=True,
    )


def solution(mesh):
    placed = (
        P(("row", "col"), "scen"),
        P(("row", "col"), "scen"),
        P(("row", "col"), "scen"),
        P(("row", "col")),
        P(("row", "col")),
        P(("row", "col")),
        P("row", "col", None, None),
        P(None, "row", "col", None, None),
        P(None, "row", "col", None, None),
        P("row", "col"),
        P("row", "col"),
    )
    return jax.shard_map(
        body,
        mesh=mesh,
        in_specs=placed,
        out_specs=(P(("row", "col"), "scen"), P(("row", "col"), "scen")),
        check_vma=False,
    )
```

```python
import functools

import jax
import jax.numpy as jnp
from jax import lax
from jax.experimental import pallas as pl
from jax.experimental.pallas import tpu as pltpu
from jax.sharding import PartitionSpec as P

NEWTON = 2
DIRECT_COUNTS = (4, 8)
LATE = 4

damping = 0.5
sigma_floor = 0.5
section_step = 0.1


def arrivals(count, direct):
    if not direct:
        return list(range(count))
    return [0, 1, 4, 2, 3, 5, 6, 7] if count == 8 else [0, 1, 2, 3]


def row_met(spot, row, direct):
    return jnp.bitwise_xor(row, spot) if direct else spot


def gather_direct(block, count):
    def swapped(mask, data):
        return lax.ppermute(data, "row", [(row, row ^ mask) for row in range(count)])

    found = {0: block}
    for mask in (4, 1, 2, 3) if count == 8 else (1, 2, 3):
        found[mask] = swapped(mask, block)
    if count == 8:
        for mask in (1, 2, 3):
            found[4 + mask] = swapped(mask, found[4])
    return [found[mask] for mask in arrivals(count, True)]


PIECES = 8


def row_pieces(size):
    tall = size // PIECES
    return [pl.ds(at * tall, tall) for at in range(PIECES)]


def narrow_kernel(wide_ref, narrow_ref, held, sem):
    copies = [
        pltpu.make_async_copy(wide_ref.at[part], held.at[part], sem.at[at])
        for at, part in enumerate(row_pieces(held.shape[0]))
    ]
    for copy in copies:
        copy.start()
    for copy, part in zip(copies, row_pieces(held.shape[0])):
        copy.wait()
        narrow_ref[part, :] = held[part, :].astype(narrow_ref.dtype)


def store_powers(outs, part, state, coef):
    outs[0][:, part] = jnp.exp(-state * coef[3])
    outs[1][:, part] = jnp.exp(state * coef[3])
    outs[2][:, part] = jnp.exp(-state * coef[4])


def later_kernel(state, change, coef, *outs):
    lanes = coef.shape[2]
    for first in range(0, state.shape[1], lanes):
        part = slice(first, first + lanes)
        store_powers(outs, part, state[:, part] + section_step * change[:, part], coef)


def prepare_kernel(spots, direct, *refs):
    far, (v_out, u_out, coef_out, *powers), near, sem = refs[:7], refs[7:13], refs[13:20], refs[20]
    copies = [
        pltpu.make_async_copy(source, held, sem.at[at])
        for at, (source, held) in enumerate(zip(far, near))
    ]
    for copy in copies:
        copy.start()
    for copy in copies:
        copy.wait()
    rank_ref, v_ref, u_ref, sigma_ref, a_ref, b_ref, state_ref = near
    kinds, rows, count, rank_count, size = u_ref.shape
    row = lax.axis_index("row")
    met = [row_met(spot, row, direct) for spot in spots]
    for at, q in enumerate(met):
        for p in range(rows):
            inside = lax.broadcasted_iota(jnp.int32, (rank_count, size), 0) < rank_ref[p, q]
            v_out[at, p] = jnp.where(inside, v_ref[p, q].astype(jnp.float32), 0.0).astype(v_out.dtype)
    for p in range(rows):
        for kind in range(kinds):
            for first in range(0, count, 4):
                group = [u_ref[kind, p, q] for q in met[first : first + 4]]
                turned = jnp.concatenate(group, axis=0).astype(jnp.float32).T
                u_out[p, kind * size : (kind + 1) * size, first * rank_count : (first + len(group)) * rank_count] = (
                    turned.astype(u_out.dtype)
                )
    lanes = coef_out.shape[2]
    for at, values in enumerate((sigma_ref[...], a_ref[...], b_ref[...], 1.0 / a_ref[...], 1.0 / b_ref[...])):
        coef_out[at] = jnp.broadcast_to(values, (lanes, size)).T
    for first in range(0, state_ref.shape[1], lanes):
        part = slice(first, first + lanes)
        store_powers(powers, part, state_ref[:, part], coef_out)


def sums_kernel(spots, direct, first, pick, before, near_any, v_ref, u_ref, d_ref, *refs):
    blocks = refs[: len(spots)]
    refs = refs[len(spots) :]
    if before:
        sums_ref, refs = refs[0], refs[1:]
    out_ref, x_all, proj, near_ref, near_sem = refs
    count, rows, rank_count, size = v_ref.shape
    kinds, slots = d_ref.shape[0], near_ref.shape[1]
    near_copy = pltpu.make_async_copy(near_any, near_ref, near_sem)
    near_copy.start()
    row, col = lax.axis_index("row"), lax.axis_index("col")
    met = [row_met(spot, row, direct) for spot in spots]
    chosen = list(range(rows)) if pick is None else [col if pick == 0 else 1 - col]
    places = [(place,) for place in range(rows)] if pick is None else [()]
    for at, block in enumerate(blocks):
        if pick is None:
            weights = v_ref[first + at].reshape(rows * rank_count, size)
        else:
            weights = v_ref[first + at, chosen[0]]
        part = jnp.dot(weights, block[...], preferred_element_type=jnp.float32).astype(proj.dtype)
        for place in range(len(chosen)):
            proj[place, at * rank_count : (at + 1) * rank_count, :] = part[
                place * rank_count : (place + 1) * rank_count
            ]
    for at, block in enumerate(blocks):
        x_all[at] = block[...]
    x_all[len(blocks)] = jnp.zeros_like(x_all[0])
    lanes = slice(first * rank_count, (first + len(blocks)) * rank_count)
    near_copy.wait()
    for place, p in enumerate(chosen):
        total = jnp.dot(u_ref[p, :, lanes], proj[place], preferred_element_type=jnp.float32)
        for s in range(slots):
            near = near_ref[p, s] - col * count
            at = len(blocks) - sum(jnp.where(near == q, len(blocks) - i, 0) for i, q in enumerate(met))
            weights = jnp.concatenate([d_ref[kind, p, s] for kind in range(kinds)], axis=0)
            total += jnp.dot(weights, x_all[at], preferred_element_type=jnp.float32)
        for kind in range(kinds):
            piece = total[kind * size : (kind + 1) * size]
            if before:
                piece += sums_ref[p, kind]
            out_ref[*places[place], kind] = piece.astype(out_ref.dtype)


def inverse(value):
    rough = pl.reciprocal(value, approx=True)
    return rough * (2.0 - value * rough)


def sinh_cosh(value):
    grown = jnp.exp(value)
    shrunk = inverse(grown)
    square = value * value
    small = value * (1.0 + square * (1 / 6 + square * (1 / 120)))
    sinh = jnp.where(square < 0.25, small, 0.5 * (grown - shrunk))
    return sinh, 0.5 * (grown + shrunk)


def friction(shear, normal, weight, unweight, decay, tau_load, sigma_base, a_wide, b_wide):
    tau = tau_load + shear
    size = jnp.abs(tau)
    stiff = jnp.maximum(sigma_base + normal, sigma_floor) * a_wide
    double = 2.0 * damping * weight
    drive = size * unweight * (0.5 / damping)
    square = drive * drive + 1.0
    slope = jnp.minimum(size * inverse(stiff), jnp.log(drive + square * lax.rsqrt(square)))
    for newton_step in range(NEWTON):
        sinh, cosh = sinh_cosh(slope)
        excess = stiff * slope + double * sinh - size
        slope = slope - excess * inverse(stiff + double * cosh)
    rate = 2.0 * weight * sinh_cosh(slope)[0]
    change = b_wide * (decay - jnp.abs(rate))
    return (jnp.where(tau < 0.0, -rate, rate), change)


def over_pieces(begin, tall, members, lanes, work):
    step = min(tall, 32)

    @pl.loop(0, tall // step)
    def _(index):
        rows = pl.ds(pl.multiple_of(begin + index * step, step), step)
        for first in range(0, members, lanes):
            work(rows, slice(first, first + lanes))


def section_one_kernel(own, other, weight, unweight, decay, tau, coef, stress, normal, rate, change, rate_half):
    size, members = tau.shape

    def work(rows, part):
        shear = own[0, rows, part] + other[0, rows, part].astype(jnp.float32)
        press = own[1, rows, part] + other[1, rows, part].astype(jnp.float32)
        stress[rows, part] = shear
        normal[rows, part] = press
        first, second = friction(
            shear,
            press,
            weight[rows, part],
            unweight[rows, part],
            decay[rows, part],
            tau[rows, part],
            coef[0, rows, :],
            coef[1, rows, :],
            coef[2, rows, :],
        )
        rate[rows, part] = first
        change[rows, part] = second
        rate_half[rows, part] = first.astype(rate_half.dtype)

    over_pieces(0, size, members, coef.shape[2], work)


def section_two_kernel(
    own, other, weight, unweight, decay, tau, coef, stress, normal, rate, change, rate_out, change_out, mean_rate, mean_change, sem
):
    size, members = tau.shape

    def work(rows, part):
        shear = own[0, rows, part] + other[0, rows, part].astype(jnp.float32)
        press = own[1, rows, part] + other[1, rows, part].astype(jnp.float32)
        first, second = friction(
            stress[rows, part] + section_step * shear,
            normal[rows, part] + section_step * press,
            weight[rows, part],
            unweight[rows, part],
            decay[rows, part],
            tau[rows, part],
            coef[0, rows, :],
            coef[1, rows, :],
            coef[2, rows, :],
        )
        mean_rate[rows, part] = (rate[rows, part] + first) * 0.5
        mean_change[rows, part] = (change[rows, part] + second) * 0.5

    copies = []
    for at, part in enumerate(row_pieces(size)):
        over_pieces(part.start, part.size, members, coef.shape[2], work)
        for kind, (held, out) in enumerate(((mean_rate, rate_out), (mean_change, change_out))):
            copies.append(pltpu.make_async_copy(held.at[part], out.at[part], sem.at[kind, at]))
            copies[-1].start()
    for copy in copies:
        copy.wait()


def on_core(kernel, outs, arrays, scratch=(), flops=0, room=16, far=(), out_far=False):
    vmem, hbm = pl.BlockSpec(memory_space=pltpu.VMEM), pl.BlockSpec(memory_space=pl.ANY)
    arrays = (*(pltpu.with_memory_space_constraint(a, pltpu.HBM) for a in far), *arrays)
    return pl.pallas_call(
        kernel,
        out_shape=outs,
        in_specs=[hbm] * len(far) + [vmem] * (len(arrays) - len(far)),
        out_specs=jax.tree.map(lambda _: hbm if out_far else vmem, outs),
        scratch_shapes=list(scratch),
        compiler_params=pltpu.CompilerParams(vmem_limit_bytes=room * 1024 * 1024),
        cost_estimate=pl.CostEstimate(
            flops=flops, bytes_accessed=sum(a.size * a.dtype.itemsize for a in arrays), transcendentals=0
        ),
    )(*arrays)


def body(
    slip_deficit,
    state_var,
    tau_load,
    sigma_base,
    a_coef,
    b_coef,
    v_basis,
    u_basis,
    dense_blocks,
    block_ranks,
    near_index,
):
    count = lax.axis_size("row")
    size, members = slip_deficit.shape
    kinds, rows, _, rank_count, _ = u_basis.shape
    direct = count in DIRECT_COUNTS
    spots = arrivals(count, direct)
    early = max(count - LATE, 0)
    room = 16 if direct else 40
    lanes = min(members, 128)
    narrow, wide = jnp.bfloat16, jnp.float32
    swap = [(0, 1), (1, 0)]

    def shaped(*shape, kind=wide):
        return jax.ShapeDtypeStruct(shape, kind)

    full = shaped(size, members)
    v_met, u_met, coef, *powers = on_core(
        functools.partial(prepare_kernel, spots, direct),
        (
            shaped(count, rows, rank_count, size, kind=narrow),
            shaped(rows, kinds * size, count * rank_count, kind=narrow),
            shaped(5, size, lanes),
            full,
            full,
            full,
        ),
        (),
        (
            pltpu.SMEM(block_ranks.shape, jnp.int32),
            pltpu.VMEM(v_basis.shape, narrow),
            pltpu.VMEM(u_basis.shape, narrow),
            *[pltpu.VMEM((1, size), wide)] * 3,
            pltpu.VMEM((size, members), wide),
            pltpu.SemaphoreType.DMA((7,)),
        ),
        room=room,
        far=(
            block_ranks,
            v_basis,
            u_basis,
            sigma_base.reshape(1, size),
            a_coef.reshape(1, size),
            b_coef.reshape(1, size),
            state_var,
        ),
    )

    def add(blocks, first, pick, before, kind):
        held = rows if pick is None else 1
        lead = (rows, kinds) if pick is None else (kinds,)
        return on_core(
            functools.partial(
                sums_kernel, spots[first : first + len(blocks)], direct, first, pick, before is not None
            ),
            shaped(*lead, size, members, kind=kind),
            (v_met, u_met, dense_blocks, *blocks, *(() if before is None else (before,))),
            (
                pltpu.VMEM((len(blocks) + 1, size, members), narrow),
                pltpu.VMEM((held, len(blocks) * rank_count, members), narrow),
                pltpu.SMEM(near_index.shape, jnp.int32),
                pltpu.SemaphoreType.DMA(()),
            ),
            2 * held * size * members * rank_count * len(blocks) * 3,
            room,
            far=(near_index,),
        )

    def lattice(field_half, beside):
        if direct:
            blocks = gather_direct(field_half, count)
        else:
            whole = lax.all_gather(field_half, "row", axis=0)
            blocks = [whole[r] for r in range(count)]
        blocks[0], beside = lax.optimization_barrier((blocks[0], beside))
        sums = add(blocks[:early], 0, None, None, wide) if early else None
        other = lax.ppermute(add(blocks[early:], early, 1, sums, narrow), "col", swap)
        return add(blocks[early:], early, 0, sums, wide), other, beside

    slip_half = on_core(
        narrow_kernel,
        shaped(size, members, kind=narrow),
        (),
        (pltpu.VMEM((size, members), wide), pltpu.SemaphoreType.DMA((PIECES,))),
        far=(slip_deficit,),
    )
    own, other, powers = lattice(slip_half, powers)
    stress, normal, rate, change, rate_half = on_core(
        section_one_kernel,
        (full, full, full, full, shaped(size, members, kind=narrow)),
        (own, other, *powers, tau_load, coef),
        flops=200 * size * members,
    )
    powers = on_core(later_kernel, (full, full, full), (state_var, change, coef))
    own, other, powers = lattice(rate_half, powers)
    return on_core(
        section_two_kernel,
        (full, full),
        (own, other, *powers, tau_load, coef, stress, normal, rate, change),
        (
            pltpu.VMEM((size, members), wide),
            pltpu.VMEM((size, members), wide),
            pltpu.SemaphoreType.DMA((2, PIECES)),
        ),
        flops=200 * size * members,
        out_far=True,
    )


def solution(mesh):
    placed = (
        P(("row", "col"), "scen"),
        P(("row", "col"), "scen"),
        P(("row", "col"), "scen"),
        P(("row", "col")),
        P(("row", "col")),
        P(("row", "col")),
        P("row", "col", None, None),
        P(None, "row", "col", None, None),
        P(None, "row", "col", None, None),
        P("row", "col"),
        P("row", "col"),
    )
    return jax.shard_map(
        body,
        mesh=mesh,
        in_specs=placed,
        out_specs=(P(("row", "col"), "scen"), P(("row", "col"), "scen")),
        check_vma=False,
    )
```

```python
import functools

import jax
import jax.numpy as jnp
from jax import lax
from jax.experimental import pallas as pl
from jax.experimental.pallas import tpu as pltpu
from jax.sharding import PartitionSpec as P

NEWTON = 2
DIRECT_COUNTS = (4, 8)
LATE = 4

damping = 0.5
sigma_floor = 0.5
section_step = 0.1


def arrivals(count, direct):
    if not direct:
        return list(range(count))
    return [0, 1, 4, 2, 3, 5, 6, 7] if count == 8 else [0, 1, 2, 3]


def row_met(spot, row, direct):
    return jnp.bitwise_xor(row, spot) if direct else spot


def gather_direct(block, count):
    def swapped(mask, data):
        return lax.ppermute(data, "row", [(row, row ^ mask) for row in range(count)])

    found = {0: block}
    for mask in (4, 1, 2, 3) if count == 8 else (1, 2, 3):
        found[mask] = swapped(mask, block)
    if count == 8:
        for mask in (1, 2, 3):
            found[4 + mask] = swapped(mask, found[4])
    return [found[mask] for mask in arrivals(count, True)]


IN_PIECES = 8
OUT_PIECES = 4


def row_pieces(size, pieces):
    tall = size // pieces
    return [pl.ds(at * tall, tall) for at in range(pieces)]


def narrow_kernel(wide_ref, narrow_ref, held, sem):
    copies = [
        pltpu.make_async_copy(wide_ref.at[part], held.at[part], sem.at[at])
        for at, part in enumerate(row_pieces(held.shape[0], IN_PIECES))
    ]
    for copy in copies:
        copy.start()
    for copy, part in zip(copies, row_pieces(held.shape[0], IN_PIECES)):
        copy.wait()
        narrow_ref[part, :] = held[part, :].astype(narrow_ref.dtype)


def store_powers(outs, part, state, coef):
    outs[0][:, part] = jnp.exp(-state * coef[3])
    outs[1][:, part] = jnp.exp(state * coef[3])
    outs[2][:, part] = jnp.exp(-state * coef[4])


def later_kernel(state, change, coef, *outs):
    lanes = coef.shape[2]
    for first in range(0, state.shape[1], lanes):
        part = slice(first, first + lanes)
        store_powers(outs, part, state[:, part] + section_step * change[:, part], coef)


def prepare_kernel(spots, direct, *refs):
    far, (v_out, u_out, coef_out, *powers), near, sem = refs[:7], refs[7:13], refs[13:20], refs[20]
    copies = [
        pltpu.make_async_copy(source, held, sem.at[at])
        for at, (source, held) in enumerate(zip(far, near))
    ]
    for copy in copies:
        copy.start()
    for copy in copies:
        copy.wait()
    rank_ref, v_ref, u_ref, sigma_ref, a_ref, b_ref, state_ref = near
    kinds, rows, count, rank_count, size = u_ref.shape
    row = lax.axis_index("row")
    met = [row_met(spot, row, direct) for spot in spots]
    for at, q in enumerate(met):
        for p in range(rows):
            inside = lax.broadcasted_iota(jnp.int32, (rank_count, size), 0) < rank_ref[p, q]
            v_out[at, p] = jnp.where(inside, v_ref[p, q].astype(jnp.float32), 0.0).astype(v_out.dtype)
    for p in range(rows):
        for kind in range(kinds):
            for first in range(0, count, 4):
                group = [u_ref[kind, p, q] for q in met[first : first + 4]]
                turned = jnp.concatenate(group, axis=0).astype(jnp.float32).T
                u_out[p, kind * size : (kind + 1) * size, first * rank_count : (first + len(group)) * rank_count] = (
                    turned.astype(u_out.dtype)
                )
    lanes = coef_out.shape[2]
    for at, values in enumerate((sigma_ref[...], a_ref[...], b_ref[...], 1.0 / a_ref[...], 1.0 / b_ref[...])):
        coef_out[at] = jnp.broadcast_to(values, (lanes, size)).T
    for first in range(0, state_ref.shape[1], lanes):
        part = slice(first, first + lanes)
        store_powers(powers, part, state_ref[:, part], coef_out)


def sums_kernel(spots, direct, first, pick, before, near_any, v_ref, u_ref, d_ref, *refs):
    blocks = refs[: len(spots)]
    refs = refs[len(spots) :]
    if before:
        sums_ref, refs = refs[0], refs[1:]
    out_ref, x_all, proj, near_ref, near_sem = refs
    count, rows, rank_count, size = v_ref.shape
    kinds, slots = d_ref.shape[0], near_ref.shape[1]
    near_copy = pltpu.make_async_copy(near_any, near_ref, near_sem)
    near_copy.start()
    row, col = lax.axis_index("row"), lax.axis_index("col")
    met = [row_met(spot, row, direct) for spot in spots]
    chosen = list(range(rows)) if pick is None else [col if pick == 0 else 1 - col]
    places = [(place,) for place in range(rows)] if pick is None else [()]
    for at, block in enumerate(blocks):
        if pick is None:
            weights = v_ref[first + at].reshape(rows * rank_count, size)
        else:
            weights = v_ref[first + at, chosen[0]]
        part = jnp.dot(weights, block[...], preferred_element_type=jnp.float32).astype(proj.dtype)
        for place in range(len(chosen)):
            proj[place, at * rank_count : (at + 1) * rank_count, :] = part[
                place * rank_count : (place + 1) * rank_count
            ]
    for at, block in enumerate(blocks):
        x_all[at] = block[...]
    x_all[len(blocks)] = jnp.zeros_like(x_all[0])
    lanes = slice(first * rank_count, (first + len(blocks)) * rank_count)
    near_copy.wait()
    for place, p in enumerate(chosen):
        weights, fields = [u_ref[p, :, lanes]], [proj[place]]
        for s in range(slots):
            near = near_ref[p, s] - col * count
            at = len(blocks) - sum(jnp.where(near == q, len(blocks) - i, 0) for i, q in enumerate(met))
            weights.append(jnp.concatenate([d_ref[kind, p, s] for kind in range(kinds)], axis=0))
            fields.append(x_all[at])
        total = jnp.dot(
            jnp.concatenate(weights, axis=1),
            jnp.concatenate(fields, axis=0),
            preferred_element_type=jnp.float32,
        )
        for kind in range(kinds):
            piece = total[kind * size : (kind + 1) * size]
            if before:
                piece += sums_ref[p, kind]
            out_ref[*places[place], kind] = piece.astype(out_ref.dtype)


def inverse(value):
    rough = pl.reciprocal(value, approx=True)
    return rough * (2.0 - value * rough)


def sinh_cosh(value):
    grown = jnp.exp(value)
    shrunk = inverse(grown)
    square = value * value
    small = value * (1.0 + square * (1 / 6 + square * (1 / 120)))
    sinh = jnp.where(square < 0.25, small, 0.5 * (grown - shrunk))
    return sinh, 0.5 * (grown + shrunk)


def friction(shear, normal, weight, unweight, decay, tau_load, sigma_base, a_wide, b_wide):
    tau = tau_load + shear
    size = jnp.abs(tau)
    stiff = jnp.maximum(sigma_base + normal, sigma_floor) * a_wide
    double = 2.0 * damping * weight
    drive = size * unweight * (0.5 / damping)
    square = drive * drive + 1.0
    slope = jnp.minimum(size * inverse(stiff), jnp.log(drive + square * lax.rsqrt(square)))
    for newton_step in range(NEWTON):
        sinh, cosh = sinh_cosh(slope)
        excess = stiff * slope + double * sinh - size
        slope = slope - excess * inverse(stiff + double * cosh)
    rate = 2.0 * weight * sinh_cosh(slope)[0]
    change = b_wide * (decay - jnp.abs(rate))
    return (jnp.where(tau < 0.0, -rate, rate), change)


def over_pieces(begin, tall, members, lanes, work):
    step = min(tall, 64)

    @pl.loop(0, tall // step)
    def _(index):
        rows = pl.ds(pl.multiple_of(begin + index * step, step), step)
        for first in range(0, members, lanes):
            work(rows, slice(first, first + lanes))


def section_one_kernel(own, other, weight, unweight, decay, tau, coef, stress, normal, rate, change, rate_half):
    size, members = tau.shape

    def work(rows, part):
        shear = own[0, rows, part] + other[0, rows, part].astype(jnp.float32)
        press = own[1, rows, part] + other[1, rows, part].astype(jnp.float32)
        stress[rows, part] = shear
        normal[rows, part] = press
        first, second = friction(
            shear,
            press,
            weight[rows, part],
            unweight[rows, part],
            decay[rows, part],
            tau[rows, part],
            coef[0, rows, :],
            coef[1, rows, :],
            coef[2, rows, :],
        )
        rate[rows, part] = first
        change[rows, part] = second
        rate_half[rows, part] = first.astype(rate_half.dtype)

    over_pieces(0, size, members, coef.shape[2], work)


def section_two_kernel(
    own, other, weight, unweight, decay, tau, coef, stress, normal, rate, change, rate_out, change_out, mean_rate, mean_change, sem
):
    size, members = tau.shape

    def work(rows, part):
        shear = own[0, rows, part] + other[0, rows, part].astype(jnp.float32)
        press = own[1, rows, part] + other[1, rows, part].astype(jnp.float32)
        first, second = friction(
            stress[rows, part] + section_step * shear,
            normal[rows, part] + section_step * press,
            weight[rows, part],
            unweight[rows, part],
            decay[rows, part],
            tau[rows, part],
            coef[0, rows, :],
            coef[1, rows, :],
            coef[2, rows, :],
        )
        mean_rate[rows, part] = (rate[rows, part] + first) * 0.5
        mean_change[rows, part] = (change[rows, part] + second) * 0.5

    copies = []
    for at, part in enumerate(row_pieces(size, OUT_PIECES)):
        over_pieces(part.start, part.size, members, coef.shape[2], work)
        for kind, (held, out) in enumerate(((mean_rate, rate_out), (mean_change, change_out))):
            copies.append(pltpu.make_async_copy(held.at[part], out.at[part], sem.at[kind, at]))
            copies[-1].start()
    for copy in copies:
        copy.wait()


def on_core(kernel, outs, arrays, scratch=(), flops=0, room=16, far=(), out_far=False):
    vmem, hbm = pl.BlockSpec(memory_space=pltpu.VMEM), pl.BlockSpec(memory_space=pl.ANY)
    arrays = (*(pltpu.with_memory_space_constraint(a, pltpu.HBM) for a in far), *arrays)
    return pl.pallas_call(
        kernel,
        out_shape=outs,
        in_specs=[hbm] * len(far) + [vmem] * (len(arrays) - len(far)),
        out_specs=jax.tree.map(lambda _: hbm if out_far else vmem, outs),
        scratch_shapes=list(scratch),
        compiler_params=pltpu.CompilerParams(vmem_limit_bytes=room * 1024 * 1024),
        cost_estimate=pl.CostEstimate(
            flops=flops, bytes_accessed=sum(a.size * a.dtype.itemsize for a in arrays), transcendentals=0
        ),
    )(*arrays)


def body(
    slip_deficit,
    state_var,
    tau_load,
    sigma_base,
    a_coef,
    b_coef,
    v_basis,
    u_basis,
    dense_blocks,
    block_ranks,
    near_index,
):
    count = lax.axis_size("row")
    size, members = slip_deficit.shape
    kinds, rows, _, rank_count, _ = u_basis.shape
    direct = count in DIRECT_COUNTS
    spots = arrivals(count, direct)
    early = max(count - LATE, 0)
    room = 16 if direct else 40
    lanes = min(members, 128)
    narrow, wide = jnp.bfloat16, jnp.float32
    swap = [(0, 1), (1, 0)]

    def shaped(*shape, kind=wide):
        return jax.ShapeDtypeStruct(shape, kind)

    full = shaped(size, members)
    v_met, u_met, coef, *powers = on_core(
        functools.partial(prepare_kernel, spots, direct),
        (
            shaped(count, rows, rank_count, size, kind=narrow),
            shaped(rows, kinds * size, count * rank_count, kind=narrow),
            shaped(5, size, lanes),
            full,
            full,
            full,
        ),
        (),
        (
            pltpu.SMEM(block_ranks.shape, jnp.int32),
            pltpu.VMEM(v_basis.shape, narrow),
            pltpu.VMEM(u_basis.shape, narrow),
            *[pltpu.VMEM((1, size), wide)] * 3,
            pltpu.VMEM((size, members), wide),
            pltpu.SemaphoreType.DMA((7,)),
        ),
        room=room,
        far=(
            block_ranks,
            v_basis,
            u_basis,
            sigma_base.reshape(1, size),
            a_coef.reshape(1, size),
            b_coef.reshape(1, size),
            state_var,
        ),
    )

    def add(blocks, first, pick, before, kind):
        held = rows if pick is None else 1
        lead = (rows, kinds) if pick is None else (kinds,)
        return on_core(
            functools.partial(
                sums_kernel, spots[first : first + len(blocks)], direct, first, pick, before is not None
            ),
            shaped(*lead, size, members, kind=kind),
            (v_met, u_met, dense_blocks, *blocks, *(() if before is None else (before,))),
            (
                pltpu.VMEM((len(blocks) + 1, size, members), narrow),
                pltpu.VMEM((held, len(blocks) * rank_count, members), narrow),
                pltpu.SMEM(near_index.shape, jnp.int32),
                pltpu.SemaphoreType.DMA(()),
            ),
            2 * held * size * members * rank_count * len(blocks) * 3,
            room,
            far=(near_index,),
        )

    def lattice(field_half, beside):
        if direct:
            blocks = gather_direct(field_half, count)
        else:
            whole = lax.all_gather(field_half, "row", axis=0)
            blocks = [whole[r] for r in range(count)]
        blocks[0], beside = lax.optimization_barrier((blocks[0], beside))
        sums = add(blocks[:early], 0, None, None, wide) if early else None
        other = lax.ppermute(add(blocks[early:], early, 1, sums, narrow), "col", swap)
        return add(blocks[early:], early, 0, sums, wide), other, beside

    slip_half = on_core(
        narrow_kernel,
        shaped(size, members, kind=narrow),
        (),
        (pltpu.VMEM((size, members), wide), pltpu.SemaphoreType.DMA((IN_PIECES,))),
        far=(slip_deficit,),
    )
    own, other, powers = lattice(slip_half, powers)
    stress, normal, rate, change, rate_half = on_core(
        section_one_kernel,
        (full, full, full, full, shaped(size, members, kind=narrow)),
        (own, other, *powers, tau_load, coef),
        flops=200 * size * members,
    )
    powers = on_core(later_kernel, (full, full, full), (state_var, change, coef))
    own, other, powers = lattice(rate_half, powers)
    return on_core(
        section_two_kernel,
        (full, full),
        (own, other, *powers, tau_load, coef, stress, normal, rate, change),
        (
            pltpu.VMEM((size, members), wide),
            pltpu.VMEM((size, members), wide),
            pltpu.SemaphoreType.DMA((2, OUT_PIECES)),
        ),
        flops=200 * size * members,
        out_far=True,
    )


def solution(mesh):
    placed = (
        P(("row", "col"), "scen"),
        P(("row", "col"), "scen"),
        P(("row", "col"), "scen"),
        P(("row", "col")),
        P(("row", "col")),
        P(("row", "col")),
        P("row", "col", None, None),
        P(None, "row", "col", None, None),
        P(None, "row", "col", None, None),
        P("row", "col"),
        P("row", "col"),
    )
    return jax.shard_map(
        body,
        mesh=mesh,
        in_specs=placed,
        out_specs=(P(("row", "col"), "scen"), P(("row", "col"), "scen")),
        check_vma=False,
    )
```

```python
import functools

import jax
import jax.numpy as jnp
from jax import lax
from jax.experimental import pallas as pl
from jax.experimental.pallas import tpu as pltpu
from jax.sharding import PartitionSpec as P

NEWTON = 2
DIRECT_COUNTS = (4, 8)
LATE = 4

damping = 0.5
sigma_floor = 0.5
section_step = 0.1


def arrivals(count, direct):
    if not direct:
        return list(range(count))
    return [0, 1, 4, 2, 3, 5, 6, 7] if count == 8 else [0, 1, 2, 3]


def row_met(spot, row, direct):
    return jnp.bitwise_xor(row, spot) if direct else spot


def gather_direct(block, count):
    def swapped(mask, data):
        return lax.ppermute(data, "row", [(row, row ^ mask) for row in range(count)])

    found = {0: block}
    for mask in (4, 1, 2, 3) if count == 8 else (1, 2, 3):
        found[mask] = swapped(mask, block)
    if count == 8:
        for mask in (1, 2, 3):
            found[4 + mask] = swapped(mask, found[4])
    return [found[mask] for mask in arrivals(count, True)]


IN_PIECES = 8
OUT_PIECES = 4


def row_pieces(size, pieces):
    tall = size // pieces
    return [pl.ds(at * tall, tall) for at in range(pieces)]


def narrow_kernel(wide_ref, narrow_ref, held, sem):
    copies = [
        pltpu.make_async_copy(wide_ref.at[part], held.at[part], sem.at[at])
        for at, part in enumerate(row_pieces(held.shape[0], IN_PIECES))
    ]
    for copy in copies:
        copy.start()
    for copy, part in zip(copies, row_pieces(held.shape[0], IN_PIECES)):
        copy.wait()
        narrow_ref[part, :] = held[part, :].astype(narrow_ref.dtype)


def store_powers(outs, part, state, coef):
    outs[0][:, part] = jnp.exp(-state * coef[3])
    outs[1][:, part] = jnp.exp(state * coef[3])
    outs[2][:, part] = jnp.exp(-state * coef[4])


def later_kernel(state, change, coef, *outs):
    lanes = coef.shape[2]
    for first in range(0, state.shape[1], lanes):
        part = slice(first, first + lanes)
        store_powers(outs, part, state[:, part] + section_step * change[:, part], coef)


def prepare_kernel(spots, direct, *refs):
    far, (v_out, u_out, coef_out, *powers), near, sem = refs[:7], refs[7:13], refs[13:20], refs[20]
    copies = [
        pltpu.make_async_copy(source, held, sem.at[at])
        for at, (source, held) in enumerate(zip(far, near))
    ]
    for copy in copies:
        copy.start()
    for copy in copies:
        copy.wait()
    rank_ref, v_ref, u_ref, sigma_ref, a_ref, b_ref, state_ref = near
    kinds, rows, count, rank_count, size = u_ref.shape
    row = lax.axis_index("row")
    met = [row_met(spot, row, direct) for spot in spots]
    for at, q in enumerate(met):
        for p in range(rows):
            inside = lax.broadcasted_iota(jnp.int32, (rank_count, size), 0) < rank_ref[p, q]
            v_out[at, p] = jnp.where(inside, v_ref[p, q].astype(jnp.float32), 0.0).astype(v_out.dtype)
    for p in range(rows):
        for kind in range(kinds):
            for first in range(0, count, 4):
                group = [u_ref[kind, p, q] for q in met[first : first + 4]]
                turned = jnp.concatenate(group, axis=0).astype(jnp.float32).T
                u_out[p, kind * size : (kind + 1) * size, first * rank_count : (first + len(group)) * rank_count] = (
                    turned.astype(u_out.dtype)
                )
    lanes = coef_out.shape[2]
    for at, values in enumerate((sigma_ref[...], a_ref[...], b_ref[...], 1.0 / a_ref[...], 1.0 / b_ref[...])):
        coef_out[at] = jnp.broadcast_to(values, (lanes, size)).T
    for first in range(0, state_ref.shape[1], lanes):
        part = slice(first, first + lanes)
        store_powers(powers, part, state_ref[:, part], coef_out)


def sums_kernel(spots, direct, first, pick, before, near_ref, v_ref, u_ref, d_ref, *refs):
    blocks = refs[: len(spots)]
    refs = refs[len(spots) :]
    if before:
        sums_ref, refs = refs[0], refs[1:]
    out_ref, proj = refs
    count, rows, rank_count, size = v_ref.shape
    kinds, slots = d_ref.shape[0], near_ref.shape[1]
    row, col = lax.axis_index("row"), lax.axis_index("col")
    met = [row_met(spot, row, direct) for spot in spots]
    chosen = list(range(rows)) if pick is None else [col if pick == 0 else 1 - col]
    places = [(place,) for place in range(rows)] if pick is None else [()]
    for at, block in enumerate(blocks):
        if pick is None:
            weights = v_ref[first + at].reshape(rows * rank_count, size)
        else:
            weights = v_ref[first + at, chosen[0]]
        part = jnp.dot(weights, block[...], preferred_element_type=jnp.float32).astype(proj.dtype)
        for place in range(len(chosen)):
            proj[place, at * rank_count : (at + 1) * rank_count, :] = part[
                place * rank_count : (place + 1) * rank_count
            ]
    lanes = slice(first * rank_count, (first + len(blocks)) * rank_count)
    for place, p in enumerate(chosen):
        weights, fields = [u_ref[p, :, lanes]], [proj[place]]
        for s in range(slots):
            near = near_ref[pl.ds(p, 1), s : s + 1] - col * count
            field = None
            for q, block in zip(met, blocks):
                mask = jnp.where(near == q, 1.0, 0.0).astype(block.dtype)
                part = block[...] * mask
                field = part if field is None else field + part
            weights.append(jnp.concatenate([d_ref[kind, p, s] for kind in range(kinds)], axis=0))
            fields.append(field)
        total = jnp.dot(
            jnp.concatenate(weights, axis=1),
            jnp.concatenate(fields, axis=0),
            preferred_element_type=jnp.float32,
        )
        for kind in range(kinds):
            piece = total[kind * size : (kind + 1) * size]
            if before:
                piece += sums_ref[p, kind]
            out_ref[*places[place], kind] = piece.astype(out_ref.dtype)


def inverse(value):
    rough = pl.reciprocal(value, approx=True)
    return rough * (2.0 - value * rough)


def sinh_cosh(value):
    grown = jnp.exp(value)
    shrunk = inverse(grown)
    square = value * value
    small = value * (1.0 + square * (1 / 6 + square * (1 / 120)))
    sinh = jnp.where(square < 0.25, small, 0.5 * (grown - shrunk))
    return sinh, 0.5 * (grown + shrunk)


def friction(shear, normal, weight, unweight, decay, tau_load, sigma_base, a_wide, b_wide):
    tau = tau_load + shear
    size = jnp.abs(tau)
    stiff = jnp.maximum(sigma_base + normal, sigma_floor) * a_wide
    double = 2.0 * damping * weight
    drive = size * unweight * (0.5 / damping)
    square = drive * drive + 1.0
    slope = jnp.minimum(size * inverse(stiff), jnp.log(drive + square * lax.rsqrt(square)))
    for newton_step in range(NEWTON):
        sinh, cosh = sinh_cosh(slope)
        excess = stiff * slope + double * sinh - size
        slope = slope - excess * inverse(stiff + double * cosh)
    rate = 2.0 * weight * sinh_cosh(slope)[0]
    change = b_wide * (decay - jnp.abs(rate))
    return (jnp.where(tau < 0.0, -rate, rate), change)


def over_pieces(begin, tall, members, lanes, work):
    step = min(tall, 64)

    @pl.loop(0, tall // step)
    def _(index):
        rows = pl.ds(pl.multiple_of(begin + index * step, step), step)
        for first in range(0, members, lanes):
            work(rows, slice(first, first + lanes))


def section_one_kernel(own, other, weight, unweight, decay, tau, coef, stress, normal, rate, change, rate_half):
    size, members = tau.shape

    def work(rows, part):
        shear = own[0, rows, part] + other[0, rows, part].astype(jnp.float32)
        press = own[1, rows, part] + other[1, rows, part].astype(jnp.float32)
        stress[rows, part] = shear
        normal[rows, part] = press
        first, second = friction(
            shear,
            press,
            weight[rows, part],
            unweight[rows, part],
            decay[rows, part],
            tau[rows, part],
            coef[0, rows, :],
            coef[1, rows, :],
            coef[2, rows, :],
        )
        rate[rows, part] = first
        change[rows, part] = second
        rate_half[rows, part] = first.astype(rate_half.dtype)

    over_pieces(0, size, members, coef.shape[2], work)


def section_two_kernel(
    own, other, weight, unweight, decay, tau, coef, stress, normal, rate, change, rate_out, change_out, mean_rate, mean_change, sem
):
    size, members = tau.shape

    def work(rows, part):
        shear = own[0, rows, part] + other[0, rows, part].astype(jnp.float32)
        press = own[1, rows, part] + other[1, rows, part].astype(jnp.float32)
        first, second = friction(
            stress[rows, part] + section_step * shear,
            normal[rows, part] + section_step * press,
            weight[rows, part],
            unweight[rows, part],
            decay[rows, part],
            tau[rows, part],
            coef[0, rows, :],
            coef[1, rows, :],
            coef[2, rows, :],
        )
        mean_rate[rows, part] = (rate[rows, part] + first) * 0.5
        mean_change[rows, part] = (change[rows, part] + second) * 0.5

    copies = []
    for at, part in enumerate(row_pieces(size, OUT_PIECES)):
        over_pieces(part.start, part.size, members, coef.shape[2], work)
        for kind, (held, out) in enumerate(((mean_rate, rate_out), (mean_change, change_out))):
            copies.append(pltpu.make_async_copy(held.at[part], out.at[part], sem.at[kind, at]))
            copies[-1].start()
    for copy in copies:
        copy.wait()


def on_core(kernel, outs, arrays, scratch=(), flops=0, room=16, far=(), out_far=False):
    vmem, hbm = pl.BlockSpec(memory_space=pltpu.VMEM), pl.BlockSpec(memory_space=pl.ANY)
    arrays = (*(pltpu.with_memory_space_constraint(a, pltpu.HBM) for a in far), *arrays)
    return pl.pallas_call(
        kernel,
        out_shape=outs,
        in_specs=[hbm] * len(far) + [vmem] * (len(arrays) - len(far)),
        out_specs=jax.tree.map(lambda _: hbm if out_far else vmem, outs),
        scratch_shapes=list(scratch),
        compiler_params=pltpu.CompilerParams(vmem_limit_bytes=room * 1024 * 1024),
        cost_estimate=pl.CostEstimate(
            flops=flops, bytes_accessed=sum(a.size * a.dtype.itemsize for a in arrays), transcendentals=0
        ),
    )(*arrays)


def body(
    slip_deficit,
    state_var,
    tau_load,
    sigma_base,
    a_coef,
    b_coef,
    v_basis,
    u_basis,
    dense_blocks,
    block_ranks,
    near_index,
):
    count = lax.axis_size("row")
    size, members = slip_deficit.shape
    kinds, rows, _, rank_count, _ = u_basis.shape
    direct = count in DIRECT_COUNTS
    spots = arrivals(count, direct)
    early = max(count - LATE, 0)
    room = 16 if direct else 40
    lanes = min(members, 128)
    narrow, wide = jnp.bfloat16, jnp.float32
    swap = [(0, 1), (1, 0)]

    def shaped(*shape, kind=wide):
        return jax.ShapeDtypeStruct(shape, kind)

    full = shaped(size, members)
    v_met, u_met, coef, *powers = on_core(
        functools.partial(prepare_kernel, spots, direct),
        (
            shaped(count, rows, rank_count, size, kind=narrow),
            shaped(rows, kinds * size, count * rank_count, kind=narrow),
            shaped(5, size, lanes),
            full,
            full,
            full,
        ),
        (),
        (
            pltpu.SMEM(block_ranks.shape, jnp.int32),
            pltpu.VMEM(v_basis.shape, narrow),
            pltpu.VMEM(u_basis.shape, narrow),
            *[pltpu.VMEM((1, size), wide)] * 3,
            pltpu.VMEM((size, members), wide),
            pltpu.SemaphoreType.DMA((7,)),
        ),
        room=room,
        far=(
            block_ranks,
            v_basis,
            u_basis,
            sigma_base.reshape(1, size),
            a_coef.reshape(1, size),
            b_coef.reshape(1, size),
            state_var,
        ),
    )

    def add(blocks, first, pick, before, kind):
        held = rows if pick is None else 1
        lead = (rows, kinds) if pick is None else (kinds,)
        return on_core(
            functools.partial(
                sums_kernel, spots[first : first + len(blocks)], direct, first, pick, before is not None
            ),
            shaped(*lead, size, members, kind=kind),
            (near_index, v_met, u_met, dense_blocks, *blocks, *(() if before is None else (before,))),
            (
                pltpu.VMEM((held, len(blocks) * rank_count, members), narrow),
            ),
            2 * held * size * members * rank_count * len(blocks) * 3,
            room,
        )

    def lattice(field_half, beside):
        if direct:
            blocks = gather_direct(field_half, count)
        else:
            whole = lax.all_gather(field_half, "row", axis=0)
            blocks = [whole[r] for r in range(count)]
        blocks[0], beside = lax.optimization_barrier((blocks[0], beside))
        sums = add(blocks[:early], 0, None, None, wide) if early else None
        other = lax.ppermute(add(blocks[early:], early, 1, sums, narrow), "col", swap)
        return add(blocks[early:], early, 0, sums, wide), other, beside

    slip_half = on_core(
        narrow_kernel,
        shaped(size, members, kind=narrow),
        (),
        (pltpu.VMEM((size, members), wide), pltpu.SemaphoreType.DMA((IN_PIECES,))),
        far=(slip_deficit,),
    )
    own, other, powers = lattice(slip_half, powers)
    stress, normal, rate, change, rate_half = on_core(
        section_one_kernel,
        (full, full, full, full, shaped(size, members, kind=narrow)),
        (own, other, *powers, tau_load, coef),
        flops=200 * size * members,
    )
    powers = on_core(later_kernel, (full, full, full), (state_var, change, coef))
    own, other, powers = lattice(rate_half, powers)
    return on_core(
        section_two_kernel,
        (full, full),
        (own, other, *powers, tau_load, coef, stress, normal, rate, change),
        (
            pltpu.VMEM((size, members), wide),
            pltpu.VMEM((size, members), wide),
            pltpu.SemaphoreType.DMA((2, OUT_PIECES)),
        ),
        flops=200 * size * members,
        out_far=True,
    )


def solution(mesh):
    placed = (
        P(("row", "col"), "scen"),
        P(("row", "col"), "scen"),
        P(("row", "col"), "scen"),
        P(("row", "col")),
        P(("row", "col")),
        P(("row", "col")),
        P("row", "col", None, None),
        P(None, "row", "col", None, None),
        P(None, "row", "col", None, None),
        P("row", "col"),
        P("row", "col"),
    )
    return jax.shard_map(
        body,
        mesh=mesh,
        in_specs=placed,
        out_specs=(P(("row", "col"), "scen"), P(("row", "col"), "scen")),
        check_vma=False,
    )
```

```python
import functools

import jax
import jax.numpy as jnp
from jax import lax
from jax.experimental import pallas as pl
from jax.experimental.pallas import tpu as pltpu
from jax.sharding import PartitionSpec as P

NEWTON = 2
SQUARE = 4

damping = 0.5
sigma_floor = 0.5
section_step = 0.1


def rows_met(first, last, row, count):
    if count != 2 * SQUARE:
        return list(range(first, last))
    base = row - lax.rem(row, SQUARE)
    return [(base if at < SQUARE else SQUARE - base) + at % SQUARE for at in range(first, last)]


def copies_kernel(block_ref, out_ref):
    for at in range(SQUARE):
        out_ref[at] = block_ref[...]


IN_PIECES = 8
OUT_PIECES = 4


def row_pieces(size, pieces):
    tall = size // pieces
    return [pl.ds(at * tall, tall) for at in range(pieces)]


def narrow_kernel(wide_ref, narrow_ref, copies_ref, held, sem):
    copies = [
        pltpu.make_async_copy(wide_ref.at[part], held.at[part], sem.at[at])
        for at, part in enumerate(row_pieces(held.shape[0], IN_PIECES))
    ]
    for copy in copies:
        copy.start()
    for copy, part in zip(copies, row_pieces(held.shape[0], IN_PIECES)):
        copy.wait()
        value = held[part, :].astype(narrow_ref.dtype)
        narrow_ref[part, :] = value
        for at in range(copies_ref.shape[0]):
            copies_ref[at, part, :] = value


def store_powers(outs, part, state, coef):
    outs[0][:, part] = jnp.exp(-state * coef[3])
    outs[1][:, part] = jnp.exp(state * coef[3])
    outs[2][:, part] = jnp.exp(-state * coef[4])


def later_kernel(state, change, coef, *outs):
    lanes = coef.shape[2]
    for first in range(0, state.shape[1], lanes):
        part = slice(first, first + lanes)
        store_powers(outs, part, state[:, part] + section_step * change[:, part], coef)


def prepare_kernel(*refs):
    far, (v_out, u_out, coef_out, *powers), near, sem = refs[:7], refs[7:13], refs[13:20], refs[20]
    copies = [
        pltpu.make_async_copy(source, held, sem.at[at])
        for at, (source, held) in enumerate(zip(far, near))
    ]
    for copy in copies:
        copy.start()
    for copy in copies:
        copy.wait()
    rank_ref, v_ref, u_ref, sigma_ref, a_ref, b_ref, state_ref = near
    kinds, rows, count, rank_count, size = u_ref.shape
    met = rows_met(0, count, lax.axis_index("row"), count)
    for at, q in enumerate(met):
        for p in range(rows):
            inside = lax.broadcasted_iota(jnp.int32, (rank_count, size), 0) < rank_ref[p, q]
            v_out[at, p] = jnp.where(inside, v_ref[p, q].astype(jnp.float32), 0.0).astype(v_out.dtype)
    for p in range(rows):
        for kind in range(kinds):
            for first in range(0, count, 4):
                group = [u_ref[kind, p, q] for q in met[first : first + 4]]
                turned = jnp.concatenate(group, axis=0).astype(jnp.float32).T
                u_out[p, kind * size : (kind + 1) * size, first * rank_count : (first + len(group)) * rank_count] = (
                    turned.astype(u_out.dtype)
                )
    lanes = coef_out.shape[2]
    for at, values in enumerate((sigma_ref[...], a_ref[...], b_ref[...], 1.0 / a_ref[...], 1.0 / b_ref[...])):
        coef_out[at] = jnp.broadcast_to(values, (lanes, size)).T
    for first in range(0, state_ref.shape[1], lanes):
        part = slice(first, first + lanes)
        store_powers(powers, part, state_ref[:, part], coef_out)


def sums_kernel(first, pick, before, near_ref, v_ref, u_ref, d_ref, field_ref, *refs):
    if before:
        sums_ref, refs = refs[0], refs[1:]
    out_ref, proj = refs
    blocks = [field_ref.at[at] for at in range(field_ref.shape[0])]
    count, rows, rank_count, size = v_ref.shape
    kinds, slots = d_ref.shape[0], near_ref.shape[1]
    row, col = lax.axis_index("row"), lax.axis_index("col")
    met = rows_met(first, first + len(blocks), row, count)
    chosen = list(range(rows)) if pick is None else [col if pick == 0 else 1 - col]
    places = [(place,) for place in range(rows)] if pick is None else [()]
    for at, block in enumerate(blocks):
        if pick is None:
            weights = v_ref[first + at].reshape(rows * rank_count, size)
        else:
            weights = v_ref[first + at, chosen[0]]
        part = jnp.dot(weights, block[...], preferred_element_type=jnp.float32).astype(proj.dtype)
        for place in range(len(chosen)):
            proj[place, at * rank_count : (at + 1) * rank_count, :] = part[
                place * rank_count : (place + 1) * rank_count
            ]
    lanes = slice(first * rank_count, (first + len(blocks)) * rank_count)
    for place, p in enumerate(chosen):
        weights, fields = [u_ref[p, :, lanes]], [proj[place]]
        for s in range(slots):
            near = near_ref[pl.ds(p, 1), s : s + 1] - col * count
            field = None
            for q, block in zip(met, blocks):
                mask = jnp.where(near == q, 1.0, 0.0).astype(block.dtype)
                part = block[...] * mask
                field = part if field is None else field + part
            weights.append(jnp.concatenate([d_ref[kind, p, s] for kind in range(kinds)], axis=0))
            fields.append(field)
        total = jnp.dot(
            jnp.concatenate(weights, axis=1),
            jnp.concatenate(fields, axis=0),
            preferred_element_type=jnp.float32,
        )
        for kind in range(kinds):
            piece = total[kind * size : (kind + 1) * size]
            if before:
                piece += sums_ref[p, kind]
            out_ref[*places[place], kind] = piece.astype(out_ref.dtype)


def inverse(value):
    rough = pl.reciprocal(value, approx=True)
    return rough * (2.0 - value * rough)


def sinh_cosh(value):
    grown = jnp.exp(value)
    shrunk = inverse(grown)
    square = value * value
    small = value * (1.0 + square * (1 / 6 + square * (1 / 120)))
    sinh = jnp.where(square < 0.25, small, 0.5 * (grown - shrunk))
    return sinh, 0.5 * (grown + shrunk)


def friction(shear, normal, weight, unweight, decay, tau_load, sigma_base, a_wide, b_wide):
    tau = tau_load + shear
    size = jnp.abs(tau)
    stiff = jnp.maximum(sigma_base + normal, sigma_floor) * a_wide
    double = 2.0 * damping * weight
    drive = size * unweight * (0.5 / damping)
    square = drive * drive + 1.0
    slope = jnp.minimum(size * inverse(stiff), jnp.log(drive + square * lax.rsqrt(square)))
    for newton_step in range(NEWTON):
        sinh, cosh = sinh_cosh(slope)
        excess = stiff * slope + double * sinh - size
        slope = slope - excess * inverse(stiff + double * cosh)
    rate = 2.0 * weight * sinh_cosh(slope)[0]
    change = b_wide * (decay - jnp.abs(rate))
    return (jnp.where(tau < 0.0, -rate, rate), change)


def over_pieces(begin, tall, members, lanes, work):
    step = min(tall, 64)

    @pl.loop(0, tall // step)
    def _(index):
        rows = pl.ds(pl.multiple_of(begin + index * step, step), step)
        for first in range(0, members, lanes):
            work(rows, slice(first, first + lanes))


def section_one_kernel(own, other, weight, unweight, decay, tau, coef, stress, normal, rate, change, rate_half, rate_copies):
    size, members = tau.shape

    def work(rows, part):
        shear = own[0, rows, part] + other[0, rows, part].astype(jnp.float32)
        press = own[1, rows, part] + other[1, rows, part].astype(jnp.float32)
        stress[rows, part] = shear
        normal[rows, part] = press
        first, second = friction(
            shear,
            press,
            weight[rows, part],
            unweight[rows, part],
            decay[rows, part],
            tau[rows, part],
            coef[0, rows, :],
            coef[1, rows, :],
            coef[2, rows, :],
        )
        rate[rows, part] = first
        change[rows, part] = second
        half = first.astype(rate_half.dtype)
        rate_half[rows, part] = half
        for at in range(rate_copies.shape[0]):
            rate_copies[at, rows, part] = half

    over_pieces(0, size, members, coef.shape[2], work)


def section_two_kernel(
    own, other, weight, unweight, decay, tau, coef, stress, normal, rate, change, rate_out, change_out, mean_rate, mean_change, sem
):
    size, members = tau.shape

    def work(rows, part):
        shear = own[0, rows, part] + other[0, rows, part].astype(jnp.float32)
        press = own[1, rows, part] + other[1, rows, part].astype(jnp.float32)
        first, second = friction(
            stress[rows, part] + section_step * shear,
            normal[rows, part] + section_step * press,
            weight[rows, part],
            unweight[rows, part],
            decay[rows, part],
            tau[rows, part],
            coef[0, rows, :],
            coef[1, rows, :],
            coef[2, rows, :],
        )
        mean_rate[rows, part] = (rate[rows, part] + first) * 0.5
        mean_change[rows, part] = (change[rows, part] + second) * 0.5

    copies = []
    for at, part in enumerate(row_pieces(size, OUT_PIECES)):
        over_pieces(part.start, part.size, members, coef.shape[2], work)
        for kind, (held, out) in enumerate(((mean_rate, rate_out), (mean_change, change_out))):
            copies.append(pltpu.make_async_copy(held.at[part], out.at[part], sem.at[kind, at]))
            copies[-1].start()
    for copy in copies:
        copy.wait()


def on_core(kernel, outs, arrays, scratch=(), flops=0, room=16, far=(), out_far=False):
    vmem, hbm = pl.BlockSpec(memory_space=pltpu.VMEM), pl.BlockSpec(memory_space=pl.ANY)
    arrays = (*(pltpu.with_memory_space_constraint(a, pltpu.HBM) for a in far), *arrays)
    return pl.pallas_call(
        kernel,
        out_shape=outs,
        in_specs=[hbm] * len(far) + [vmem] * (len(arrays) - len(far)),
        out_specs=jax.tree.map(lambda _: hbm if out_far else vmem, outs),
        scratch_shapes=list(scratch),
        compiler_params=pltpu.CompilerParams(vmem_limit_bytes=room * 1024 * 1024),
        cost_estimate=pl.CostEstimate(
            flops=flops, bytes_accessed=sum(a.size * a.dtype.itemsize for a in arrays), transcendentals=0
        ),
    )(*arrays)


def body(
    slip_deficit,
    state_var,
    tau_load,
    sigma_base,
    a_coef,
    b_coef,
    v_basis,
    u_basis,
    dense_blocks,
    block_ranks,
    near_index,
):
    count = lax.axis_size("row")
    size, members = slip_deficit.shape
    kinds, rows, _, rank_count, _ = u_basis.shape
    direct = count == 2 * SQUARE
    early = max(count - SQUARE, 0)
    room = 16 if direct else 40
    lanes = min(members, 128)
    narrow, wide = jnp.bfloat16, jnp.float32
    swap = [(0, 1), (1, 0)]

    def shaped(*shape, kind=wide):
        return jax.ShapeDtypeStruct(shape, kind)

    full = shaped(size, members)
    v_met, u_met, coef, *powers = on_core(
        prepare_kernel,
        (
            shaped(count, rows, rank_count, size, kind=narrow),
            shaped(rows, kinds * size, count * rank_count, kind=narrow),
            shaped(5, size, lanes),
            full,
            full,
            full,
        ),
        (),
        (
            pltpu.SMEM(block_ranks.shape, jnp.int32),
            pltpu.VMEM(v_basis.shape, narrow),
            pltpu.VMEM(u_basis.shape, narrow),
            *[pltpu.VMEM((1, size), wide)] * 3,
            pltpu.VMEM((size, members), wide),
            pltpu.SemaphoreType.DMA((7,)),
        ),
        room=room,
        far=(
            block_ranks,
            v_basis,
            u_basis,
            sigma_base.reshape(1, size),
            a_coef.reshape(1, size),
            b_coef.reshape(1, size),
            state_var,
        ),
    )

    def add(field, first, pick, before, kind):
        held = rows if pick is None else 1
        lead = (rows, kinds) if pick is None else (kinds,)
        blocks = field.shape[0]
        return on_core(
            functools.partial(sums_kernel, first, pick, before is not None),
            shaped(*lead, size, members, kind=kind),
            (near_index, v_met, u_met, dense_blocks, field, *(() if before is None else (before,))),
            (pltpu.VMEM((held, blocks * rank_count, members), narrow),),
            2 * held * size * members * rank_count * blocks * 3,
            room,
        )

    def gather(block, copies):
        squares = [list(range(first, first + SQUARE)) for first in range(0, count, SQUARE)]

        def within(data):
            return lax.all_to_all(data, "row", 0, 0, axis_index_groups=squares)

        across = lax.ppermute(block, "row", [(row, (row + SQUARE) % count) for row in range(count)])
        near = within(copies)
        return near, within(on_core(copies_kernel, shaped(*copies.shape, kind=narrow), (across,)))

    def lattice(block, copies, beside):
        if direct:
            near, last = gather(block, copies)
        else:
            whole = lax.all_gather(block, "row", axis=0)
            near, last = whole[:early], whole[early:]
        near, beside = lax.optimization_barrier((near, beside))
        sums = add(near, 0, None, None, wide) if early else None
        other = lax.ppermute(add(last, early, 1, sums, narrow), "col", swap)
        return add(last, early, 0, sums, wide), other, beside

    sent = (shaped(size, members, kind=narrow), shaped(SQUARE if direct else 1, size, members, kind=narrow))
    slip_half = on_core(
        narrow_kernel,
        sent,
        (),
        (pltpu.VMEM((size, members), wide), pltpu.SemaphoreType.DMA((IN_PIECES,))),
        far=(slip_deficit,),
    )
    own, other, powers = lattice(*slip_half, powers)
    stress, normal, rate, change, *rate_half = on_core(
        section_one_kernel,
        (full, full, full, full, *sent),
        (own, other, *powers, tau_load, coef),
        flops=200 * size * members,
    )
    powers = on_core(later_kernel, (full, full, full), (state_var, change, coef))
    own, other, powers = lattice(*rate_half, powers)
    return on_core(
        section_two_kernel,
        (full, full),
        (own, other, *powers, tau_load, coef, stress, normal, rate, change),
        (
            pltpu.VMEM((size, members), wide),
            pltpu.VMEM((size, members), wide),
            pltpu.SemaphoreType.DMA((2, OUT_PIECES)),
        ),
        flops=200 * size * members,
        out_far=True,
    )


def solution(mesh):
    placed = (
        P(("row", "col"), "scen"),
        P(("row", "col"), "scen"),
        P(("row", "col"), "scen"),
        P(("row", "col")),
        P(("row", "col")),
        P(("row", "col")),
        P("row", "col", None, None),
        P(None, "row", "col", None, None),
        P(None, "row", "col", None, None),
        P("row", "col"),
        P("row", "col"),
    )
    return jax.shard_map(
        body,
        mesh=mesh,
        in_specs=placed,
        out_specs=(P(("row", "col"), "scen"), P(("row", "col"), "scen")),
        check_vma=False,
    )
```

```python
import functools

import jax
import jax.numpy as jnp
from jax import lax
from jax.experimental import pallas as pl
from jax.experimental.pallas import tpu as pltpu
from jax.sharding import PartitionSpec as P

NEWTON = 2
DIRECT_COUNTS = (4, 8)
TILE = 128

damping = 0.5
sigma_floor = 0.5
section_step = 0.1


def arrivals(count, direct):
    if not direct:
        cuts = [0, max(count - 4, 0), count]
        return [list(range(first, last)) for first, last in zip(cuts, cuts[1:]) if last > first]
    return [[0, 1, 4, 2, 3], [6, 5, 7]] if count == 8 else [[0, 1], [2, 3]]


def row_met(spot, row, direct):
    return jnp.bitwise_xor(row, spot) if direct else spot


def gather_direct(block, count):
    def swapped(mask, data):
        return lax.ppermute(data, "row", [(row, row ^ mask) for row in range(count)])

    found = {0: block}
    for mask in (4, 1, 2) if count == 8 else (1, 2):
        found[mask] = swapped(mask, block)
    found[3] = swapped(2, found[1])
    if count == 8:
        for mask in (1, 2, 3):
            found[4 + mask] = swapped(mask, found[4])
    return [[found[mask] for mask in group] for group in arrivals(count, True)]


IN_PIECES = 8
OUT_PIECES = 4


def row_pieces(size, pieces):
    tall = size // pieces
    return [pl.ds(at * tall, tall) for at in range(pieces)]


def narrow_kernel(wide_ref, narrow_ref, held, sem):
    copies = [
        pltpu.make_async_copy(wide_ref.at[part], held.at[part], sem.at[at])
        for at, part in enumerate(row_pieces(held.shape[0], IN_PIECES))
    ]
    for copy in copies:
        copy.start()
    for copy, part in zip(copies, row_pieces(held.shape[0], IN_PIECES)):
        copy.wait()
        narrow_ref[part, :] = held[part, :].astype(narrow_ref.dtype)


def store_powers(outs, part, state, coef):
    outs[0][:, part] = jnp.exp(-state * coef[3])
    outs[1][:, part] = jnp.exp(state * coef[3])
    outs[2][:, part] = jnp.exp(-state * coef[4])


def later_kernel(state, change, coef, *outs):
    lanes = coef.shape[2]
    for first in range(0, state.shape[1], lanes):
        part = slice(first, first + lanes)
        store_powers(outs, part, state[:, part] + section_step * change[:, part], coef)


def prepare_kernel(groups, direct, *refs):
    far, (v_out, u_out, coef_out, *powers), near, sem = refs[:7], refs[7:13], refs[13:20], refs[20]
    copies = [
        pltpu.make_async_copy(source, held, sem.at[at])
        for at, (source, held) in enumerate(zip(far, near))
    ]
    for copy in copies:
        copy.start()
    for copy in copies:
        copy.wait()
    rank_ref, v_ref, u_ref, sigma_ref, a_ref, b_ref, state_ref = near
    kinds, rows, count, rank_count, size = u_ref.shape
    row = lax.axis_index("row")
    met = [row_met(spot, row, direct) for group in groups for spot in group]
    for at, q in enumerate(met):
        for p in range(rows):
            inside = lax.broadcasted_iota(jnp.int32, (rank_count, size), 0) < rank_ref[p, q]
            v_out[at, p] = jnp.where(inside, v_ref[p, q].astype(jnp.float32), 0.0).astype(v_out.dtype)
    for p in range(rows):
        for kind in range(kinds):
            first = start = 0
            for spots in groups:
                group = [u_ref[kind, p, q] for q in met[first : first + len(spots)]]
                spare = -len(group) * rank_count % TILE
                if spare:
                    group.append(jnp.zeros((spare, size), u_ref.dtype))
                turned = jnp.concatenate(group, axis=0).astype(jnp.float32).T
                stop = start + turned.shape[1]
                u_out[p, kind * size : (kind + 1) * size, start:stop] = turned.astype(u_out.dtype)
                first, start = first + len(spots), stop
    lanes = coef_out.shape[2]
    for at, values in enumerate((sigma_ref[...], a_ref[...], b_ref[...], 1.0 / a_ref[...], 1.0 / b_ref[...])):
        coef_out[at] = jnp.broadcast_to(values, (lanes, size)).T
    for first in range(0, state_ref.shape[1], lanes):
        part = slice(first, first + lanes)
        store_powers(powers, part, state_ref[:, part], coef_out)


def sums_kernel(spots, direct, first, start, pick, before, near_ref, v_ref, u_ref, d_ref, *refs):
    blocks = refs[: len(spots)]
    refs = refs[len(spots) :]
    if before:
        sums_ref, refs = refs[0], refs[1:]
    out_ref, proj = refs
    count, rows, rank_count, size = v_ref.shape
    kinds, slots = d_ref.shape[0], near_ref.shape[1]
    row, col = lax.axis_index("row"), lax.axis_index("col")
    met = [row_met(spot, row, direct) for spot in spots]
    chosen = list(range(rows)) if pick is None else [col if pick == 0 else 1 - col]
    places = [(place,) for place in range(rows)] if pick is None else [()]
    for at, block in enumerate(blocks):
        if pick is None:
            weights = v_ref[first + at].reshape(rows * rank_count, size)
        else:
            weights = v_ref[first + at, chosen[0]]
        part = jnp.dot(weights, block[...], preferred_element_type=jnp.float32).astype(proj.dtype)
        for place in range(len(chosen)):
            proj[place, at * rank_count : (at + 1) * rank_count, :] = part[
                place * rank_count : (place + 1) * rank_count
            ]
    width = proj.shape[1]
    lanes = slice(start, start + width)
    if width > len(blocks) * rank_count:
        for place in range(len(chosen)):
            proj[place, len(blocks) * rank_count :, :] = jnp.zeros(
                (width - len(blocks) * rank_count, proj.shape[2]), proj.dtype
            )
    for place, p in enumerate(chosen):
        weights, fields = [u_ref[p, :, lanes]], [proj[place]]
        for s in range(slots):
            near = near_ref[pl.ds(p, 1), s : s + 1] - col * count
            field = None
            for q, block in zip(met, blocks):
                mask = jnp.where(near == q, 1.0, 0.0).astype(block.dtype)
                part = block[...] * mask
                field = part if field is None else field + part
            weights.append(jnp.concatenate([d_ref[kind, p, s] for kind in range(kinds)], axis=0))
            fields.append(field)
        total = jnp.dot(
            jnp.concatenate(weights, axis=1),
            jnp.concatenate(fields, axis=0),
            preferred_element_type=jnp.float32,
        )
        for kind in range(kinds):
            piece = total[kind * size : (kind + 1) * size]
            if before:
                piece += sums_ref[p, kind]
            out_ref[*places[place], kind] = piece.astype(out_ref.dtype)


def inverse(value):
    rough = pl.reciprocal(value, approx=True)
    return rough * (2.0 - value * rough)


def sinh_cosh(value):
    grown = jnp.exp(value)
    shrunk = inverse(grown)
    square = value * value
    small = value * (1.0 + square * (1 / 6 + square * (1 / 120)))
    sinh = jnp.where(square < 0.25, small, 0.5 * (grown - shrunk))
    return sinh, 0.5 * (grown + shrunk)


def friction(shear, normal, weight, unweight, decay, tau_load, sigma_base, a_wide, b_wide):
    tau = tau_load + shear
    size = jnp.abs(tau)
    stiff = jnp.maximum(sigma_base + normal, sigma_floor) * a_wide
    double = 2.0 * damping * weight
    drive = size * unweight * (0.5 / damping)
    square = drive * drive + 1.0
    slope = jnp.minimum(size * inverse(stiff), jnp.log(drive + square * lax.rsqrt(square)))
    for newton_step in range(NEWTON):
        sinh, cosh = sinh_cosh(slope)
        excess = stiff * slope + double * sinh - size
        slope = slope - excess * inverse(stiff + double * cosh)
    rate = 2.0 * weight * sinh_cosh(slope)[0]
    change = b_wide * (decay - jnp.abs(rate))
    return (jnp.where(tau < 0.0, -rate, rate), change)


def over_pieces(begin, tall, members, lanes, work):
    step = min(tall, 64)

    @pl.loop(0, tall // step)
    def _(index):
        rows = pl.ds(pl.multiple_of(begin + index * step, step), step)
        for first in range(0, members, lanes):
            work(rows, slice(first, first + lanes))


def section_one_kernel(own, other, weight, unweight, decay, tau, coef, stress, normal, rate, change, rate_half):
    size, members = tau.shape

    def work(rows, part):
        shear = own[0, rows, part] + other[0, rows, part].astype(jnp.float32)
        press = own[1, rows, part] + other[1, rows, part].astype(jnp.float32)
        stress[rows, part] = shear
        normal[rows, part] = press
        first, second = friction(
            shear,
            press,
            weight[rows, part],
            unweight[rows, part],
            decay[rows, part],
            tau[rows, part],
            coef[0, rows, :],
            coef[1, rows, :],
            coef[2, rows, :],
        )
        rate[rows, part] = first
        change[rows, part] = second
        rate_half[rows, part] = first.astype(rate_half.dtype)

    over_pieces(0, size, members, coef.shape[2], work)


def section_two_kernel(
    own, other, weight, unweight, decay, tau, coef, stress, normal, rate, change, rate_out, change_out, mean_rate, mean_change, sem
):
    size, members = tau.shape

    def work(rows, part):
        shear = own[0, rows, part] + other[0, rows, part].astype(jnp.float32)
        press = own[1, rows, part] + other[1, rows, part].astype(jnp.float32)
        first, second = friction(
            stress[rows, part] + section_step * shear,
            normal[rows, part] + section_step * press,
            weight[rows, part],
            unweight[rows, part],
            decay[rows, part],
            tau[rows, part],
            coef[0, rows, :],
            coef[1, rows, :],
            coef[2, rows, :],
        )
        mean_rate[rows, part] = (rate[rows, part] + first) * 0.5
        mean_change[rows, part] = (change[rows, part] + second) * 0.5

    copies = []
    for at, part in enumerate(row_pieces(size, OUT_PIECES)):
        over_pieces(part.start, part.size, members, coef.shape[2], work)
        for kind, (held, out) in enumerate(((mean_rate, rate_out), (mean_change, change_out))):
            copies.append(pltpu.make_async_copy(held.at[part], out.at[part], sem.at[kind, at]))
            copies[-1].start()
    for copy in copies:
        copy.wait()


def on_core(kernel, outs, arrays, scratch=(), flops=0, room=16, far=(), out_far=False):
    vmem, hbm = pl.BlockSpec(memory_space=pltpu.VMEM), pl.BlockSpec(memory_space=pl.ANY)
    arrays = (*(pltpu.with_memory_space_constraint(a, pltpu.HBM) for a in far), *arrays)
    return pl.pallas_call(
        kernel,
        out_shape=outs,
        in_specs=[hbm] * len(far) + [vmem] * (len(arrays) - len(far)),
        out_specs=jax.tree.map(lambda _: hbm if out_far else vmem, outs),
        scratch_shapes=list(scratch),
        compiler_params=pltpu.CompilerParams(vmem_limit_bytes=room * 1024 * 1024),
        cost_estimate=pl.CostEstimate(
            flops=flops, bytes_accessed=sum(a.size * a.dtype.itemsize for a in arrays), transcendentals=0
        ),
    )(*arrays)


def body(
    slip_deficit,
    state_var,
    tau_load,
    sigma_base,
    a_coef,
    b_coef,
    v_basis,
    u_basis,
    dense_blocks,
    block_ranks,
    near_index,
):
    count = lax.axis_size("row")
    size, members = slip_deficit.shape
    kinds, rows, _, rank_count, _ = u_basis.shape
    direct = count in DIRECT_COUNTS
    groups = arrivals(count, direct)
    firsts = [sum(len(group) for group in groups[:at]) for at in range(len(groups))]
    tiles = [-(-len(group) * rank_count // TILE) * TILE for group in groups]
    starts = [sum(tiles[:at]) for at in range(len(groups))]
    room = 16 if direct else 40
    lanes = min(members, 128)
    narrow, wide = jnp.bfloat16, jnp.float32
    swap = [(0, 1), (1, 0)]

    def shaped(*shape, kind=wide):
        return jax.ShapeDtypeStruct(shape, kind)

    full = shaped(size, members)
    v_met, u_met, coef, *powers = on_core(
        functools.partial(prepare_kernel, groups, direct),
        (
            shaped(count, rows, rank_count, size, kind=narrow),
            shaped(rows, kinds * size, sum(tiles), kind=narrow),
            shaped(5, size, lanes),
            full,
            full,
            full,
        ),
        (),
        (
            pltpu.SMEM(block_ranks.shape, jnp.int32),
            pltpu.VMEM(v_basis.shape, narrow),
            pltpu.VMEM(u_basis.shape, narrow),
            *[pltpu.VMEM((1, size), wide)] * 3,
            pltpu.VMEM((size, members), wide),
            pltpu.SemaphoreType.DMA((7,)),
        ),
        room=room,
        far=(
            block_ranks,
            v_basis,
            u_basis,
            sigma_base.reshape(1, size),
            a_coef.reshape(1, size),
            b_coef.reshape(1, size),
            state_var,
        ),
    )

    def add(blocks, at, pick, before, kind):
        held = rows if pick is None else 1
        lead = (rows, kinds) if pick is None else (kinds,)
        return on_core(
            functools.partial(
                sums_kernel, groups[at], direct, firsts[at], starts[at], pick, before is not None
            ),
            shaped(*lead, size, members, kind=kind),
            (near_index, v_met, u_met, dense_blocks, *blocks, *(() if before is None else (before,))),
            (
                pltpu.VMEM((held, tiles[at], members), narrow),
            ),
            2 * held * size * members * rank_count * len(blocks) * 3,
            room,
        )

    def lattice(field_half, beside):
        if direct:
            found = gather_direct(field_half, count)
        else:
            whole = lax.all_gather(field_half, "row", axis=0)
            found = [[whole[r] for r in group] for group in groups]
        found[0][0], beside = lax.optimization_barrier((found[0][0], beside))
        sums, end = None, len(groups) - 1
        for at in range(end):
            sums = add(found[at], at, None, sums, wide)
        other = lax.ppermute(add(found[end], end, 1, sums, narrow), "col", swap)
        return add(found[end], end, 0, sums, wide), other, beside

    slip_half = on_core(
        narrow_kernel,
        shaped(size, members, kind=narrow),
        (),
        (pltpu.VMEM((size, members), wide), pltpu.SemaphoreType.DMA((IN_PIECES,))),
        far=(slip_deficit,),
    )
    own, other, powers = lattice(slip_half, powers)
    stress, normal, rate, change, rate_half = on_core(
        section_one_kernel,
        (full, full, full, full, shaped(size, members, kind=narrow)),
        (own, other, *powers, tau_load, coef),
        flops=200 * size * members,
    )
    powers = on_core(later_kernel, (full, full, full), (state_var, change, coef))
    own, other, powers = lattice(rate_half, powers)
    return on_core(
        section_two_kernel,
        (full, full),
        (own, other, *powers, tau_load, coef, stress, normal, rate, change),
        (
            pltpu.VMEM((size, members), wide),
            pltpu.VMEM((size, members), wide),
            pltpu.SemaphoreType.DMA((2, OUT_PIECES)),
        ),
        flops=200 * size * members,
        out_far=True,
    )


def solution(mesh):
    placed = (
        P(("row", "col"), "scen"),
        P(("row", "col"), "scen"),
        P(("row", "col"), "scen"),
        P(("row", "col")),
        P(("row", "col")),
        P(("row", "col")),
        P("row", "col", None, None),
        P(None, "row", "col", None, None),
        P(None, "row", "col", None, None),
        P("row", "col"),
        P("row", "col"),
    )
    return jax.shard_map(
        body,
        mesh=mesh,
        in_specs=placed,
        out_specs=(P(("row", "col"), "scen"), P(("row", "col"), "scen")),
        check_vma=False,
    )
```

```python
import functools

import jax
import jax.numpy as jnp
from jax import lax
from jax.experimental import pallas as pl
from jax.experimental.pallas import tpu as pltpu
from jax.sharding import PartitionSpec as P

NEWTON = 2
DIRECT_COUNTS = (4, 8)
LATE = 4

damping = 0.5
sigma_floor = 0.5
section_step = 0.1


def arrivals(count, direct):
    if not direct:
        return list(range(count))
    return [0, 4, 2, 1, 3, 6, 7, 5] if count == 8 else [0, 1, 2, 3]


def row_met(spot, row, direct):
    return jnp.bitwise_xor(row, spot) if direct else spot


def gather_direct(block, count):
    def swapped(mask, data):
        return lax.ppermute(data, "row", [(row, row ^ mask) for row in range(count)])

    found = {0: block}
    for mask in (4, 1, 2, 3) if count == 8 else (1, 2, 3):
        found[mask] = swapped(mask, block)
    if count == 8:
        for mask in (1, 2, 3):
            found[4 + mask] = swapped(mask, found[4])
    return [found[mask] for mask in arrivals(count, True)]


IN_PIECES = 8
OUT_PIECES = 4


def row_pieces(size, pieces):
    tall = size // pieces
    return [pl.ds(at * tall, tall) for at in range(pieces)]


def narrow_kernel(wide_ref, narrow_ref, held, sem):
    copies = [
        pltpu.make_async_copy(wide_ref.at[part], held.at[part], sem.at[at])
        for at, part in enumerate(row_pieces(held.shape[0], IN_PIECES))
    ]
    for copy in copies:
        copy.start()
    for copy, part in zip(copies, row_pieces(held.shape[0], IN_PIECES)):
        copy.wait()
        narrow_ref[part, :] = held[part, :].astype(narrow_ref.dtype)


def store_powers(outs, part, state, coef):
    outs[0][:, part] = jnp.exp(-state * coef[3])
    outs[1][:, part] = jnp.exp(state * coef[3])
    outs[2][:, part] = jnp.exp(-state * coef[4])


def later_kernel(state, change, coef, *outs):
    lanes = coef.shape[2]
    for first in range(0, state.shape[1], lanes):
        part = slice(first, first + lanes)
        store_powers(outs, part, state[:, part] + section_step * change[:, part], coef)


def prepare_kernel(spots, direct, *refs):
    far, (v_out, u_out, coef_out, *powers), near, sem = refs[:7], refs[7:13], refs[13:20], refs[20]
    copies = [
        pltpu.make_async_copy(source, held, sem.at[at])
        for at, (source, held) in enumerate(zip(far, near))
    ]
    for copy in copies:
        copy.start()
    for copy in copies:
        copy.wait()
    rank_ref, v_ref, u_ref, sigma_ref, a_ref, b_ref, state_ref = near
    kinds, rows, count, rank_count, size = u_ref.shape
    row = lax.axis_index("row")
    met = [row_met(spot, row, direct) for spot in spots]
    for at, q in enumerate(met):
        for p in range(rows):
            inside = lax.broadcasted_iota(jnp.int32, (rank_count, size), 0) < rank_ref[p, q]
            v_out[at, p] = jnp.where(inside, v_ref[p, q].astype(jnp.float32), 0.0).astype(v_out.dtype)
    for p in range(rows):
        for kind in range(kinds):
            for first in range(0, count, 4):
                group = [u_ref[kind, p, q] for q in met[first : first + 4]]
                turned = jnp.concatenate(group, axis=0).astype(jnp.float32).T
                u_out[p, kind * size : (kind + 1) * size, first * rank_count : (first + len(group)) * rank_count] = (
                    turned.astype(u_out.dtype)
                )
    lanes = coef_out.shape[2]
    for at, values in enumerate((sigma_ref[...], a_ref[...], b_ref[...], 1.0 / a_ref[...], 1.0 / b_ref[...])):
        coef_out[at] = jnp.broadcast_to(values, (lanes, size)).T
    for first in range(0, state_ref.shape[1], lanes):
        part = slice(first, first + lanes)
        store_powers(powers, part, state_ref[:, part], coef_out)


def sums_kernel(spots, direct, first, pick, before, near_ref, v_ref, u_ref, d_ref, *refs):
    blocks = refs[: len(spots)]
    refs = refs[len(spots) :]
    if before:
        sums_ref, refs = refs[0], refs[1:]
    out_ref, proj = refs
    count, rows, rank_count, size = v_ref.shape
    kinds, slots = d_ref.shape[0], near_ref.shape[1]
    row, col = lax.axis_index("row"), lax.axis_index("col")
    met = [row_met(spot, row, direct) for spot in spots]
    chosen = list(range(rows)) if pick is None else [col if pick == 0 else 1 - col]
    places = [(place,) for place in range(rows)] if pick is None else [()]
    for at, block in enumerate(blocks):
        if pick is None:
            weights = v_ref[first + at].reshape(rows * rank_count, size)
        else:
            weights = v_ref[first + at, chosen[0]]
        part = jnp.dot(weights, block[...], preferred_element_type=jnp.float32).astype(proj.dtype)
        for place in range(len(chosen)):
            proj[place, at * rank_count : (at + 1) * rank_count, :] = part[
                place * rank_count : (place + 1) * rank_count
            ]
    lanes = slice(first * rank_count, (first + len(blocks)) * rank_count)
    for place, p in enumerate(chosen):
        weights, fields = [u_ref[p, :, lanes]], [proj[place]]
        for s in range(slots):
            near = near_ref[pl.ds(p, 1), s : s + 1] - col * count
            field = None
            for q, block in zip(met, blocks):
                mask = jnp.where(near == q, 1.0, 0.0).astype(block.dtype)
                part = block[...] * mask
                field = part if field is None else field + part
            weights.append(jnp.concatenate([d_ref[kind, p, s] for kind in range(kinds)], axis=0))
            fields.append(field)
        total = jnp.dot(
            jnp.concatenate(weights, axis=1),
            jnp.concatenate(fields, axis=0),
            preferred_element_type=jnp.float32,
        )
        for kind in range(kinds):
            piece = total[kind * size : (kind + 1) * size]
            if before:
                piece += sums_ref[p, kind]
            out_ref[*places[place], kind] = piece.astype(out_ref.dtype)


def inverse(value):
    rough = pl.reciprocal(value, approx=True)
    return rough * (2.0 - value * rough)


def sinh_cosh(value):
    grown = jnp.exp(value)
    shrunk = inverse(grown)
    square = value * value
    small = value * (1.0 + square * (1 / 6 + square * (1 / 120)))
    sinh = jnp.where(square < 0.25, small, 0.5 * (grown - shrunk))
    return sinh, 0.5 * (grown + shrunk)


def friction(shear, normal, weight, unweight, decay, tau_load, sigma_base, a_wide, b_wide):
    tau = tau_load + shear
    size = jnp.abs(tau)
    stiff = jnp.maximum(sigma_base + normal, sigma_floor) * a_wide
    double = 2.0 * damping * weight
    drive = size * unweight * (0.5 / damping)
    square = drive * drive + 1.0
    slope = jnp.minimum(size * inverse(stiff), jnp.log(drive + square * lax.rsqrt(square)))
    for newton_step in range(NEWTON):
        sinh, cosh = sinh_cosh(slope)
        excess = stiff * slope + double * sinh - size
        slope = slope - excess * inverse(stiff + double * cosh)
    rate = 2.0 * weight * sinh_cosh(slope)[0]
    change = b_wide * (decay - jnp.abs(rate))
    return (jnp.where(tau < 0.0, -rate, rate), change)


def over_pieces(begin, tall, members, lanes, work):
    step = min(tall, 64)

    @pl.loop(0, tall // step)
    def _(index):
        rows = pl.ds(pl.multiple_of(begin + index * step, step), step)
        for first in range(0, members, lanes):
            work(rows, slice(first, first + lanes))


def section_one_kernel(own, other, weight, unweight, decay, tau, coef, stress, normal, rate, change, rate_half):
    size, members = tau.shape

    def work(rows, part):
        shear = own[0, rows, part] + other[0, rows, part].astype(jnp.float32)
        press = own[1, rows, part] + other[1, rows, part].astype(jnp.float32)
        stress[rows, part] = shear
        normal[rows, part] = press
        first, second = friction(
            shear,
            press,
            weight[rows, part],
            unweight[rows, part],
            decay[rows, part],
            tau[rows, part],
            coef[0, rows, :],
            coef[1, rows, :],
            coef[2, rows, :],
        )
        rate[rows, part] = first
        change[rows, part] = second
        rate_half[rows, part] = first.astype(rate_half.dtype)

    over_pieces(0, size, members, coef.shape[2], work)


def section_two_kernel(
    own, other, weight, unweight, decay, tau, coef, stress, normal, rate, change, rate_out, change_out, mean_rate, mean_change, sem
):
    size, members = tau.shape

    def work(rows, part):
        shear = own[0, rows, part] + other[0, rows, part].astype(jnp.float32)
        press = own[1, rows, part] + other[1, rows, part].astype(jnp.float32)
        first, second = friction(
            stress[rows, part] + section_step * shear,
            normal[rows, part] + section_step * press,
            weight[rows, part],
            unweight[rows, part],
            decay[rows, part],
            tau[rows, part],
            coef[0, rows, :],
            coef[1, rows, :],
            coef[2, rows, :],
        )
        mean_rate[rows, part] = (rate[rows, part] + first) * 0.5
        mean_change[rows, part] = (change[rows, part] + second) * 0.5

    copies = []
    for at, part in enumerate(row_pieces(size, OUT_PIECES)):
        over_pieces(part.start, part.size, members, coef.shape[2], work)
        for kind, (held, out) in enumerate(((mean_rate, rate_out), (mean_change, change_out))):
            copies.append(pltpu.make_async_copy(held.at[part], out.at[part], sem.at[kind, at]))
            copies[-1].start()
    for copy in copies:
        copy.wait()


def on_core(kernel, outs, arrays, scratch=(), flops=0, room=16, far=(), out_far=False):
    vmem, hbm = pl.BlockSpec(memory_space=pltpu.VMEM), pl.BlockSpec(memory_space=pl.ANY)
    arrays = (*(pltpu.with_memory_space_constraint(a, pltpu.HBM) for a in far), *arrays)
    return pl.pallas_call(
        kernel,
        out_shape=outs,
        in_specs=[hbm] * len(far) + [vmem] * (len(arrays) - len(far)),
        out_specs=jax.tree.map(lambda _: hbm if out_far else vmem, outs),
        scratch_shapes=list(scratch),
        compiler_params=pltpu.CompilerParams(vmem_limit_bytes=room * 1024 * 1024),
        cost_estimate=pl.CostEstimate(
            flops=flops, bytes_accessed=sum(a.size * a.dtype.itemsize for a in arrays), transcendentals=0
        ),
    )(*arrays)


def body(
    slip_deficit,
    state_var,
    tau_load,
    sigma_base,
    a_coef,
    b_coef,
    v_basis,
    u_basis,
    dense_blocks,
    block_ranks,
    near_index,
):
    count = lax.axis_size("row")
    size, members = slip_deficit.shape
    kinds, rows, _, rank_count, _ = u_basis.shape
    direct = count in DIRECT_COUNTS
    spots = arrivals(count, direct)
    early = max(count - LATE, 0)
    room = 16 if direct else 40
    lanes = min(members, 128)
    narrow, wide = jnp.bfloat16, jnp.float32
    swap = [(0, 1), (1, 0)]

    def shaped(*shape, kind=wide):
        return jax.ShapeDtypeStruct(shape, kind)

    full = shaped(size, members)
    v_met, u_met, coef, *powers = on_core(
        functools.partial(prepare_kernel, spots, direct),
        (
            shaped(count, rows, rank_count, size, kind=narrow),
            shaped(rows, kinds * size, count * rank_count, kind=narrow),
            shaped(5, size, lanes),
            full,
            full,
            full,
        ),
        (),
        (
            pltpu.SMEM(block_ranks.shape, jnp.int32),
            pltpu.VMEM(v_basis.shape, narrow),
            pltpu.VMEM(u_basis.shape, narrow),
            *[pltpu.VMEM((1, size), wide)] * 3,
            pltpu.VMEM((size, members), wide),
            pltpu.SemaphoreType.DMA((7,)),
        ),
        room=room,
        far=(
            block_ranks,
            v_basis,
            u_basis,
            sigma_base.reshape(1, size),
            a_coef.reshape(1, size),
            b_coef.reshape(1, size),
            state_var,
        ),
    )

    def add(blocks, first, pick, before, kind):
        held = rows if pick is None else 1
        lead = (rows, kinds) if pick is None else (kinds,)
        return on_core(
            functools.partial(
                sums_kernel, spots[first : first + len(blocks)], direct, first, pick, before is not None
            ),
            shaped(*lead, size, members, kind=kind),
            (near_index, v_met, u_met, dense_blocks, *blocks, *(() if before is None else (before,))),
            (
                pltpu.VMEM((held, len(blocks) * rank_count, members), narrow),
            ),
            2 * held * size * members * rank_count * len(blocks) * 3,
            room,
        )

    def lattice(field_half, beside):
        if direct:
            blocks = gather_direct(field_half, count)
        else:
            whole = lax.all_gather(field_half, "row", axis=0)
            blocks = [whole[r] for r in range(count)]
        blocks[0], beside = lax.optimization_barrier((blocks[0], beside))
        sums = add(blocks[:early], 0, None, None, wide) if early else None
        other = lax.ppermute(add(blocks[early:], early, 1, sums, narrow), "col", swap)
        return add(blocks[early:], early, 0, sums, wide), other, beside

    slip_half = on_core(
        narrow_kernel,
        shaped(size, members, kind=narrow),
        (),
        (pltpu.VMEM((size, members), wide), pltpu.SemaphoreType.DMA((IN_PIECES,))),
        far=(slip_deficit,),
    )
    own, other, powers = lattice(slip_half, powers)
    stress, normal, rate, change, rate_half = on_core(
        section_one_kernel,
        (full, full, full, full, shaped(size, members, kind=narrow)),
        (own, other, *powers, tau_load, coef),
        flops=200 * size * members,
    )
    powers = on_core(later_kernel, (full, full, full), (state_var, change, coef))
    own, other, powers = lattice(rate_half, powers)
    return on_core(
        section_two_kernel,
        (full, full),
        (own, other, *powers, tau_load, coef, stress, normal, rate, change),
        (
            pltpu.VMEM((size, members), wide),
            pltpu.VMEM((size, members), wide),
            pltpu.SemaphoreType.DMA((2, OUT_PIECES)),
        ),
        flops=200 * size * members,
        out_far=True,
    )


def solution(mesh):
    placed = (
        P(("row", "col"), "scen"),
        P(("row", "col"), "scen"),
        P(("row", "col"), "scen"),
        P(("row", "col")),
        P(("row", "col")),
        P(("row", "col")),
        P("row", "col", None, None),
        P(None, "row", "col", None, None),
        P(None, "row", "col", None, None),
        P("row", "col"),
        P("row", "col"),
    )
    return jax.shard_map(
        body,
        mesh=mesh,
        in_specs=placed,
        out_specs=(P(("row", "col"), "scen"), P(("row", "col"), "scen")),
        check_vma=False,
    )
```

```python
import functools

import jax
import jax.numpy as jnp
from jax import lax
from jax.experimental import pallas as pl
from jax.experimental.pallas import tpu as pltpu
from jax.sharding import PartitionSpec as P

NEWTON = 2
DIRECT_COUNTS = (4, 8)
LATE = 4

damping = 0.5
sigma_floor = 0.5
section_step = 0.1


def arrivals(count, direct):
    if not direct:
        return list(range(count))
    return [0, 1, 4, 2, 7, 6, 3, 5] if count == 8 else [0, 1, 2, 3]


def row_met(spot, row, direct):
    return jnp.bitwise_xor(row, spot) if direct else spot


def gather_direct(block, count):
    def swapped(mask, data):
        return lax.ppermute(data, "row", [(row, row ^ mask) for row in range(count)])

    found = {0: block}
    for mask in (4, 2, 1, 7) if count == 8 else (2, 1):
        found[mask] = swapped(mask, block)
    if count == 8:
        for mask in (1, 2):
            found[4 + mask] = swapped(mask, found[4])
    found[3] = swapped(1, found[2])
    return [found[mask] for mask in arrivals(count, True)]


IN_PIECES = 8
OUT_PIECES = 4


def row_pieces(size, pieces):
    tall = size // pieces
    return [pl.ds(at * tall, tall) for at in range(pieces)]


def narrow_kernel(wide_ref, narrow_ref, held, sem):
    copies = [
        pltpu.make_async_copy(wide_ref.at[part], held.at[part], sem.at[at])
        for at, part in enumerate(row_pieces(held.shape[0], IN_PIECES))
    ]
    for copy in copies:
        copy.start()
    for copy, part in zip(copies, row_pieces(held.shape[0], IN_PIECES)):
        copy.wait()
        narrow_ref[part, :] = held[part, :].astype(narrow_ref.dtype)


def store_powers(outs, part, state, coef):
    outs[0][:, part] = jnp.exp(-state * coef[3])
    outs[1][:, part] = jnp.exp(state * coef[3])
    outs[2][:, part] = jnp.exp(-state * coef[4])


def later_kernel(state, change, coef, *outs):
    lanes = coef.shape[2]
    for first in range(0, state.shape[1], lanes):
        part = slice(first, first + lanes)
        store_powers(outs, part, state[:, part] + section_step * change[:, part], coef)


def prepare_kernel(spots, direct, *refs):
    far, (v_out, u_out, coef_out, *powers), near, sem = refs[:7], refs[7:13], refs[13:20], refs[20]
    copies = [
        pltpu.make_async_copy(source, held, sem.at[at])
        for at, (source, held) in enumerate(zip(far, near))
    ]
    for copy in copies:
        copy.start()
    for copy in copies:
        copy.wait()
    rank_ref, v_ref, u_ref, sigma_ref, a_ref, b_ref, state_ref = near
    kinds, rows, count, rank_count, size = u_ref.shape
    row = lax.axis_index("row")
    met = [row_met(spot, row, direct) for spot in spots]
    for at, q in enumerate(met):
        for p in range(rows):
            inside = lax.broadcasted_iota(jnp.int32, (rank_count, size), 0) < rank_ref[p, q]
            v_out[at, p] = jnp.where(inside, v_ref[p, q].astype(jnp.float32), 0.0).astype(v_out.dtype)
    for p in range(rows):
        for kind in range(kinds):
            for first in range(0, count, 4):
                group = [u_ref[kind, p, q] for q in met[first : first + 4]]
                turned = jnp.concatenate(group, axis=0).astype(jnp.float32).T
                u_out[p, kind * size : (kind + 1) * size, first * rank_count : (first + len(group)) * rank_count] = (
                    turned.astype(u_out.dtype)
                )
    lanes = coef_out.shape[2]
    for at, values in enumerate((sigma_ref[...], a_ref[...], b_ref[...], 1.0 / a_ref[...], 1.0 / b_ref[...])):
        coef_out[at] = jnp.broadcast_to(values, (lanes, size)).T
    for first in range(0, state_ref.shape[1], lanes):
        part = slice(first, first + lanes)
        store_powers(powers, part, state_ref[:, part], coef_out)


def sums_kernel(spots, direct, first, pick, before, near_ref, v_ref, u_ref, d_ref, *refs):
    blocks = refs[: len(spots)]
    refs = refs[len(spots) :]
    if before:
        sums_ref, refs = refs[0], refs[1:]
    out_ref, proj = refs
    count, rows, rank_count, size = v_ref.shape
    kinds, slots = d_ref.shape[0], near_ref.shape[1]
    row, col = lax.axis_index("row"), lax.axis_index("col")
    met = [row_met(spot, row, direct) for spot in spots]
    chosen = list(range(rows)) if pick is None else [col if pick == 0 else 1 - col]
    places = [(place,) for place in range(rows)] if pick is None else [()]
    for at, block in enumerate(blocks):
        if pick is None:
            weights = v_ref[first + at].reshape(rows * rank_count, size)
        else:
            weights = v_ref[first + at, chosen[0]]
        part = jnp.dot(weights, block[...], preferred_element_type=jnp.float32).astype(proj.dtype)
        for place in range(len(chosen)):
            proj[place, at * rank_count : (at + 1) * rank_count, :] = part[
                place * rank_count : (place + 1) * rank_count
            ]
    lanes = slice(first * rank_count, (first + len(blocks)) * rank_count)
    for place, p in enumerate(chosen):
        weights, fields = [u_ref[p, :, lanes]], [proj[place]]
        for s in range(slots):
            near = near_ref[pl.ds(p, 1), s : s + 1] - col * count
            field = None
            for q, block in zip(met, blocks):
                mask = jnp.where(near == q, 1.0, 0.0).astype(block.dtype)
                part = block[...] * mask
                field = part if field is None else field + part
            weights.append(jnp.concatenate([d_ref[kind, p, s] for kind in range(kinds)], axis=0))
            fields.append(field)
        total = jnp.dot(
            jnp.concatenate(weights, axis=1),
            jnp.concatenate(fields, axis=0),
            preferred_element_type=jnp.float32,
        )
        for kind in range(kinds):
            piece = total[kind * size : (kind + 1) * size]
            if before:
                piece += sums_ref[p, kind]
            out_ref[*places[place], kind] = piece.astype(out_ref.dtype)


def inverse(value):
    rough = pl.reciprocal(value, approx=True)
    return rough * (2.0 - value * rough)


def sinh_cosh(value):
    grown = jnp.exp(value)
    shrunk = inverse(grown)
    square = value * value
    small = value * (1.0 + square * (1 / 6 + square * (1 / 120)))
    sinh = jnp.where(square < 0.25, small, 0.5 * (grown - shrunk))
    return sinh, 0.5 * (grown + shrunk)


def friction(shear, normal, weight, unweight, decay, tau_load, sigma_base, a_wide, b_wide):
    tau = tau_load + shear
    size = jnp.abs(tau)
    stiff = jnp.maximum(sigma_base + normal, sigma_floor) * a_wide
    double = 2.0 * damping * weight
    drive = size * unweight * (0.5 / damping)
    square = drive * drive + 1.0
    slope = jnp.minimum(size * inverse(stiff), jnp.log(drive + square * lax.rsqrt(square)))
    for newton_step in range(NEWTON):
        sinh, cosh = sinh_cosh(slope)
        excess = stiff * slope + double * sinh - size
        slope = slope - excess * inverse(stiff + double * cosh)
    rate = 2.0 * weight * sinh_cosh(slope)[0]
    change = b_wide * (decay - jnp.abs(rate))
    return (jnp.where(tau < 0.0, -rate, rate), change)


def over_pieces(begin, tall, members, lanes, work):
    step = min(tall, 64)

    @pl.loop(0, tall // step)
    def _(index):
        rows = pl.ds(pl.multiple_of(begin + index * step, step), step)
        for first in range(0, members, lanes):
            work(rows, slice(first, first + lanes))


def section_one_kernel(own, other, weight, unweight, decay, tau, coef, stress, normal, rate, change, rate_half):
    size, members = tau.shape

    def work(rows, part):
        shear = own[0, rows, part] + other[0, rows, part].astype(jnp.float32)
        press = own[1, rows, part] + other[1, rows, part].astype(jnp.float32)
        stress[rows, part] = shear
        normal[rows, part] = press
        first, second = friction(
            shear,
            press,
            weight[rows, part],
            unweight[rows, part],
            decay[rows, part],
            tau[rows, part],
            coef[0, rows, :],
            coef[1, rows, :],
            coef[2, rows, :],
        )
        rate[rows, part] = first
        change[rows, part] = second
        rate_half[rows, part] = first.astype(rate_half.dtype)

    over_pieces(0, size, members, coef.shape[2], work)


def section_two_kernel(
    own, other, weight, unweight, decay, tau, coef, stress, normal, rate, change, rate_out, change_out, mean_rate, mean_change, sem
):
    size, members = tau.shape

    def work(rows, part):
        shear = own[0, rows, part] + other[0, rows, part].astype(jnp.float32)
        press = own[1, rows, part] + other[1, rows, part].astype(jnp.float32)
        first, second = friction(
            stress[rows, part] + section_step * shear,
            normal[rows, part] + section_step * press,
            weight[rows, part],
            unweight[rows, part],
            decay[rows, part],
            tau[rows, part],
            coef[0, rows, :],
            coef[1, rows, :],
            coef[2, rows, :],
        )
        mean_rate[rows, part] = (rate[rows, part] + first) * 0.5
        mean_change[rows, part] = (change[rows, part] + second) * 0.5

    copies = []
    for at, part in enumerate(row_pieces(size, OUT_PIECES)):
        over_pieces(part.start, part.size, members, coef.shape[2], work)
        for kind, (held, out) in enumerate(((mean_rate, rate_out), (mean_change, change_out))):
            copies.append(pltpu.make_async_copy(held.at[part], out.at[part], sem.at[kind, at]))
            copies[-1].start()
    for copy in copies:
        copy.wait()


def on_core(kernel, outs, arrays, scratch=(), flops=0, room=16, far=(), out_far=False):
    vmem, hbm = pl.BlockSpec(memory_space=pltpu.VMEM), pl.BlockSpec(memory_space=pl.ANY)
    arrays = (*(pltpu.with_memory_space_constraint(a, pltpu.HBM) for a in far), *arrays)
    return pl.pallas_call(
        kernel,
        out_shape=outs,
        in_specs=[hbm] * len(far) + [vmem] * (len(arrays) - len(far)),
        out_specs=jax.tree.map(lambda _: hbm if out_far else vmem, outs),
        scratch_shapes=list(scratch),
        compiler_params=pltpu.CompilerParams(vmem_limit_bytes=room * 1024 * 1024),
        cost_estimate=pl.CostEstimate(
            flops=flops, bytes_accessed=sum(a.size * a.dtype.itemsize for a in arrays), transcendentals=0
        ),
    )(*arrays)


def body(
    slip_deficit,
    state_var,
    tau_load,
    sigma_base,
    a_coef,
    b_coef,
    v_basis,
    u_basis,
    dense_blocks,
    block_ranks,
    near_index,
):
    count = lax.axis_size("row")
    size, members = slip_deficit.shape
    kinds, rows, _, rank_count, _ = u_basis.shape
    direct = count in DIRECT_COUNTS
    spots = arrivals(count, direct)
    early = max(count - LATE, 0)
    room = 16 if direct else 40
    lanes = min(members, 128)
    narrow, wide = jnp.bfloat16, jnp.float32
    swap = [(0, 1), (1, 0)]

    def shaped(*shape, kind=wide):
        return jax.ShapeDtypeStruct(shape, kind)

    full = shaped(size, members)
    v_met, u_met, coef, *powers = on_core(
        functools.partial(prepare_kernel, spots, direct),
        (
            shaped(count, rows, rank_count, size, kind=narrow),
            shaped(rows, kinds * size, count * rank_count, kind=narrow),
            shaped(5, size, lanes),
            full,
            full,
            full,
        ),
        (),
        (
            pltpu.SMEM(block_ranks.shape, jnp.int32),
            pltpu.VMEM(v_basis.shape, narrow),
            pltpu.VMEM(u_basis.shape, narrow),
            *[pltpu.VMEM((1, size), wide)] * 3,
            pltpu.VMEM((size, members), wide),
            pltpu.SemaphoreType.DMA((7,)),
        ),
        room=room,
        far=(
            block_ranks,
            v_basis,
            u_basis,
            sigma_base.reshape(1, size),
            a_coef.reshape(1, size),
            b_coef.reshape(1, size),
            state_var,
        ),
    )

    def add(blocks, first, pick, before, kind):
        held = rows if pick is None else 1
        lead = (rows, kinds) if pick is None else (kinds,)
        return on_core(
            functools.partial(
                sums_kernel, spots[first : first + len(blocks)], direct, first, pick, before is not None
            ),
            shaped(*lead, size, members, kind=kind),
            (near_index, v_met, u_met, dense_blocks, *blocks, *(() if before is None else (before,))),
            (
                pltpu.VMEM((held, len(blocks) * rank_count, members), narrow),
            ),
            2 * held * size * members * rank_count * len(blocks) * 3,
            room,
        )

    def lattice(field_half, beside):
        if direct:
            blocks = gather_direct(field_half, count)
        else:
            whole = lax.all_gather(field_half, "row", axis=0)
            blocks = [whole[r] for r in range(count)]
        blocks[0], beside = lax.optimization_barrier((blocks[0], beside))
        sums = add(blocks[:early], 0, None, None, wide) if early else None
        other = lax.ppermute(add(blocks[early:], early, 1, sums, narrow), "col", swap)
        return add(blocks[early:], early, 0, sums, wide), other, beside

    slip_half = on_core(
        narrow_kernel,
        shaped(size, members, kind=narrow),
        (),
        (pltpu.VMEM((size, members), wide), pltpu.SemaphoreType.DMA((IN_PIECES,))),
        far=(slip_deficit,),
    )
    own, other, powers = lattice(slip_half, powers)
    stress, normal, rate, change, rate_half = on_core(
        section_one_kernel,
        (full, full, full, full, shaped(size, members, kind=narrow)),
        (own, other, *powers, tau_load, coef),
        flops=200 * size * members,
    )
    powers = on_core(later_kernel, (full, full, full), (state_var, change, coef))
    own, other, powers = lattice(rate_half, powers)
    return on_core(
        section_two_kernel,
        (full, full),
        (own, other, *powers, tau_load, coef, stress, normal, rate, change),
        (
            pltpu.VMEM((size, members), wide),
            pltpu.VMEM((size, members), wide),
            pltpu.SemaphoreType.DMA((2, OUT_PIECES)),
        ),
        flops=200 * size * members,
        out_far=True,
    )


def solution(mesh):
    placed = (
        P(("row", "col"), "scen"),
        P(("row", "col"), "scen"),
        P(("row", "col"), "scen"),
        P(("row", "col")),
        P(("row", "col")),
        P(("row", "col")),
        P("row", "col", None, None),
        P(None, "row", "col", None, None),
        P(None, "row", "col", None, None),
        P("row", "col"),
        P("row", "col"),
    )
    return jax.shard_map(
        body,
        mesh=mesh,
        in_specs=placed,
        out_specs=(P(("row", "col"), "scen"), P(("row", "col"), "scen")),
        check_vma=False,
    )
```

```python
import functools

import jax
import jax.numpy as jnp
from jax import lax
from jax.experimental import pallas as pl
from jax.experimental.pallas import tpu as pltpu
from jax.sharding import PartitionSpec as P

NEWTON = 2
DIRECT_COUNTS = (4, 8)
LATE = 4

damping = 0.5
sigma_floor = 0.5
section_step = 0.1


def arrivals(count, direct):
    if not direct:
        return list(range(count))
    return [0, 1, 4, 2, 3, 6, 5, 7] if count == 8 else [0, 1, 2, 3]


def row_met(spot, row, direct):
    return jnp.bitwise_xor(row, spot) if direct else spot


def gather_direct(block, count):
    def swapped(mask, data):
        return lax.ppermute(data, "row", [(row, row ^ mask) for row in range(count)])

    found = {0: block}
    for mask in (4, 1, 2, 3) if count == 8 else (1, 2, 3):
        found[mask] = swapped(mask, block)
    if count == 8:
        for mask in (1, 2, 3):
            found[4 + mask] = swapped(mask, found[4])
    return [found[mask] for mask in arrivals(count, True)]


IN_PIECES = 8
OUT_PIECES = 4


def row_pieces(size, pieces):
    tall = size // pieces
    return [pl.ds(at * tall, tall) for at in range(pieces)]


def narrow_kernel(wide_ref, narrow_ref, held, sem):
    copies = [
        pltpu.make_async_copy(wide_ref.at[part], held.at[part], sem.at[at])
        for at, part in enumerate(row_pieces(held.shape[0], IN_PIECES))
    ]
    for copy in copies:
        copy.start()
    for copy, part in zip(copies, row_pieces(held.shape[0], IN_PIECES)):
        copy.wait()
        narrow_ref[part, :] = held[part, :].astype(narrow_ref.dtype)


def store_powers(outs, part, state, coef):
    outs[0][:, part] = jnp.exp(-state * coef[3])
    outs[1][:, part] = jnp.exp(state * coef[3])
    outs[2][:, part] = jnp.exp(-state * coef[4])


def later_kernel(own, other, state, decay, rate, coef, stress, normal, change, *outs):
    stress[...] = own[0] + other[0].astype(jnp.float32)
    normal[...] = own[1] + other[1].astype(jnp.float32)
    lanes = coef.shape[2]
    for first in range(0, state.shape[1], lanes):
        part = slice(first, first + lanes)
        step = state_change(rate[:, part], decay[:, part], coef[2])
        change[:, part] = step
        store_powers(outs, part, state[:, part] + section_step * step, coef)


def prepare_kernel(spots, direct, *refs):
    far, (v_out, u_out, coef_out, *powers), near, sem = refs[:7], refs[7:13], refs[13:20], refs[20]
    copies = [
        pltpu.make_async_copy(source, held, sem.at[at])
        for at, (source, held) in enumerate(zip(far, near))
    ]
    for copy in copies:
        copy.start()
    for copy in copies:
        copy.wait()
    rank_ref, v_ref, u_ref, sigma_ref, a_ref, b_ref, state_ref = near
    kinds, rows, count, rank_count, size = u_ref.shape
    row = lax.axis_index("row")
    met = [row_met(spot, row, direct) for spot in spots]
    for at, q in enumerate(met):
        for p in range(rows):
            inside = lax.broadcasted_iota(jnp.int32, (rank_count, size), 0) < rank_ref[p, q]
            v_out[at, p] = jnp.where(inside, v_ref[p, q].astype(jnp.float32), 0.0).astype(v_out.dtype)
    for p in range(rows):
        for kind in range(kinds):
            for first in range(0, count, 4):
                group = [u_ref[kind, p, q] for q in met[first : first + 4]]
                turned = jnp.concatenate(group, axis=0).astype(jnp.float32).T
                u_out[p, kind * size : (kind + 1) * size, first * rank_count : (first + len(group)) * rank_count] = (
                    turned.astype(u_out.dtype)
                )
    lanes = coef_out.shape[2]
    for at, values in enumerate((sigma_ref[...], a_ref[...], b_ref[...], 1.0 / a_ref[...], 1.0 / b_ref[...])):
        coef_out[at] = jnp.broadcast_to(values, (lanes, size)).T
    for first in range(0, state_ref.shape[1], lanes):
        part = slice(first, first + lanes)
        store_powers(powers, part, state_ref[:, part], coef_out)


def sums_kernel(spots, direct, first, pick, before, near_ref, v_ref, u_ref, d_ref, *refs):
    blocks = refs[: len(spots)]
    refs = refs[len(spots) :]
    if before:
        sums_ref, refs = refs[0], refs[1:]
    out_ref, proj = refs
    count, rows, rank_count, size = v_ref.shape
    kinds, slots = d_ref.shape[0], near_ref.shape[1]
    row, col = lax.axis_index("row"), lax.axis_index("col")
    met = [row_met(spot, row, direct) for spot in spots]
    chosen = list(range(rows)) if pick is None else [col if pick == 0 else 1 - col]
    places = [(place,) for place in range(rows)] if pick is None else [()]
    for at, block in enumerate(blocks):
        if pick is None:
            weights = v_ref[first + at].reshape(rows * rank_count, size)
        else:
            weights = v_ref[first + at, chosen[0]]
        part = jnp.dot(weights, block[...], preferred_element_type=jnp.float32).astype(proj.dtype)
        for place in range(len(chosen)):
            proj[place, at * rank_count : (at + 1) * rank_count, :] = part[
                place * rank_count : (place + 1) * rank_count
            ]
    lanes = slice(first * rank_count, (first + len(blocks)) * rank_count)
    for place, p in enumerate(chosen):
        weights, fields = [u_ref[p, :, lanes]], [proj[place]]
        for s in range(slots):
            near = near_ref[pl.ds(p, 1), s : s + 1] - col * count
            field = None
            for q, block in zip(met, blocks):
                mask = jnp.where(near == q, 1.0, 0.0).astype(block.dtype)
                part = block[...] * mask
                field = part if field is None else field + part
            weights.append(jnp.concatenate([d_ref[kind, p, s] for kind in range(kinds)], axis=0))
            fields.append(field)
        total = jnp.dot(
            jnp.concatenate(weights, axis=1),
            jnp.concatenate(fields, axis=0),
            preferred_element_type=jnp.float32,
        )
        for kind in range(kinds):
            piece = total[kind * size : (kind + 1) * size]
            if before:
                piece += sums_ref[p, kind]
            out_ref[*places[place], kind] = piece.astype(out_ref.dtype)


def inverse(value):
    rough = pl.reciprocal(value, approx=True)
    return rough * (2.0 - value * rough)


def sinh_cosh(value):
    grown = jnp.exp(value)
    shrunk = inverse(grown)
    square = value * value
    small = value * (1.0 + square * (1 / 6 + square * (1 / 120)))
    sinh = jnp.where(square < 0.25, small, 0.5 * (grown - shrunk))
    return sinh, 0.5 * (grown + shrunk)


def friction(shear, normal, weight, unweight, tau_load, sigma_base, a_wide):
    tau = tau_load + shear
    size = jnp.abs(tau)
    stiff = jnp.maximum(sigma_base + normal, sigma_floor) * a_wide
    double = 2.0 * damping * weight
    drive = size * unweight * (0.5 / damping)
    square = drive * drive + 1.0
    slope = jnp.minimum(size * inverse(stiff), jnp.log(drive + square * lax.rsqrt(square)))
    for newton_step in range(NEWTON):
        sinh, cosh = sinh_cosh(slope)
        excess = stiff * slope + double * sinh - size
        slope = slope - excess * inverse(stiff + double * cosh)
    rate = 2.0 * weight * sinh_cosh(slope)[0]
    return jnp.where(tau < 0.0, -rate, rate)


def state_change(rate, decay, b_wide):
    return b_wide * (decay - jnp.abs(rate))


def over_pieces(begin, tall, members, lanes, work):
    step = min(tall, 64)

    @pl.loop(0, tall // step)
    def _(index):
        rows = pl.ds(pl.multiple_of(begin + index * step, step), step)
        for first in range(0, members, lanes):
            work(rows, slice(first, first + lanes))


def section_one_kernel(own, other, weight, unweight, tau, coef, rate, rate_half):
    size, members = tau.shape

    def work(rows, part):
        first = friction(
            own[0, rows, part] + other[0, rows, part].astype(jnp.float32),
            own[1, rows, part] + other[1, rows, part].astype(jnp.float32),
            weight[rows, part],
            unweight[rows, part],
            tau[rows, part],
            coef[0, rows, :],
            coef[1, rows, :],
        )
        rate[rows, part] = first
        rate_half[rows, part] = first.astype(rate_half.dtype)

    over_pieces(0, size, members, coef.shape[2], work)


def section_two_kernel(
    own, other, weight, unweight, decay, tau, coef, stress, normal, rate, change, rate_out, change_out, mean_rate, mean_change, sem
):
    size, members = tau.shape

    def work(rows, part):
        shear = own[0, rows, part] + other[0, rows, part].astype(jnp.float32)
        press = own[1, rows, part] + other[1, rows, part].astype(jnp.float32)
        later = friction(
            stress[rows, part] + section_step * shear,
            normal[rows, part] + section_step * press,
            weight[rows, part],
            unweight[rows, part],
            tau[rows, part],
            coef[0, rows, :],
            coef[1, rows, :],
        )
        second = state_change(later, decay[rows, part], coef[2, rows, :])
        mean_rate[rows, part] = (rate[rows, part] + later) * 0.5
        mean_change[rows, part] = (change[rows, part] + second) * 0.5

    copies = []
    for at, part in enumerate(row_pieces(size, OUT_PIECES)):
        over_pieces(part.start, part.size, members, coef.shape[2], work)
        for kind, (held, out) in enumerate(((mean_rate, rate_out), (mean_change, change_out))):
            copies.append(pltpu.make_async_copy(held.at[part], out.at[part], sem.at[kind, at]))
            copies[-1].start()
    for copy in copies:
        copy.wait()


def on_core(kernel, outs, arrays, scratch=(), flops=0, room=16, far=(), out_far=False):
    vmem, hbm = pl.BlockSpec(memory_space=pltpu.VMEM), pl.BlockSpec(memory_space=pl.ANY)
    arrays = (*(pltpu.with_memory_space_constraint(a, pltpu.HBM) for a in far), *arrays)
    return pl.pallas_call(
        kernel,
        out_shape=outs,
        in_specs=[hbm] * len(far) + [vmem] * (len(arrays) - len(far)),
        out_specs=jax.tree.map(lambda _: hbm if out_far else vmem, outs),
        scratch_shapes=list(scratch),
        compiler_params=pltpu.CompilerParams(vmem_limit_bytes=room * 1024 * 1024),
        cost_estimate=pl.CostEstimate(
            flops=flops, bytes_accessed=sum(a.size * a.dtype.itemsize for a in arrays), transcendentals=0
        ),
    )(*arrays)


def body(
    slip_deficit,
    state_var,
    tau_load,
    sigma_base,
    a_coef,
    b_coef,
    v_basis,
    u_basis,
    dense_blocks,
    block_ranks,
    near_index,
):
    count = lax.axis_size("row")
    size, members = slip_deficit.shape
    kinds, rows, _, rank_count, _ = u_basis.shape
    direct = count in DIRECT_COUNTS
    spots = arrivals(count, direct)
    early = max(count - LATE, 0)
    room = 16 if direct else 40
    lanes = min(members, 128)
    narrow, wide = jnp.bfloat16, jnp.float32
    swap = [(0, 1), (1, 0)]

    def shaped(*shape, kind=wide):
        return jax.ShapeDtypeStruct(shape, kind)

    full = shaped(size, members)
    v_met, u_met, coef, *powers = on_core(
        functools.partial(prepare_kernel, spots, direct),
        (
            shaped(count, rows, rank_count, size, kind=narrow),
            shaped(rows, kinds * size, count * rank_count, kind=narrow),
            shaped(5, size, lanes),
            full,
            full,
            full,
        ),
        (),
        (
            pltpu.SMEM(block_ranks.shape, jnp.int32),
            pltpu.VMEM(v_basis.shape, narrow),
            pltpu.VMEM(u_basis.shape, narrow),
            *[pltpu.VMEM((1, size), wide)] * 3,
            pltpu.VMEM((size, members), wide),
            pltpu.SemaphoreType.DMA((7,)),
        ),
        room=room,
        far=(
            block_ranks,
            v_basis,
            u_basis,
            sigma_base.reshape(1, size),
            a_coef.reshape(1, size),
            b_coef.reshape(1, size),
            state_var,
        ),
    )

    def add(blocks, first, pick, before, kind):
        held = rows if pick is None else 1
        lead = (rows, kinds) if pick is None else (kinds,)
        return on_core(
            functools.partial(
                sums_kernel, spots[first : first + len(blocks)], direct, first, pick, before is not None
            ),
            shaped(*lead, size, members, kind=kind),
            (near_index, v_met, u_met, dense_blocks, *blocks, *(() if before is None else (before,))),
            (
                pltpu.VMEM((held, len(blocks) * rank_count, members), narrow),
            ),
            2 * held * size * members * rank_count * len(blocks) * 3,
            room,
        )

    def lattice(field_half, beside):
        if direct:
            blocks = gather_direct(field_half, count)
        else:
            whole = lax.all_gather(field_half, "row", axis=0)
            blocks = [whole[r] for r in range(count)]
        blocks[0], beside = lax.optimization_barrier((blocks[0], beside))
        sums = add(blocks[:early], 0, None, None, wide) if early else None
        other = lax.ppermute(add(blocks[early:], early, 1, sums, narrow), "col", swap)
        return add(blocks[early:], early, 0, sums, wide), other, beside

    slip_half = on_core(
        narrow_kernel,
        shaped(size, members, kind=narrow),
        (),
        (pltpu.VMEM((size, members), wide), pltpu.SemaphoreType.DMA((IN_PIECES,))),
        far=(slip_deficit,),
    )
    own, other, powers = lattice(slip_half, powers)
    rate, rate_half = on_core(
        section_one_kernel,
        (full, shaped(size, members, kind=narrow)),
        (own, other, *powers[:2], tau_load, coef),
        flops=200 * size * members,
    )
    beside = on_core(later_kernel, (full,) * 6, (own, other, state_var, powers[2], rate, coef))
    own, other, (stress, normal, change, *powers) = lattice(rate_half, beside)
    return on_core(
        section_two_kernel,
        (full, full),
        (own, other, *powers, tau_load, coef, stress, normal, rate, change),
        (
            pltpu.VMEM((size, members), wide),
            pltpu.VMEM((size, members), wide),
            pltpu.SemaphoreType.DMA((2, OUT_PIECES)),
        ),
        flops=200 * size * members,
        out_far=True,
    )


def solution(mesh):
    placed = (
        P(("row", "col"), "scen"),
        P(("row", "col"), "scen"),
        P(("row", "col"), "scen"),
        P(("row", "col")),
        P(("row", "col")),
        P(("row", "col")),
        P("row", "col", None, None),
        P(None, "row", "col", None, None),
        P(None, "row", "col", None, None),
        P("row", "col"),
        P("row", "col"),
    )
    return jax.shard_map(
        body,
        mesh=mesh,
        in_specs=placed,
        out_specs=(P(("row", "col"), "scen"), P(("row", "col"), "scen")),
        check_vma=False,
    )
```

```python
import functools

import jax
import jax.numpy as jnp
from jax import lax
from jax.experimental import pallas as pl
from jax.experimental.pallas import tpu as pltpu
from jax.sharding import PartitionSpec as P

NEWTON = 2
DIRECT_COUNTS = (4, 8)
TILE = 128

damping = 0.5
sigma_floor = 0.5
section_step = 0.1


def arrivals(count, direct):
    if not direct:
        cuts = [0, max(count - 4, 0), count]
        return [list(range(first, last)) for first, last in zip(cuts, cuts[1:]) if last > first]
    return [[0, 1, 4], [2, 3], [7, 6, 5]] if count == 8 else [[0, 1], [2, 3]]


def row_met(spot, row, direct):
    return jnp.bitwise_xor(row, spot) if direct else spot


def gather_direct(block, count):
    def swapped(mask, data):
        return lax.ppermute(data, "row", [(row, row ^ mask) for row in range(count)])

    found = {0: block}
    for mask in (4, 1, 2, 3, 7) if count == 8 else (1, 2, 3):
        found[mask] = swapped(mask, block)
    if count == 8:
        for mask in (1, 2):
            found[4 + mask] = swapped(mask, found[4])
    return [[found[mask] for mask in group] for group in arrivals(count, True)]


IN_PIECES = 8
OUT_PIECES = 4


def row_pieces(size, pieces):
    tall = size // pieces
    return [pl.ds(at * tall, tall) for at in range(pieces)]


def narrow_kernel(wide_ref, narrow_ref, held, sem):
    copies = [
        pltpu.make_async_copy(wide_ref.at[part], held.at[part], sem.at[at])
        for at, part in enumerate(row_pieces(held.shape[0], IN_PIECES))
    ]
    for copy in copies:
        copy.start()
    for copy, part in zip(copies, row_pieces(held.shape[0], IN_PIECES)):
        copy.wait()
        narrow_ref[part, :] = held[part, :].astype(narrow_ref.dtype)


def store_powers(outs, part, state, coef):
    outs[0][:, part] = jnp.exp(-state * coef[3])
    outs[1][:, part] = jnp.exp(state * coef[3])
    outs[2][:, part] = jnp.exp(-state * coef[4])


def later_kernel(state, change, coef, *outs):
    lanes = coef.shape[2]
    for first in range(0, state.shape[1], lanes):
        part = slice(first, first + lanes)
        store_powers(outs, part, state[:, part] + section_step * change[:, part], coef)


def prepare_kernel(groups, direct, *refs):
    far, (v_out, u_out, coef_out, *powers), near, sem = refs[:7], refs[7:13], refs[13:20], refs[20]
    copies = [
        pltpu.make_async_copy(source, held, sem.at[at])
        for at, (source, held) in enumerate(zip(far, near))
    ]
    for copy in copies:
        copy.start()
    for copy in copies:
        copy.wait()
    rank_ref, v_ref, u_ref, sigma_ref, a_ref, b_ref, state_ref = near
    kinds, rows, count, rank_count, size = u_ref.shape
    row = lax.axis_index("row")
    met = [row_met(spot, row, direct) for group in groups for spot in group]
    for at, q in enumerate(met):
        for p in range(rows):
            inside = lax.broadcasted_iota(jnp.int32, (rank_count, size), 0) < rank_ref[p, q]
            v_out[at, p] = jnp.where(inside, v_ref[p, q].astype(jnp.float32), 0.0).astype(v_out.dtype)
    for p in range(rows):
        for kind in range(kinds):
            first = start = 0
            for spots in groups:
                group = [u_ref[kind, p, q] for q in met[first : first + len(spots)]]
                spare = -len(group) * rank_count % TILE
                if spare:
                    group.append(jnp.zeros((spare, size), u_ref.dtype))
                turned = jnp.concatenate(group, axis=0).astype(jnp.float32).T
                stop = start + turned.shape[1]
                u_out[p, kind * size : (kind + 1) * size, start:stop] = turned.astype(u_out.dtype)
                first, start = first + len(spots), stop
    lanes = coef_out.shape[2]
    for at, values in enumerate((sigma_ref[...], a_ref[...], b_ref[...], 1.0 / a_ref[...], 1.0 / b_ref[...])):
        coef_out[at] = jnp.broadcast_to(values, (lanes, size)).T
    for first in range(0, state_ref.shape[1], lanes):
        part = slice(first, first + lanes)
        store_powers(powers, part, state_ref[:, part], coef_out)


def sums_kernel(spots, direct, first, start, pick, before, near_ref, v_ref, u_ref, d_ref, *refs):
    blocks = refs[: len(spots)]
    refs = refs[len(spots) :]
    if before:
        sums_ref, refs = refs[0], refs[1:]
    out_ref, proj = refs
    count, rows, rank_count, size = v_ref.shape
    kinds, slots = d_ref.shape[0], near_ref.shape[1]
    row, col = lax.axis_index("row"), lax.axis_index("col")
    met = [row_met(spot, row, direct) for spot in spots]
    chosen = list(range(rows)) if pick is None else [col if pick == 0 else 1 - col]
    places = [(place,) for place in range(rows)] if pick is None else [()]
    for at, block in enumerate(blocks):
        if pick is None:
            weights = v_ref[first + at].reshape(rows * rank_count, size)
        else:
            weights = v_ref[first + at, chosen[0]]
        part = jnp.dot(weights, block[...], preferred_element_type=jnp.float32).astype(proj.dtype)
        for place in range(len(chosen)):
            proj[place, at * rank_count : (at + 1) * rank_count, :] = part[
                place * rank_count : (place + 1) * rank_count
            ]
    width = proj.shape[1]
    lanes = slice(start, start + width)
    if width > len(blocks) * rank_count:
        for place in range(len(chosen)):
            proj[place, len(blocks) * rank_count :, :] = jnp.zeros(
                (width - len(blocks) * rank_count, proj.shape[2]), proj.dtype
            )
    for place, p in enumerate(chosen):
        weights, fields = [u_ref[p, :, lanes]], [proj[place]]
        for s in range(slots):
            near = near_ref[pl.ds(p, 1), s : s + 1] - col * count
            field = None
            for q, block in zip(met, blocks):
                mask = jnp.where(near == q, 1.0, 0.0).astype(block.dtype)
                part = block[...] * mask
                field = part if field is None else field + part
            weights.append(jnp.concatenate([d_ref[kind, p, s] for kind in range(kinds)], axis=0))
            fields.append(field)
        total = jnp.dot(
            jnp.concatenate(weights, axis=1),
            jnp.concatenate(fields, axis=0),
            preferred_element_type=jnp.float32,
        )
        for kind in range(kinds):
            piece = total[kind * size : (kind + 1) * size]
            if before:
                piece += sums_ref[p, kind]
            out_ref[*places[place], kind] = piece.astype(out_ref.dtype)


def inverse(value):
    rough = pl.reciprocal(value, approx=True)
    return rough * (2.0 - value * rough)


def sinh_cosh(value):
    grown = jnp.exp(value)
    shrunk = inverse(grown)
    square = value * value
    small = value * (1.0 + square * (1 / 6 + square * (1 / 120)))
    sinh = jnp.where(square < 0.25, small, 0.5 * (grown - shrunk))
    return sinh, 0.5 * (grown + shrunk)


def friction(shear, normal, weight, unweight, decay, tau_load, sigma_base, a_wide, b_wide):
    tau = tau_load + shear
    size = jnp.abs(tau)
    stiff = jnp.maximum(sigma_base + normal, sigma_floor) * a_wide
    double = 2.0 * damping * weight
    drive = size * unweight * (0.5 / damping)
    square = drive * drive + 1.0
    slope = jnp.minimum(size * inverse(stiff), jnp.log(drive + square * lax.rsqrt(square)))
    for newton_step in range(NEWTON):
        sinh, cosh = sinh_cosh(slope)
        excess = stiff * slope + double * sinh - size
        slope = slope - excess * inverse(stiff + double * cosh)
    rate = 2.0 * weight * sinh_cosh(slope)[0]
    change = b_wide * (decay - jnp.abs(rate))
    return (jnp.where(tau < 0.0, -rate, rate), change)


def over_pieces(begin, tall, members, lanes, work):
    step = min(tall, 64)

    @pl.loop(0, tall // step)
    def _(index):
        rows = pl.ds(pl.multiple_of(begin + index * step, step), step)
        for first in range(0, members, lanes):
            work(rows, slice(first, first + lanes))


def section_one_kernel(own, other, weight, unweight, decay, tau, coef, stress, normal, rate, change, rate_half):
    size, members = tau.shape

    def work(rows, part):
        shear = own[0, rows, part] + other[0, rows, part].astype(jnp.float32)
        press = own[1, rows, part] + other[1, rows, part].astype(jnp.float32)
        stress[rows, part] = shear
        normal[rows, part] = press
        first, second = friction(
            shear,
            press,
            weight[rows, part],
            unweight[rows, part],
            decay[rows, part],
            tau[rows, part],
            coef[0, rows, :],
            coef[1, rows, :],
            coef[2, rows, :],
        )
        rate[rows, part] = first
        change[rows, part] = second
        rate_half[rows, part] = first.astype(rate_half.dtype)

    over_pieces(0, size, members, coef.shape[2], work)


def section_two_kernel(
    own, other, weight, unweight, decay, tau, coef, stress, normal, rate, change, rate_out, change_out, mean_rate, mean_change, sem
):
    size, members = tau.shape

    def work(rows, part):
        shear = own[0, rows, part] + other[0, rows, part].astype(jnp.float32)
        press = own[1, rows, part] + other[1, rows, part].astype(jnp.float32)
        first, second = friction(
            stress[rows, part] + section_step * shear,
            normal[rows, part] + section_step * press,
            weight[rows, part],
            unweight[rows, part],
            decay[rows, part],
            tau[rows, part],
            coef[0, rows, :],
            coef[1, rows, :],
            coef[2, rows, :],
        )
        mean_rate[rows, part] = (rate[rows, part] + first) * 0.5
        mean_change[rows, part] = (change[rows, part] + second) * 0.5

    copies = []
    for at, part in enumerate(row_pieces(size, OUT_PIECES)):
        over_pieces(part.start, part.size, members, coef.shape[2], work)
        for kind, (held, out) in enumerate(((mean_rate, rate_out), (mean_change, change_out))):
            copies.append(pltpu.make_async_copy(held.at[part], out.at[part], sem.at[kind, at]))
            copies[-1].start()
    for copy in copies:
        copy.wait()


def on_core(kernel, outs, arrays, scratch=(), flops=0, room=16, far=(), out_far=False):
    vmem, hbm = pl.BlockSpec(memory_space=pltpu.VMEM), pl.BlockSpec(memory_space=pl.ANY)
    arrays = (*(pltpu.with_memory_space_constraint(a, pltpu.HBM) for a in far), *arrays)
    return pl.pallas_call(
        kernel,
        out_shape=outs,
        in_specs=[hbm] * len(far) + [vmem] * (len(arrays) - len(far)),
        out_specs=jax.tree.map(lambda _: hbm if out_far else vmem, outs),
        scratch_shapes=list(scratch),
        compiler_params=pltpu.CompilerParams(vmem_limit_bytes=room * 1024 * 1024),
        cost_estimate=pl.CostEstimate(
            flops=flops, bytes_accessed=sum(a.size * a.dtype.itemsize for a in arrays), transcendentals=0
        ),
    )(*arrays)


def body(
    slip_deficit,
    state_var,
    tau_load,
    sigma_base,
    a_coef,
    b_coef,
    v_basis,
    u_basis,
    dense_blocks,
    block_ranks,
    near_index,
):
    count = lax.axis_size("row")
    size, members = slip_deficit.shape
    kinds, rows, _, rank_count, _ = u_basis.shape
    direct = count in DIRECT_COUNTS
    groups = arrivals(count, direct)
    firsts = [sum(len(group) for group in groups[:at]) for at in range(len(groups))]
    tiles = [-(-len(group) * rank_count // TILE) * TILE for group in groups]
    starts = [sum(tiles[:at]) for at in range(len(groups))]
    room = 16 if direct else 40
    lanes = min(members, 128)
    narrow, wide = jnp.bfloat16, jnp.float32
    swap = [(0, 1), (1, 0)]

    def shaped(*shape, kind=wide):
        return jax.ShapeDtypeStruct(shape, kind)

    full = shaped(size, members)
    v_met, u_met, coef, *powers = on_core(
        functools.partial(prepare_kernel, groups, direct),
        (
            shaped(count, rows, rank_count, size, kind=narrow),
            shaped(rows, kinds * size, sum(tiles), kind=narrow),
            shaped(5, size, lanes),
            full,
            full,
            full,
        ),
        (),
        (
            pltpu.SMEM(block_ranks.shape, jnp.int32),
            pltpu.VMEM(v_basis.shape, narrow),
            pltpu.VMEM(u_basis.shape, narrow),
            *[pltpu.VMEM((1, size), wide)] * 3,
            pltpu.VMEM((size, members), wide),
            pltpu.SemaphoreType.DMA((7,)),
        ),
        room=room,
        far=(
            block_ranks,
            v_basis,
            u_basis,
            sigma_base.reshape(1, size),
            a_coef.reshape(1, size),
            b_coef.reshape(1, size),
            state_var,
        ),
    )

    def add(blocks, at, pick, before, kind):
        held = rows if pick is None else 1
        lead = (rows, kinds) if pick is None else (kinds,)
        return on_core(
            functools.partial(
                sums_kernel, groups[at], direct, firsts[at], starts[at], pick, before is not None
            ),
            shaped(*lead, size, members, kind=kind),
            (near_index, v_met, u_met, dense_blocks, *blocks, *(() if before is None else (before,))),
            (
                pltpu.VMEM((held, tiles[at], members), narrow),
            ),
            2 * held * size * members * rank_count * len(blocks) * 3,
            room,
        )

    def lattice(field_half, beside):
        if direct:
            found = gather_direct(field_half, count)
        else:
            whole = lax.all_gather(field_half, "row", axis=0)
            found = [[whole[r] for r in group] for group in groups]
        found[0][0], beside = lax.optimization_barrier((found[0][0], beside))
        sums, end = None, len(groups) - 1
        for at in range(end):
            sums = add(found[at], at, None, sums, wide)
        other = lax.ppermute(add(found[end], end, 1, sums, narrow), "col", swap)
        return add(found[end], end, 0, sums, wide), other, beside

    slip_half = on_core(
        narrow_kernel,
        shaped(size, members, kind=narrow),
        (),
        (pltpu.VMEM((size, members), wide), pltpu.SemaphoreType.DMA((IN_PIECES,))),
        far=(slip_deficit,),
    )
    own, other, powers = lattice(slip_half, powers)
    stress, normal, rate, change, rate_half = on_core(
        section_one_kernel,
        (full, full, full, full, shaped(size, members, kind=narrow)),
        (own, other, *powers, tau_load, coef),
        flops=200 * size * members,
    )
    powers = on_core(later_kernel, (full, full, full), (state_var, change, coef))
    own, other, powers = lattice(rate_half, powers)
    return on_core(
        section_two_kernel,
        (full, full),
        (own, other, *powers, tau_load, coef, stress, normal, rate, change),
        (
            pltpu.VMEM((size, members), wide),
            pltpu.VMEM((size, members), wide),
            pltpu.SemaphoreType.DMA((2, OUT_PIECES)),
        ),
        flops=200 * size * members,
        out_far=True,
    )


def solution(mesh):
    placed = (
        P(("row", "col"), "scen"),
        P(("row", "col"), "scen"),
        P(("row", "col"), "scen"),
        P(("row", "col")),
        P(("row", "col")),
        P(("row", "col")),
        P("row", "col", None, None),
        P(None, "row", "col", None, None),
        P(None, "row", "col", None, None),
        P("row", "col"),
        P("row", "col"),
    )
    return jax.shard_map(
        body,
        mesh=mesh,
        in_specs=placed,
        out_specs=(P(("row", "col"), "scen"), P(("row", "col"), "scen")),
        check_vma=False,
    )
```

```python
import functools

import jax
import jax.numpy as jnp
from jax import lax
from jax.experimental import pallas as pl
from jax.experimental.pallas import tpu as pltpu
from jax.sharding import PartitionSpec as P

NEWTON = 2
DIRECT_COUNTS = (4, 8)
LATE = 4

damping = 0.5
sigma_floor = 0.5
section_step = 0.1


def arrivals(count, direct):
    if not direct:
        return list(range(count))
    return [0, 1, 4, 2, 3, 6, 5, 7] if count == 8 else [0, 1, 2, 3]


def row_met(spot, row, direct):
    return jnp.bitwise_xor(row, spot) if direct else spot


def gather_direct(block, count):
    def swapped(mask, data):
        return lax.ppermute(data, "row", [(row, row ^ mask) for row in range(count)])

    found = {0: block}
    for mask in (4, 1, 2, 3) if count == 8 else (1, 2, 3):
        found[mask] = swapped(mask, block)
    if count == 8:
        for mask in (1, 2, 3):
            found[4 + mask] = swapped(mask, found[4])
    return [found[mask] for mask in arrivals(count, True)]


IN_PIECES = 8
OUT_PIECES = 4


def row_pieces(size, pieces):
    tall = size // pieces
    return [pl.ds(at * tall, tall) for at in range(pieces)]


def narrow_kernel(wide_ref, narrow_ref, held, sem):
    copies = [
        pltpu.make_async_copy(wide_ref.at[part], held.at[part], sem.at[at])
        for at, part in enumerate(row_pieces(held.shape[0], IN_PIECES))
    ]
    for copy in copies:
        copy.start()
    for copy, part in zip(copies, row_pieces(held.shape[0], IN_PIECES)):
        copy.wait()
        narrow_ref[part, :] = held[part, :].astype(narrow_ref.dtype)


def store_powers(outs, part, state, coef):
    outs[0][:, part] = jnp.exp(-state * coef[3])
    outs[1][:, part] = jnp.exp(state * coef[3])
    outs[2][:, part] = jnp.exp(-state * coef[4])


def later_kernel(own, other, state, decay, rate, coef, stress, normal, change, *outs):
    stress[...] = own[0] + other[0].astype(jnp.float32)
    normal[...] = own[1] + other[1].astype(jnp.float32)
    lanes = coef.shape[2]
    for first in range(0, state.shape[1], lanes):
        part = slice(first, first + lanes)
        step = state_change(rate[:, part], decay[:, part], coef[2])
        change[:, part] = step
        store_powers(outs, part, state[:, part] + section_step * step, coef)


def prepare_kernel(spots, direct, *refs):
    far, (v_out, u_out, coef_out, *powers), near, sem = refs[:7], refs[7:13], refs[13:20], refs[20]
    copies = [
        pltpu.make_async_copy(source, held, sem.at[at])
        for at, (source, held) in enumerate(zip(far, near))
    ]
    for copy in copies:
        copy.start()
    for copy in copies:
        copy.wait()
    rank_ref, v_ref, u_ref, sigma_ref, a_ref, b_ref, state_ref = near
    kinds, rows, count, rank_count, size = u_ref.shape
    row = lax.axis_index("row")
    met = [row_met(spot, row, direct) for spot in spots]
    for at, q in enumerate(met):
        for p in range(rows):
            inside = lax.broadcasted_iota(jnp.int32, (rank_count, size), 0) < rank_ref[p, q]
            v_out[at, p] = jnp.where(inside, v_ref[p, q].astype(jnp.float32), 0.0).astype(v_out.dtype)
    for p in range(rows):
        for kind in range(kinds):
            for first in range(0, count, 4):
                group = [u_ref[kind, p, q] for q in met[first : first + 4]]
                turned = jnp.concatenate(group, axis=0).astype(jnp.float32).T
                u_out[p, kind * size : (kind + 1) * size, first * rank_count : (first + len(group)) * rank_count] = (
                    turned.astype(u_out.dtype)
                )
    lanes = coef_out.shape[2]
    for at, values in enumerate((sigma_ref[...], a_ref[...], b_ref[...], 1.0 / a_ref[...], 1.0 / b_ref[...])):
        coef_out[at] = jnp.broadcast_to(values, (lanes, size)).T
    for first in range(0, state_ref.shape[1], lanes):
        part = slice(first, first + lanes)
        store_powers(powers, part, state_ref[:, part], coef_out)


def sums_kernel(spots, direct, first, pick, before, near_ref, v_ref, u_ref, d_ref, *refs):
    blocks = refs[: len(spots)]
    refs = refs[len(spots) :]
    if before:
        sums_ref, refs = refs[0], refs[1:]
    out_ref, proj = refs
    count, rows, rank_count, size = v_ref.shape
    kinds, slots = d_ref.shape[0], near_ref.shape[1]
    row, col = lax.axis_index("row"), lax.axis_index("col")
    met = [row_met(spot, row, direct) for spot in spots]
    chosen = list(range(rows)) if pick is None else [col if pick == 0 else 1 - col]
    places = [(place,) for place in range(rows)] if pick is None else [()]
    for at, block in enumerate(blocks):
        if pick is None:
            weights = v_ref[first + at].reshape(rows * rank_count, size)
        else:
            weights = v_ref[first + at, chosen[0]]
        part = jnp.dot(weights, block[...], preferred_element_type=jnp.float32).astype(proj.dtype)
        for place in range(len(chosen)):
            proj[place, at * rank_count : (at + 1) * rank_count, :] = part[
                place * rank_count : (place + 1) * rank_count
            ]
    lanes = slice(first * rank_count, (first + len(blocks)) * rank_count)
    for place, p in enumerate(chosen):
        weights, fields = [u_ref[p, :, lanes]], [proj[place]]
        for s in range(slots):
            near = near_ref[pl.ds(p, 1), s : s + 1] - col * count
            field = None
            for q, block in zip(met, blocks):
                mask = jnp.where(near == q, 1.0, 0.0).astype(block.dtype)
                part = block[...] * mask
                field = part if field is None else field + part
            weights.append(jnp.concatenate([d_ref[kind, p, s] for kind in range(kinds)], axis=0))
            fields.append(field)
        total = jnp.dot(
            jnp.concatenate(weights, axis=1),
            jnp.concatenate(fields, axis=0),
            preferred_element_type=jnp.float32,
        )
        for kind in range(kinds):
            piece = total[kind * size : (kind + 1) * size]
            if before:
                piece += sums_ref[p, kind]
            out_ref[*places[place], kind] = piece.astype(out_ref.dtype)


def inverse(value):
    rough = pl.reciprocal(value, approx=True)
    return rough * (2.0 - value * rough)


def rough_inverse(value):
    return pl.reciprocal(value, approx=True)


def scaled_sinh_cosh(value, scale):
    grown = jnp.exp(value)
    half = 0.5 * scale
    up, down = half * grown, half * inverse(grown)
    square = value * value
    small = scale * value * (1.0 + square * (1 / 6 + square * (1 / 120)))
    return jnp.where(square < 0.25, small, up - down), up + down


def friction(shear, normal, weight, unweight, tau_load, sigma_base, a_wide):
    tau = tau_load + shear
    size = jnp.abs(tau)
    stiff = jnp.maximum(sigma_base + normal, sigma_floor) * a_wide
    double = 2.0 * damping * weight
    drive = size * unweight * (0.5 / damping)
    square = drive * drive + 1.0
    slope = jnp.minimum(size * rough_inverse(stiff), jnp.log(drive + square * lax.rsqrt(square)))
    for newton_step in range(NEWTON):
        sinh, cosh = scaled_sinh_cosh(slope, double)
        slope = slope - (stiff * slope + sinh - size) * rough_inverse(stiff + cosh)
    rate = scaled_sinh_cosh(slope, double)[0] * (1.0 / damping)
    return jnp.where(tau < 0.0, -rate, rate)


def state_change(rate, decay, b_wide):
    return b_wide * (decay - jnp.abs(rate))


def over_pieces(begin, tall, members, lanes, work):
    step = min(tall, 64)

    @pl.loop(0, tall // step)
    def _(index):
        rows = pl.ds(pl.multiple_of(begin + index * step, step), step)
        for first in range(0, members, lanes):
            work(rows, slice(first, first + lanes))


def section_one_kernel(own, other, weight, unweight, tau, coef, rate, rate_half):
    size, members = tau.shape

    def work(rows, part):
        first = friction(
            own[0, rows, part] + other[0, rows, part].astype(jnp.float32),
            own[1, rows, part] + other[1, rows, part].astype(jnp.float32),
            weight[rows, part],
            unweight[rows, part],
            tau[rows, part],
            coef[0, rows, :],
            coef[1, rows, :],
        )
        rate[rows, part] = first
        rate_half[rows, part] = first.astype(rate_half.dtype)

    over_pieces(0, size, members, coef.shape[2], work)


def section_two_kernel(
    own, other, weight, unweight, decay, tau, coef, stress, normal, rate, change, rate_out, change_out, mean_rate, mean_change, sem
):
    size, members = tau.shape

    def work(rows, part):
        shear = own[0, rows, part] + other[0, rows, part].astype(jnp.float32)
        press = own[1, rows, part] + other[1, rows, part].astype(jnp.float32)
        later = friction(
            stress[rows, part] + section_step * shear,
            normal[rows, part] + section_step * press,
            weight[rows, part],
            unweight[rows, part],
            tau[rows, part],
            coef[0, rows, :],
            coef[1, rows, :],
        )
        second = state_change(later, decay[rows, part], coef[2, rows, :])
        mean_rate[rows, part] = (rate[rows, part] + later) * 0.5
        mean_change[rows, part] = (change[rows, part] + second) * 0.5

    copies = []
    for at, part in enumerate(row_pieces(size, OUT_PIECES)):
        over_pieces(part.start, part.size, members, coef.shape[2], work)
        for kind, (held, out) in enumerate(((mean_rate, rate_out), (mean_change, change_out))):
            copies.append(pltpu.make_async_copy(held.at[part], out.at[part], sem.at[kind, at]))
            copies[-1].start()
    for copy in copies:
        copy.wait()


def on_core(kernel, outs, arrays, scratch=(), flops=0, room=16, far=(), out_far=False):
    vmem, hbm = pl.BlockSpec(memory_space=pltpu.VMEM), pl.BlockSpec(memory_space=pl.ANY)
    arrays = (*(pltpu.with_memory_space_constraint(a, pltpu.HBM) for a in far), *arrays)
    return pl.pallas_call(
        kernel,
        out_shape=outs,
        in_specs=[hbm] * len(far) + [vmem] * (len(arrays) - len(far)),
        out_specs=jax.tree.map(lambda _: hbm if out_far else vmem, outs),
        scratch_shapes=list(scratch),
        compiler_params=pltpu.CompilerParams(vmem_limit_bytes=room * 1024 * 1024),
        cost_estimate=pl.CostEstimate(
            flops=flops, bytes_accessed=sum(a.size * a.dtype.itemsize for a in arrays), transcendentals=0
        ),
    )(*arrays)


def body(
    slip_deficit,
    state_var,
    tau_load,
    sigma_base,
    a_coef,
    b_coef,
    v_basis,
    u_basis,
    dense_blocks,
    block_ranks,
    near_index,
):
    count = lax.axis_size("row")
    size, members = slip_deficit.shape
    kinds, rows, _, rank_count, _ = u_basis.shape
    direct = count in DIRECT_COUNTS
    spots = arrivals(count, direct)
    early = max(count - LATE, 0)
    room = 16 if direct else 40
    lanes = min(members, 128)
    narrow, wide = jnp.bfloat16, jnp.float32
    swap = [(0, 1), (1, 0)]

    def shaped(*shape, kind=wide):
        return jax.ShapeDtypeStruct(shape, kind)

    full = shaped(size, members)
    v_met, u_met, coef, *powers = on_core(
        functools.partial(prepare_kernel, spots, direct),
        (
            shaped(count, rows, rank_count, size, kind=narrow),
            shaped(rows, kinds * size, count * rank_count, kind=narrow),
            shaped(5, size, lanes),
            full,
            full,
            full,
        ),
        (),
        (
            pltpu.SMEM(block_ranks.shape, jnp.int32),
            pltpu.VMEM(v_basis.shape, narrow),
            pltpu.VMEM(u_basis.shape, narrow),
            *[pltpu.VMEM((1, size), wide)] * 3,
            pltpu.VMEM((size, members), wide),
            pltpu.SemaphoreType.DMA((7,)),
        ),
        room=room,
        far=(
            block_ranks,
            v_basis,
            u_basis,
            sigma_base.reshape(1, size),
            a_coef.reshape(1, size),
            b_coef.reshape(1, size),
            state_var,
        ),
    )

    def add(blocks, first, pick, before, kind):
        held = rows if pick is None else 1
        lead = (rows, kinds) if pick is None else (kinds,)
        return on_core(
            functools.partial(
                sums_kernel, spots[first : first + len(blocks)], direct, first, pick, before is not None
            ),
            shaped(*lead, size, members, kind=kind),
            (near_index, v_met, u_met, dense_blocks, *blocks, *(() if before is None else (before,))),
            (
                pltpu.VMEM((held, len(blocks) * rank_count, members), narrow),
            ),
            2 * held * size * members * rank_count * len(blocks) * 3,
            room,
        )

    def lattice(field_half, beside):
        if direct:
            blocks = gather_direct(field_half, count)
        else:
            whole = lax.all_gather(field_half, "row", axis=0)
            blocks = [whole[r] for r in range(count)]
        blocks[0], beside = lax.optimization_barrier((blocks[0], beside))
        sums = add(blocks[:early], 0, None, None, wide) if early else None
        other = lax.ppermute(add(blocks[early:], early, 1, sums, narrow), "col", swap)
        return add(blocks[early:], early, 0, sums, wide), other, beside

    slip_half = on_core(
        narrow_kernel,
        shaped(size, members, kind=narrow),
        (),
        (pltpu.VMEM((size, members), wide), pltpu.SemaphoreType.DMA((IN_PIECES,))),
        far=(slip_deficit,),
    )
    own, other, powers = lattice(slip_half, powers)
    rate, rate_half = on_core(
        section_one_kernel,
        (full, shaped(size, members, kind=narrow)),
        (own, other, *powers[:2], tau_load, coef),
        flops=200 * size * members,
    )
    beside = on_core(later_kernel, (full,) * 6, (own, other, state_var, powers[2], rate, coef))
    own, other, (stress, normal, change, *powers) = lattice(rate_half, beside)
    return on_core(
        section_two_kernel,
        (full, full),
        (own, other, *powers, tau_load, coef, stress, normal, rate, change),
        (
            pltpu.VMEM((size, members), wide),
            pltpu.VMEM((size, members), wide),
            pltpu.SemaphoreType.DMA((2, OUT_PIECES)),
        ),
        flops=200 * size * members,
        out_far=True,
    )


def solution(mesh):
    placed = (
        P(("row", "col"), "scen"),
        P(("row", "col"), "scen"),
        P(("row", "col"), "scen"),
        P(("row", "col")),
        P(("row", "col")),
        P(("row", "col")),
        P("row", "col", None, None),
        P(None, "row", "col", None, None),
        P(None, "row", "col", None, None),
        P("row", "col"),
        P("row", "col"),
    )
    return jax.shard_map(
        body,
        mesh=mesh,
        in_specs=placed,
        out_specs=(P(("row", "col"), "scen"), P(("row", "col"), "scen")),
        check_vma=False,
    )
```

```python
import functools

import jax
import jax.numpy as jnp
from jax import lax
from jax.experimental import pallas as pl
from jax.experimental.pallas import tpu as pltpu
from jax.sharding import PartitionSpec as P

NEWTON = 2
DIRECT_COUNTS = (4, 8)
LATE = 4

damping = 0.5
sigma_floor = 0.5
section_step = 0.1


def arrivals(count, direct):
    if not direct:
        return list(range(count))
    return [0, 1, 4, 2, 3, 6, 5, 7] if count == 8 else [0, 1, 2, 3]


def row_met(spot, row, direct):
    return jnp.bitwise_xor(row, spot) if direct else spot


def gather_direct(block, count):
    def swapped(mask, data):
        return lax.ppermute(data, "row", [(row, row ^ mask) for row in range(count)])

    found = {0: block}
    for mask in (4, 1, 2, 3) if count == 8 else (1, 2, 3):
        found[mask] = swapped(mask, block)
    if count == 8:
        for mask in (1, 2, 3):
            found[4 + mask] = swapped(mask, found[4])
    return [found[mask] for mask in arrivals(count, True)]


IN_PIECES = 8
OUT_PIECES = 4


def row_pieces(size, pieces):
    tall = size // pieces
    return [pl.ds(at * tall, tall) for at in range(pieces)]


def narrow_kernel(wide_ref, narrow_ref, held, sem):
    copies = [
        pltpu.make_async_copy(wide_ref.at[part], held.at[part], sem.at[at])
        for at, part in enumerate(row_pieces(held.shape[0], IN_PIECES))
    ]
    for copy in copies:
        copy.start()
    for copy, part in zip(copies, row_pieces(held.shape[0], IN_PIECES)):
        copy.wait()
        narrow_ref[part, :] = held[part, :].astype(narrow_ref.dtype)


def store_powers(outs, part, state, coef):
    outs[0][:, part] = jnp.exp(-state * coef[3])
    outs[1][:, part] = jnp.exp(state * coef[3])
    outs[2][:, part] = jnp.exp(-state * coef[4])


def later_kernel(own, other, state, decay, rate, coef, stress, normal, change, *outs):
    stress[...] = own[0] + other[0].astype(jnp.float32)
    normal[...] = own[1] + other[1].astype(jnp.float32)
    lanes = coef.shape[2]
    for first in range(0, state.shape[1], lanes):
        part = slice(first, first + lanes)
        step = state_change(rate[:, part], decay[:, part], coef[2])
        change[:, part] = step
        store_powers(outs, part, state[:, part] + section_step * step, coef)


def prepare_kernel(spots, direct, *refs):
    far, (v_out, u_out, coef_out, *powers), near, sem = refs[:7], refs[7:13], refs[13:20], refs[20]
    copies = [
        pltpu.make_async_copy(source, held, sem.at[at])
        for at, (source, held) in enumerate(zip(far, near))
    ]
    for copy in copies:
        copy.start()
    for copy in copies:
        copy.wait()
    rank_ref, v_ref, u_ref, sigma_ref, a_ref, b_ref, state_ref = near
    kinds, rows, count, rank_count, size = u_ref.shape
    row = lax.axis_index("row")
    met = [row_met(spot, row, direct) for spot in spots]
    for at, q in enumerate(met):
        for p in range(rows):
            inside = lax.broadcasted_iota(jnp.int32, (rank_count, size), 0) < rank_ref[p, q]
            v_out[at, p] = jnp.where(inside, v_ref[p, q].astype(jnp.float32), 0.0).astype(v_out.dtype)
    for p in range(rows):
        for kind in range(kinds):
            for first in range(0, count, 4):
                group = [u_ref[kind, p, q] for q in met[first : first + 4]]
                turned = jnp.concatenate(group, axis=0).astype(jnp.float32).T
                u_out[p, kind * size : (kind + 1) * size, first * rank_count : (first + len(group)) * rank_count] = (
                    turned.astype(u_out.dtype)
                )
    lanes = coef_out.shape[2]
    for at, values in enumerate((sigma_ref[...], a_ref[...], b_ref[...], 1.0 / a_ref[...], 1.0 / b_ref[...])):
        coef_out[at] = jnp.broadcast_to(values, (lanes, size)).T
    for first in range(0, state_ref.shape[1], lanes):
        part = slice(first, first + lanes)
        store_powers(powers, part, state_ref[:, part], coef_out)


def sums_kernel(spots, direct, first, pick, before, near_ref, v_ref, u_ref, d_ref, *refs):
    blocks = refs[: len(spots)]
    refs = refs[len(spots) :]
    if before:
        sums_ref, refs = refs[0], refs[1:]
    out_ref, proj = refs
    count, rows, rank_count, size = v_ref.shape
    kinds, slots = d_ref.shape[0], near_ref.shape[1]
    row, col = lax.axis_index("row"), lax.axis_index("col")
    met = [row_met(spot, row, direct) for spot in spots]
    chosen = list(range(rows)) if pick is None else [col if pick == 0 else 1 - col]
    places = [(place,) for place in range(rows)] if pick is None else [()]
    for at, block in enumerate(blocks):
        if pick is None:
            weights = v_ref[first + at].reshape(rows * rank_count, size)
        else:
            weights = v_ref[first + at, chosen[0]]
        part = jnp.dot(weights, block[...], preferred_element_type=jnp.float32).astype(proj.dtype)
        for place in range(len(chosen)):
            proj[place, at * rank_count : (at + 1) * rank_count, :] = part[
                place * rank_count : (place + 1) * rank_count
            ]
    lanes = slice(first * rank_count, (first + len(blocks)) * rank_count)
    for place, p in enumerate(chosen):
        weights, fields = [u_ref[p, :, lanes]], [proj[place]]
        for s in range(slots):
            near = near_ref[pl.ds(p, 1), s : s + 1] - col * count
            field = None
            for q, block in zip(met, blocks):
                mask = jnp.where(near == q, 1.0, 0.0).astype(block.dtype)
                part = block[...] * mask
                field = part if field is None else field + part
            weights.append(jnp.concatenate([d_ref[kind, p, s] for kind in range(kinds)], axis=0))
            fields.append(field)
        total = jnp.dot(
            jnp.concatenate(weights, axis=1),
            jnp.concatenate(fields, axis=0),
            preferred_element_type=jnp.float32,
        )
        for kind in range(kinds):
            piece = total[kind * size : (kind + 1) * size]
            if before:
                piece += sums_ref[p, kind]
            out_ref[*places[place], kind] = piece.astype(out_ref.dtype)


def inverse(value):
    rough = pl.reciprocal(value, approx=True)
    return rough * (2.0 - value * rough)


def rough_inverse(value):
    return pl.reciprocal(value, approx=True)


def scaled_sinh_cosh(value, scale):
    grown = jnp.exp(value)
    half = 0.5 * scale
    up, down = half * grown, half * inverse(grown)
    square = value * value
    small = scale * value * (1.0 + square * (1 / 6 + square * (1 / 120)))
    return jnp.where(square < 0.25, small, up - down), up + down


def friction(shear, normal, weight, unweight, tau_load, sigma_base, a_wide):
    tau = tau_load + shear
    size = jnp.abs(tau)
    stiff = jnp.maximum(sigma_base + normal, sigma_floor) * a_wide
    double = 2.0 * damping * weight
    drive = size * unweight * (0.5 / damping)
    square = drive * drive + 1.0
    slope = jnp.minimum(size * rough_inverse(stiff), jnp.log(drive + square * lax.rsqrt(square)))
    for newton_step in range(NEWTON):
        sinh, cosh = scaled_sinh_cosh(slope, double)
        slope = slope - (stiff * slope + sinh - size) * rough_inverse(stiff + cosh)
    rate = scaled_sinh_cosh(slope, double)[0] * (1.0 / damping)
    return jnp.where(tau < 0.0, -rate, rate)


def state_change(rate, decay, b_wide):
    return b_wide * (decay - jnp.abs(rate))


def over_pieces(begin, tall, members, lanes, work):
    step = min(tall, 64)
    for at in range(begin, begin + tall, step):
        for first in range(0, members, lanes):
            work(pl.ds(at, step), slice(first, first + lanes))


def section_one_kernel(own, other, weight, unweight, tau, coef, rate, rate_half):
    size, members = tau.shape

    def work(rows, part):
        first = friction(
            own[0, rows, part] + other[0, rows, part].astype(jnp.float32),
            own[1, rows, part] + other[1, rows, part].astype(jnp.float32),
            weight[rows, part],
            unweight[rows, part],
            tau[rows, part],
            coef[0, rows, :],
            coef[1, rows, :],
        )
        rate[rows, part] = first
        rate_half[rows, part] = first.astype(rate_half.dtype)

    over_pieces(0, size, members, coef.shape[2], work)


def section_two_kernel(
    own, other, weight, unweight, decay, tau, coef, stress, normal, rate, change, rate_out, change_out, mean_rate, mean_change, sem
):
    size, members = tau.shape

    def work(rows, part):
        shear = own[0, rows, part] + other[0, rows, part].astype(jnp.float32)
        press = own[1, rows, part] + other[1, rows, part].astype(jnp.float32)
        later = friction(
            stress[rows, part] + section_step * shear,
            normal[rows, part] + section_step * press,
            weight[rows, part],
            unweight[rows, part],
            tau[rows, part],
            coef[0, rows, :],
            coef[1, rows, :],
        )
        second = state_change(later, decay[rows, part], coef[2, rows, :])
        mean_rate[rows, part] = (rate[rows, part] + later) * 0.5
        mean_change[rows, part] = (change[rows, part] + second) * 0.5

    copies = []
    for at, part in enumerate(row_pieces(size, OUT_PIECES)):
        over_pieces(part.start, part.size, members, coef.shape[2], work)
        for kind, (held, out) in enumerate(((mean_rate, rate_out), (mean_change, change_out))):
            copies.append(pltpu.make_async_copy(held.at[part], out.at[part], sem.at[kind, at]))
            copies[-1].start()
    for copy in copies:
        copy.wait()


def on_core(kernel, outs, arrays, scratch=(), flops=0, room=16, far=(), out_far=False):
    vmem, hbm = pl.BlockSpec(memory_space=pltpu.VMEM), pl.BlockSpec(memory_space=pl.ANY)
    arrays = (*(pltpu.with_memory_space_constraint(a, pltpu.HBM) for a in far), *arrays)
    return pl.pallas_call(
        kernel,
        out_shape=outs,
        in_specs=[hbm] * len(far) + [vmem] * (len(arrays) - len(far)),
        out_specs=jax.tree.map(lambda _: hbm if out_far else vmem, outs),
        scratch_shapes=list(scratch),
        compiler_params=pltpu.CompilerParams(vmem_limit_bytes=room * 1024 * 1024),
        cost_estimate=pl.CostEstimate(
            flops=flops, bytes_accessed=sum(a.size * a.dtype.itemsize for a in arrays), transcendentals=0
        ),
    )(*arrays)


def body(
    slip_deficit,
    state_var,
    tau_load,
    sigma_base,
    a_coef,
    b_coef,
    v_basis,
    u_basis,
    dense_blocks,
    block_ranks,
    near_index,
):
    count = lax.axis_size("row")
    size, members = slip_deficit.shape
    kinds, rows, _, rank_count, _ = u_basis.shape
    direct = count in DIRECT_COUNTS
    spots = arrivals(count, direct)
    early = max(count - LATE, 0)
    room = 16 if direct else 40
    lanes = min(members, 128)
    narrow, wide = jnp.bfloat16, jnp.float32
    swap = [(0, 1), (1, 0)]

    def shaped(*shape, kind=wide):
        return jax.ShapeDtypeStruct(shape, kind)

    full = shaped(size, members)
    v_met, u_met, coef, *powers = on_core(
        functools.partial(prepare_kernel, spots, direct),
        (
            shaped(count, rows, rank_count, size, kind=narrow),
            shaped(rows, kinds * size, count * rank_count, kind=narrow),
            shaped(5, size, lanes),
            full,
            full,
            full,
        ),
        (),
        (
            pltpu.SMEM(block_ranks.shape, jnp.int32),
            pltpu.VMEM(v_basis.shape, narrow),
            pltpu.VMEM(u_basis.shape, narrow),
            *[pltpu.VMEM((1, size), wide)] * 3,
            pltpu.VMEM((size, members), wide),
            pltpu.SemaphoreType.DMA((7,)),
        ),
        room=room,
        far=(
            block_ranks,
            v_basis,
            u_basis,
            sigma_base.reshape(1, size),
            a_coef.reshape(1, size),
            b_coef.reshape(1, size),
            state_var,
        ),
    )

    def add(blocks, first, pick, before, kind):
        held = rows if pick is None else 1
        lead = (rows, kinds) if pick is None else (kinds,)
        return on_core(
            functools.partial(
                sums_kernel, spots[first : first + len(blocks)], direct, first, pick, before is not None
            ),
            shaped(*lead, size, members, kind=kind),
            (near_index, v_met, u_met, dense_blocks, *blocks, *(() if before is None else (before,))),
            (
                pltpu.VMEM((held, len(blocks) * rank_count, members), narrow),
            ),
            2 * held * size * members * rank_count * len(blocks) * 3,
            room,
        )

    def lattice(field_half, beside):
        if direct:
            blocks = gather_direct(field_half, count)
        else:
            whole = lax.all_gather(field_half, "row", axis=0)
            blocks = [whole[r] for r in range(count)]
        blocks[0], beside = lax.optimization_barrier((blocks[0], beside))
        sums = add(blocks[:early], 0, None, None, wide) if early else None
        other = lax.ppermute(add(blocks[early:], early, 1, sums, narrow), "col", swap)
        return add(blocks[early:], early, 0, sums, wide), other, beside

    slip_half = on_core(
        narrow_kernel,
        shaped(size, members, kind=narrow),
        (),
        (pltpu.VMEM((size, members), wide), pltpu.SemaphoreType.DMA((IN_PIECES,))),
        far=(slip_deficit,),
    )
    own, other, powers = lattice(slip_half, powers)
    rate, rate_half = on_core(
        section_one_kernel,
        (full, shaped(size, members, kind=narrow)),
        (own, other, *powers[:2], tau_load, coef),
        flops=200 * size * members,
    )
    beside = on_core(later_kernel, (full,) * 6, (own, other, state_var, powers[2], rate, coef))
    own, other, (stress, normal, change, *powers) = lattice(rate_half, beside)
    return on_core(
        section_two_kernel,
        (full, full),
        (own, other, *powers, tau_load, coef, stress, normal, rate, change),
        (
            pltpu.VMEM((size, members), wide),
            pltpu.VMEM((size, members), wide),
            pltpu.SemaphoreType.DMA((2, OUT_PIECES)),
        ),
        flops=200 * size * members,
        out_far=True,
    )


def solution(mesh):
    placed = (
        P(("row", "col"), "scen"),
        P(("row", "col"), "scen"),
        P(("row", "col"), "scen"),
        P(("row", "col")),
        P(("row", "col")),
        P(("row", "col")),
        P("row", "col", None, None),
        P(None, "row", "col", None, None),
        P(None, "row", "col", None, None),
        P("row", "col"),
        P("row", "col"),
    )
    return jax.shard_map(
        body,
        mesh=mesh,
        in_specs=placed,
        out_specs=(P(("row", "col"), "scen"), P(("row", "col"), "scen")),
        check_vma=False,
    )
```

```python
import functools

import jax
import jax.numpy as jnp
from jax import lax
from jax.experimental import pallas as pl
from jax.experimental.pallas import tpu as pltpu
from jax.sharding import PartitionSpec as P

NEWTON = 2
DIRECT_COUNTS = (4, 8)
LATE = 4

damping = 0.5
sigma_floor = 0.5
section_step = 0.1


def arrivals(count, direct):
    if not direct:
        return list(range(count))
    return [0, 4, 2, 1, 3, 6, 5, 7] if count == 8 else [0, 1, 2, 3]


def row_met(spot, row, direct):
    return jnp.bitwise_xor(row, spot) if direct else spot


def gather_direct(block, count):
    def swapped(mask, data):
        return lax.ppermute(data, "row", [(row, row ^ mask) for row in range(count)])

    found = {0: block}
    for mask in (4, 1, 2, 3) if count == 8 else (1, 2, 3):
        found[mask] = swapped(mask, block)
    if count == 8:
        for mask in (1, 2, 3):
            found[4 + mask] = swapped(mask, found[4])
    return [found[mask] for mask in arrivals(count, True)]


IN_PIECES = 8
OUT_PIECES = 4


def row_pieces(size, pieces):
    tall = size // pieces
    return [pl.ds(at * tall, tall) for at in range(pieces)]


def narrow_kernel(wide_ref, narrow_ref, held, sem):
    copies = [
        pltpu.make_async_copy(wide_ref.at[part], held.at[part], sem.at[at])
        for at, part in enumerate(row_pieces(held.shape[0], IN_PIECES))
    ]
    for copy in copies:
        copy.start()
    for copy, part in zip(copies, row_pieces(held.shape[0], IN_PIECES)):
        copy.wait()
        narrow_ref[part, :] = held[part, :].astype(narrow_ref.dtype)


def store_powers(outs, part, state, coef):
    outs[0][:, part] = jnp.exp(-state * coef[3])
    outs[1][:, part] = jnp.exp(state * coef[3])
    outs[2][:, part] = jnp.exp(-state * coef[4])


def later_kernel(own, other, state, decay, rate, coef, stress, normal, change, *outs):
    stress[...] = own[0] + other[0].astype(jnp.float32)
    normal[...] = own[1] + other[1].astype(jnp.float32)
    lanes = coef.shape[2]
    for first in range(0, state.shape[1], lanes):
        part = slice(first, first + lanes)
        step = state_change(rate[:, part], decay[:, part], coef[2])
        change[:, part] = step
        store_powers(outs, part, state[:, part] + section_step * step, coef)


def prepare_kernel(spots, direct, *refs):
    far, (v_out, u_out, coef_out, *powers), near, sem = refs[:7], refs[7:13], refs[13:20], refs[20]
    copies = [
        pltpu.make_async_copy(source, held, sem.at[at])
        for at, (source, held) in enumerate(zip(far, near))
    ]
    for copy in copies:
        copy.start()
    for copy in copies:
        copy.wait()
    rank_ref, v_ref, u_ref, sigma_ref, a_ref, b_ref, state_ref = near
    kinds, rows, count, rank_count, size = u_ref.shape
    row = lax.axis_index("row")
    met = [row_met(spot, row, direct) for spot in spots]
    for at, q in enumerate(met):
        for p in range(rows):
            inside = lax.broadcasted_iota(jnp.int32, (rank_count, size), 0) < rank_ref[p, q]
            v_out[at, p] = jnp.where(inside, v_ref[p, q].astype(jnp.float32), 0.0).astype(v_out.dtype)
    for p in range(rows):
        for kind in range(kinds):
            for first in range(0, count, 4):
                group = [u_ref[kind, p, q] for q in met[first : first + 4]]
                turned = jnp.concatenate(group, axis=0).astype(jnp.float32).T
                u_out[p, kind * size : (kind + 1) * size, first * rank_count : (first + len(group)) * rank_count] = (
                    turned.astype(u_out.dtype)
                )
    lanes = coef_out.shape[2]
    for at, values in enumerate((sigma_ref[...], a_ref[...], b_ref[...], 1.0 / a_ref[...], 1.0 / b_ref[...])):
        coef_out[at] = jnp.broadcast_to(values, (lanes, size)).T
    for first in range(0, state_ref.shape[1], lanes):
        part = slice(first, first + lanes)
        store_powers(powers, part, state_ref[:, part], coef_out)


def sums_kernel(spots, direct, first, pick, before, near_ref, v_ref, u_ref, d_ref, *refs):
    blocks = refs[: len(spots)]
    refs = refs[len(spots) :]
    if before:
        sums_ref, refs = refs[0], refs[1:]
    out_ref, proj = refs
    count, rows, rank_count, size = v_ref.shape
    kinds, slots = d_ref.shape[0], near_ref.shape[1]
    row, col = lax.axis_index("row"), lax.axis_index("col")
    met = [row_met(spot, row, direct) for spot in spots]
    chosen = list(range(rows)) if pick is None else [col if pick == 0 else 1 - col]
    places = [(place,) for place in range(rows)] if pick is None else [()]
    for at, block in enumerate(blocks):
        if pick is None:
            weights = v_ref[first + at].reshape(rows * rank_count, size)
        else:
            weights = v_ref[first + at, chosen[0]]
        part = jnp.dot(weights, block[...], preferred_element_type=jnp.float32).astype(proj.dtype)
        for place in range(len(chosen)):
            proj[place, at * rank_count : (at + 1) * rank_count, :] = part[
                place * rank_count : (place + 1) * rank_count
            ]
    lanes = slice(first * rank_count, (first + len(blocks)) * rank_count)
    for place, p in enumerate(chosen):
        weights, fields = [u_ref[p, :, lanes]], [proj[place]]
        for s in range(slots):
            near = near_ref[pl.ds(p, 1), s : s + 1] - col * count
            field = None
            for q, block in zip(met, blocks):
                mask = jnp.where(near == q, 1.0, 0.0).astype(block.dtype)
                part = block[...] * mask
                field = part if field is None else field + part
            weights.append(jnp.concatenate([d_ref[kind, p, s] for kind in range(kinds)], axis=0))
            fields.append(field)
        total = jnp.dot(
            jnp.concatenate(weights, axis=1),
            jnp.concatenate(fields, axis=0),
            preferred_element_type=jnp.float32,
        )
        for kind in range(kinds):
            piece = total[kind * size : (kind + 1) * size]
            if before:
                piece += sums_ref[p, kind]
            out_ref[*places[place], kind] = piece.astype(out_ref.dtype)


def inverse(value):
    rough = pl.reciprocal(value, approx=True)
    return rough * (2.0 - value * rough)


def rough_inverse(value):
    return pl.reciprocal(value, approx=True)


def scaled_sinh_cosh(value, scale):
    grown = jnp.exp(value)
    half = 0.5 * scale
    up, down = half * grown, half * inverse(grown)
    square = value * value
    small = scale * value * (1.0 + square * (1 / 6 + square * (1 / 120)))
    return jnp.where(square < 0.25, small, up - down), up + down


def friction(shear, normal, weight, unweight, tau_load, sigma_base, a_wide):
    tau = tau_load + shear
    size = jnp.abs(tau)
    stiff = jnp.maximum(sigma_base + normal, sigma_floor) * a_wide
    double = 2.0 * damping * weight
    drive = size * unweight * (0.5 / damping)
    square = drive * drive + 1.0
    slope = jnp.minimum(size * rough_inverse(stiff), jnp.log(drive + square * lax.rsqrt(square)))
    for newton_step in range(NEWTON):
        sinh, cosh = scaled_sinh_cosh(slope, double)
        slope = slope - (stiff * slope + sinh - size) * rough_inverse(stiff + cosh)
    rate = scaled_sinh_cosh(slope, double)[0] * (1.0 / damping)
    return jnp.where(tau < 0.0, -rate, rate)


def state_change(rate, decay, b_wide):
    return b_wide * (decay - jnp.abs(rate))


def over_pieces(begin, tall, members, lanes, work):
    step = min(tall, 64)
    for at in range(begin, begin + tall, step):
        for first in range(0, members, lanes):
            work(pl.ds(at, step), slice(first, first + lanes))


def section_one_kernel(own, other, weight, unweight, tau, coef, rate, rate_half):
    size, members = tau.shape

    def work(rows, part):
        first = friction(
            own[0, rows, part] + other[0, rows, part].astype(jnp.float32),
            own[1, rows, part] + other[1, rows, part].astype(jnp.float32),
            weight[rows, part],
            unweight[rows, part],
            tau[rows, part],
            coef[0, rows, :],
            coef[1, rows, :],
        )
        rate[rows, part] = first
        rate_half[rows, part] = first.astype(rate_half.dtype)

    over_pieces(0, size, members, coef.shape[2], work)


def section_two_kernel(
    own, other, weight, unweight, decay, tau, coef, stress, normal, rate, change, rate_out, change_out, mean_rate, mean_change, sem
):
    size, members = tau.shape

    def work(rows, part):
        shear = own[0, rows, part] + other[0, rows, part].astype(jnp.float32)
        press = own[1, rows, part] + other[1, rows, part].astype(jnp.float32)
        later = friction(
            stress[rows, part] + section_step * shear,
            normal[rows, part] + section_step * press,
            weight[rows, part],
            unweight[rows, part],
            tau[rows, part],
            coef[0, rows, :],
            coef[1, rows, :],
        )
        second = state_change(later, decay[rows, part], coef[2, rows, :])
        mean_rate[rows, part] = (rate[rows, part] + later) * 0.5
        mean_change[rows, part] = (change[rows, part] + second) * 0.5

    copies = []
    for at, part in enumerate(row_pieces(size, OUT_PIECES)):
        over_pieces(part.start, part.size, members, coef.shape[2], work)
        for kind, (held, out) in enumerate(((mean_rate, rate_out), (mean_change, change_out))):
            copies.append(pltpu.make_async_copy(held.at[part], out.at[part], sem.at[kind, at]))
            copies[-1].start()
    for copy in copies:
        copy.wait()


def on_core(kernel, outs, arrays, scratch=(), flops=0, room=16, far=(), out_far=False):
    vmem, hbm = pl.BlockSpec(memory_space=pltpu.VMEM), pl.BlockSpec(memory_space=pl.ANY)
    arrays = (*(pltpu.with_memory_space_constraint(a, pltpu.HBM) for a in far), *arrays)
    return pl.pallas_call(
        kernel,
        out_shape=outs,
        in_specs=[hbm] * len(far) + [vmem] * (len(arrays) - len(far)),
        out_specs=jax.tree.map(lambda _: hbm if out_far else vmem, outs),
        scratch_shapes=list(scratch),
        compiler_params=pltpu.CompilerParams(vmem_limit_bytes=room * 1024 * 1024),
        cost_estimate=pl.CostEstimate(
            flops=flops, bytes_accessed=sum(a.size * a.dtype.itemsize for a in arrays), transcendentals=0
        ),
    )(*arrays)


def body(
    slip_deficit,
    state_var,
    tau_load,
    sigma_base,
    a_coef,
    b_coef,
    v_basis,
    u_basis,
    dense_blocks,
    block_ranks,
    near_index,
):
    count = lax.axis_size("row")
    size, members = slip_deficit.shape
    kinds, rows, _, rank_count, _ = u_basis.shape
    direct = count in DIRECT_COUNTS
    spots = arrivals(count, direct)
    early = max(count - LATE, 0)
    room = 16 if direct else 40
    lanes = min(members, 128)
    narrow, wide = jnp.bfloat16, jnp.float32
    swap = [(0, 1), (1, 0)]

    def shaped(*shape, kind=wide):
        return jax.ShapeDtypeStruct(shape, kind)

    full = shaped(size, members)
    v_met, u_met, coef, *powers = on_core(
        functools.partial(prepare_kernel, spots, direct),
        (
            shaped(count, rows, rank_count, size, kind=narrow),
            shaped(rows, kinds * size, count * rank_count, kind=narrow),
            shaped(5, size, lanes),
            full,
            full,
            full,
        ),
        (),
        (
            pltpu.SMEM(block_ranks.shape, jnp.int32),
            pltpu.VMEM(v_basis.shape, narrow),
            pltpu.VMEM(u_basis.shape, narrow),
            *[pltpu.VMEM((1, size), wide)] * 3,
            pltpu.VMEM((size, members), wide),
            pltpu.SemaphoreType.DMA((7,)),
        ),
        room=room,
        far=(
            block_ranks,
            v_basis,
            u_basis,
            sigma_base.reshape(1, size),
            a_coef.reshape(1, size),
            b_coef.reshape(1, size),
            state_var,
        ),
    )

    def add(blocks, first, pick, before, kind):
        held = rows if pick is None else 1
        lead = (rows, kinds) if pick is None else (kinds,)
        return on_core(
            functools.partial(
                sums_kernel, spots[first : first + len(blocks)], direct, first, pick, before is not None
            ),
            shaped(*lead, size, members, kind=kind),
            (near_index, v_met, u_met, dense_blocks, *blocks, *(() if before is None else (before,))),
            (
                pltpu.VMEM((held, len(blocks) * rank_count, members), narrow),
            ),
            2 * held * size * members * rank_count * len(blocks) * 3,
            room,
        )

    def lattice(field_half, beside):
        if direct:
            blocks = gather_direct(field_half, count)
        else:
            whole = lax.all_gather(field_half, "row", axis=0)
            blocks = [whole[r] for r in range(count)]
        blocks[0], beside = lax.optimization_barrier((blocks[0], beside))
        sums = add(blocks[:early], 0, None, None, wide) if early else None
        other = lax.ppermute(add(blocks[early:], early, 1, sums, narrow), "col", swap)
        return add(blocks[early:], early, 0, sums, wide), other, beside

    slip_half = on_core(
        narrow_kernel,
        shaped(size, members, kind=narrow),
        (),
        (pltpu.VMEM((size, members), wide), pltpu.SemaphoreType.DMA((IN_PIECES,))),
        far=(slip_deficit,),
    )
    own, other, powers = lattice(slip_half, powers)
    rate, rate_half = on_core(
        section_one_kernel,
        (full, shaped(size, members, kind=narrow)),
        (own, other, *powers[:2], tau_load, coef),
        flops=200 * size * members,
    )
    beside = on_core(later_kernel, (full,) * 6, (own, other, state_var, powers[2], rate, coef))
    own, other, (stress, normal, change, *powers) = lattice(rate_half, beside)
    return on_core(
        section_two_kernel,
        (full, full),
        (own, other, *powers, tau_load, coef, stress, normal, rate, change),
        (
            pltpu.VMEM((size, members), wide),
            pltpu.VMEM((size, members), wide),
            pltpu.SemaphoreType.DMA((2, OUT_PIECES)),
        ),
        flops=200 * size * members,
        out_far=True,
    )


def solution(mesh):
    placed = (
        P(("row", "col"), "scen"),
        P(("row", "col"), "scen"),
        P(("row", "col"), "scen"),
        P(("row", "col")),
        P(("row", "col")),
        P(("row", "col")),
        P("row", "col", None, None),
        P(None, "row", "col", None, None),
        P(None, "row", "col", None, None),
        P("row", "col"),
        P("row", "col"),
    )
    return jax.shard_map(
        body,
        mesh=mesh,
        in_specs=placed,
        out_specs=(P(("row", "col"), "scen"), P(("row", "col"), "scen")),
        check_vma=False,
    )
```

```python
import functools

import jax
import jax.numpy as jnp
from jax import lax
from jax.experimental import pallas as pl
from jax.experimental.pallas import tpu as pltpu
from jax.sharding import PartitionSpec as P

NEWTON = 2
DIRECT_COUNTS = (4, 8)
TILE = 128

damping = 0.5
sigma_floor = 0.5
section_step = 0.1


def arrivals(count, direct):
    if not direct:
        cuts = [0, max(count - 4, 0), count]
        return [list(range(first, last)) for first, last in zip(cuts, cuts[1:]) if last > first]
    return [[0, 1, 4, 3, 2], [6, 5, 7]] if count == 8 else [[0, 1], [2, 3]]


def row_met(spot, row, direct):
    return jnp.bitwise_xor(row, spot) if direct else spot


def gather_direct(block, count):
    def swapped(mask, data):
        return lax.ppermute(data, "row", [(row, row ^ mask) for row in range(count)])

    found = {0: block}
    for mask in (4, 1, 2, 3) if count == 8 else (1, 2, 3):
        found[mask] = swapped(mask, block)
    if count == 8:
        for mask in (1, 2, 3):
            found[4 + mask] = swapped(mask, found[4])
    return [[found[mask] for mask in group] for group in arrivals(count, True)]


IN_PIECES = 8
OUT_PIECES = 4


def row_pieces(size, pieces):
    tall = size // pieces
    return [pl.ds(at * tall, tall) for at in range(pieces)]


def narrow_kernel(wide_ref, narrow_ref, held, sem):
    copies = [
        pltpu.make_async_copy(wide_ref.at[part], held.at[part], sem.at[at])
        for at, part in enumerate(row_pieces(held.shape[0], IN_PIECES))
    ]
    for copy in copies:
        copy.start()
    for copy, part in zip(copies, row_pieces(held.shape[0], IN_PIECES)):
        copy.wait()
        narrow_ref[part, :] = held[part, :].astype(narrow_ref.dtype)


def store_powers(outs, part, state, coef):
    outs[0][:, part] = jnp.exp(-state * coef[3])
    outs[1][:, part] = jnp.exp(state * coef[3])
    outs[2][:, part] = jnp.exp(-state * coef[4])


def later_kernel(own, other, state, decay, rate, coef, stress, normal, change, *outs):
    stress[...] = own[0] + other[0].astype(jnp.float32)
    normal[...] = own[1] + other[1].astype(jnp.float32)
    lanes = coef.shape[2]
    for first in range(0, state.shape[1], lanes):
        part = slice(first, first + lanes)
        step = state_change(rate[:, part], decay[:, part], coef[2])
        change[:, part] = step
        store_powers(outs, part, state[:, part] + section_step * step, coef)


def prepare_kernel(groups, direct, *refs):
    far, (v_out, u_out, coef_out, *powers), near, sem = refs[:7], refs[7:13], refs[13:20], refs[20]
    copies = [
        pltpu.make_async_copy(source, held, sem.at[at])
        for at, (source, held) in enumerate(zip(far, near))
    ]
    for copy in copies:
        copy.start()
    for copy in copies:
        copy.wait()
    rank_ref, v_ref, u_ref, sigma_ref, a_ref, b_ref, state_ref = near
    kinds, rows, count, rank_count, size = u_ref.shape
    row = lax.axis_index("row")
    met = [row_met(spot, row, direct) for group in groups for spot in group]
    for at, q in enumerate(met):
        for p in range(rows):
            inside = lax.broadcasted_iota(jnp.int32, (rank_count, size), 0) < rank_ref[p, q]
            v_out[at, p] = jnp.where(inside, v_ref[p, q].astype(jnp.float32), 0.0).astype(v_out.dtype)
    for p in range(rows):
        for kind in range(kinds):
            first = start = 0
            for spots in groups:
                group = [u_ref[kind, p, q] for q in met[first : first + len(spots)]]
                spare = -len(group) * rank_count % TILE
                if spare:
                    group.append(jnp.zeros((spare, size), u_ref.dtype))
                turned = jnp.concatenate(group, axis=0).astype(jnp.float32).T
                stop = start + turned.shape[1]
                u_out[p, kind * size : (kind + 1) * size, start:stop] = turned.astype(u_out.dtype)
                first, start = first + len(spots), stop
    lanes = coef_out.shape[2]
    for at, values in enumerate((sigma_ref[...], a_ref[...], b_ref[...], 1.0 / a_ref[...], 1.0 / b_ref[...])):
        coef_out[at] = jnp.broadcast_to(values, (lanes, size)).T
    for first in range(0, state_ref.shape[1], lanes):
        part = slice(first, first + lanes)
        store_powers(powers, part, state_ref[:, part], coef_out)


def sums_kernel(spots, direct, first, start, pick, before, near_ref, v_ref, u_ref, d_ref, *refs):
    blocks = refs[: len(spots)]
    refs = refs[len(spots) :]
    if before:
        sums_ref, refs = refs[0], refs[1:]
    out_ref, proj = refs
    count, rows, rank_count, size = v_ref.shape
    kinds, slots = d_ref.shape[0], near_ref.shape[1]
    row, col = lax.axis_index("row"), lax.axis_index("col")
    met = [row_met(spot, row, direct) for spot in spots]
    chosen = list(range(rows)) if pick is None else [col if pick == 0 else 1 - col]
    places = [(place,) for place in range(rows)] if pick is None else [()]
    for at, block in enumerate(blocks):
        if pick is None:
            weights = v_ref[first + at].reshape(rows * rank_count, size)
        else:
            weights = v_ref[first + at, chosen[0]]
        part = jnp.dot(weights, block[...], preferred_element_type=jnp.float32).astype(proj.dtype)
        for place in range(len(chosen)):
            proj[place, at * rank_count : (at + 1) * rank_count, :] = part[
                place * rank_count : (place + 1) * rank_count
            ]
    width = proj.shape[1]
    lanes = slice(start, start + width)
    if width > len(blocks) * rank_count:
        for place in range(len(chosen)):
            proj[place, len(blocks) * rank_count :, :] = jnp.zeros(
                (width - len(blocks) * rank_count, proj.shape[2]), proj.dtype
            )
    for place, p in enumerate(chosen):
        weights, fields = [u_ref[p, :, lanes]], [proj[place]]
        for s in range(slots):
            near = near_ref[pl.ds(p, 1), s : s + 1] - col * count
            field = None
            for q, block in zip(met, blocks):
                mask = jnp.where(near == q, 1.0, 0.0).astype(block.dtype)
                part = block[...] * mask
                field = part if field is None else field + part
            weights.append(jnp.concatenate([d_ref[kind, p, s] for kind in range(kinds)], axis=0))
            fields.append(field)
        total = jnp.dot(
            jnp.concatenate(weights, axis=1),
            jnp.concatenate(fields, axis=0),
            preferred_element_type=jnp.float32,
        )
        for kind in range(kinds):
            piece = total[kind * size : (kind + 1) * size]
            if before:
                piece += sums_ref[p, kind]
            out_ref[*places[place], kind] = piece.astype(out_ref.dtype)


def inverse(value):
    rough = pl.reciprocal(value, approx=True)
    return rough * (2.0 - value * rough)


def rough_inverse(value):
    return pl.reciprocal(value, approx=True)


def scaled_sinh_cosh(value, scale):
    grown = jnp.exp(value)
    half = 0.5 * scale
    up, down = half * grown, half * inverse(grown)
    square = value * value
    small = scale * value * (1.0 + square * (1 / 6 + square * (1 / 120)))
    return jnp.where(square < 0.25, small, up - down), up + down


def friction(shear, normal, weight, unweight, tau_load, sigma_base, a_wide):
    tau = tau_load + shear
    size = jnp.abs(tau)
    stiff = jnp.maximum(sigma_base + normal, sigma_floor) * a_wide
    double = 2.0 * damping * weight
    drive = size * unweight * (0.5 / damping)
    square = drive * drive + 1.0
    slope = jnp.minimum(size * rough_inverse(stiff), jnp.log(drive + square * lax.rsqrt(square)))
    for newton_step in range(NEWTON):
        sinh, cosh = scaled_sinh_cosh(slope, double)
        slope = slope - (stiff * slope + sinh - size) * rough_inverse(stiff + cosh)
    rate = scaled_sinh_cosh(slope, double)[0] * (1.0 / damping)
    return jnp.where(tau < 0.0, -rate, rate)


def state_change(rate, decay, b_wide):
    return b_wide * (decay - jnp.abs(rate))


def over_pieces(begin, tall, members, lanes, work):
    step = min(tall, 64)
    for at in range(begin, begin + tall, step):
        for first in range(0, members, lanes):
            work(pl.ds(at, step), slice(first, first + lanes))


def section_one_kernel(own, other, weight, unweight, tau, coef, rate, rate_half):
    size, members = tau.shape

    def work(rows, part):
        first = friction(
            own[0, rows, part] + other[0, rows, part].astype(jnp.float32),
            own[1, rows, part] + other[1, rows, part].astype(jnp.float32),
            weight[rows, part],
            unweight[rows, part],
            tau[rows, part],
            coef[0, rows, :],
            coef[1, rows, :],
        )
        rate[rows, part] = first
        rate_half[rows, part] = first.astype(rate_half.dtype)

    over_pieces(0, size, members, coef.shape[2], work)


def section_two_kernel(
    own, other, weight, unweight, decay, tau, coef, stress, normal, rate, change, rate_out, change_out, mean_rate, mean_change, sem
):
    size, members = tau.shape

    def work(rows, part):
        shear = own[0, rows, part] + other[0, rows, part].astype(jnp.float32)
        press = own[1, rows, part] + other[1, rows, part].astype(jnp.float32)
        later = friction(
            stress[rows, part] + section_step * shear,
            normal[rows, part] + section_step * press,
            weight[rows, part],
            unweight[rows, part],
            tau[rows, part],
            coef[0, rows, :],
            coef[1, rows, :],
        )
        second = state_change(later, decay[rows, part], coef[2, rows, :])
        mean_rate[rows, part] = (rate[rows, part] + later) * 0.5
        mean_change[rows, part] = (change[rows, part] + second) * 0.5

    copies = []
    for at, part in enumerate(row_pieces(size, OUT_PIECES)):
        over_pieces(part.start, part.size, members, coef.shape[2], work)
        for kind, (held, out) in enumerate(((mean_rate, rate_out), (mean_change, change_out))):
            copies.append(pltpu.make_async_copy(held.at[part], out.at[part], sem.at[kind, at]))
            copies[-1].start()
    for copy in copies:
        copy.wait()


def on_core(kernel, outs, arrays, scratch=(), flops=0, room=16, far=(), out_far=False):
    vmem, hbm = pl.BlockSpec(memory_space=pltpu.VMEM), pl.BlockSpec(memory_space=pl.ANY)
    arrays = (*(pltpu.with_memory_space_constraint(a, pltpu.HBM) for a in far), *arrays)
    return pl.pallas_call(
        kernel,
        out_shape=outs,
        in_specs=[hbm] * len(far) + [vmem] * (len(arrays) - len(far)),
        out_specs=jax.tree.map(lambda _: hbm if out_far else vmem, outs),
        scratch_shapes=list(scratch),
        compiler_params=pltpu.CompilerParams(vmem_limit_bytes=room * 1024 * 1024),
        cost_estimate=pl.CostEstimate(
            flops=flops, bytes_accessed=sum(a.size * a.dtype.itemsize for a in arrays), transcendentals=0
        ),
    )(*arrays)


def body(
    slip_deficit,
    state_var,
    tau_load,
    sigma_base,
    a_coef,
    b_coef,
    v_basis,
    u_basis,
    dense_blocks,
    block_ranks,
    near_index,
):
    count = lax.axis_size("row")
    size, members = slip_deficit.shape
    kinds, rows, _, rank_count, _ = u_basis.shape
    direct = count in DIRECT_COUNTS
    groups = arrivals(count, direct)
    firsts = [sum(len(group) for group in groups[:at]) for at in range(len(groups))]
    tiles = [-(-len(group) * rank_count // TILE) * TILE for group in groups]
    starts = [sum(tiles[:at]) for at in range(len(groups))]
    room = 16 if direct else 40
    lanes = min(members, 128)
    narrow, wide = jnp.bfloat16, jnp.float32
    swap = [(0, 1), (1, 0)]

    def shaped(*shape, kind=wide):
        return jax.ShapeDtypeStruct(shape, kind)

    full = shaped(size, members)
    v_met, u_met, coef, *powers = on_core(
        functools.partial(prepare_kernel, groups, direct),
        (
            shaped(count, rows, rank_count, size, kind=narrow),
            shaped(rows, kinds * size, sum(tiles), kind=narrow),
            shaped(5, size, lanes),
            full,
            full,
            full,
        ),
        (),
        (
            pltpu.SMEM(block_ranks.shape, jnp.int32),
            pltpu.VMEM(v_basis.shape, narrow),
            pltpu.VMEM(u_basis.shape, narrow),
            *[pltpu.VMEM((1, size), wide)] * 3,
            pltpu.VMEM((size, members), wide),
            pltpu.SemaphoreType.DMA((7,)),
        ),
        room=room,
        far=(
            block_ranks,
            v_basis,
            u_basis,
            sigma_base.reshape(1, size),
            a_coef.reshape(1, size),
            b_coef.reshape(1, size),
            state_var,
        ),
    )

    def add(blocks, at, pick, before, kind):
        held = rows if pick is None else 1
        lead = (rows, kinds) if pick is None else (kinds,)
        return on_core(
            functools.partial(
                sums_kernel, groups[at], direct, firsts[at], starts[at], pick, before is not None
            ),
            shaped(*lead, size, members, kind=kind),
            (near_index, v_met, u_met, dense_blocks, *blocks, *(() if before is None else (before,))),
            (
                pltpu.VMEM((held, tiles[at], members), narrow),
            ),
            2 * held * size * members * rank_count * len(blocks) * 3,
            room,
        )

    def lattice(field_half, beside):
        if direct:
            found = gather_direct(field_half, count)
        else:
            whole = lax.all_gather(field_half, "row", axis=0)
            found = [[whole[r] for r in group] for group in groups]
        found[0][0], beside = lax.optimization_barrier((found[0][0], beside))
        sums, end = None, len(groups) - 1
        for at in range(end):
            sums = add(found[at], at, None, sums, wide)
        other = lax.ppermute(add(found[end], end, 1, sums, narrow), "col", swap)
        return add(found[end], end, 0, sums, wide), other, beside

    slip_half = on_core(
        narrow_kernel,
        shaped(size, members, kind=narrow),
        (),
        (pltpu.VMEM((size, members), wide), pltpu.SemaphoreType.DMA((IN_PIECES,))),
        far=(slip_deficit,),
    )
    own, other, powers = lattice(slip_half, powers)
    rate, rate_half = on_core(
        section_one_kernel,
        (full, shaped(size, members, kind=narrow)),
        (own, other, *powers[:2], tau_load, coef),
        flops=200 * size * members,
    )
    beside = on_core(later_kernel, (full,) * 6, (own, other, state_var, powers[2], rate, coef))
    own, other, (stress, normal, change, *powers) = lattice(rate_half, beside)
    return on_core(
        section_two_kernel,
        (full, full),
        (own, other, *powers, tau_load, coef, stress, normal, rate, change),
        (
            pltpu.VMEM((size, members), wide),
            pltpu.VMEM((size, members), wide),
            pltpu.SemaphoreType.DMA((2, OUT_PIECES)),
        ),
        flops=200 * size * members,
        out_far=True,
    )


def solution(mesh):
    placed = (
        P(("row", "col"), "scen"),
        P(("row", "col"), "scen"),
        P(("row", "col"), "scen"),
        P(("row", "col")),
        P(("row", "col")),
        P(("row", "col")),
        P("row", "col", None, None),
        P(None, "row", "col", None, None),
        P(None, "row", "col", None, None),
        P("row", "col"),
        P("row", "col"),
    )
    return jax.shard_map(
        body,
        mesh=mesh,
        in_specs=placed,
        out_specs=(P(("row", "col"), "scen"), P(("row", "col"), "scen")),
        check_vma=False,
    )
```

```python
import functools

import jax
import jax.numpy as jnp
from jax import lax
from jax.experimental import pallas as pl
from jax.experimental.pallas import tpu as pltpu
from jax.sharding import PartitionSpec as P

NEWTON = 2
DIRECT_COUNTS = (4, 8)
TILE = 128

damping = 0.5
sigma_floor = 0.5
section_step = 0.1


def arrivals(count, direct):
    if not direct:
        cuts = [0, max(count - 4, 0), count]
        return [list(range(first, last)) for first, last in zip(cuts, cuts[1:]) if last > first]
    return [[0, 1, 4, 2, 3], [6, 5, 7]] if count == 8 else [[0, 1], [2, 3]]


def row_met(spot, row, direct):
    return jnp.bitwise_xor(row, spot) if direct else spot


def gather_direct(block, count):
    def swapped(mask, data):
        return lax.ppermute(data, "row", [(row, row ^ mask) for row in range(count)])

    found = {0: block}
    for mask in (4, 1, 2, 3) if count == 8 else (1, 2, 3):
        found[mask] = swapped(mask, block)
    if count == 8:
        for mask in (1, 2, 3):
            found[4 + mask] = swapped(mask, found[4])
    return [[found[mask] for mask in group] for group in arrivals(count, True)]


IN_PIECES = 8
OUT_PIECES = 4


def row_pieces(size, pieces):
    tall = size // pieces
    return [pl.ds(at * tall, tall) for at in range(pieces)]


def narrow_kernel(wide_ref, narrow_ref, held, sem):
    copies = [
        pltpu.make_async_copy(wide_ref.at[part], held.at[part], sem.at[at])
        for at, part in enumerate(row_pieces(held.shape[0], IN_PIECES))
    ]
    for copy in copies:
        copy.start()
    for copy, part in zip(copies, row_pieces(held.shape[0], IN_PIECES)):
        copy.wait()
        narrow_ref[part, :] = held[part, :].astype(narrow_ref.dtype)


def store_powers(outs, part, state, coef):
    outs[0][:, part] = jnp.exp(-state * coef[3])
    outs[1][:, part] = jnp.exp(state * coef[3])
    outs[2][:, part] = jnp.exp(-state * coef[4])


def later_kernel(own, other, state, decay, rate, coef, stress, normal, change, *outs):
    stress[...] = own[0] + other[0].astype(jnp.float32)
    normal[...] = own[1] + other[1].astype(jnp.float32)
    lanes = coef.shape[2]
    for first in range(0, state.shape[1], lanes):
        part = slice(first, first + lanes)
        step = state_change(rate[:, part], decay[:, part], coef[2])
        change[:, part] = step
        store_powers(outs, part, state[:, part] + section_step * step, coef)


def prepare_kernel(groups, direct, *refs):
    far, (v_out, u_out, coef_out, *powers), near, sem = refs[:7], refs[7:13], refs[13:20], refs[20]
    copies = [
        pltpu.make_async_copy(source, held, sem.at[at])
        for at, (source, held) in enumerate(zip(far, near))
    ]
    for copy in copies:
        copy.start()
    for copy in copies:
        copy.wait()
    rank_ref, v_ref, u_ref, sigma_ref, a_ref, b_ref, state_ref = near
    kinds, rows, count, rank_count, size = u_ref.shape
    row = lax.axis_index("row")
    met = [row_met(spot, row, direct) for group in groups for spot in group]
    for at, q in enumerate(met):
        for p in range(rows):
            inside = lax.broadcasted_iota(jnp.int32, (rank_count, size), 0) < rank_ref[p, q]
            v_out[at, p] = jnp.where(inside, v_ref[p, q].astype(jnp.float32), 0.0).astype(v_out.dtype)
    for p in range(rows):
        for kind in range(kinds):
            first = start = 0
            for spots in groups:
                group = [u_ref[kind, p, q] for q in met[first : first + len(spots)]]
                spare = -len(group) * rank_count % TILE
                if spare:
                    group.append(jnp.zeros((spare, size), u_ref.dtype))
                turned = jnp.concatenate(group, axis=0).astype(jnp.float32).T
                stop = start + turned.shape[1]
                u_out[p, kind * size : (kind + 1) * size, start:stop] = turned.astype(u_out.dtype)
                first, start = first + len(spots), stop
    lanes = coef_out.shape[2]
    for at, values in enumerate((sigma_ref[...], a_ref[...], b_ref[...], 1.0 / a_ref[...], 1.0 / b_ref[...])):
        coef_out[at] = jnp.broadcast_to(values, (lanes, size)).T
    for first in range(0, state_ref.shape[1], lanes):
        part = slice(first, first + lanes)
        store_powers(powers, part, state_ref[:, part], coef_out)


def sums_kernel(spots, direct, first, start, pick, before, near_ref, v_ref, u_ref, d_ref, *refs):
    blocks = refs[: len(spots)]
    refs = refs[len(spots) :]
    if before:
        sums_ref, refs = refs[0], refs[1:]
    out_ref, proj = refs
    count, rows, rank_count, size = v_ref.shape
    kinds, slots = d_ref.shape[0], near_ref.shape[1]
    row, col = lax.axis_index("row"), lax.axis_index("col")
    met = [row_met(spot, row, direct) for spot in spots]
    chosen = list(range(rows)) if pick is None else [col if pick == 0 else 1 - col]
    places = [(place,) for place in range(rows)] if pick is None else [()]
    for at, block in enumerate(blocks):
        if pick is None:
            weights = v_ref[first + at].reshape(rows * rank_count, size)
        else:
            weights = v_ref[first + at, chosen[0]]
        part = jnp.dot(weights, block[...], preferred_element_type=jnp.float32).astype(proj.dtype)
        for place in range(len(chosen)):
            proj[place, at * rank_count : (at + 1) * rank_count, :] = part[
                place * rank_count : (place + 1) * rank_count
            ]
    width = proj.shape[1]
    lanes = slice(start, start + width)
    if width > len(blocks) * rank_count:
        for place in range(len(chosen)):
            proj[place, len(blocks) * rank_count :, :] = jnp.zeros(
                (width - len(blocks) * rank_count, proj.shape[2]), proj.dtype
            )
    for place, p in enumerate(chosen):
        weights, fields = [u_ref[p, :, lanes]], [proj[place]]
        for s in range(slots):
            near = near_ref[pl.ds(p, 1), s : s + 1] - col * count
            field = None
            for q, block in zip(met, blocks):
                mask = jnp.where(near == q, 1.0, 0.0).astype(block.dtype)
                part = block[...] * mask
                field = part if field is None else field + part
            weights.append(jnp.concatenate([d_ref[kind, p, s] for kind in range(kinds)], axis=0))
            fields.append(field)
        total = jnp.dot(
            jnp.concatenate(weights, axis=1),
            jnp.concatenate(fields, axis=0),
            preferred_element_type=jnp.float32,
        )
        for kind in range(kinds):
            piece = total[kind * size : (kind + 1) * size]
            if before:
                piece += sums_ref[p, kind]
            out_ref[*places[place], kind] = piece.astype(out_ref.dtype)


def inverse(value):
    rough = pl.reciprocal(value, approx=True)
    return rough * (2.0 - value * rough)


def rough_inverse(value):
    return pl.reciprocal(value, approx=True)


def scaled_sinh_cosh(value, scale):
    grown = jnp.exp(value)
    half = 0.5 * scale
    up, down = half * grown, half * inverse(grown)
    square = value * value
    small = scale * value * (1.0 + square * (1 / 6 + square * (1 / 120)))
    return jnp.where(square < 0.25, small, up - down), up + down


def friction(shear, normal, weight, unweight, tau_load, sigma_base, a_wide):
    tau = tau_load + shear
    size = jnp.abs(tau)
    stiff = jnp.maximum(sigma_base + normal, sigma_floor) * a_wide
    double = 2.0 * damping * weight
    drive = size * unweight * (0.5 / damping)
    square = drive * drive + 1.0
    slope = jnp.minimum(size * rough_inverse(stiff), jnp.log(drive + square * lax.rsqrt(square)))
    for newton_step in range(NEWTON):
        sinh, cosh = scaled_sinh_cosh(slope, double)
        slope = slope - (stiff * slope + sinh - size) * rough_inverse(stiff + cosh)
    rate = scaled_sinh_cosh(slope, double)[0] * (1.0 / damping)
    return jnp.where(tau < 0.0, -rate, rate)


def state_change(rate, decay, b_wide):
    return b_wide * (decay - jnp.abs(rate))


def over_pieces(begin, tall, members, lanes, work):
    step = min(tall, 64)
    for at in range(begin, begin + tall, step):
        for first in range(0, members, lanes):
            work(pl.ds(at, step), slice(first, first + lanes))


def section_one_kernel(own, other, weight, unweight, tau, coef, rate, rate_half):
    size, members = tau.shape

    def work(rows, part):
        first = friction(
            own[0, rows, part] + other[0, rows, part].astype(jnp.float32),
            own[1, rows, part] + other[1, rows, part].astype(jnp.float32),
            weight[rows, part],
            unweight[rows, part],
            tau[rows, part],
            coef[0, rows, :],
            coef[1, rows, :],
        )
        rate[rows, part] = first
        rate_half[rows, part] = first.astype(rate_half.dtype)

    over_pieces(0, size, members, coef.shape[2], work)


def section_two_kernel(
    own, other, weight, unweight, decay, tau, coef, stress, normal, rate, change, rate_out, change_out, mean_rate, mean_change, sem
):
    size, members = tau.shape

    def work(rows, part):
        shear = own[0, rows, part] + other[0, rows, part].astype(jnp.float32)
        press = own[1, rows, part] + other[1, rows, part].astype(jnp.float32)
        later = friction(
            stress[rows, part] + section_step * shear,
            normal[rows, part] + section_step * press,
            weight[rows, part],
            unweight[rows, part],
            tau[rows, part],
            coef[0, rows, :],
            coef[1, rows, :],
        )
        second = state_change(later, decay[rows, part], coef[2, rows, :])
        mean_rate[rows, part] = (rate[rows, part] + later) * 0.5
        mean_change[rows, part] = (change[rows, part] + second) * 0.5

    copies = []
    for at, part in enumerate(row_pieces(size, OUT_PIECES)):
        over_pieces(part.start, part.size, members, coef.shape[2], work)
        for kind, (held, out) in enumerate(((mean_rate, rate_out), (mean_change, change_out))):
            copies.append(pltpu.make_async_copy(held.at[part], out.at[part], sem.at[kind, at]))
            copies[-1].start()
    for copy in copies:
        copy.wait()


def on_core(kernel, outs, arrays, scratch=(), flops=0, room=16, far=(), out_far=False):
    vmem, hbm = pl.BlockSpec(memory_space=pltpu.VMEM), pl.BlockSpec(memory_space=pl.ANY)
    arrays = (*(pltpu.with_memory_space_constraint(a, pltpu.HBM) for a in far), *arrays)
    return pl.pallas_call(
        kernel,
        out_shape=outs,
        in_specs=[hbm] * len(far) + [vmem] * (len(arrays) - len(far)),
        out_specs=jax.tree.map(lambda _: hbm if out_far else vmem, outs),
        scratch_shapes=list(scratch),
        compiler_params=pltpu.CompilerParams(vmem_limit_bytes=room * 1024 * 1024),
        cost_estimate=pl.CostEstimate(
            flops=flops, bytes_accessed=sum(a.size * a.dtype.itemsize for a in arrays), transcendentals=0
        ),
    )(*arrays)


def body(
    slip_deficit,
    state_var,
    tau_load,
    sigma_base,
    a_coef,
    b_coef,
    v_basis,
    u_basis,
    dense_blocks,
    block_ranks,
    near_index,
):
    count = lax.axis_size("row")
    size, members = slip_deficit.shape
    kinds, rows, _, rank_count, _ = u_basis.shape
    direct = count in DIRECT_COUNTS
    groups = arrivals(count, direct)
    firsts = [sum(len(group) for group in groups[:at]) for at in range(len(groups))]
    tiles = [-(-len(group) * rank_count // TILE) * TILE for group in groups]
    starts = [sum(tiles[:at]) for at in range(len(groups))]
    room = 16 if direct else 40
    lanes = min(members, 128)
    narrow, wide = jnp.bfloat16, jnp.float32
    swap = [(0, 1), (1, 0)]

    def shaped(*shape, kind=wide):
        return jax.ShapeDtypeStruct(shape, kind)

    full = shaped(size, members)
    v_met, u_met, coef, *powers = on_core(
        functools.partial(prepare_kernel, groups, direct),
        (
            shaped(count, rows, rank_count, size, kind=narrow),
            shaped(rows, kinds * size, sum(tiles), kind=narrow),
            shaped(5, size, lanes),
            full,
            full,
            full,
        ),
        (),
        (
            pltpu.SMEM(block_ranks.shape, jnp.int32),
            pltpu.VMEM(v_basis.shape, narrow),
            pltpu.VMEM(u_basis.shape, narrow),
            *[pltpu.VMEM((1, size), wide)] * 3,
            pltpu.VMEM((size, members), wide),
            pltpu.SemaphoreType.DMA((7,)),
        ),
        room=room,
        far=(
            block_ranks,
            v_basis,
            u_basis,
            sigma_base.reshape(1, size),
            a_coef.reshape(1, size),
            b_coef.reshape(1, size),
            state_var,
        ),
    )

    def add(blocks, at, pick, before, kind):
        held = rows if pick is None else 1
        lead = (rows, kinds) if pick is None else (kinds,)
        return on_core(
            functools.partial(
                sums_kernel, groups[at], direct, firsts[at], starts[at], pick, before is not None
            ),
            shaped(*lead, size, members, kind=kind),
            (near_index, v_met, u_met, dense_blocks, *blocks, *(() if before is None else (before,))),
            (
                pltpu.VMEM((held, tiles[at], members), narrow),
            ),
            2 * held * size * members * rank_count * len(blocks) * 3,
            room,
        )

    def lattice(field_half, beside):
        if direct:
            found = gather_direct(field_half, count)
        else:
            whole = lax.all_gather(field_half, "row", axis=0)
            found = [[whole[r] for r in group] for group in groups]
        found[0][0], beside = lax.optimization_barrier((found[0][0], beside))
        sums, end = None, len(groups) - 1
        for at in range(end):
            sums = add(found[at], at, None, sums, wide)
        other = lax.ppermute(add(found[end], end, 1, sums, narrow), "col", swap)
        return add(found[end], end, 0, sums, wide), other, beside

    slip_half = on_core(
        narrow_kernel,
        shaped(size, members, kind=narrow),
        (),
        (pltpu.VMEM((size, members), wide), pltpu.SemaphoreType.DMA((IN_PIECES,))),
        far=(slip_deficit,),
    )
    own, other, powers = lattice(slip_half, powers)
    rate, rate_half = on_core(
        section_one_kernel,
        (full, shaped(size, members, kind=narrow)),
        (own, other, *powers[:2], tau_load, coef),
        flops=200 * size * members,
    )
    beside = on_core(later_kernel, (full,) * 6, (own, other, state_var, powers[2], rate, coef))
    own, other, (stress, normal, change, *powers) = lattice(rate_half, beside)
    return on_core(
        section_two_kernel,
        (full, full),
        (own, other, *powers, tau_load, coef, stress, normal, rate, change),
        (
            pltpu.VMEM((size, members), wide),
            pltpu.VMEM((size, members), wide),
            pltpu.SemaphoreType.DMA((2, OUT_PIECES)),
        ),
        flops=200 * size * members,
        out_far=True,
    )


def solution(mesh):
    placed = (
        P(("row", "col"), "scen"),
        P(("row", "col"), "scen"),
        P(("row", "col"), "scen"),
        P(("row", "col")),
        P(("row", "col")),
        P(("row", "col")),
        P("row", "col", None, None),
        P(None, "row", "col", None, None),
        P(None, "row", "col", None, None),
        P("row", "col"),
        P("row", "col"),
    )
    return jax.shard_map(
        body,
        mesh=mesh,
        in_specs=placed,
        out_specs=(P(("row", "col"), "scen"), P(("row", "col"), "scen")),
        check_vma=False,
    )
```

```python
import functools

import jax
import jax.numpy as jnp
from jax import lax
from jax.experimental import pallas as pl
from jax.experimental.pallas import tpu as pltpu
from jax.sharding import PartitionSpec as P

NEWTON = 2
DIRECT_COUNTS = (4, 8)
TILE = 128

damping = 0.5
sigma_floor = 0.5
section_step = 0.1


def arrivals(count, direct):
    if not direct:
        cuts = [0, max(count - 4, 0), count]
        return [list(range(first, last)) for first, last in zip(cuts, cuts[1:]) if last > first]
    return [[0, 1, 4, 2, 3], [5, 6, 7]] if count == 8 else [[0, 1], [2, 3]]


def row_met(spot, row, direct):
    return jnp.bitwise_xor(row, spot) if direct else spot


def gather_direct(block, count):
    def swapped(mask, data):
        return lax.ppermute(data, "row", [(row, row ^ mask) for row in range(count)])

    found = {0: block}
    for mask in (4, 1, 2, 3) if count == 8 else (1, 2, 3):
        found[mask] = swapped(mask, block)
    if count == 8:
        for mask in (1, 2, 3):
            found[4 + mask] = swapped(mask, found[4])
    return [[found[mask] for mask in group] for group in arrivals(count, True)]


IN_PIECES = 8
OUT_PIECES = 4


def row_pieces(size, pieces):
    tall = size // pieces
    return [pl.ds(at * tall, tall) for at in range(pieces)]


def narrow_kernel(wide_ref, narrow_ref, held, sem):
    copies = [
        pltpu.make_async_copy(wide_ref.at[part], held.at[part], sem.at[at])
        for at, part in enumerate(row_pieces(held.shape[0], IN_PIECES))
    ]
    for copy in copies:
        copy.start()
    for copy, part in zip(copies, row_pieces(held.shape[0], IN_PIECES)):
        copy.wait()
        narrow_ref[part, :] = held[part, :].astype(narrow_ref.dtype)


def store_powers(outs, part, state, coef):
    outs[0][:, part] = jnp.exp(-state * coef[3])
    outs[1][:, part] = jnp.exp(state * coef[3])
    outs[2][:, part] = jnp.exp(-state * coef[4])


def later_kernel(own, other, state, decay, rate, coef, stress, normal, change, *outs):
    stress[...] = own[0] + other[0].astype(jnp.float32)
    normal[...] = own[1] + other[1].astype(jnp.float32)
    lanes = coef.shape[2]
    for first in range(0, state.shape[1], lanes):
        part = slice(first, first + lanes)
        step = state_change(rate[:, part], decay[:, part], coef[2])
        change[:, part] = step
        store_powers(outs, part, state[:, part] + section_step * step, coef)


def prepare_kernel(groups, direct, *refs):
    far, (v_out, u_out, coef_out, *powers), near, sem = refs[:7], refs[7:13], refs[13:20], refs[20]
    copies = [
        pltpu.make_async_copy(source, held, sem.at[at])
        for at, (source, held) in enumerate(zip(far, near))
    ]
    for copy in copies:
        copy.start()
    for copy in copies:
        copy.wait()
    rank_ref, v_ref, u_ref, sigma_ref, a_ref, b_ref, state_ref = near
    kinds, rows, count, rank_count, size = u_ref.shape
    row = lax.axis_index("row")
    met = [row_met(spot, row, direct) for group in groups for spot in group]
    for at, q in enumerate(met):
        for p in range(rows):
            inside = lax.broadcasted_iota(jnp.int32, (rank_count, size), 0) < rank_ref[p, q]
            v_out[at, p] = jnp.where(inside, v_ref[p, q].astype(jnp.float32), 0.0).astype(v_out.dtype)
    for p in range(rows):
        for kind in range(kinds):
            first = start = 0
            for spots in groups:
                group = [u_ref[kind, p, q] for q in met[first : first + len(spots)]]
                spare = -len(group) * rank_count % TILE
                if spare:
                    group.append(jnp.zeros((spare, size), u_ref.dtype))
                turned = jnp.concatenate(group, axis=0).astype(jnp.float32).T
                stop = start + turned.shape[1]
                u_out[p, kind * size : (kind + 1) * size, start:stop] = turned.astype(u_out.dtype)
                first, start = first + len(spots), stop
    lanes = coef_out.shape[2]
    for at, values in enumerate((sigma_ref[...], a_ref[...], b_ref[...], 1.0 / a_ref[...], 1.0 / b_ref[...])):
        coef_out[at] = jnp.broadcast_to(values, (lanes, size)).T
    for first in range(0, state_ref.shape[1], lanes):
        part = slice(first, first + lanes)
        store_powers(powers, part, state_ref[:, part], coef_out)


def sums_kernel(spots, direct, first, start, pick, before, near_ref, v_ref, u_ref, d_ref, *refs):
    blocks = refs[: len(spots)]
    refs = refs[len(spots) :]
    if before:
        sums_ref, refs = refs[0], refs[1:]
    out_ref, proj = refs
    count, rows, rank_count, size = v_ref.shape
    kinds, slots = d_ref.shape[0], near_ref.shape[1]
    row, col = lax.axis_index("row"), lax.axis_index("col")
    met = [row_met(spot, row, direct) for spot in spots]
    chosen = list(range(rows)) if pick is None else [col if pick == 0 else 1 - col]
    places = [(place,) for place in range(rows)] if pick is None else [()]
    for at, block in enumerate(blocks):
        if pick is None:
            weights = v_ref[first + at].reshape(rows * rank_count, size)
        else:
            weights = v_ref[first + at, chosen[0]]
        part = jnp.dot(weights, block[...], preferred_element_type=jnp.float32).astype(proj.dtype)
        for place in range(len(chosen)):
            proj[place, at * rank_count : (at + 1) * rank_count, :] = part[
                place * rank_count : (place + 1) * rank_count
            ]
    width = proj.shape[1]
    lanes = slice(start, start + width)
    if width > len(blocks) * rank_count:
        for place in range(len(chosen)):
            proj[place, len(blocks) * rank_count :, :] = jnp.zeros(
                (width - len(blocks) * rank_count, proj.shape[2]), proj.dtype
            )
    for place, p in enumerate(chosen):
        weights, fields = [u_ref[p, :, lanes]], [proj[place]]
        for s in range(slots):
            near = near_ref[pl.ds(p, 1), s : s + 1] - col * count
            field = None
            for q, block in zip(met, blocks):
                mask = jnp.where(near == q, 1.0, 0.0).astype(block.dtype)
                part = block[...] * mask
                field = part if field is None else field + part
            weights.append(jnp.concatenate([d_ref[kind, p, s] for kind in range(kinds)], axis=0))
            fields.append(field)
        total = jnp.dot(
            jnp.concatenate(weights, axis=1),
            jnp.concatenate(fields, axis=0),
            preferred_element_type=jnp.float32,
        )
        for kind in range(kinds):
            piece = total[kind * size : (kind + 1) * size]
            if before:
                piece += sums_ref[p, kind]
            out_ref[*places[place], kind] = piece.astype(out_ref.dtype)


def inverse(value):
    rough = pl.reciprocal(value, approx=True)
    return rough * (2.0 - value * rough)


def rough_inverse(value):
    return pl.reciprocal(value, approx=True)


def scaled_sinh_cosh(value, scale):
    grown = jnp.exp(value)
    half = 0.5 * scale
    up, down = half * grown, half * inverse(grown)
    square = value * value
    small = scale * value * (1.0 + square * (1 / 6 + square * (1 / 120)))
    return jnp.where(square < 0.25, small, up - down), up + down


def friction(shear, normal, weight, unweight, tau_load, sigma_base, a_wide):
    tau = tau_load + shear
    size = jnp.abs(tau)
    stiff = jnp.maximum(sigma_base + normal, sigma_floor) * a_wide
    double = 2.0 * damping * weight
    drive = size * unweight * (0.5 / damping)
    square = drive * drive + 1.0
    slope = jnp.minimum(size * rough_inverse(stiff), jnp.log(drive + square * lax.rsqrt(square)))
    for newton_step in range(NEWTON):
        sinh, cosh = scaled_sinh_cosh(slope, double)
        slope = slope - (stiff * slope + sinh - size) * rough_inverse(stiff + cosh)
    rate = scaled_sinh_cosh(slope, double)[0] * (1.0 / damping)
    return jnp.where(tau < 0.0, -rate, rate)


def state_change(rate, decay, b_wide):
    return b_wide * (decay - jnp.abs(rate))


def over_pieces(begin, tall, members, lanes, work):
    step = min(tall, 64)
    for at in range(begin, begin + tall, step):
        for first in range(0, members, lanes):
            work(pl.ds(at, step), slice(first, first + lanes))


def section_one_kernel(own, other, weight, unweight, tau, coef, rate, rate_half):
    size, members = tau.shape

    def work(rows, part):
        first = friction(
            own[0, rows, part] + other[0, rows, part].astype(jnp.float32),
            own[1, rows, part] + other[1, rows, part].astype(jnp.float32),
            weight[rows, part],
            unweight[rows, part],
            tau[rows, part],
            coef[0, rows, :],
            coef[1, rows, :],
        )
        rate[rows, part] = first
        rate_half[rows, part] = first.astype(rate_half.dtype)

    over_pieces(0, size, members, coef.shape[2], work)


def section_two_kernel(
    own, other, weight, unweight, decay, tau, coef, stress, normal, rate, change, rate_out, change_out, mean_rate, mean_change, sem
):
    size, members = tau.shape

    def work(rows, part):
        shear = own[0, rows, part] + other[0, rows, part].astype(jnp.float32)
        press = own[1, rows, part] + other[1, rows, part].astype(jnp.float32)
        later = friction(
            stress[rows, part] + section_step * shear,
            normal[rows, part] + section_step * press,
            weight[rows, part],
            unweight[rows, part],
            tau[rows, part],
            coef[0, rows, :],
            coef[1, rows, :],
        )
        second = state_change(later, decay[rows, part], coef[2, rows, :])
        mean_rate[rows, part] = (rate[rows, part] + later) * 0.5
        mean_change[rows, part] = (change[rows, part] + second) * 0.5

    copies = []
    for at, part in enumerate(row_pieces(size, OUT_PIECES)):
        over_pieces(part.start, part.size, members, coef.shape[2], work)
        for kind, (held, out) in enumerate(((mean_rate, rate_out), (mean_change, change_out))):
            copies.append(pltpu.make_async_copy(held.at[part], out.at[part], sem.at[kind, at]))
            copies[-1].start()
    for copy in copies:
        copy.wait()


def on_core(kernel, outs, arrays, scratch=(), flops=0, room=16, far=(), out_far=False):
    vmem, hbm = pl.BlockSpec(memory_space=pltpu.VMEM), pl.BlockSpec(memory_space=pl.ANY)
    arrays = (*(pltpu.with_memory_space_constraint(a, pltpu.HBM) for a in far), *arrays)
    return pl.pallas_call(
        kernel,
        out_shape=outs,
        in_specs=[hbm] * len(far) + [vmem] * (len(arrays) - len(far)),
        out_specs=jax.tree.map(lambda _: hbm if out_far else vmem, outs),
        scratch_shapes=list(scratch),
        compiler_params=pltpu.CompilerParams(vmem_limit_bytes=room * 1024 * 1024),
        cost_estimate=pl.CostEstimate(
            flops=flops, bytes_accessed=sum(a.size * a.dtype.itemsize for a in arrays), transcendentals=0
        ),
    )(*arrays)


def body(
    slip_deficit,
    state_var,
    tau_load,
    sigma_base,
    a_coef,
    b_coef,
    v_basis,
    u_basis,
    dense_blocks,
    block_ranks,
    near_index,
):
    count = lax.axis_size("row")
    size, members = slip_deficit.shape
    kinds, rows, _, rank_count, _ = u_basis.shape
    direct = count in DIRECT_COUNTS
    groups = arrivals(count, direct)
    firsts = [sum(len(group) for group in groups[:at]) for at in range(len(groups))]
    tiles = [-(-len(group) * rank_count // TILE) * TILE for group in groups]
    starts = [sum(tiles[:at]) for at in range(len(groups))]
    room = 16 if direct else 40
    lanes = min(members, 128)
    narrow, wide = jnp.bfloat16, jnp.float32
    swap = [(0, 1), (1, 0)]

    def shaped(*shape, kind=wide):
        return jax.ShapeDtypeStruct(shape, kind)

    full = shaped(size, members)
    v_met, u_met, coef, *powers = on_core(
        functools.partial(prepare_kernel, groups, direct),
        (
            shaped(count, rows, rank_count, size, kind=narrow),
            shaped(rows, kinds * size, sum(tiles), kind=narrow),
            shaped(5, size, lanes),
            full,
            full,
            full,
        ),
        (),
        (
            pltpu.SMEM(block_ranks.shape, jnp.int32),
            pltpu.VMEM(v_basis.shape, narrow),
            pltpu.VMEM(u_basis.shape, narrow),
            *[pltpu.VMEM((1, size), wide)] * 3,
            pltpu.VMEM((size, members), wide),
            pltpu.SemaphoreType.DMA((7,)),
        ),
        room=room,
        far=(
            block_ranks,
            v_basis,
            u_basis,
            sigma_base.reshape(1, size),
            a_coef.reshape(1, size),
            b_coef.reshape(1, size),
            state_var,
        ),
    )

    def add(blocks, at, pick, before, kind):
        held = rows if pick is None else 1
        lead = (rows, kinds) if pick is None else (kinds,)
        return on_core(
            functools.partial(
                sums_kernel, groups[at], direct, firsts[at], starts[at], pick, before is not None
            ),
            shaped(*lead, size, members, kind=kind),
            (near_index, v_met, u_met, dense_blocks, *blocks, *(() if before is None else (before,))),
            (
                pltpu.VMEM((held, tiles[at], members), narrow),
            ),
            2 * held * size * members * rank_count * len(blocks) * 3,
            room,
        )

    def lattice(field_half, beside):
        if direct:
            found = gather_direct(field_half, count)
        else:
            whole = lax.all_gather(field_half, "row", axis=0)
            found = [[whole[r] for r in group] for group in groups]
        found[0][0], beside = lax.optimization_barrier((found[0][0], beside))
        sums, end = None, len(groups) - 1
        for at in range(end):
            sums = add(found[at], at, None, sums, wide)
        other = lax.ppermute(add(found[end], end, 1, sums, narrow), "col", swap)
        return add(found[end], end, 0, sums, wide), other, beside

    slip_half = on_core(
        narrow_kernel,
        shaped(size, members, kind=narrow),
        (),
        (pltpu.VMEM((size, members), wide), pltpu.SemaphoreType.DMA((IN_PIECES,))),
        far=(slip_deficit,),
    )
    own, other, powers = lattice(slip_half, powers)
    rate, rate_half = on_core(
        section_one_kernel,
        (full, shaped(size, members, kind=narrow)),
        (own, other, *powers[:2], tau_load, coef),
        flops=200 * size * members,
    )
    beside = on_core(later_kernel, (full,) * 6, (own, other, state_var, powers[2], rate, coef))
    own, other, (stress, normal, change, *powers) = lattice(rate_half, beside)
    return on_core(
        section_two_kernel,
        (full, full),
        (own, other, *powers, tau_load, coef, stress, normal, rate, change),
        (
            pltpu.VMEM((size, members), wide),
            pltpu.VMEM((size, members), wide),
            pltpu.SemaphoreType.DMA((2, OUT_PIECES)),
        ),
        flops=200 * size * members,
        out_far=True,
    )


def solution(mesh):
    placed = (
        P(("row", "col"), "scen"),
        P(("row", "col"), "scen"),
        P(("row", "col"), "scen"),
        P(("row", "col")),
        P(("row", "col")),
        P(("row", "col")),
        P("row", "col", None, None),
        P(None, "row", "col", None, None),
        P(None, "row", "col", None, None),
        P("row", "col"),
        P("row", "col"),
    )
    return jax.shard_map(
        body,
        mesh=mesh,
        in_specs=placed,
        out_specs=(P(("row", "col"), "scen"), P(("row", "col"), "scen")),
        check_vma=False,
    )
```

```python
import functools

import jax
import jax.numpy as jnp
from jax import lax
from jax.experimental import pallas as pl
from jax.experimental.pallas import tpu as pltpu
from jax.sharding import PartitionSpec as P

NEWTON = 2
DIRECT_COUNTS = (4, 8)
TILE = 128

damping = 0.5
sigma_floor = 0.5
section_step = 0.1


def arrivals(count, direct):
    if not direct:
        cuts = [0, max(count - 4, 0), count]
        return [list(range(first, last)) for first, last in zip(cuts, cuts[1:]) if last > first]
    return [[0, 1, 4, 2, 3], [6, 5, 7]] if count == 8 else [[0, 1], [2, 3]]


def row_met(spot, row, direct):
    return jnp.bitwise_xor(row, spot) if direct else spot


def gather_direct(block, count):
    def swapped(mask, data):
        return lax.ppermute(data, "row", [(row, row ^ mask) for row in range(count)])

    found = {0: block}
    for mask in (4, 1, 2, 3) if count == 8 else (1, 2, 3):
        found[mask] = swapped(mask, block)
    if count == 8:
        for mask in (1, 2, 3):
            found[4 + mask] = swapped(mask, found[4])
    return [[found[mask] for mask in group] for group in arrivals(count, True)]


IN_PIECES = 8
OUT_SHARES = (2, 4, 8, 8)


def row_pieces(size, pieces):
    tall = size // pieces
    return [pl.ds(at * tall, tall) for at in range(pieces)]


def shrinking_pieces(size):
    talls = [size // share for share in OUT_SHARES]
    return [pl.ds(sum(talls[:at]), tall) for at, tall in enumerate(talls)]


def narrow_kernel(wide_ref, narrow_ref, held, sem):
    copies = [
        pltpu.make_async_copy(wide_ref.at[part], held.at[part], sem.at[at])
        for at, part in enumerate(row_pieces(held.shape[0], IN_PIECES))
    ]
    for copy in copies:
        copy.start()
    for copy, part in zip(copies, row_pieces(held.shape[0], IN_PIECES)):
        copy.wait()
        narrow_ref[part, :] = held[part, :].astype(narrow_ref.dtype)


def store_powers(outs, part, state, coef):
    outs[0][:, part] = jnp.exp(-state * coef[3])
    outs[1][:, part] = jnp.exp(state * coef[3])
    outs[2][:, part] = jnp.exp(-state * coef[4])


def later_kernel(own, other, state, decay, rate, coef, stress, normal, change, *outs):
    stress[...] = own[0] + other[0].astype(jnp.float32)
    normal[...] = own[1] + other[1].astype(jnp.float32)
    lanes = coef.shape[2]
    for first in range(0, state.shape[1], lanes):
        part = slice(first, first + lanes)
        step = state_change(rate[:, part], decay[:, part], coef[2])
        change[:, part] = step
        store_powers(outs, part, state[:, part] + section_step * step, coef)


def prepare_kernel(groups, direct, *refs):
    far, (v_out, u_out, coef_out, *powers), near, sem = refs[:7], refs[7:13], refs[13:20], refs[20]
    copies = [
        pltpu.make_async_copy(source, held, sem.at[at])
        for at, (source, held) in enumerate(zip(far, near))
    ]
    for copy in copies:
        copy.start()
    for copy in copies:
        copy.wait()
    rank_ref, v_ref, u_ref, sigma_ref, a_ref, b_ref, state_ref = near
    kinds, rows, count, rank_count, size = u_ref.shape
    row = lax.axis_index("row")
    met = [row_met(spot, row, direct) for group in groups for spot in group]
    for at, q in enumerate(met):
        for p in range(rows):
            inside = lax.broadcasted_iota(jnp.int32, (rank_count, size), 0) < rank_ref[p, q]
            v_out[at, p] = jnp.where(inside, v_ref[p, q].astype(jnp.float32), 0.0).astype(v_out.dtype)
    for p in range(rows):
        for kind in range(kinds):
            first = start = 0
            for spots in groups:
                group = [u_ref[kind, p, q] for q in met[first : first + len(spots)]]
                spare = -len(group) * rank_count % TILE
                if spare:
                    group.append(jnp.zeros((spare, size), u_ref.dtype))
                turned = jnp.concatenate(group, axis=0).astype(jnp.float32).T
                stop = start + turned.shape[1]
                u_out[p, kind * size : (kind + 1) * size, start:stop] = turned.astype(u_out.dtype)
                first, start = first + len(spots), stop
    lanes = coef_out.shape[2]
    for at, values in enumerate((sigma_ref[...], a_ref[...], b_ref[...], 1.0 / a_ref[...], 1.0 / b_ref[...])):
        coef_out[at] = jnp.broadcast_to(values, (lanes, size)).T
    for first in range(0, state_ref.shape[1], lanes):
        part = slice(first, first + lanes)
        store_powers(powers, part, state_ref[:, part], coef_out)


def sums_kernel(spots, direct, first, start, pick, before, near_ref, v_ref, u_ref, d_ref, *refs):
    blocks = refs[: len(spots)]
    refs = refs[len(spots) :]
    if before:
        sums_ref, refs = refs[0], refs[1:]
    out_ref, proj = refs
    count, rows, rank_count, size = v_ref.shape
    kinds, slots = d_ref.shape[0], near_ref.shape[1]
    row, col = lax.axis_index("row"), lax.axis_index("col")
    met = [row_met(spot, row, direct) for spot in spots]
    chosen = list(range(rows)) if pick is None else [col if pick == 0 else 1 - col]
    places = [(place,) for place in range(rows)] if pick is None else [()]
    for at, block in enumerate(blocks):
        if pick is None:
            weights = v_ref[first + at].reshape(rows * rank_count, size)
        else:
            weights = v_ref[first + at, chosen[0]]
        part = jnp.dot(weights, block[...], preferred_element_type=jnp.float32).astype(proj.dtype)
        for place in range(len(chosen)):
            proj[place, at * rank_count : (at + 1) * rank_count, :] = part[
                place * rank_count : (place + 1) * rank_count
            ]
    width = proj.shape[1]
    lanes = slice(start, start + width)
    if width > len(blocks) * rank_count:
        for place in range(len(chosen)):
            proj[place, len(blocks) * rank_count :, :] = jnp.zeros(
                (width - len(blocks) * rank_count, proj.shape[2]), proj.dtype
            )
    for place, p in enumerate(chosen):
        weights, fields = [u_ref[p, :, lanes]], [proj[place]]
        for s in range(slots):
            near = near_ref[pl.ds(p, 1), s : s + 1] - col * count
            field = None
            for q, block in zip(met, blocks):
                mask = jnp.where(near == q, 1.0, 0.0).astype(block.dtype)
                part = block[...] * mask
                field = part if field is None else field + part
            weights.append(jnp.concatenate([d_ref[kind, p, s] for kind in range(kinds)], axis=0))
            fields.append(field)
        total = jnp.dot(
            jnp.concatenate(weights, axis=1),
            jnp.concatenate(fields, axis=0),
            preferred_element_type=jnp.float32,
        )
        for kind in range(kinds):
            piece = total[kind * size : (kind + 1) * size]
            if before:
                piece += sums_ref[p, kind]
            out_ref[*places[place], kind] = piece.astype(out_ref.dtype)


def inverse(value):
    rough = pl.reciprocal(value, approx=True)
    return rough * (2.0 - value * rough)


def rough_inverse(value):
    return pl.reciprocal(value, approx=True)


def scaled_sinh_cosh(value, scale):
    grown = jnp.exp(value)
    half = 0.5 * scale
    up, down = half * grown, half * inverse(grown)
    square = value * value
    small = scale * value * (1.0 + square * (1 / 6 + square * (1 / 120)))
    return jnp.where(square < 0.25, small, up - down), up + down


def friction(shear, normal, weight, unweight, tau_load, sigma_base, a_wide):
    tau = tau_load + shear
    size = jnp.abs(tau)
    stiff = jnp.maximum(sigma_base + normal, sigma_floor) * a_wide
    double = 2.0 * damping * weight
    drive = size * unweight * (0.5 / damping)
    square = drive * drive + 1.0
    slope = jnp.minimum(size * rough_inverse(stiff), jnp.log(drive + square * lax.rsqrt(square)))
    for newton_step in range(NEWTON):
        sinh, cosh = scaled_sinh_cosh(slope, double)
        slope = slope - (stiff * slope + sinh - size) * rough_inverse(stiff + cosh)
    rate = scaled_sinh_cosh(slope, double)[0] * (1.0 / damping)
    return jnp.where(tau < 0.0, -rate, rate)


def state_change(rate, decay, b_wide):
    return b_wide * (decay - jnp.abs(rate))


def over_pieces(begin, tall, members, lanes, work):
    step = min(tall, 64)
    for at in range(begin, begin + tall, step):
        for first in range(0, members, lanes):
            work(pl.ds(at, step), slice(first, first + lanes))


def section_one_kernel(own, other, weight, unweight, tau, coef, rate, rate_half):
    size, members = tau.shape

    def work(rows, part):
        first = friction(
            own[0, rows, part] + other[0, rows, part].astype(jnp.float32),
            own[1, rows, part] + other[1, rows, part].astype(jnp.float32),
            weight[rows, part],
            unweight[rows, part],
            tau[rows, part],
            coef[0, rows, :],
            coef[1, rows, :],
        )
        rate[rows, part] = first
        rate_half[rows, part] = first.astype(rate_half.dtype)

    over_pieces(0, size, members, coef.shape[2], work)


def section_two_kernel(
    own, other, weight, unweight, decay, tau, coef, stress, normal, rate, change, rate_out, change_out, mean_rate, mean_change, sem
):
    size, members = tau.shape

    def work(rows, part):
        shear = own[0, rows, part] + other[0, rows, part].astype(jnp.float32)
        press = own[1, rows, part] + other[1, rows, part].astype(jnp.float32)
        later = friction(
            stress[rows, part] + section_step * shear,
            normal[rows, part] + section_step * press,
            weight[rows, part],
            unweight[rows, part],
            tau[rows, part],
            coef[0, rows, :],
            coef[1, rows, :],
        )
        second = state_change(later, decay[rows, part], coef[2, rows, :])
        mean_rate[rows, part] = (rate[rows, part] + later) * 0.5
        mean_change[rows, part] = (change[rows, part] + second) * 0.5

    copies = []
    for at, part in enumerate(shrinking_pieces(size)):
        over_pieces(part.start, part.size, members, coef.shape[2], work)
        for kind, (held, out) in enumerate(((mean_rate, rate_out), (mean_change, change_out))):
            copies.append(pltpu.make_async_copy(held.at[part], out.at[part], sem.at[kind, at]))
            copies[-1].start()
    for copy in copies:
        copy.wait()


def on_core(kernel, outs, arrays, scratch=(), flops=0, room=16, far=(), out_far=False):
    vmem, hbm = pl.BlockSpec(memory_space=pltpu.VMEM), pl.BlockSpec(memory_space=pl.ANY)
    arrays = (*(pltpu.with_memory_space_constraint(a, pltpu.HBM) for a in far), *arrays)
    return pl.pallas_call(
        kernel,
        out_shape=outs,
        in_specs=[hbm] * len(far) + [vmem] * (len(arrays) - len(far)),
        out_specs=jax.tree.map(lambda _: hbm if out_far else vmem, outs),
        scratch_shapes=list(scratch),
        compiler_params=pltpu.CompilerParams(vmem_limit_bytes=room * 1024 * 1024),
        cost_estimate=pl.CostEstimate(
            flops=flops, bytes_accessed=sum(a.size * a.dtype.itemsize for a in arrays), transcendentals=0
        ),
    )(*arrays)


def body(
    slip_deficit,
    state_var,
    tau_load,
    sigma_base,
    a_coef,
    b_coef,
    v_basis,
    u_basis,
    dense_blocks,
    block_ranks,
    near_index,
):
    count = lax.axis_size("row")
    size, members = slip_deficit.shape
    kinds, rows, _, rank_count, _ = u_basis.shape
    direct = count in DIRECT_COUNTS
    groups = arrivals(count, direct)
    firsts = [sum(len(group) for group in groups[:at]) for at in range(len(groups))]
    tiles = [-(-len(group) * rank_count // TILE) * TILE for group in groups]
    starts = [sum(tiles[:at]) for at in range(len(groups))]
    room = 16 if direct else 40
    lanes = min(members, 128)
    narrow, wide = jnp.bfloat16, jnp.float32
    swap = [(0, 1), (1, 0)]

    def shaped(*shape, kind=wide):
        return jax.ShapeDtypeStruct(shape, kind)

    full = shaped(size, members)
    v_met, u_met, coef, *powers = on_core(
        functools.partial(prepare_kernel, groups, direct),
        (
            shaped(count, rows, rank_count, size, kind=narrow),
            shaped(rows, kinds * size, sum(tiles), kind=narrow),
            shaped(5, size, lanes),
            full,
            full,
            full,
        ),
        (),
        (
            pltpu.SMEM(block_ranks.shape, jnp.int32),
            pltpu.VMEM(v_basis.shape, narrow),
            pltpu.VMEM(u_basis.shape, narrow),
            *[pltpu.VMEM((1, size), wide)] * 3,
            pltpu.VMEM((size, members), wide),
            pltpu.SemaphoreType.DMA((7,)),
        ),
        room=room,
        far=(
            block_ranks,
            v_basis,
            u_basis,
            sigma_base.reshape(1, size),
            a_coef.reshape(1, size),
            b_coef.reshape(1, size),
            state_var,
        ),
    )

    def add(blocks, at, pick, before, kind):
        held = rows if pick is None else 1
        lead = (rows, kinds) if pick is None else (kinds,)
        return on_core(
            functools.partial(
                sums_kernel, groups[at], direct, firsts[at], starts[at], pick, before is not None
            ),
            shaped(*lead, size, members, kind=kind),
            (near_index, v_met, u_met, dense_blocks, *blocks, *(() if before is None else (before,))),
            (
                pltpu.VMEM((held, tiles[at], members), narrow),
            ),
            2 * held * size * members * rank_count * len(blocks) * 3,
            room,
        )

    def lattice(field_half, beside):
        if direct:
            found = gather_direct(field_half, count)
        else:
            whole = lax.all_gather(field_half, "row", axis=0)
            found = [[whole[r] for r in group] for group in groups]
        found[0][0], beside = lax.optimization_barrier((found[0][0], beside))
        sums, end = None, len(groups) - 1
        for at in range(end):
            sums = add(found[at], at, None, sums, wide)
        other = lax.ppermute(add(found[end], end, 1, sums, narrow), "col", swap)
        return add(found[end], end, 0, sums, wide), other, beside

    slip_half = on_core(
        narrow_kernel,
        shaped(size, members, kind=narrow),
        (),
        (pltpu.VMEM((size, members), wide), pltpu.SemaphoreType.DMA((IN_PIECES,))),
        far=(slip_deficit,),
    )
    own, other, powers = lattice(slip_half, powers)
    rate, rate_half = on_core(
        section_one_kernel,
        (full, shaped(size, members, kind=narrow)),
        (own, other, *powers[:2], tau_load, coef),
        flops=200 * size * members,
    )
    beside = on_core(later_kernel, (full,) * 6, (own, other, state_var, powers[2], rate, coef))
    own, other, (stress, normal, change, *powers) = lattice(rate_half, beside)
    return on_core(
        section_two_kernel,
        (full, full),
        (own, other, *powers, tau_load, coef, stress, normal, rate, change),
        (
            pltpu.VMEM((size, members), wide),
            pltpu.VMEM((size, members), wide),
            pltpu.SemaphoreType.DMA((2, len(OUT_SHARES))),
        ),
        flops=200 * size * members,
        out_far=True,
    )


def solution(mesh):
    placed = (
        P(("row", "col"), "scen"),
        P(("row", "col"), "scen"),
        P(("row", "col"), "scen"),
        P(("row", "col")),
        P(("row", "col")),
        P(("row", "col")),
        P("row", "col", None, None),
        P(None, "row", "col", None, None),
        P(None, "row", "col", None, None),
        P("row", "col"),
        P("row", "col"),
    )
    return jax.shard_map(
        body,
        mesh=mesh,
        in_specs=placed,
        out_specs=(P(("row", "col"), "scen"), P(("row", "col"), "scen")),
        check_vma=False,
    )
```

```python
import functools

import jax
import jax.numpy as jnp
from jax import lax
from jax.experimental import pallas as pl
from jax.experimental.pallas import tpu as pltpu
from jax.sharding import PartitionSpec as P

NEWTON = 2
DIRECT_COUNTS = (4, 8)
TILE = 128

damping = 0.5
sigma_floor = 0.5
section_step = 0.1


def arrivals(count, direct):
    if not direct:
        cuts = [0, max(count - 4, 0), count]
        return [list(range(first, last)) for first, last in zip(cuts, cuts[1:]) if last > first]
    return [[0, 1, 4, 2, 3], [6, 5, 7]] if count == 8 else [[0, 1], [2, 3]]


def row_met(spot, row, direct):
    return jnp.bitwise_xor(row, spot) if direct else spot


def gather_direct(block, count):
    def swapped(mask, data):
        return lax.ppermute(data, "row", [(row, row ^ mask) for row in range(count)])

    found = {0: block}
    for mask in (4, 1, 2, 3) if count == 8 else (1, 2, 3):
        found[mask] = swapped(mask, block)
    if count == 8:
        for mask in (1, 2, 3):
            found[4 + mask] = swapped(mask, found[4])
    return [[found[mask] for mask in group] for group in arrivals(count, True)]


IN_PIECES = 8
OUT_PIECES = 2


def row_pieces(size, pieces):
    tall = size // pieces
    return [pl.ds(at * tall, tall) for at in range(pieces)]


def narrow_kernel(wide_ref, narrow_ref, held, sem):
    copies = [
        pltpu.make_async_copy(wide_ref.at[part], held.at[part], sem.at[at])
        for at, part in enumerate(row_pieces(held.shape[0], IN_PIECES))
    ]
    for copy in copies:
        copy.start()
    for copy, part in zip(copies, row_pieces(held.shape[0], IN_PIECES)):
        copy.wait()
        narrow_ref[part, :] = held[part, :].astype(narrow_ref.dtype)


def store_powers(outs, part, state, coef):
    outs[0][:, part] = jnp.exp(-state * coef[3])
    outs[1][:, part] = jnp.exp(state * coef[3])
    outs[2][:, part] = jnp.exp(-state * coef[4])


def later_kernel(own, other, state, decay, rate, coef, stress, normal, change, *outs):
    stress[...] = own[0] + other[0].astype(jnp.float32)
    normal[...] = own[1] + other[1].astype(jnp.float32)
    lanes = coef.shape[2]
    for first in range(0, state.shape[1], lanes):
        part = slice(first, first + lanes)
        step = state_change(rate[:, part], decay[:, part], coef[2])
        change[:, part] = step
        store_powers(outs, part, state[:, part] + section_step * step, coef)


def prepare_kernel(groups, direct, *refs):
    far, (v_out, u_out, coef_out, *powers), near, sem = refs[:7], refs[7:13], refs[13:20], refs[20]
    copies = [
        pltpu.make_async_copy(source, held, sem.at[at])
        for at, (source, held) in enumerate(zip(far, near))
    ]
    for copy in copies:
        copy.start()
    for copy in copies:
        copy.wait()
    rank_ref, v_ref, u_ref, sigma_ref, a_ref, b_ref, state_ref = near
    kinds, rows, count, rank_count, size = u_ref.shape
    row = lax.axis_index("row")
    met = [row_met(spot, row, direct) for group in groups for spot in group]
    for at, q in enumerate(met):
        for p in range(rows):
            inside = lax.broadcasted_iota(jnp.int32, (rank_count, size), 0) < rank_ref[p, q]
            v_out[at, p] = jnp.where(inside, v_ref[p, q].astype(jnp.float32), 0.0).astype(v_out.dtype)
    for p in range(rows):
        for kind in range(kinds):
            first = start = 0
            for spots in groups:
                group = [u_ref[kind, p, q] for q in met[first : first + len(spots)]]
                spare = -len(group) * rank_count % TILE
                if spare:
                    group.append(jnp.zeros((spare, size), u_ref.dtype))
                turned = jnp.concatenate(group, axis=0).astype(jnp.float32).T
                stop = start + turned.shape[1]
                u_out[p, kind * size : (kind + 1) * size, start:stop] = turned.astype(u_out.dtype)
                first, start = first + len(spots), stop
    lanes = coef_out.shape[2]
    for at, values in enumerate((sigma_ref[...], a_ref[...], b_ref[...], 1.0 / a_ref[...], 1.0 / b_ref[...])):
        coef_out[at] = jnp.broadcast_to(values, (lanes, size)).T
    for first in range(0, state_ref.shape[1], lanes):
        part = slice(first, first + lanes)
        store_powers(powers, part, state_ref[:, part], coef_out)


def sums_kernel(spots, direct, first, start, pick, before, near_ref, v_ref, u_ref, d_ref, *refs):
    blocks = refs[: len(spots)]
    refs = refs[len(spots) :]
    if before:
        sums_ref, refs = refs[0], refs[1:]
    out_ref, proj = refs
    count, rows, rank_count, size = v_ref.shape
    kinds, slots = d_ref.shape[0], near_ref.shape[1]
    row, col = lax.axis_index("row"), lax.axis_index("col")
    met = [row_met(spot, row, direct) for spot in spots]
    chosen = list(range(rows)) if pick is None else [col if pick == 0 else 1 - col]
    places = [(place,) for place in range(rows)] if pick is None else [()]
    for at, block in enumerate(blocks):
        if pick is None:
            weights = v_ref[first + at].reshape(rows * rank_count, size)
        else:
            weights = v_ref[first + at, chosen[0]]
        part = jnp.dot(weights, block[...], preferred_element_type=jnp.float32).astype(proj.dtype)
        for place in range(len(chosen)):
            proj[place, at * rank_count : (at + 1) * rank_count, :] = part[
                place * rank_count : (place + 1) * rank_count
            ]
    width = proj.shape[1]
    lanes = slice(start, start + width)
    if width > len(blocks) * rank_count:
        for place in range(len(chosen)):
            proj[place, len(blocks) * rank_count :, :] = jnp.zeros(
                (width - len(blocks) * rank_count, proj.shape[2]), proj.dtype
            )
    for place, p in enumerate(chosen):
        weights, fields = [u_ref[p, :, lanes]], [proj[place]]
        for s in range(slots):
            near = near_ref[pl.ds(p, 1), s : s + 1] - col * count
            field = None
            for q, block in zip(met, blocks):
                mask = jnp.where(near == q, 1.0, 0.0).astype(block.dtype)
                part = block[...] * mask
                field = part if field is None else field + part
            weights.append(jnp.concatenate([d_ref[kind, p, s] for kind in range(kinds)], axis=0))
            fields.append(field)
        total = jnp.dot(
            jnp.concatenate(weights, axis=1),
            jnp.concatenate(fields, axis=0),
            preferred_element_type=jnp.float32,
        )
        for kind in range(kinds):
            piece = total[kind * size : (kind + 1) * size]
            if before:
                piece += sums_ref[p, kind]
            out_ref[*places[place], kind] = piece.astype(out_ref.dtype)


def inverse(value):
    rough = pl.reciprocal(value, approx=True)
    return rough * (2.0 - value * rough)


def rough_inverse(value):
    return pl.reciprocal(value, approx=True)


def scaled_sinh_cosh(value, scale):
    grown = jnp.exp(value)
    half = 0.5 * scale
    up, down = half * grown, half * inverse(grown)
    square = value * value
    small = scale * value * (1.0 + square * (1 / 6 + square * (1 / 120)))
    return jnp.where(square < 0.25, small, up - down), up + down


def friction(shear, normal, weight, unweight, tau_load, sigma_base, a_wide):
    tau = tau_load + shear
    size = jnp.abs(tau)
    stiff = jnp.maximum(sigma_base + normal, sigma_floor) * a_wide
    double = 2.0 * damping * weight
    drive = size * unweight * (0.5 / damping)
    square = drive * drive + 1.0
    slope = jnp.minimum(size * rough_inverse(stiff), jnp.log(drive + square * lax.rsqrt(square)))
    for newton_step in range(NEWTON):
        sinh, cosh = scaled_sinh_cosh(slope, double)
        slope = slope - (stiff * slope + sinh - size) * rough_inverse(stiff + cosh)
    rate = scaled_sinh_cosh(slope, double)[0] * (1.0 / damping)
    return jnp.where(tau < 0.0, -rate, rate)


def state_change(rate, decay, b_wide):
    return b_wide * (decay - jnp.abs(rate))


def over_pieces(begin, tall, members, lanes, work):
    step = min(tall, 64)
    for at in range(begin, begin + tall, step):
        for first in range(0, members, lanes):
            work(pl.ds(at, step), slice(first, first + lanes))


def section_one_kernel(own, other, weight, unweight, tau, coef, rate, rate_half):
    size, members = tau.shape

    def work(rows, part):
        first = friction(
            own[0, rows, part] + other[0, rows, part].astype(jnp.float32),
            own[1, rows, part] + other[1, rows, part].astype(jnp.float32),
            weight[rows, part],
            unweight[rows, part],
            tau[rows, part],
            coef[0, rows, :],
            coef[1, rows, :],
        )
        rate[rows, part] = first
        rate_half[rows, part] = first.astype(rate_half.dtype)

    over_pieces(0, size, members, coef.shape[2], work)


def section_two_kernel(
    own, other, weight, unweight, decay, tau, coef, stress, normal, rate, change, rate_out, change_out, mean_rate, mean_change, sem
):
    size, members = tau.shape

    def work(rows, part):
        shear = own[0, rows, part] + other[0, rows, part].astype(jnp.float32)
        press = own[1, rows, part] + other[1, rows, part].astype(jnp.float32)
        later = friction(
            stress[rows, part] + section_step * shear,
            normal[rows, part] + section_step * press,
            weight[rows, part],
            unweight[rows, part],
            tau[rows, part],
            coef[0, rows, :],
            coef[1, rows, :],
        )
        second = state_change(later, decay[rows, part], coef[2, rows, :])
        mean_rate[rows, part] = (rate[rows, part] + later) * 0.5
        mean_change[rows, part] = (change[rows, part] + second) * 0.5

    copies = []
    for at, part in enumerate(row_pieces(size, OUT_PIECES)):
        over_pieces(part.start, part.size, members, coef.shape[2], work)
        for kind, (held, out) in enumerate(((mean_rate, rate_out), (mean_change, change_out))):
            copies.append(pltpu.make_async_copy(held.at[part], out.at[part], sem.at[kind, at]))
            copies[-1].start()
    for copy in copies:
        copy.wait()


def on_core(kernel, outs, arrays, scratch=(), flops=0, room=16, far=(), out_far=False):
    vmem, hbm = pl.BlockSpec(memory_space=pltpu.VMEM), pl.BlockSpec(memory_space=pl.ANY)
    arrays = (*(pltpu.with_memory_space_constraint(a, pltpu.HBM) for a in far), *arrays)
    return pl.pallas_call(
        kernel,
        out_shape=outs,
        in_specs=[hbm] * len(far) + [vmem] * (len(arrays) - len(far)),
        out_specs=jax.tree.map(lambda _: hbm if out_far else vmem, outs),
        scratch_shapes=list(scratch),
        compiler_params=pltpu.CompilerParams(vmem_limit_bytes=room * 1024 * 1024),
        cost_estimate=pl.CostEstimate(
            flops=flops, bytes_accessed=sum(a.size * a.dtype.itemsize for a in arrays), transcendentals=0
        ),
    )(*arrays)


def body(
    slip_deficit,
    state_var,
    tau_load,
    sigma_base,
    a_coef,
    b_coef,
    v_basis,
    u_basis,
    dense_blocks,
    block_ranks,
    near_index,
):
    count = lax.axis_size("row")
    size, members = slip_deficit.shape
    kinds, rows, _, rank_count, _ = u_basis.shape
    direct = count in DIRECT_COUNTS
    groups = arrivals(count, direct)
    firsts = [sum(len(group) for group in groups[:at]) for at in range(len(groups))]
    tiles = [-(-len(group) * rank_count // TILE) * TILE for group in groups]
    starts = [sum(tiles[:at]) for at in range(len(groups))]
    room = 16 if direct else 40
    lanes = min(members, 128)
    narrow, wide = jnp.bfloat16, jnp.float32
    swap = [(0, 1), (1, 0)]

    def shaped(*shape, kind=wide):
        return jax.ShapeDtypeStruct(shape, kind)

    full = shaped(size, members)
    v_met, u_met, coef, *powers = on_core(
        functools.partial(prepare_kernel, groups, direct),
        (
            shaped(count, rows, rank_count, size, kind=narrow),
            shaped(rows, kinds * size, sum(tiles), kind=narrow),
            shaped(5, size, lanes),
            full,
            full,
            full,
        ),
        (),
        (
            pltpu.SMEM(block_ranks.shape, jnp.int32),
            pltpu.VMEM(v_basis.shape, narrow),
            pltpu.VMEM(u_basis.shape, narrow),
            *[pltpu.VMEM((1, size), wide)] * 3,
            pltpu.VMEM((size, members), wide),
            pltpu.SemaphoreType.DMA((7,)),
        ),
        room=room,
        far=(
            block_ranks,
            v_basis,
            u_basis,
            sigma_base.reshape(1, size),
            a_coef.reshape(1, size),
            b_coef.reshape(1, size),
            state_var,
        ),
    )

    def add(blocks, at, pick, before, kind):
        held = rows if pick is None else 1
        lead = (rows, kinds) if pick is None else (kinds,)
        return on_core(
            functools.partial(
                sums_kernel, groups[at], direct, firsts[at], starts[at], pick, before is not None
            ),
            shaped(*lead, size, members, kind=kind),
            (near_index, v_met, u_met, dense_blocks, *blocks, *(() if before is None else (before,))),
            (
                pltpu.VMEM((held, tiles[at], members), narrow),
            ),
            2 * held * size * members * rank_count * len(blocks) * 3,
            room,
        )

    def lattice(field_half, beside):
        if direct:
            found = gather_direct(field_half, count)
        else:
            whole = lax.all_gather(field_half, "row", axis=0)
            found = [[whole[r] for r in group] for group in groups]
        found[0][0], beside = lax.optimization_barrier((found[0][0], beside))
        sums, end = None, len(groups) - 1
        for at in range(end):
            sums = add(found[at], at, None, sums, wide)
        other = lax.ppermute(add(found[end], end, 1, sums, narrow), "col", swap)
        return add(found[end], end, 0, sums, wide), other, beside

    slip_half = on_core(
        narrow_kernel,
        shaped(size, members, kind=narrow),
        (),
        (pltpu.VMEM((size, members), wide), pltpu.SemaphoreType.DMA((IN_PIECES,))),
        far=(slip_deficit,),
    )
    own, other, powers = lattice(slip_half, powers)
    rate, rate_half = on_core(
        section_one_kernel,
        (full, shaped(size, members, kind=narrow)),
        (own, other, *powers[:2], tau_load, coef),
        flops=200 * size * members,
    )
    beside = on_core(later_kernel, (full,) * 6, (own, other, state_var, powers[2], rate, coef))
    own, other, (stress, normal, change, *powers) = lattice(rate_half, beside)
    return on_core(
        section_two_kernel,
        (full, full),
        (own, other, *powers, tau_load, coef, stress, normal, rate, change),
        (
            pltpu.VMEM((size, members), wide),
            pltpu.VMEM((size, members), wide),
            pltpu.SemaphoreType.DMA((2, OUT_PIECES)),
        ),
        flops=200 * size * members,
        out_far=True,
    )


def solution(mesh):
    placed = (
        P(("row", "col"), "scen"),
        P(("row", "col"), "scen"),
        P(("row", "col"), "scen"),
        P(("row", "col")),
        P(("row", "col")),
        P(("row", "col")),
        P("row", "col", None, None),
        P(None, "row", "col", None, None),
        P(None, "row", "col", None, None),
        P("row", "col"),
        P("row", "col"),
    )
    return jax.shard_map(
        body,
        mesh=mesh,
        in_specs=placed,
        out_specs=(P(("row", "col"), "scen"), P(("row", "col"), "scen")),
        check_vma=False,
    )
```

```python
import functools

import jax
import jax.numpy as jnp
from jax import lax
from jax.experimental import pallas as pl
from jax.experimental.pallas import tpu as pltpu
from jax.sharding import PartitionSpec as P

NEWTON = 2
DIRECT_COUNTS = (4, 8)
TILE = 128

damping = 0.5
sigma_floor = 0.5
section_step = 0.1


def arrivals(count, direct):
    if not direct:
        cuts = [0, max(count - 4, 0), count]
        return [list(range(first, last)) for first, last in zip(cuts, cuts[1:]) if last > first]
    return [[0, 1, 4, 2, 3], [6, 5, 7]] if count == 8 else [[0, 1], [2, 3]]


def row_met(spot, row, direct):
    return jnp.bitwise_xor(row, spot) if direct else spot


def gather_direct(block, count):
    def swapped(mask, data):
        return lax.ppermute(data, "row", [(row, row ^ mask) for row in range(count)])

    found = {0: block}
    for mask in (4, 1, 2, 3) if count == 8 else (1, 2, 3):
        found[mask] = swapped(mask, block)
    if count == 8:
        for mask in (1, 2, 3):
            found[4 + mask] = swapped(mask, found[4])
    return [[found[mask] for mask in group] for group in arrivals(count, True)]


IN_PIECES = 8
OUT_PIECES = 4


def row_pieces(size, pieces):
    tall = size // pieces
    return [pl.ds(at * tall, tall) for at in range(pieces)]


def narrow_kernel(wide_ref, narrow_ref, held, sem):
    copies = [
        pltpu.make_async_copy(wide_ref.at[part], held.at[part], sem.at[at])
        for at, part in enumerate(row_pieces(held.shape[0], IN_PIECES))
    ]
    for copy in copies:
        copy.start()
    for copy, part in zip(copies, row_pieces(held.shape[0], IN_PIECES)):
        copy.wait()
        narrow_ref[part, :] = held[part, :].astype(narrow_ref.dtype)


def store_powers(outs, part, state, coef):
    outs[0][:, part] = jnp.exp(-state * coef[3])
    outs[1][:, part] = jnp.exp(state * coef[3])
    outs[2][:, part] = jnp.exp(-state * coef[4])


def later_kernel(own, other, state, decay, rate, coef, stress, normal, change, *outs):
    stress[...] = own[0] + other[0].astype(jnp.float32)
    normal[...] = own[1] + other[1].astype(jnp.float32)
    lanes = coef.shape[2]
    for first in range(0, state.shape[1], lanes):
        part = slice(first, first + lanes)
        step = state_change(rate[:, part], decay[:, part], coef[2])
        change[:, part] = step
        store_powers(outs, part, state[:, part] + section_step * step, coef)


def prepare_kernel(groups, direct, *refs):
    far, (v_out, u_out, coef_out, *powers), near, sem = refs[:7], refs[7:13], refs[13:20], refs[20]
    copies = [
        pltpu.make_async_copy(source, held, sem.at[at])
        for at, (source, held) in enumerate(zip(far, near))
    ]
    for copy in copies:
        copy.start()
    for copy in copies:
        copy.wait()
    rank_ref, v_ref, u_ref, sigma_ref, a_ref, b_ref, state_ref = near
    kinds, rows, count, rank_count, size = u_ref.shape
    row = lax.axis_index("row")
    met = [row_met(spot, row, direct) for group in groups for spot in group]
    for at, q in enumerate(met):
        for p in range(rows):
            inside = lax.broadcasted_iota(jnp.int32, (rank_count, size), 0) < rank_ref[p, q]
            v_out[at, p] = jnp.where(inside, v_ref[p, q].astype(jnp.float32), 0.0).astype(v_out.dtype)
    for p in range(rows):
        for kind in range(kinds):
            first = start = 0
            for spots in groups:
                group = [u_ref[kind, p, q] for q in met[first : first + len(spots)]]
                spare = -len(group) * rank_count % TILE
                if spare:
                    group.append(jnp.zeros((spare, size), u_ref.dtype))
                turned = jnp.concatenate(group, axis=0).astype(jnp.float32).T
                stop = start + turned.shape[1]
                u_out[p, kind * size : (kind + 1) * size, start:stop] = turned.astype(u_out.dtype)
                first, start = first + len(spots), stop
    lanes = coef_out.shape[2]
    for at, values in enumerate((sigma_ref[...], a_ref[...], b_ref[...], 1.0 / a_ref[...], 1.0 / b_ref[...])):
        coef_out[at] = jnp.broadcast_to(values, (lanes, size)).T
    for first in range(0, state_ref.shape[1], lanes):
        part = slice(first, first + lanes)
        store_powers(powers, part, state_ref[:, part], coef_out)


def sums_kernel(spots, direct, first, start, pick, before, near_ref, v_ref, u_ref, d_ref, *refs):
    blocks = refs[: len(spots)]
    refs = refs[len(spots) :]
    if before:
        sums_ref, refs = refs[0], refs[1:]
    out_ref, proj = refs
    count, rows, rank_count, size = v_ref.shape
    kinds, slots = d_ref.shape[0], near_ref.shape[1]
    row, col = lax.axis_index("row"), lax.axis_index("col")
    met = [row_met(spot, row, direct) for spot in spots]
    chosen = list(range(rows)) if pick is None else [col if pick == 0 else 1 - col]
    places = [(place,) for place in range(rows)] if pick is None else [()]
    for at, block in enumerate(blocks):
        if pick is None:
            weights = v_ref[first + at].reshape(rows * rank_count, size)
        else:
            weights = v_ref[first + at, chosen[0]]
        part = jnp.dot(weights, block[...], preferred_element_type=jnp.float32).astype(proj.dtype)
        for place in range(len(chosen)):
            proj[place, at * rank_count : (at + 1) * rank_count, :] = part[
                place * rank_count : (place + 1) * rank_count
            ]
    width = proj.shape[1]
    lanes = slice(start, start + width)
    if width > len(blocks) * rank_count:
        for place in range(len(chosen)):
            proj[place, len(blocks) * rank_count :, :] = jnp.zeros(
                (width - len(blocks) * rank_count, proj.shape[2]), proj.dtype
            )
    for place, p in enumerate(chosen):
        weights, fields = [u_ref[p, :, lanes]], [proj[place]]
        for s in range(slots):
            near = near_ref[pl.ds(p, 1), s : s + 1] - col * count
            field = None
            for q, block in zip(met, blocks):
                mask = jnp.where(near == q, 1.0, 0.0).astype(block.dtype)
                part = block[...] * mask
                field = part if field is None else field + part
            weights.append(jnp.concatenate([d_ref[kind, p, s] for kind in range(kinds)], axis=0))
            fields.append(field)
        total = jnp.dot(
            jnp.concatenate(weights, axis=1),
            jnp.concatenate(fields, axis=0),
            preferred_element_type=jnp.float32,
        )
        for kind in range(kinds):
            piece = total[kind * size : (kind + 1) * size]
            if before:
                piece += sums_ref[p, kind]
            out_ref[*places[place], kind] = piece.astype(out_ref.dtype)


def inverse(value):
    rough = pl.reciprocal(value, approx=True)
    return rough * (2.0 - value * rough)


def rough_inverse(value):
    return pl.reciprocal(value, approx=True)


def scaled_sinh_cosh(value, scale):
    grown = jnp.exp(value)
    half = 0.5 * scale
    up, down = half * grown, half * inverse(grown)
    square = value * value
    small = scale * value * (1.0 + square * (1 / 6 + square * (1 / 120)))
    return jnp.where(square < 0.25, small, up - down), up + down


def friction(shear, normal, weight, unweight, tau_load, sigma_base, a_wide):
    tau = tau_load + shear
    size = jnp.abs(tau)
    stiff = jnp.maximum(sigma_base + normal, sigma_floor) * a_wide
    double = 2.0 * damping * weight
    drive = size * unweight * (0.5 / damping)
    square = drive * drive + 1.0
    slope = jnp.minimum(size * rough_inverse(stiff), jnp.log(drive + square * lax.rsqrt(square)))
    for newton_step in range(NEWTON):
        sinh, cosh = scaled_sinh_cosh(slope, double)
        slope = slope - (stiff * slope + sinh - size) * rough_inverse(stiff + cosh)
    rate = scaled_sinh_cosh(slope, double)[0] * (1.0 / damping)
    return jnp.where(tau < 0.0, -rate, rate)


def state_change(rate, decay, b_wide):
    return b_wide * (decay - jnp.abs(rate))


def over_pieces(begin, tall, members, lanes, work):
    step = min(tall, 128)
    for at in range(begin, begin + tall, step):
        for first in range(0, members, lanes):
            work(pl.ds(at, step), slice(first, first + lanes))


def section_one_kernel(own, other, weight, unweight, tau, coef, rate, rate_half):
    size, members = tau.shape

    def work(rows, part):
        first = friction(
            own[0, rows, part] + other[0, rows, part].astype(jnp.float32),
            own[1, rows, part] + other[1, rows, part].astype(jnp.float32),
            weight[rows, part],
            unweight[rows, part],
            tau[rows, part],
            coef[0, rows, :],
            coef[1, rows, :],
        )
        rate[rows, part] = first
        rate_half[rows, part] = first.astype(rate_half.dtype)

    over_pieces(0, size, members, coef.shape[2], work)


def section_two_kernel(
    own, other, weight, unweight, decay, tau, coef, stress, normal, rate, change, rate_out, change_out, mean_rate, mean_change, sem
):
    size, members = tau.shape

    def work(rows, part):
        shear = own[0, rows, part] + other[0, rows, part].astype(jnp.float32)
        press = own[1, rows, part] + other[1, rows, part].astype(jnp.float32)
        later = friction(
            stress[rows, part] + section_step * shear,
            normal[rows, part] + section_step * press,
            weight[rows, part],
            unweight[rows, part],
            tau[rows, part],
            coef[0, rows, :],
            coef[1, rows, :],
        )
        second = state_change(later, decay[rows, part], coef[2, rows, :])
        mean_rate[rows, part] = (rate[rows, part] + later) * 0.5
        mean_change[rows, part] = (change[rows, part] + second) * 0.5

    copies = []
    for at, part in enumerate(row_pieces(size, OUT_PIECES)):
        over_pieces(part.start, part.size, members, coef.shape[2], work)
        for kind, (held, out) in enumerate(((mean_rate, rate_out), (mean_change, change_out))):
            copies.append(pltpu.make_async_copy(held.at[part], out.at[part], sem.at[kind, at]))
            copies[-1].start()
    for copy in copies:
        copy.wait()


def on_core(kernel, outs, arrays, scratch=(), flops=0, room=16, far=(), out_far=False):
    vmem, hbm = pl.BlockSpec(memory_space=pltpu.VMEM), pl.BlockSpec(memory_space=pl.ANY)
    arrays = (*(pltpu.with_memory_space_constraint(a, pltpu.HBM) for a in far), *arrays)
    return pl.pallas_call(
        kernel,
        out_shape=outs,
        in_specs=[hbm] * len(far) + [vmem] * (len(arrays) - len(far)),
        out_specs=jax.tree.map(lambda _: hbm if out_far else vmem, outs),
        scratch_shapes=list(scratch),
        compiler_params=pltpu.CompilerParams(vmem_limit_bytes=room * 1024 * 1024),
        cost_estimate=pl.CostEstimate(
            flops=flops, bytes_accessed=sum(a.size * a.dtype.itemsize for a in arrays), transcendentals=0
        ),
    )(*arrays)


def body(
    slip_deficit,
    state_var,
    tau_load,
    sigma_base,
    a_coef,
    b_coef,
    v_basis,
    u_basis,
    dense_blocks,
    block_ranks,
    near_index,
):
    count = lax.axis_size("row")
    size, members = slip_deficit.shape
    kinds, rows, _, rank_count, _ = u_basis.shape
    direct = count in DIRECT_COUNTS
    groups = arrivals(count, direct)
    firsts = [sum(len(group) for group in groups[:at]) for at in range(len(groups))]
    tiles = [-(-len(group) * rank_count // TILE) * TILE for group in groups]
    starts = [sum(tiles[:at]) for at in range(len(groups))]
    room = 16 if direct else 40
    lanes = min(members, 128)
    narrow, wide = jnp.bfloat16, jnp.float32
    swap = [(0, 1), (1, 0)]

    def shaped(*shape, kind=wide):
        return jax.ShapeDtypeStruct(shape, kind)

    full = shaped(size, members)
    v_met, u_met, coef, *powers = on_core(
        functools.partial(prepare_kernel, groups, direct),
        (
            shaped(count, rows, rank_count, size, kind=narrow),
            shaped(rows, kinds * size, sum(tiles), kind=narrow),
            shaped(5, size, lanes),
            full,
            full,
            full,
        ),
        (),
        (
            pltpu.SMEM(block_ranks.shape, jnp.int32),
            pltpu.VMEM(v_basis.shape, narrow),
            pltpu.VMEM(u_basis.shape, narrow),
            *[pltpu.VMEM((1, size), wide)] * 3,
            pltpu.VMEM((size, members), wide),
            pltpu.SemaphoreType.DMA((7,)),
        ),
        room=room,
        far=(
            block_ranks,
            v_basis,
            u_basis,
            sigma_base.reshape(1, size),
            a_coef.reshape(1, size),
            b_coef.reshape(1, size),
            state_var,
        ),
    )

    def add(blocks, at, pick, before, kind):
        held = rows if pick is None else 1
        lead = (rows, kinds) if pick is None else (kinds,)
        return on_core(
            functools.partial(
                sums_kernel, groups[at], direct, firsts[at], starts[at], pick, before is not None
            ),
            shaped(*lead, size, members, kind=kind),
            (near_index, v_met, u_met, dense_blocks, *blocks, *(() if before is None else (before,))),
            (
                pltpu.VMEM((held, tiles[at], members), narrow),
            ),
            2 * held * size * members * rank_count * len(blocks) * 3,
            room,
        )

    def lattice(field_half, beside):
        if direct:
            found = gather_direct(field_half, count)
        else:
            whole = lax.all_gather(field_half, "row", axis=0)
            found = [[whole[r] for r in group] for group in groups]
        found[0][0], beside = lax.optimization_barrier((found[0][0], beside))
        sums, end = None, len(groups) - 1
        for at in range(end):
            sums = add(found[at], at, None, sums, wide)
        other = lax.ppermute(add(found[end], end, 1, sums, narrow), "col", swap)
        return add(found[end], end, 0, sums, wide), other, beside

    slip_half = on_core(
        narrow_kernel,
        shaped(size, members, kind=narrow),
        (),
        (pltpu.VMEM((size, members), wide), pltpu.SemaphoreType.DMA((IN_PIECES,))),
        far=(slip_deficit,),
    )
    own, other, powers = lattice(slip_half, powers)
    rate, rate_half = on_core(
        section_one_kernel,
        (full, shaped(size, members, kind=narrow)),
        (own, other, *powers[:2], tau_load, coef),
        flops=200 * size * members,
    )
    beside = on_core(later_kernel, (full,) * 6, (own, other, state_var, powers[2], rate, coef))
    own, other, (stress, normal, change, *powers) = lattice(rate_half, beside)
    return on_core(
        section_two_kernel,
        (full, full),
        (own, other, *powers, tau_load, coef, stress, normal, rate, change),
        (
            pltpu.VMEM((size, members), wide),
            pltpu.VMEM((size, members), wide),
            pltpu.SemaphoreType.DMA((2, OUT_PIECES)),
        ),
        flops=200 * size * members,
        out_far=True,
    )


def solution(mesh):
    placed = (
        P(("row", "col"), "scen"),
        P(("row", "col"), "scen"),
        P(("row", "col"), "scen"),
        P(("row", "col")),
        P(("row", "col")),
        P(("row", "col")),
        P("row", "col", None, None),
        P(None, "row", "col", None, None),
        P(None, "row", "col", None, None),
        P("row", "col"),
        P("row", "col"),
    )
    return jax.shard_map(
        body,
        mesh=mesh,
        in_specs=placed,
        out_specs=(P(("row", "col"), "scen"), P(("row", "col"), "scen")),
        check_vma=False,
    )
```
